32 devices in a mesh: groups: 2 (over x), shard: 16 (over z, y, core).
Axes of the slice: x: 2, y: 2, z: 4, core: 2. Of those that a mesh axis runs over, the one named last changes fastest.
Arguments:
- embeddings: bfloat16 [1280, 1024], P(('groups', 'shard')), parts along dimension 0, may hold values from -250 to 250
- probes: int32 [1280, 8], P(('groups', 'shard')), parts along dimension 0, may hold values from 0 to 15, all different within a row; in each aligned block of 40 rows (0 to 39, 40 to 79, ...) at most 40 rows name the same one
- assigned: int32 [1280], P(('groups', 'shard')), parts along dimension 0, may hold values from 0 to 1023
- prior_counts: int32 [32768], P(('groups', 'shard')), parts along dimension 0, may hold values from 1 to 16
- centroids: bfloat16 [32768, 1024], P(('groups', 'shard')), parts along dimension 0, may hold values from -30 to 30
- candidates: int32 [32768, 1], P(('groups', 'shard')), parts along dimension 0, may hold values from 0 to 47; in each aligned block of 1024 rows (0 to 1023, 1024 to 2047, ...) at most 32 rows name the same one
- centroids2: bfloat16 [12288, 1024], P(('groups', 'shard')), parts along dimension 0, may hold values from -30 to 30
Outputs:
- density: float32 [1280], P(('groups', 'shard')), parts along dimension 0
- new_centroids: bfloat16 [32768, 1024], P(('groups', 'shard')), parts along dimension 0
- new_counts: int32 [32768], P(('groups', 'shard')), parts along dimension 0
- level_two: float32 [32768], P(('groups', 'shard')), parts along dimension 0
The draws below stay inside these ranges and needn't reach their ends.
There are 2 independent parts, one for each index of `groups`. The reference program is written for one: setup_inputs(seed, part) draws one part's arguments, and reference() takes and returns one part's arrays. A program takes and returns all parts, laid end to end along the dimension named above; each array names one. Nothing has to cross between parts.
Inputs may be any that keep to these rules, and one draw needn't show every extreme that they name: `probes`: each row names 8 different blocks. Among the 40 embeddings of one device no block is named more than 40 times, and in every draw some block is named exactly 40 times by one device's embeddings. `candidates`: among the 1024 level-1 centroids of one device no level-2 block is named more than 32 times, and in every draw some is named exactly 32 times.
All inputs are finite; a program needn't handle non-finite values.
Results may differ from the reference program's by a relative error of at most 0.0015.
Values may be sent and summed in bfloat16 or wider, within the bound.
No kernel may reach another device: no remote copies, remote signals or barrier semaphores. Data moves between devices by JAX's collectives and lax.ppermute only.
A program may use at most 64 MiB of HBM per device.

```python
import math
import jax
import jax.numpy as jnp
import numpy as np
from jax import lax

D = 1024
BLOCK = 1024
PROBES = 8
BLOCKS_DEV = 1
EMB_DEV = 40
BLOCK2 = 128
BLOCKS = 16
CENTROIDS = 16384
EMBEDS = 640
CAP = 40
BLOCKS2 = 48
CENTROIDS2 = 6144
CAP2 = 32
N_SHARD = 16


def topic_table(key):
    themes = D // 4
    return jax.random.truncated_normal(key, -4.0, 4.0, (themes, D), jnp.float32)


def structured_rows(key, table, rows, strength_lo, strength_hi, scale_lo, scale_hi):
    keys = jax.random.split(key, 4)
    picked = jax.random.randint(keys[0], (rows,), 0, table.shape[0])
    strength = jnp.exp(jax.random.uniform(keys[1], (rows, 1), jnp.float32, math.log(strength_lo), math.log(strength_hi)))
    noise = jax.random.truncated_normal(keys[2], -4.0, 4.0, (rows, D), jnp.float32)
    scale = jnp.exp(jax.random.uniform(keys[3], (rows, 1), jnp.float32, math.log(scale_lo), math.log(scale_hi)))
    return scale * (table[picked] * strength + noise) / jnp.sqrt(1.0 + strength * strength)


def draw_embeddings(key, part):
    table = topic_table(key)
    key = jax.random.fold_in(key, 21)
    value = structured_rows(key, table, EMBEDS, 1.0, 6.0, 1.0, 10.0)
    return value.astype(jnp.bfloat16)


def draw_centroids(key, part):
    table = topic_table(key)
    key = jax.random.fold_in(key, 22)
    value = structured_rows(key, table, CENTROIDS, 0.5, 6.0, 0.5, 5.0)
    return value.astype(jnp.bfloat16)


def draw_centroids2(key, part):
    table = topic_table(key)
    key = jax.random.fold_in(key, 23)
    value = structured_rows(key, table, CENTROIDS2, 0.5, 6.0, 0.5, 5.0)
    return value.astype(jnp.bfloat16)


def place_ends(values, rng, smallest, high):
    spot = [jax.random.randint(jax.random.fold_in(rng, axis), (), 0, length) for axis, length in enumerate(values.shape)]
    widest = values.shape.index(max(values.shape))
    beside = spot[:widest] + [(spot[widest] + 1) % values.shape[widest]] + spot[widest + 1:]
    return values.at[tuple(spot)].set(smallest).at[tuple(beside)].set(high)


def shared_out(key, own, number, rows, amount, top, most, slope):
    ranking = jax.random.permutation(key, amount)
    packed, common = shares(amount, rows * top, most, slope, True), shares(amount, rows * top, most, slope, False)
    places = jnp.arange(amount)

    def named(lengths, offset_by):
        used = int((lengths > 0).sum())
        fixed = max(1, used // 4)
        shifted = fixed + (places - fixed + offset_by * (used - fixed)) % max(1, amount - fixed)
        return jnp.zeros((amount,), jnp.int32).at[ranking[jnp.where(places < fixed, places, shifted)]].set(jnp.asarray(lengths, jnp.int32))

    lengths = jnp.where(number % 4 == 0, named(packed, number // 4), named(common, number - number // 4 - 1))
    mixed = jax.random.permutation(jax.random.fold_in(own, 3), amount)
    giver, sink = mixed[0:amount // 2 * 2:2], mixed[1:amount // 2 * 2:2]
    slack = jnp.minimum(lengths[giver] - 1, most - lengths[sink]) // 2
    slack = jnp.where((giver == ranking[0]) | (sink == ranking[0]) | (lengths[sink] == 0), 0, jnp.maximum(slack, 0))
    shifted = jax.random.randint(jax.random.fold_in(own, 4), (amount // 2,), 0, 1 << 20) % (slack + 1)
    lengths = lengths.at[giver].add(-shifted).at[sink].add(shifted)
    items = jnp.searchsorted(jnp.cumsum(lengths), jnp.arange(rows * top), side="right").astype(jnp.int32)
    grid = items.reshape(top, rows).T
    grid = grid[jax.random.permutation(jax.random.fold_in(own, 1), rows)]
    offset_by = jax.random.randint(jax.random.fold_in(own, 2), (rows, 1), 0, top)
    return jnp.take_along_axis(grid, (jnp.arange(top)[None, :] + offset_by) % top, axis=1)


def shares(amount, total, reach, lean, full):
    weights = [(1 << 20) // math.isqrt(rank ** lean) + 1 for rank in range(1, amount + 1)]
    largest = reach if full else min(reach, max(-(-total // amount), total * weights[0] // sum(weights)))
    least = 1 if total - largest >= amount - 1 else 0
    given, rest = [largest] + [least] * (amount - 1), total - largest - least * (amount - 1)
    while rest > 0:
        movable = [i for i in range(1, amount) if given[i] < largest] or [i for i in range(1, amount) if given[i] < reach]
        whole, left = sum([weights[i] for i in movable]), rest
        for i in movable:
            addition = min(reach - given[i], max(1, left * weights[i] // whole), rest)
            given[i] = given[i] + addition
            rest = rest - addition
    return np.array(given)


def setup_inputs(seed: int = 0, part: int = 0) -> dict:
    key_of = jax.random.split(jax.random.key(seed), 8)
    part_splits = jax.random.split(jax.random.fold_in(key_of[7], part), 8)
    embeddings = draw_embeddings(jax.random.fold_in(jax.random.fold_in(key_of[7], part), 71), part)
    probes_keys = jax.random.split(jax.random.fold_in(part_splits[1], 1), EMBEDS // EMB_DEV)
    probes_turns = jax.random.permutation(jax.random.fold_in(part_splits[1], 3), EMBEDS // EMB_DEV)
    probes = jax.vmap(lambda own, number: shared_out(jax.random.fold_in(part_splits[1], 2), own, number, EMB_DEV, BLOCKS, PROBES, CAP, 2))(probes_keys, probes_turns).reshape((EMBEDS, PROBES))
    assigned = place_ends(jax.random.randint(part_splits[2], (EMBEDS,), 0, BLOCK), jax.random.fold_in(part_splits[2], 1), 0, BLOCK - 1).astype(jnp.int32)
    prior_counts = place_ends(jax.random.randint(part_splits[3], (CENTROIDS,), 1, 17), jax.random.fold_in(part_splits[3], 1), 1, 16).astype(jnp.int32)
    centroids = draw_centroids(jax.random.fold_in(jax.random.fold_in(key_of[7], part), 71), part)
    candidates_keys = jax.random.split(jax.random.fold_in(part_splits[5], 1), CENTROIDS // (BLOCKS_DEV * BLOCK))
    candidates_turns = jax.random.permutation(jax.random.fold_in(part_splits[5], 3), CENTROIDS // (BLOCKS_DEV * BLOCK))
    candidates = jax.vmap(lambda own, number: shared_out(jax.random.fold_in(part_splits[5], 2), own, number, BLOCKS_DEV * BLOCK, BLOCKS2, 1, CAP2, 1))(candidates_keys, candidates_turns).reshape((CENTROIDS, 1))
    centroids2 = draw_centroids2(jax.random.fold_in(jax.random.fold_in(key_of[7], part), 71), part)
    return {"embeddings": embeddings, "probes": probes, "assigned": assigned, "prior_counts": prior_counts, "centroids": centroids, "candidates": candidates, "centroids2": centroids2}


def unit_rows(values):
    wide = values.astype(jnp.float32)
    power = lax.optimization_barrier(jnp.mean(wide * wide, axis=-1, keepdims=True)) + 1e-06
    return (wide * lax.rsqrt(power)).astype(jnp.bfloat16)

def kernel_sums(rows, unit):
    scores = jnp.dot(rows.astype(jnp.float32), unit.astype(jnp.float32).T, precision=lax.Precision.HIGHEST)
    return lax.optimization_barrier(jnp.sum(jnp.exp((scores / rows.shape[1] - 1.0) / 0.1), axis=1))

def block_update(rows, slots, width):
    selector = (slots[:, None] == jnp.arange(width, dtype=jnp.int32)[None, :]).astype(jnp.float32)
    sums = jnp.dot(selector.T, rows.astype(jnp.float32), precision=lax.Precision.HIGHEST)
    counts = lax.optimization_barrier(jnp.sum(selector.astype(jnp.int32), axis=0))
    return (sums, counts)

def reference(embeddings, probes, assigned, prior_counts, centroids, candidates, centroids2):
    width = embeddings.shape[1]
    scaled = unit_rows(embeddings)
    total = EMBEDS * PROBES
    flat = probes.reshape(-1)
    owner = jnp.arange(total, dtype=jnp.int32) // PROBES
    first = jnp.arange(total, dtype=jnp.int32) % PROBES == 0
    limit = N_SHARD * CAP

    def level_one(block):
        found = jnp.nonzero(flat == block, size=limit, fill_value=total)[0].astype(jnp.int32)
        valid = found < total
        clipped = jnp.minimum(found, total - 1).astype(jnp.int32)
        source = owner[clipped]
        rows = scaled[source]
        slots = jnp.where(valid & first[clipped], assigned[source], -1).astype(jnp.int32)
        start = (block * BLOCK).astype(jnp.int32)
        old = lax.dynamic_slice_in_dim(centroids, start, BLOCK, 0)
        prior = lax.dynamic_slice_in_dim(prior_counts, start, BLOCK, 0)
        part = jnp.where(valid, kernel_sums(rows, unit_rows(old)), jnp.float32(0.0))
        sums, counts = block_update(rows, slots, BLOCK)
        fresh = prior + counts
        updated = (prior.astype(jnp.float32)[:, None] * old.astype(jnp.float32) + sums) / fresh.astype(jnp.float32)[:, None]
        return (part, clipped, updated.astype(jnp.bfloat16), fresh, unit_rows(updated))
    parts, places, fresh_rows, fresh_counts, units = lax.map(level_one, jnp.arange(BLOCKS, dtype=jnp.int32))
    slot_sum = jnp.zeros((total,), jnp.float32).at[places.reshape(-1)].add(parts.reshape(-1))
    density = jnp.log(lax.optimization_barrier(jnp.sum(slot_sum.reshape(EMBEDS, PROBES), axis=1)) / (PROBES * BLOCK))
    flat_units = units.reshape(CENTROIDS, width)
    chosen = candidates[:, 0]
    limit_two = N_SHARD * CAP2

    def level_two_block(block):
        found = jnp.nonzero(chosen == block, size=limit_two, fill_value=CENTROIDS)[0].astype(jnp.int32)
        valid = found < CENTROIDS
        clipped = jnp.minimum(found, CENTROIDS - 1).astype(jnp.int32)
        rows = flat_units[clipped]
        start = (block * BLOCK2).astype(jnp.int32)
        other = lax.dynamic_slice_in_dim(centroids2, start, BLOCK2, 0)
        part = jnp.where(valid, kernel_sums(rows, unit_rows(other)), jnp.float32(0.0))
        return (part, clipped)
    parts_two, places_two = lax.map(level_two_block, jnp.arange(BLOCKS2, dtype=jnp.int32))
    sums_two = jnp.zeros((CENTROIDS,), jnp.float32).at[places_two.reshape(-1)].add(parts_two.reshape(-1))
    level_two = jnp.log(sums_two / BLOCK2)
    return (density, fresh_rows.reshape(CENTROIDS, width), fresh_counts.reshape(-1), level_two)
```

```python
import functools

import jax
import jax.numpy as jnp
from jax import lax
from jax.experimental import pallas as pl
from jax.experimental.pallas import tpu as pltpu
from jax.sharding import PartitionSpec as P

BLOCK = 1024
BLOCKS_DEV = 1
BLOCK2 = 128
BLOCKS2_DEV = 3


def unit_rows(values):
    wide = values.astype(jnp.float32)
    power = jnp.mean(wide * wide, axis=-1, keepdims=True) + 1e-06
    return (wide * lax.rsqrt(power)).astype(jnp.bfloat16)


def kernel_sums(rows, unit):
    scores = lax.dot_general(
        rows, unit, (((1,), (1,)), ((), ())), preferred_element_type=jnp.float32
    )
    return jnp.sum(jnp.exp((scores / rows.shape[1] - 1.0) / 0.1), axis=1)


def block_update(rows, slots, width):
    matches = slots[:, None] == jnp.arange(width, dtype=jnp.int32)[None, :]
    sums = lax.dot_general(
        matches.astype(jnp.bfloat16),
        rows,
        (((0,), (0,)), ((), ())),
        preferred_element_type=jnp.float32,
    )
    counts = jnp.sum(matches.astype(jnp.int32), axis=0)
    return (sums, counts)


def slot_ranks(targets, buckets):
    matches = (targets[:, None] == jnp.arange(buckets, dtype=jnp.int32)[None, :]).astype(jnp.int32)
    return jnp.sum(jnp.cumsum(matches, axis=0) * matches, axis=1) - 1


def general_body(embeddings, probes, assigned, prior_counts, centroids, candidates, centroids2):
    devices = lax.axis_size("shard")
    emb_rows, width = embeddings.shape
    probe_count = probes.shape[1]
    capacity = max(2, 2 * emb_rows * probe_count // (BLOCKS_DEV * devices))
    scaled = unit_rows(embeddings)
    units_old = unit_rows(centroids).reshape(BLOCKS_DEV, BLOCK, width)
    total = emb_rows * probe_count
    buckets = BLOCKS_DEV * devices
    flat = probes.reshape(-1)
    place = flat * capacity + slot_ranks(flat, buckets)
    leading = jnp.arange(total, dtype=jnp.int32) % probe_count == 0
    repeated = jnp.repeat(scaled, probe_count, axis=0)
    slot_values = jnp.where(leading, jnp.repeat(assigned, probe_count), -1)
    send_rows = jnp.zeros((buckets * capacity, width), jnp.bfloat16).at[place].set(repeated)
    send_slots = jnp.full((buckets * capacity,), -1, jnp.int32).at[place].set(slot_values)
    got_rows, got_slots = (
        lax.all_to_all(
            send_rows.reshape(devices, BLOCKS_DEV * capacity, width),
            "shard",
            split_axis=0,
            concat_axis=0,
            tiled=True,
        ),
        lax.all_to_all(
            send_slots.reshape(devices, BLOCKS_DEV * capacity),
            "shard",
            split_axis=0,
            concat_axis=0,
            tiled=True,
        ),
    )
    got_rows = got_rows.reshape(devices, BLOCKS_DEV, capacity, width)
    got_slots = got_slots.reshape(devices, BLOCKS_DEV, capacity)
    local = 0
    picked = got_rows[:, local].reshape(devices * capacity, width)
    slots = got_slots[:, local].reshape(-1)
    weights = [kernel_sums(picked, units_old[local]).reshape(devices, capacity)]
    more_sums, more_counts = block_update(picked, slots, BLOCK)
    sum_list = [more_sums]
    count_list = [more_counts]
    sums = jnp.stack(sum_list)
    counts = jnp.stack(count_list)
    returned = lax.all_to_all(
        jnp.stack(weights, axis=1).reshape(devices, BLOCKS_DEV * capacity),
        "shard",
        split_axis=0,
        concat_axis=0,
        tiled=True,
    )
    totals = jnp.sum(returned.reshape(-1)[place].reshape(emb_rows, probe_count), axis=1)
    density = jnp.log(totals / (probe_count * BLOCK))
    prior = prior_counts.reshape(BLOCKS_DEV, BLOCK)
    fresh = prior + counts
    updated = (
        prior.astype(jnp.float32)[:, :, None]
        * centroids.reshape(BLOCKS_DEV, BLOCK, width).astype(jnp.float32)
        + sums
    ) / fresh.astype(jnp.float32)[:, :, None]
    new_centroids = updated.astype(jnp.bfloat16).reshape(BLOCKS_DEV * BLOCK, width)
    units_new = unit_rows(updated).reshape(BLOCKS_DEV * BLOCK, width)
    rows_two = units_new.shape[0]
    second_capacity = max(2, 3 * rows_two // (2 * BLOCKS2_DEV * devices))
    buckets_two = BLOCKS2_DEV * devices
    chosen = candidates[:, 0]
    place_two = chosen * second_capacity + slot_ranks(chosen, buckets_two)
    send_two = (
        jnp.zeros((buckets_two * second_capacity, width), jnp.bfloat16).at[place_two].set(units_new)
    )
    send_two = send_two.reshape(devices, BLOCKS2_DEV, second_capacity, width)
    units_two = unit_rows(centroids2).reshape(BLOCKS2_DEV, BLOCK2, width)
    arrived = lax.all_to_all(send_two, "shard", split_axis=0, concat_axis=0, tiled=True)
    items = arrived.shape[2]
    weights_two = [
        kernel_sums(arrived[:, local].reshape(-1, width), units_two[local]).reshape(
            arrived.shape[0], items
        )
        for local in range(BLOCKS2_DEV)
    ]
    returned_two = lax.all_to_all(
        jnp.stack(weights_two, axis=1), "shard", split_axis=0, concat_axis=0, tiled=True
    )
    level_two = jnp.log(returned_two.reshape(-1)[place_two] / BLOCK2)
    return (density, new_centroids, fresh.reshape(-1), level_two)


NT = (((1,), (1,)), ((), ()))
PARAMS = pltpu.CompilerParams(vmem_limit_bytes=48 * 1024 * 1024)
META = 16


def position():
    me = lax.axis_index("shard")
    return me, me // 4, (me // 2) % 2, me % 2


def unit_wide(wide):
    power = jnp.mean(wide * wide, axis=-1, keepdims=True) + 1e-06
    return (wide * lax.rsqrt(power)).astype(jnp.bfloat16)


def weights(scores, width):
    return jnp.exp(scores * (10.0 / width) - 10.0)


def one_hot(hits):
    return jnp.where(hits, 1.0, 0.0).astype(jnp.bfloat16)


def column(row):
    return jnp.transpose(jnp.broadcast_to(row, (8, row.shape[1])))[:, 0:1]


def pack_kernel(cap, per, cand_ref, prior_ref, cent_ref, far_own, far1, far2, far3, main1, main2, main3, info):
    me, z, y, core = position()
    cand = cand_ref[...]
    rows = cand.shape[1]
    buckets = 16 * per
    dev = sum((cand >= per * step).astype(jnp.int32) for step in range(1, 16))
    near = dev >> 2
    plane = jnp.where(z >= 2, 3 - near, near)
    rel = (((dev >> 1) & 1) ^ y) * 2 + ((dev & 1) ^ core)
    named = cand == lax.broadcasted_iota(jnp.int32, (buckets, rows), 0)
    before = lax.broadcasted_iota(jnp.int32, (rows, rows), 0) <= lax.broadcasted_iota(jnp.int32, (rows, rows), 1)
    counted = jnp.dot(one_hot(named), one_hot(before), preferred_element_type=jnp.float32)
    rank = jnp.sum(jnp.where(named, counted, 0.0), axis=0, keepdims=True).astype(jnp.int32) - 1
    kind = plane * per + cand - dev * per
    unit_slot = (cand - dev * per) * cap + rank
    part = per * cap
    slot_far = jnp.where(plane == 3, rel * part + unit_slot, -1)
    slot_main = jnp.where(plane < 3, rel * 3 * part + plane * part + unit_slot, -1)
    info[0:1, :] = slot_main
    info[1:2, :] = kind
    info[2:3, :] = rel * cap + rank
    ident = lax.broadcasted_iota(jnp.int32, (1, rows), 1) + 1
    line = lax.broadcasted_iota(jnp.int32, (META, rows), 0)
    cent = cent_ref[...]
    for r, (far, main) in enumerate(((far_own, None), (far1, main1), (far2, main2), (far3, main3))):
        facts = jnp.where(line == 4 * r + 1, ident & 31, jnp.where(line == 4 * r + 2, prior_ref[...], 0))
        facts = jnp.where(line == 4 * r, ident >> 5, facts).astype(jnp.float32).astype(jnp.bfloat16)
        far[part : part + META, :] = jnp.zeros((META, cent.shape[1]), jnp.bfloat16)
        pick = one_hot(slot_far == lax.broadcasted_iota(jnp.int32, (part, rows), 0) + r * part)
        far[0:part, :] = jnp.dot(pick, cent, preferred_element_type=jnp.float32).astype(jnp.bfloat16)
        far[part : part + META, 0:part] = lax.dot_general(
            facts, pick, NT, preferred_element_type=jnp.float32
        ).astype(jnp.bfloat16)
        if main is not None:
            pick = one_hot(slot_main == lax.broadcasted_iota(jnp.int32, (3 * part, rows), 0) + r * 3 * part)
            main[...] = jnp.dot(pick, cent, preferred_element_type=jnp.float32).astype(jnp.bfloat16)
            far[part : part + META, 128 : 128 + 3 * part] = lax.dot_general(
                facts, pick, NT, preferred_element_type=jnp.float32
            ).astype(jnp.bfloat16)


def first_kernel(part, emb_ref, aux_ref, cent_ref, prior_ref, info, scaled, share, fresh_rows, fresh_counts, own_main, units):
    me, z, y, core = position()
    count, width = emb_ref.shape
    probe_count = 8
    rows = cent_ref.shape[0]
    scaled[...] = unit_wide(emb_ref[...].astype(jnp.float32))
    probes = aux_ref[0:probe_count, :]
    target = jnp.where(probes[0:1, :] == me, aux_ref[probe_count : probe_count + 1, :], -1)
    member = jnp.sum((probes == me).astype(jnp.float32), axis=0, keepdims=True)
    prior = column(prior_ref[...].astype(jnp.float32))
    step = 256
    total = jnp.zeros((1, count), jnp.float32)
    for start in range(0, rows, step):
        old = cent_ref[start : start + step, :].astype(jnp.float32)
        scores = lax.dot_general(unit_wide(old), scaled[...], NT, preferred_element_type=jnp.float32)
        total = total + jnp.sum(weights(scores, width), axis=0, keepdims=True)
        hits = one_hot(target == lax.broadcasted_iota(jnp.int32, (step, count), 0) + start)
        sums = jnp.dot(hits, scaled[...], preferred_element_type=jnp.float32)
        gained = jnp.sum(hits.astype(jnp.float32), axis=1, keepdims=True)
        ahead = prior[start : start + step, :]
        updated = (ahead * old + sums) / (ahead + gained)
        fresh_rows[start : start + step, :] = updated.astype(jnp.bfloat16)
        units[start : start + step, :] = unit_wide(updated)
        gained_row = lax.dot_general(
            jnp.ones((8, count), jnp.bfloat16), hits, NT, preferred_element_type=jnp.float32
        )
        fresh_counts[0:1, start : start + step] = prior_ref[0:1, start : start + step] + gained_row[0:1, :].astype(jnp.int32)
    share[...] = jnp.where(member > 0.0, total, 0.0)
    pick = one_hot(info[0:1, :] == lax.broadcasted_iota(jnp.int32, (3 * part, rows), 0))
    own_main[...] = jnp.dot(pick, units[...], preferred_element_type=jnp.float32).astype(jnp.bfloat16)


def forward_kernel(part, far0, far1, far2, far3, block, out):
    me, z, y, core = position()
    end = (z == 0) | (z == 3)

    @pl.when(end)
    def _():
        facts = jnp.zeros((META, out.shape[1]), jnp.float32)
        for r, far in enumerate((far0, far1, far2, far3)):
            out[r * part : (r + 1) * part, :] = far[0:part, :]
            facts = facts + far[part : part + META, :].astype(jnp.float32)
        out[4 * part : 4 * part + META, :] = facts.astype(jnp.bfloat16)

    @pl.when(jnp.logical_not(end))
    def _():
        out[0 : 4 * part, :] = block[...]
        out[4 * part : 4 * part + META, :] = jnp.zeros((META, out.shape[1]), jnp.bfloat16)


def second_kernel(
    cap, per, scaled, aux_ref, own_main, far0, far1, far2, far3, main1, main2, main3,
    own_set, near_set, cross_set, passed, last_set, out, packed, two,
):
    me, z, y, core = position()
    end = (z == 0) | (z == 3)
    part = per * cap
    block = own_set.shape[0] // per
    width = own_set.shape[1]
    probe0 = aux_ref[0:1, :]
    slots = aux_ref[8:9, :]

    def place(w, r, rows):
        for j in range(per):
            packed[w, j, r * cap : (r + 1) * cap, :] = rows[j * cap : (j + 1) * cap, :]

    def corrected(raw, facts, source):
        facts = jnp.transpose(facts)
        ident = (facts[:, 0:1] * 32.0 + facts[:, 1:2]).astype(jnp.int32)
        ahead = facts[:, 2:3]
        hits = one_hot(ident == jnp.where(probe0 == source, slots + 1, -1))
        sums = jnp.dot(hits, scaled[...], preferred_element_type=jnp.float32)
        gained = jnp.sum(hits.astype(jnp.float32), axis=1, keepdims=True)
        updated = (ahead * raw.astype(jnp.float32) + sums) / jnp.maximum(ahead + gained, 1.0)
        return unit_wide(updated)

    def facts_of(ref, row, r, first):
        lines = ref[row : row + META, :].astype(jnp.float32)
        return lines[4 * r : 4 * r + 4, first : first + part]

    for w in range(3):
        place(w, 0, own_main[w * part : (w + 1) * part, :])
    for r, (far, main) in enumerate(((far0, None), (far1, main1), (far2, main2), (far3, main3))):
        source = me ^ r
        place(3, r, corrected(far[0:part, :], facts_of(far, part, r, 0), source))
        if main is not None:
            for w in range(3):
                place(w, r, corrected(main[w * part : (w + 1) * part, :], facts_of(far, part, r, 128 + w * part), source))
        place(4, r, corrected(passed[r * part : (r + 1) * part, :], facts_of(passed, 4 * part, r, 0), me ^ 4 ^ r))
    two[0] = unit_wide(jnp.where(end, own_set[...], near_set[...]).astype(jnp.float32))
    two[1] = unit_wide(jnp.where(end, near_set[...], own_set[...]).astype(jnp.float32))
    two[2] = unit_wide(jnp.where(end, passed[0 : 4 * part, :], cross_set[...]).astype(jnp.float32))
    two[3] = unit_wide(last_set[...].astype(jnp.float32))
    for w in range(5):
        for j in range(per):
            scores = lax.dot_general(
                two[min(w, 3), j * block : (j + 1) * block, :], packed[w, j], NT, preferred_element_type=jnp.float32
            )
            out[w * per + j : w * per + j + 1, :] = jnp.sum(weights(scores, width), axis=0, keepdims=True)


def last_kernel(cap, per, block, info, res0, res1, res2, res3, up0, up1, up2, up3, out):
    me, z, y, core = position()
    end = (z == 0) | (z == 3)
    lane = lax.broadcasted_iota(jnp.int32, (16, 4 * cap), 1) // cap
    line = lax.broadcasted_iota(jnp.int32, (16, 4 * cap), 0)
    values = jnp.zeros((16, 4 * cap), jnp.float32)
    for r, (res, up) in enumerate(((res0, up0), (res1, up1), (res2, up2), (res3, up3))):
        here = res[...]
        there = jnp.concatenate([here[0 : 3 * per], up[4 * per : 5 * per], here[4 * per :]], axis=0)
        values = jnp.where((lane == r) & (line < 4 * per), jnp.where(end, there, here), values)
    rows = info.shape[1]
    chosen = jnp.where(info[2:3, :] == lax.broadcasted_iota(jnp.int32, (4 * cap, rows), 0), 1.0, 0.0)
    spread = jnp.dot(values, chosen, precision=lax.Precision.HIGHEST, preferred_element_type=jnp.float32)
    found = jnp.where(info[1:2, :] == lax.broadcasted_iota(jnp.int32, (16, rows), 0), spread, 0.0)
    out[...] = jnp.log(jnp.sum(found, axis=0, keepdims=True) / block)


def call(kernel, outs, scratch=(), **kw):
    return pl.pallas_call(
        kernel,
        out_shape=outs,
        scratch_shapes=list(scratch),
        compiler_params=PARAMS,
        **kw,
    )


def line_body(embeddings, probes, assigned, prior_counts, centroids, candidates, centroids2):
    emb_rows, width = embeddings.shape
    probe_count = probes.shape[1]
    rows = centroids.shape[0]
    per = BLOCKS2_DEV
    cap = max(2, 3 * rows // (2 * per * 16))
    part = per * cap
    bf16, f32, i32 = jnp.bfloat16, jnp.float32, jnp.int32
    shape = jax.ShapeDtypeStruct

    def exchange(value, pairs):
        return lax.ppermute(value, "shard", pairs)

    near = [(i, i ^ 4) for i in range(16)]
    cross = [(i, 12 - 4 * (i // 4) + i % 4) for i in range(4, 12)]
    near_set = exchange(centroids2, near)
    cross_set = exchange(centroids2, cross)
    everyone = lax.all_gather(embeddings, "shard", axis=0, tiled=True)
    aux = jnp.concatenate(
        [probes.T, assigned[None, :], jnp.zeros((16 - probe_count - 1, emb_rows), i32)], axis=0
    )
    aux = lax.all_gather(aux, "shard", axis=0)
    aux = jnp.transpose(aux, (1, 0, 2)).reshape(16, 16 * emb_rows)
    cand_row = candidates.reshape(1, rows)
    prior_row = prior_counts.reshape(1, rows)
    far = shape((part + META, width), bf16)
    main = shape((3 * part, width), bf16)
    far0, far1, far2, far3, main1, main2, main3, info = call(
        functools.partial(pack_kernel, cap, per),
        (far, far, far, far, main, main, main, shape((8, rows), i32)),
    )(cand_row, prior_row, centroids)

    def beside(r):
        return [(i, i ^ r) for i in range(16)]

    far1, far2, far3 = (exchange(value, beside(r)) for r, value in ((1, far1), (2, far2), (3, far3)))
    main1, main2, main3 = (exchange(value, beside(r)) for r, value in ((1, main1), (2, main2), (3, main3)))
    last_set = exchange(near_set, cross)
    passing = call(functools.partial(forward_kernel, part), shape((4 * part + META, width), bf16))(
        far0, far1, far2, far3, cross_set
    )
    passed = exchange(passing, near)
    scaled, share, new_centroids, counts, own_main = call(
        functools.partial(first_kernel, part),
        (
            shape((16 * emb_rows, width), bf16),
            shape((1, 16 * emb_rows), f32),
            shape((rows, width), bf16),
            shape((1, rows), i32),
            main,
        ),
        [pltpu.VMEM((rows, width), bf16)],
    )(everyone, aux, centroids, prior_row, info)
    totals = lax.psum_scatter(share.reshape(-1), "shard", scatter_dimension=0, tiled=True)
    density = jnp.log(totals / (probe_count * BLOCK))
    result = call(
        functools.partial(second_kernel, cap, per),
        shape((16, 4 * cap), f32),
        [pltpu.VMEM((5, per, 4 * cap, width), bf16), pltpu.VMEM((4, per * BLOCK2, width), bf16)],
    )(
        scaled, aux, own_main, far0, far1, far2, far3, main1, main2, main3,
        centroids2, near_set, cross_set, passed, last_set,
    )
    beside_results = [result] + [exchange(result, beside(r)) for r in (1, 2, 3)]
    passed_results = [exchange(result, [(i, i ^ 4 ^ r) for i in range(4, 12)]) for r in range(4)]
    level_two = call(functools.partial(last_kernel, cap, per, BLOCK2), shape((1, rows), f32))(
        info, *beside_results, *passed_results
    )
    return (density, new_centroids, counts.reshape(-1), level_two.reshape(-1))


def solution(mesh):
    placed = (
        P(("groups", "shard"), None),
        P(("groups", "shard"), None),
        P(("groups", "shard")),
        P(("groups", "shard")),
        P(("groups", "shard"), None),
        P(("groups", "shard"), None),
        P(("groups", "shard"), None),
    )
    body = line_body if mesh.shape["shard"] == 16 else general_body
    return jax.shard_map(
        body,
        mesh=mesh,
        in_specs=placed,
        out_specs=(
            P(("groups", "shard")),
            P(("groups", "shard"), None),
            P(("groups", "shard")),
            P(("groups", "shard")),
        ),
        check_vma=False,
    )
```

```python
import functools

import jax
import jax.numpy as jnp
from jax import lax
from jax.experimental import pallas as pl
from jax.experimental.pallas import tpu as pltpu
from jax.sharding import PartitionSpec as P

BLOCK = 1024
BLOCKS_DEV = 1
BLOCK2 = 128
BLOCKS2_DEV = 3


def unit_rows(values):
    wide = values.astype(jnp.float32)
    power = jnp.mean(wide * wide, axis=-1, keepdims=True) + 1e-06
    return (wide * lax.rsqrt(power)).astype(jnp.bfloat16)


def kernel_sums(rows, unit):
    scores = lax.dot_general(
        rows, unit, (((1,), (1,)), ((), ())), preferred_element_type=jnp.float32
    )
    return jnp.sum(jnp.exp((scores / rows.shape[1] - 1.0) / 0.1), axis=1)


def block_update(rows, slots, width):
    matches = slots[:, None] == jnp.arange(width, dtype=jnp.int32)[None, :]
    sums = lax.dot_general(
        matches.astype(jnp.bfloat16),
        rows,
        (((0,), (0,)), ((), ())),
        preferred_element_type=jnp.float32,
    )
    counts = jnp.sum(matches.astype(jnp.int32), axis=0)
    return (sums, counts)


def slot_ranks(targets, buckets):
    matches = (targets[:, None] == jnp.arange(buckets, dtype=jnp.int32)[None, :]).astype(jnp.int32)
    return jnp.sum(jnp.cumsum(matches, axis=0) * matches, axis=1) - 1


def general_body(embeddings, probes, assigned, prior_counts, centroids, candidates, centroids2):
    devices = lax.axis_size("shard")
    emb_rows, width = embeddings.shape
    probe_count = probes.shape[1]
    capacity = max(2, 2 * emb_rows * probe_count // (BLOCKS_DEV * devices))
    scaled = unit_rows(embeddings)
    units_old = unit_rows(centroids).reshape(BLOCKS_DEV, BLOCK, width)
    total = emb_rows * probe_count
    buckets = BLOCKS_DEV * devices
    flat = probes.reshape(-1)
    place = flat * capacity + slot_ranks(flat, buckets)
    leading = jnp.arange(total, dtype=jnp.int32) % probe_count == 0
    repeated = jnp.repeat(scaled, probe_count, axis=0)
    slot_values = jnp.where(leading, jnp.repeat(assigned, probe_count), -1)
    send_rows = jnp.zeros((buckets * capacity, width), jnp.bfloat16).at[place].set(repeated)
    send_slots = jnp.full((buckets * capacity,), -1, jnp.int32).at[place].set(slot_values)
    got_rows, got_slots = (
        lax.all_to_all(
            send_rows.reshape(devices, BLOCKS_DEV * capacity, width),
            "shard",
            split_axis=0,
            concat_axis=0,
            tiled=True,
        ),
        lax.all_to_all(
            send_slots.reshape(devices, BLOCKS_DEV * capacity),
            "shard",
            split_axis=0,
            concat_axis=0,
            tiled=True,
        ),
    )
    got_rows = got_rows.reshape(devices, BLOCKS_DEV, capacity, width)
    got_slots = got_slots.reshape(devices, BLOCKS_DEV, capacity)
    local = 0
    picked = got_rows[:, local].reshape(devices * capacity, width)
    slots = got_slots[:, local].reshape(-1)
    weights = [kernel_sums(picked, units_old[local]).reshape(devices, capacity)]
    more_sums, more_counts = block_update(picked, slots, BLOCK)
    sum_list = [more_sums]
    count_list = [more_counts]
    sums = jnp.stack(sum_list)
    counts = jnp.stack(count_list)
    returned = lax.all_to_all(
        jnp.stack(weights, axis=1).reshape(devices, BLOCKS_DEV * capacity),
        "shard",
        split_axis=0,
        concat_axis=0,
        tiled=True,
    )
    totals = jnp.sum(returned.reshape(-1)[place].reshape(emb_rows, probe_count), axis=1)
    density = jnp.log(totals / (probe_count * BLOCK))
    prior = prior_counts.reshape(BLOCKS_DEV, BLOCK)
    fresh = prior + counts
    updated = (
        prior.astype(jnp.float32)[:, :, None]
        * centroids.reshape(BLOCKS_DEV, BLOCK, width).astype(jnp.float32)
        + sums
    ) / fresh.astype(jnp.float32)[:, :, None]
    new_centroids = updated.astype(jnp.bfloat16).reshape(BLOCKS_DEV * BLOCK, width)
    units_new = unit_rows(updated).reshape(BLOCKS_DEV * BLOCK, width)
    rows_two = units_new.shape[0]
    second_capacity = max(2, 3 * rows_two // (2 * BLOCKS2_DEV * devices))
    buckets_two = BLOCKS2_DEV * devices
    chosen = candidates[:, 0]
    place_two = chosen * second_capacity + slot_ranks(chosen, buckets_two)
    send_two = (
        jnp.zeros((buckets_two * second_capacity, width), jnp.bfloat16).at[place_two].set(units_new)
    )
    send_two = send_two.reshape(devices, BLOCKS2_DEV, second_capacity, width)
    units_two = unit_rows(centroids2).reshape(BLOCKS2_DEV, BLOCK2, width)
    arrived = lax.all_to_all(send_two, "shard", split_axis=0, concat_axis=0, tiled=True)
    items = arrived.shape[2]
    weights_two = [
        kernel_sums(arrived[:, local].reshape(-1, width), units_two[local]).reshape(
            arrived.shape[0], items
        )
        for local in range(BLOCKS2_DEV)
    ]
    returned_two = lax.all_to_all(
        jnp.stack(weights_two, axis=1), "shard", split_axis=0, concat_axis=0, tiled=True
    )
    level_two = jnp.log(returned_two.reshape(-1)[place_two] / BLOCK2)
    return (density, new_centroids, fresh.reshape(-1), level_two)


NT = (((1,), (1,)), ((), ()))
PARAMS = pltpu.CompilerParams(vmem_limit_bytes=48 * 1024 * 1024)
META = 16


def position():
    me = lax.axis_index("shard")
    return me, me // 4, (me // 2) % 2, me % 2


def unit_wide(wide):
    power = jnp.mean(wide * wide, axis=-1, keepdims=True) + 1e-06
    return (wide * lax.rsqrt(power)).astype(jnp.bfloat16)


def weights(scores, width):
    return jnp.exp(scores * (10.0 / width) - 10.0)


def one_hot(hits):
    return jnp.where(hits, 1.0, 0.0).astype(jnp.bfloat16)


def column(row):
    return jnp.transpose(jnp.broadcast_to(row, (8, row.shape[1])))[:, 0:1]


def pack_kernel(cap, per, cand_ref, prior_ref, cent_ref, far_own, far1, far2, far3, main1, main2, main3, info):
    me, z, y, core = position()
    cand = cand_ref[...]
    rows = cand.shape[1]
    buckets = 16 * per
    dev = sum((cand >= per * step).astype(jnp.int32) for step in range(1, 16))
    near = dev >> 2
    plane = jnp.where(z >= 2, 3 - near, near)
    rel = (((dev >> 1) & 1) ^ y) * 2 + ((dev & 1) ^ core)
    named = cand == lax.broadcasted_iota(jnp.int32, (buckets, rows), 0)
    before = lax.broadcasted_iota(jnp.int32, (rows, rows), 0) <= lax.broadcasted_iota(jnp.int32, (rows, rows), 1)
    counted = jnp.dot(one_hot(named), one_hot(before), preferred_element_type=jnp.float32)
    rank = jnp.sum(jnp.where(named, counted, 0.0), axis=0, keepdims=True).astype(jnp.int32) - 1
    kind = plane * per + cand - dev * per
    unit_slot = (cand - dev * per) * cap + rank
    part = per * cap
    slot_far = jnp.where(plane == 3, rel * part + unit_slot, -1)
    slot_main = jnp.where(plane < 3, rel * 3 * part + plane * part + unit_slot, -1)
    info[0:1, :] = slot_main
    kind = jnp.where((plane == 3) & ((z == 0) | (z == 3)), kind + per, kind)
    info[1:2, :] = rel * 4 + (kind >> 2)
    info[2:3, :] = (kind & 3) * cap + rank
    ident = lax.broadcasted_iota(jnp.int32, (1, rows), 1) + 1
    line = lax.broadcasted_iota(jnp.int32, (META, rows), 0)
    cent = cent_ref[...]
    for r, (far, main) in enumerate(((far_own, None), (far1, main1), (far2, main2), (far3, main3))):
        facts = jnp.where(line == 4 * r + 1, ident & 31, jnp.where(line == 4 * r + 2, prior_ref[...], 0))
        facts = jnp.where(line == 4 * r, ident >> 5, facts).astype(jnp.float32).astype(jnp.bfloat16)
        far[part : part + META, :] = jnp.zeros((META, cent.shape[1]), jnp.bfloat16)
        pick = one_hot(slot_far == lax.broadcasted_iota(jnp.int32, (part, rows), 0) + r * part)
        far[0:part, :] = jnp.dot(pick, cent, preferred_element_type=jnp.float32).astype(jnp.bfloat16)
        far[part : part + META, 0:part] = lax.dot_general(
            facts, pick, NT, preferred_element_type=jnp.float32
        ).astype(jnp.bfloat16)
        if main is not None:
            pick = one_hot(slot_main == lax.broadcasted_iota(jnp.int32, (3 * part, rows), 0) + r * 3 * part)
            main[...] = jnp.dot(pick, cent, preferred_element_type=jnp.float32).astype(jnp.bfloat16)
            far[part : part + META, 128 : 128 + 3 * part] = lax.dot_general(
                facts, pick, NT, preferred_element_type=jnp.float32
            ).astype(jnp.bfloat16)


def first_kernel(part, mine_ref, other_ref, cent_ref, prior_ref, info, scaled, facts, share, fresh_rows, fresh_counts, own_main, units):
    me, z, y, core = position()
    half = mine_ref.shape[0]
    count = 2 * half
    rows, width = cent_ref.shape
    scaled[0:half, :] = unit_wide(mine_ref[:, 0:width].astype(jnp.float32))
    scaled[half:count, :] = unit_wide(other_ref[:, 0:width].astype(jnp.float32))
    aux = jnp.concatenate([mine_ref[:, width:], other_ref[:, width:]], axis=0).astype(jnp.float32)
    aux = jnp.transpose(aux)[0:16, :].astype(jnp.int32)
    facts[...] = aux
    target = jnp.where(aux[0:1, :] == me, aux[8:9, :] * 32 + aux[9:10, :], -1)
    member = jnp.sum((aux[0:8, :] == me).astype(jnp.float32), axis=0, keepdims=True)
    prior = column(prior_ref[...].astype(jnp.float32))
    step = 256
    total = jnp.zeros((1, count), jnp.float32)
    for start in range(0, rows, step):
        old = cent_ref[start : start + step, :].astype(jnp.float32)
        scores = lax.dot_general(unit_wide(old), scaled[...], NT, preferred_element_type=jnp.float32)
        total = total + jnp.sum(weights(scores, width), axis=0, keepdims=True)
        hits = one_hot(target == lax.broadcasted_iota(jnp.int32, (step, count), 0) + start)
        sums = jnp.dot(hits, scaled[...], preferred_element_type=jnp.float32)
        gained = jnp.sum(hits.astype(jnp.float32), axis=1, keepdims=True)
        ahead = prior[start : start + step, :]
        updated = (ahead * old + sums) / (ahead + gained)
        fresh_rows[start : start + step, :] = updated.astype(jnp.bfloat16)
        units[start : start + step, :] = unit_wide(updated)
        gained_row = lax.dot_general(
            jnp.ones((8, count), jnp.bfloat16), hits, NT, preferred_element_type=jnp.float32
        )
        fresh_counts[0:1, start : start + step] = prior_ref[0:1, start : start + step] + gained_row[0:1, :].astype(jnp.int32)
    piece = count // 16
    lane = lax.broadcasted_iota(jnp.int32, (16, count), 1)
    line = lax.broadcasted_iota(jnp.int32, (16, count), 0)
    apart = jnp.where((member > 0.0) & (lane >= line * piece) & (lane < (line + 1) * piece), total, 0.0)
    spot = lax.broadcasted_iota(jnp.int32, (count, 128), 0)
    block = sum((spot >= piece * step).astype(jnp.int32) for step in range(1, 16))
    together = jnp.where(spot - block * piece == lax.broadcasted_iota(jnp.int32, (count, 128), 1), 1.0, 0.0)
    share[...] = jnp.dot(apart, together, precision=lax.Precision.HIGHEST, preferred_element_type=jnp.float32)
    pick = one_hot(info[0:1, :] == lax.broadcasted_iota(jnp.int32, (3 * part, rows), 0))
    own_main[...] = jnp.dot(pick, units[...], preferred_element_type=jnp.float32).astype(jnp.bfloat16)


def second_kernel(
    cap, per, scaled, facts_in, share, own_main, far0, far1, far2, far3, main1, main2, main3, up0, up1, up2, up3,
    own_set, near_set, cross_set, passed, last_set, out, packed, two,
):
    me, z, y, core = position()
    end = (z == 0) | (z == 3)
    part = per * cap
    block = own_set.shape[0] // per
    width = own_set.shape[1]
    probe0 = facts_in[0:1, :]
    slots = facts_in[8:9, :] * 32 + facts_in[9:10, :]

    def place(w, r, rows):
        for j in range(per):
            packed[w, j, r * cap : (r + 1) * cap, :] = rows[j * cap : (j + 1) * cap, :]

    def corrected(raw, facts, source):
        facts = jnp.transpose(facts)
        ident = (facts[:, 0:1] * 32.0 + facts[:, 1:2]).astype(jnp.int32)
        ahead = facts[:, 2:3]
        hits = one_hot(ident == jnp.where(probe0 == source, slots + 1, -1))
        sums = jnp.dot(hits, scaled[...], preferred_element_type=jnp.float32)
        gained = jnp.sum(hits.astype(jnp.float32), axis=1, keepdims=True)
        updated = (ahead * raw.astype(jnp.float32) + sums) / jnp.maximum(ahead + gained, 1.0)
        return unit_wide(updated)

    def facts_of(ref, r, first):
        lines = ref[part : part + META, :].astype(jnp.float32)
        return lines[4 * r : 4 * r + 4, first : first + part]

    for w in range(3):
        place(w, 0, own_main[w * part : (w + 1) * part, :])
    rows_of = ((far0, None, up0), (far1, main1, up1), (far2, main2, up2), (far3, main3, up3))
    for r, (far, main, up) in enumerate(rows_of):
        if main is not None:
            for w in range(3):
                place(w, r, corrected(main[w * part : (w + 1) * part, :], facts_of(far, r, 128 + w * part), me ^ r))

    @pl.when(jnp.logical_not(end))
    def _():
        for r, (far, main, up) in enumerate(rows_of):
            place(3, r, corrected(far[0:part, :], facts_of(far, r, 0), me ^ r))
            place(4, r, corrected(up[0:part, :], facts_of(up, r, 0), me ^ 4 ^ r))

    two[0] = unit_wide(jnp.where(end, own_set[...], near_set[...]).astype(jnp.float32))
    two[1] = unit_wide(jnp.where(end, near_set[...], own_set[...]).astype(jnp.float32))
    two[2] = unit_wide(jnp.where(end, passed[...], cross_set[...]).astype(jnp.float32))
    two[3] = unit_wide(last_set[...].astype(jnp.float32))
    lines = []
    for w in range(5):
        for j in range(per):
            scores = lax.dot_general(
                two[min(w, 3), j * block : (j + 1) * block, :], packed[w, j], NT, preferred_element_type=jnp.float32
            )
            line = jnp.sum(weights(scores, width), axis=0, keepdims=True)
            lines.append(line if w < 3 else jnp.where(end, 0.0, line))
    lines.append(jnp.zeros((1, 4 * cap), jnp.float32))
    sums = jnp.concatenate(lines, axis=0)
    lane = lax.broadcasted_iota(jnp.int32, sums.shape, 1)
    line = lax.broadcasted_iota(jnp.int32, sums.shape, 0)
    out[...] = jnp.zeros(out.shape, jnp.float32)
    for r in range(4):
        spread = jnp.zeros_like(sums)
        for s in range(4):
            turned = sums if s == r else pltpu.roll(sums, ((s - r) % 4) * cap, 1)
            spread = jnp.where((line % 4 == s) & (lane >= s * cap) & (lane < (s + 1) * cap), turned, spread)
        tile = jnp.concatenate(
            [jnp.sum(spread[4 * t : 4 * t + 4], axis=0, keepdims=True) for t in range(4)], axis=0
        )
        out[me ^ r, 0:4, :] = tile
        out[me ^ 4 ^ r, 0:4, :] = tile
    for b in range(16):
        apart = (b >> 3) | ((b >> 1) & 2) | ((b & 3) << 2)
        out[me ^ apart, 4:5, :] = share[b : b + 1, :]


def last_kernel(cap, scale_one, scale_two, info, got, density, level_two):
    me, z, y, core = position()
    end = (z == 0) | (z == 3)
    pieces = []
    total = jnp.zeros((1, 4 * cap), jnp.float32)
    for source in range(16):
        total = total + got[source, 4:5, :]
    density[...] = jnp.log(total[:, 0 : density.shape[1]] / scale_one)
    for r in range(4):
        here = got[me ^ r]
        there = got[me ^ 4 ^ r]
        pieces.append(here[0:3])
        pieces.append(jnp.where(end, there[3:4], here[3:4]))
    values = jnp.concatenate(pieces, axis=0)
    rows = info.shape[1]
    chosen = jnp.where(info[2:3, :] == lax.broadcasted_iota(jnp.int32, (4 * cap, rows), 0), 1.0, 0.0)
    spread = jnp.dot(values, chosen, precision=lax.Precision.HIGHEST, preferred_element_type=jnp.float32)
    found = jnp.where(info[1:2, :] == lax.broadcasted_iota(jnp.int32, (16, rows), 0), spread, 0.0)
    level_two[...] = jnp.log(jnp.sum(found, axis=0, keepdims=True) / scale_two)


def call(kernel, outs, scratch=(), **kw):
    return pl.pallas_call(
        kernel,
        out_shape=outs,
        scratch_shapes=list(scratch),
        compiler_params=PARAMS,
        **kw,
    )


def line_body(embeddings, probes, assigned, prior_counts, centroids, candidates, centroids2):
    emb_rows, width = embeddings.shape
    probe_count = probes.shape[1]
    rows = centroids.shape[0]
    per = BLOCKS2_DEV
    cap = max(2, 3 * rows // (2 * per * 16))
    part = per * cap
    bf16, f32, i32 = jnp.bfloat16, jnp.float32, jnp.int32
    shape = jax.ShapeDtypeStruct

    def exchange(value, apart, sources=range(16)):
        return lax.ppermute(value, "shard", [(i, i ^ apart) for i in sources])

    mids, ends = range(4, 12), (*range(4), *range(12, 16))
    facts = jnp.concatenate([probes, (assigned >> 5)[:, None], (assigned & 31)[:, None]], axis=1).astype(bf16)
    mine = jnp.concatenate([embeddings, jnp.pad(facts, ((0, 0), (0, 118)))], axis=1)
    mine = jnp.concatenate([mine] + [exchange(mine, apart) for apart in (4, 8, 12)], axis=0)
    mine = jnp.concatenate([mine, exchange(mine, 2)], axis=0)
    other = exchange(mine, 1)
    near_set = exchange(centroids2, 4)
    cross_set = exchange(centroids2, 12, mids)
    cand_row = candidates.reshape(1, rows)
    prior_row = prior_counts.reshape(1, rows)
    far = shape((part + META, width), bf16)
    main = shape((3 * part, width), bf16)
    far0, far1, far2, far3, main1, main2, main3, info = call(
        functools.partial(pack_kernel, cap, per),
        (far, far, far, far, main, main, main, shape((8, rows), i32)),
    )(cand_row, prior_row, centroids)
    main2, main3, main1 = exchange(main2, 2), exchange(main3, 3), exchange(main1, 1)
    up = [exchange(value, 4 ^ r, ends) for r, value in enumerate((far0, far1, far2, far3))]
    far2, far3, far1 = exchange(far2, 2), exchange(far3, 3), exchange(far1, 1)
    passed = exchange(cross_set, 4, mids)
    last_set = exchange(near_set, 12, mids)
    scaled, facts, share, new_centroids, counts, own_main = call(
        functools.partial(first_kernel, part),
        (
            shape((16 * emb_rows, width), bf16),
            shape((16, 16 * emb_rows), i32),
            shape((16, 4 * cap), f32),
            shape((rows, width), bf16),
            shape((1, rows), i32),
            main,
        ),
        [pltpu.VMEM((rows, width), bf16)],
    )(mine, other, centroids, prior_row, info)
    results = call(
        functools.partial(second_kernel, cap, per),
        shape((16, 8, 4 * cap), f32),
        [pltpu.VMEM((5, per, 4 * cap, width), bf16), pltpu.VMEM((4, per * BLOCK2, width), bf16)],
    )(
        scaled, facts, share, own_main, far0, far1, far2, far3, main1, main2, main3, *up,
        centroids2, near_set, cross_set, passed, last_set,
    )
    results = lax.all_to_all(results, "shard", split_axis=0, concat_axis=0, tiled=True)
    density, level_two = call(
        functools.partial(last_kernel, cap, probe_count * BLOCK, BLOCK2), (shape((1, emb_rows), f32), shape((1, rows), f32))
    )(info, results)
    return (density.reshape(-1), new_centroids, counts.reshape(-1), level_two.reshape(-1))


def solution(mesh):
    placed = (
        P(("groups", "shard"), None),
        P(("groups", "shard"), None),
        P(("groups", "shard")),
        P(("groups", "shard")),
        P(("groups", "shard"), None),
        P(("groups", "shard"), None),
        P(("groups", "shard"), None),
    )
    body = line_body if mesh.shape["shard"] == 16 else general_body
    return jax.shard_map(
        body,
        mesh=mesh,
        in_specs=placed,
        out_specs=(
            P(("groups", "shard")),
            P(("groups", "shard"), None),
            P(("groups", "shard")),
            P(("groups", "shard")),
        ),
        check_vma=False,
    )
```

```python
import functools

import jax
import jax.numpy as jnp
from jax import lax
from jax.experimental import pallas as pl
from jax.experimental.pallas import tpu as pltpu
from jax.sharding import PartitionSpec as P

BLOCK = 1024
BLOCKS_DEV = 1
BLOCK2 = 128
BLOCKS2_DEV = 3


def unit_rows(values):
    wide = values.astype(jnp.float32)
    power = jnp.mean(wide * wide, axis=-1, keepdims=True) + 1e-06
    return (wide * lax.rsqrt(power)).astype(jnp.bfloat16)


def kernel_sums(rows, unit):
    scores = lax.dot_general(
        rows, unit, (((1,), (1,)), ((), ())), preferred_element_type=jnp.float32
    )
    return jnp.sum(jnp.exp((scores / rows.shape[1] - 1.0) / 0.1), axis=1)


def block_update(rows, slots, width):
    matches = slots[:, None] == jnp.arange(width, dtype=jnp.int32)[None, :]
    sums = lax.dot_general(
        matches.astype(jnp.bfloat16),
        rows,
        (((0,), (0,)), ((), ())),
        preferred_element_type=jnp.float32,
    )
    counts = jnp.sum(matches.astype(jnp.int32), axis=0)
    return (sums, counts)


def slot_ranks(targets, buckets):
    matches = (targets[:, None] == jnp.arange(buckets, dtype=jnp.int32)[None, :]).astype(jnp.int32)
    return jnp.sum(jnp.cumsum(matches, axis=0) * matches, axis=1) - 1


def general_body(embeddings, probes, assigned, prior_counts, centroids, candidates, centroids2):
    devices = lax.axis_size("shard")
    emb_rows, width = embeddings.shape
    probe_count = probes.shape[1]
    capacity = max(2, 2 * emb_rows * probe_count // (BLOCKS_DEV * devices))
    scaled = unit_rows(embeddings)
    units_old = unit_rows(centroids).reshape(BLOCKS_DEV, BLOCK, width)
    total = emb_rows * probe_count
    buckets = BLOCKS_DEV * devices
    flat = probes.reshape(-1)
    place = flat * capacity + slot_ranks(flat, buckets)
    leading = jnp.arange(total, dtype=jnp.int32) % probe_count == 0
    repeated = jnp.repeat(scaled, probe_count, axis=0)
    slot_values = jnp.where(leading, jnp.repeat(assigned, probe_count), -1)
    send_rows = jnp.zeros((buckets * capacity, width), jnp.bfloat16).at[place].set(repeated)
    send_slots = jnp.full((buckets * capacity,), -1, jnp.int32).at[place].set(slot_values)
    got_rows, got_slots = (
        lax.all_to_all(
            send_rows.reshape(devices, BLOCKS_DEV * capacity, width),
            "shard",
            split_axis=0,
            concat_axis=0,
            tiled=True,
        ),
        lax.all_to_all(
            send_slots.reshape(devices, BLOCKS_DEV * capacity),
            "shard",
            split_axis=0,
            concat_axis=0,
            tiled=True,
        ),
    )
    got_rows = got_rows.reshape(devices, BLOCKS_DEV, capacity, width)
    got_slots = got_slots.reshape(devices, BLOCKS_DEV, capacity)
    local = 0
    picked = got_rows[:, local].reshape(devices * capacity, width)
    slots = got_slots[:, local].reshape(-1)
    weights = [kernel_sums(picked, units_old[local]).reshape(devices, capacity)]
    more_sums, more_counts = block_update(picked, slots, BLOCK)
    sum_list = [more_sums]
    count_list = [more_counts]
    sums = jnp.stack(sum_list)
    counts = jnp.stack(count_list)
    returned = lax.all_to_all(
        jnp.stack(weights, axis=1).reshape(devices, BLOCKS_DEV * capacity),
        "shard",
        split_axis=0,
        concat_axis=0,
        tiled=True,
    )
    totals = jnp.sum(returned.reshape(-1)[place].reshape(emb_rows, probe_count), axis=1)
    density = jnp.log(totals / (probe_count * BLOCK))
    prior = prior_counts.reshape(BLOCKS_DEV, BLOCK)
    fresh = prior + counts
    updated = (
        prior.astype(jnp.float32)[:, :, None]
        * centroids.reshape(BLOCKS_DEV, BLOCK, width).astype(jnp.float32)
        + sums
    ) / fresh.astype(jnp.float32)[:, :, None]
    new_centroids = updated.astype(jnp.bfloat16).reshape(BLOCKS_DEV * BLOCK, width)
    units_new = unit_rows(updated).reshape(BLOCKS_DEV * BLOCK, width)
    rows_two = units_new.shape[0]
    second_capacity = max(2, 3 * rows_two // (2 * BLOCKS2_DEV * devices))
    buckets_two = BLOCKS2_DEV * devices
    chosen = candidates[:, 0]
    place_two = chosen * second_capacity + slot_ranks(chosen, buckets_two)
    send_two = (
        jnp.zeros((buckets_two * second_capacity, width), jnp.bfloat16).at[place_two].set(units_new)
    )
    send_two = send_two.reshape(devices, BLOCKS2_DEV, second_capacity, width)
    units_two = unit_rows(centroids2).reshape(BLOCKS2_DEV, BLOCK2, width)
    arrived = lax.all_to_all(send_two, "shard", split_axis=0, concat_axis=0, tiled=True)
    items = arrived.shape[2]
    weights_two = [
        kernel_sums(arrived[:, local].reshape(-1, width), units_two[local]).reshape(
            arrived.shape[0], items
        )
        for local in range(BLOCKS2_DEV)
    ]
    returned_two = lax.all_to_all(
        jnp.stack(weights_two, axis=1), "shard", split_axis=0, concat_axis=0, tiled=True
    )
    level_two = jnp.log(returned_two.reshape(-1)[place_two] / BLOCK2)
    return (density, new_centroids, fresh.reshape(-1), level_two)


NT = (((1,), (1,)), ((), ()))
PARAMS = pltpu.CompilerParams(vmem_limit_bytes=48 * 1024 * 1024)
META = 16


def position():
    me = lax.axis_index("shard")
    return me, me // 4, (me // 2) % 2, me % 2


def unit_wide(wide):
    power = jnp.mean(wide * wide, axis=-1, keepdims=True) + 1e-06
    return (wide * lax.rsqrt(power)).astype(jnp.bfloat16)


def weights(scores, width):
    return jnp.exp(scores * (10.0 / width) - 10.0)


def one_hot(hits):
    return jnp.where(hits, 1.0, 0.0).astype(jnp.bfloat16)


def column(row):
    return jnp.transpose(jnp.broadcast_to(row, (8, row.shape[1])))[:, 0:1]


def facts_kernel(emb_ref, probes_ref, assigned_ref, out):
    count, width = emb_ref.shape
    square = (count, count)
    same = lax.broadcasted_iota(jnp.int32, square, 0) == lax.broadcasted_iota(jnp.int32, square, 1)
    slot = jnp.sum(jnp.where(same, assigned_ref[...], 0).astype(jnp.float32), axis=1, keepdims=True).astype(jnp.int32)
    probe_count = probes_ref.shape[1]
    lane = lax.broadcasted_iota(jnp.int32, (count, 128), 1)
    facts = jnp.where(lane == probe_count, slot >> 5, jnp.where(lane == probe_count + 1, slot & 31, 0))
    for p in range(probe_count):
        facts = jnp.where(lane == p, probes_ref[:, p : p + 1], facts)
    out[:, 0:width] = emb_ref[...]
    out[:, width:] = facts.astype(jnp.float32).astype(jnp.bfloat16)


def pick_rows(slot, first, count):
    return one_hot(slot == lax.broadcasted_iota(jnp.int32, (count, slot.shape[1]), 0) + first)


def pack(slot, prior, cent, r, out):
    count = out.shape[0] - META
    rows = slot.shape[1]
    ident = lax.broadcasted_iota(jnp.int32, (1, rows), 1) + 1
    line = lax.broadcasted_iota(jnp.int32, (META, rows), 0)
    facts = jnp.where(line == 0, ident >> 5, jnp.where(line == 1, ident & 31, jnp.where(line == 2, prior, 0)))
    facts = facts.astype(jnp.float32).astype(jnp.bfloat16)
    pick = pick_rows(slot, r * count, count)
    out[0:count, :] = jnp.dot(pick, cent, preferred_element_type=jnp.float32).astype(jnp.bfloat16)
    out[count:, :] = jnp.zeros((META, out.shape[1]), jnp.bfloat16)
    out[count:, 0:count] = lax.dot_general(facts, pick, NT, preferred_element_type=jnp.float32).astype(jnp.bfloat16)


def pack_kernel(cap, per, cand_any, prior_any, cent_any, rows2, rows3, info, cand_ref, prior_ref, cent_ref, sems):
    copies = [
        pltpu.make_async_copy(src, dst, sems.at[i])
        for i, (src, dst) in enumerate(((cand_any, cand_ref), (prior_any, prior_ref), (cent_any, cent_ref)))
    ]
    for copy in copies:
        copy.start()
    me, z, y, core = position()
    rows = cand_ref.shape[1]
    buckets = 16 * per
    before = lax.broadcasted_iota(jnp.int32, (rows, rows), 0) <= lax.broadcasted_iota(jnp.int32, (rows, rows), 1)
    before = one_hot(before)
    copies[0].wait()
    cand = cand_ref[...]
    dev = sum((cand >= per * step).astype(jnp.int32) for step in range(1, 16))
    near = dev >> 2
    plane = jnp.where(z >= 2, 3 - near, near)
    rel = (((dev >> 1) & 1) ^ y) * 2 + ((dev & 1) ^ core)
    named = cand == lax.broadcasted_iota(jnp.int32, (buckets, rows), 0)
    counted = jnp.dot(one_hot(named), before, preferred_element_type=jnp.float32)
    rank = jnp.sum(jnp.where(named, counted, 0.0), axis=0, keepdims=True).astype(jnp.int32) - 1
    kind = plane * per + cand - dev * per
    slot = (rel * 4 * per + kind) * cap + rank
    info[0:1, :] = slot
    info[1:2, :] = rel * 4 + (kind >> 2)
    info[2:3, :] = (kind & 3) * cap + rank
    copies[1].wait()
    copies[2].wait()
    pack(slot, prior_ref[...], cent_ref[...], 2, rows2)
    pack(slot, prior_ref[...], cent_ref[...], 3, rows3)


def pack_beside_kernel(info, prior_ref, cent_ref, rows1):
    pack(info[0:1, :], prior_ref[...], cent_ref[...], 1, rows1)


def first_kernel(mine_ref, other_ref, cent_ref, prior_ref, info, scaled, facts, share, fresh_rows, fresh_counts, own_rows, units):
    me, z, y, core = position()
    half = mine_ref.shape[0]
    count = 2 * half
    rows, width = cent_ref.shape
    scaled[0:half, :] = unit_wide(mine_ref[:, 0:width].astype(jnp.float32))
    scaled[half:count, :] = unit_wide(other_ref[:, 0:width].astype(jnp.float32))
    aux = jnp.concatenate([mine_ref[:, width:], other_ref[:, width:]], axis=0).astype(jnp.float32)
    aux = jnp.transpose(aux)[0:16, :].astype(jnp.int32)
    facts[...] = aux
    target = jnp.where(aux[0:1, :] == me, aux[8:9, :] * 32 + aux[9:10, :], -1)
    member = jnp.sum((aux[0:8, :] == me).astype(jnp.float32), axis=0, keepdims=True)
    prior = column(prior_ref[...].astype(jnp.float32))
    step = 256
    total = jnp.zeros((1, count), jnp.float32)
    for start in range(0, rows, step):
        old = cent_ref[start : start + step, :].astype(jnp.float32)
        scores = lax.dot_general(unit_wide(old), scaled[...], NT, preferred_element_type=jnp.float32)
        total = total + jnp.sum(weights(scores, width), axis=0, keepdims=True)
        hits = one_hot(target == lax.broadcasted_iota(jnp.int32, (step, count), 0) + start)
        sums = jnp.dot(hits, scaled[...], preferred_element_type=jnp.float32)
        gained = jnp.sum(hits.astype(jnp.float32), axis=1, keepdims=True)
        ahead = prior[start : start + step, :]
        updated = (ahead * old + sums) / (ahead + gained)
        fresh_rows[start : start + step, :] = updated.astype(jnp.bfloat16)
        units[start : start + step, :] = unit_wide(updated)
        gained_row = lax.dot_general(
            jnp.ones((8, count), jnp.bfloat16), hits, NT, preferred_element_type=jnp.float32
        )
        fresh_counts[0:1, start : start + step] = prior_ref[0:1, start : start + step] + gained_row[0:1, :].astype(jnp.int32)
    piece = count // 16
    lane = lax.broadcasted_iota(jnp.int32, (16, count), 1)
    line = lax.broadcasted_iota(jnp.int32, (16, count), 0)
    apart = jnp.where((member > 0.0) & (lane >= line * piece) & (lane < (line + 1) * piece), total, 0.0)
    spot = lax.broadcasted_iota(jnp.int32, (count, 128), 0)
    block = sum((spot >= piece * step).astype(jnp.int32) for step in range(1, 16))
    together = jnp.where(spot - block * piece == lax.broadcasted_iota(jnp.int32, (count, 128), 1), 1.0, 0.0)
    share[...] = jnp.dot(apart, together, precision=lax.Precision.HIGHEST, preferred_element_type=jnp.float32)
    pick = pick_rows(info[0:1, :], 0, own_rows.shape[0])
    own_rows[...] = jnp.dot(pick, units[...], preferred_element_type=jnp.float32).astype(jnp.bfloat16)


def level_sums(two, packed, w, per):
    block = two.shape[0] // per
    lines = []
    for j in range(per):
        scores = lax.dot_general(two[j * block : (j + 1) * block, :], packed[w, j], NT, preferred_element_type=jnp.float32)
        lines.append(jnp.sum(weights(scores, two.shape[1]), axis=0, keepdims=True))
    return lines


def second_kernel(cap, per, scaled, facts_in, own_rows, rows1, rows2, rows3, own_set, near_set, packed, sums):
    me, z, y, core = position()
    end = (z == 0) | (z == 3)
    part = per * cap
    probe0 = facts_in[0:1, :]
    slots = facts_in[8:9, :] * 32 + facts_in[9:10, :]
    for r, ref in enumerate((own_rows, rows1, rows2, rows3)):
        if r:
            facts = jnp.transpose(ref[4 * part :, 0 : 4 * part].astype(jnp.float32))
            target = jnp.where(probe0 == (me ^ r), slots + 1, -1)
        for w in range(4):
            rows = ref[w * part : (w + 1) * part, :]
            if r:
                known = facts[w * part : (w + 1) * part, :]
                hits = one_hot((known[:, 0:1] * 32.0 + known[:, 1:2]).astype(jnp.int32) == target)
                gained = jnp.sum(hits.astype(jnp.float32), axis=1, keepdims=True)
                added = jnp.dot(hits, scaled[...], preferred_element_type=jnp.float32)
                ahead = known[:, 2:3]
                rows = unit_wide((ahead * rows.astype(jnp.float32) + added) / jnp.maximum(ahead + gained, 1.0))
            for j in range(per):
                packed[w, j, r * cap : (r + 1) * cap, :] = rows[j * cap : (j + 1) * cap, :]
    for w in range(2):
        two = jnp.where(end, own_set[...], near_set[...]) if w == 0 else jnp.where(end, near_set[...], own_set[...])
        for j, line in enumerate(level_sums(unit_wide(two.astype(jnp.float32)), packed, w, per)):
            sums[w * per + j : w * per + j + 1, :] = line


def third_kernel(cap, per, packed, sums, cross_set, passed, last_set, far_set, out0, out1, out2, out3):
    me, z, y, core = position()
    end = (z == 0) | (z == 3)
    lines = [sums[0 : 2 * per, :]]
    for w, (at_end, at_mid) in enumerate(((passed, cross_set), (far_set, last_set))):
        two = jnp.where(end, at_end[...], at_mid[...])
        lines += level_sums(unit_wide(two.astype(jnp.float32)), packed, w + 2, per)
    together = jnp.concatenate(lines + [jnp.zeros((4, 4 * cap), jnp.float32)], axis=0)
    lane = lax.broadcasted_iota(jnp.int32, together.shape, 1)
    line = lax.broadcasted_iota(jnp.int32, together.shape, 0)
    for r, out in enumerate((out0, out1, out2, out3)):
        spread = jnp.zeros_like(together)
        for s in range(4):
            turned = together if s == r else pltpu.roll(together, ((s - r) % 4) * cap, 1)
            spread = jnp.where((line % 4 == s) & (lane >= s * cap) & (lane < (s + 1) * cap), turned, spread)
        for t in range(4):
            out[t : t + 1, :] = jnp.sum(spread[4 * t : 4 * t + 4], axis=0, keepdims=True)


def last_kernel(cap, scale, info, got0, got1, got2, got3, level_two):
    values = jnp.concatenate([got[0:4, :] for got in (got0, got1, got2, got3)], axis=0)
    rows = info.shape[1]
    chosen = jnp.where(info[2:3, :] == lax.broadcasted_iota(jnp.int32, (4 * cap, rows), 0), 1.0, 0.0)
    spread = jnp.dot(values, chosen, precision=lax.Precision.HIGHEST, preferred_element_type=jnp.float32)
    found = jnp.where(info[1:2, :] == lax.broadcasted_iota(jnp.int32, (16, rows), 0), spread, 0.0)
    level_two[...] = jnp.log(jnp.sum(found, axis=0, keepdims=True) / scale)


def call(kernel, outs, scratch=(), **kw):
    return pl.pallas_call(
        kernel,
        out_shape=outs,
        scratch_shapes=list(scratch),
        compiler_params=PARAMS,
        **kw,
    )


def line_body(embeddings, probes, assigned, prior_counts, centroids, candidates, centroids2):
    emb_rows, width = embeddings.shape
    probe_count = probes.shape[1]
    rows = centroids.shape[0]
    per = BLOCKS2_DEV
    cap = max(2, 3 * rows // (2 * per * 16))
    column_rows = 4 * per * cap
    bf16, f32, i32 = jnp.bfloat16, jnp.float32, jnp.int32
    shape = jax.ShapeDtypeStruct

    def exchange(value, apart, sources=range(16)):
        return lax.ppermute(value, "shard", [(i, i ^ apart) for i in sources])

    mids = range(4, 12)
    near_set = exchange(centroids2, 4)
    cross_set = exchange(centroids2, 12, mids)
    mine = call(facts_kernel, shape((emb_rows, width + 128), bf16))(embeddings, probes, assigned.reshape(1, emb_rows))
    mine = jnp.concatenate([mine] + [exchange(mine, apart) for apart in (4, 8, 12)], axis=0)
    mine = jnp.concatenate([mine, exchange(mine, 2)], axis=0)
    other = exchange(mine, 1)
    cand_row = candidates.reshape(1, rows)
    prior_row = prior_counts.reshape(1, rows)
    sent = shape((column_rows + META, width), bf16)
    anywhere = pl.BlockSpec(memory_space=pl.ANY)
    rows2, rows3, info = call(
        functools.partial(pack_kernel, cap, per),
        (sent, sent, shape((8, rows), i32)),
        [
            pltpu.VMEM((1, rows), i32),
            pltpu.VMEM((1, rows), i32),
            pltpu.VMEM((rows, width), bf16),
            pltpu.SemaphoreType.DMA((3,)),
        ],
        in_specs=[anywhere] * 3,
    )(cand_row, prior_row, centroids)
    rows2, rows3 = exchange(rows2, 2), exchange(rows3, 3)
    rows1 = exchange(call(pack_beside_kernel, sent)(info, prior_row, centroids), 1)
    passed = exchange(cross_set, 4, mids)
    last_set = exchange(near_set, 12, mids)
    far_set = exchange(last_set, 4, mids)
    scaled, facts, share, new_centroids, counts, own_rows = call(
        first_kernel,
        (
            shape((16 * emb_rows, width), bf16),
            shape((16, 16 * emb_rows), i32),
            shape((16, 4 * cap), f32),
            shape((rows, width), bf16),
            shape((1, rows), i32),
            shape((column_rows, width), bf16),
        ),
        [pltpu.VMEM((rows, width), bf16)],
    )(mine, other, centroids, prior_row, info)
    apart = jnp.arange(16, dtype=i32) ^ lax.axis_index("shard")
    share = share[((apart & 1) << 3) | ((apart & 2) << 1) | (apart >> 2)]
    share = lax.all_to_all(share, "shard", split_axis=0, concat_axis=0, tiled=True)
    density = jnp.log(jnp.sum(share, axis=0)[:emb_rows] / (probe_count * BLOCK))
    packed, sums = call(
        functools.partial(second_kernel, cap, per),
        (shape((4, per, 4 * cap, width), bf16), shape((8, 4 * cap), f32)),
    )(scaled, facts, own_rows, rows1, rows2, rows3, centroids2, near_set)
    tile = shape((8, 4 * cap), f32)
    tiles = call(functools.partial(third_kernel, cap, per), (tile,) * 4)(
        packed, sums, cross_set, passed, last_set, far_set
    )
    tiles = [tile if r == 0 else exchange(tile, r) for r, tile in enumerate(tiles)]
    level_two = call(functools.partial(last_kernel, cap, BLOCK2), shape((1, rows), f32))(info, *tiles)
    return (density, new_centroids, counts.reshape(-1), level_two.reshape(-1))


def solution(mesh):
    placed = (
        P(("groups", "shard"), None),
        P(("groups", "shard"), None),
        P(("groups", "shard")),
        P(("groups", "shard")),
        P(("groups", "shard"), None),
        P(("groups", "shard"), None),
        P(("groups", "shard"), None),
    )
    body = line_body if mesh.shape["shard"] == 16 else general_body
    return jax.shard_map(
        body,
        mesh=mesh,
        in_specs=placed,
        out_specs=(
            P(("groups", "shard")),
            P(("groups", "shard"), None),
            P(("groups", "shard")),
            P(("groups", "shard")),
        ),
        check_vma=False,
    )
```

```python
import functools

import jax
import jax.numpy as jnp
from jax import lax
from jax.experimental import pallas as pl
from jax.experimental.pallas import tpu as pltpu
from jax.sharding import PartitionSpec as P

BLOCK = 1024
BLOCKS_DEV = 1
BLOCK2 = 128
BLOCKS2_DEV = 3


def unit_rows(values):
    wide = values.astype(jnp.float32)
    power = jnp.mean(wide * wide, axis=-1, keepdims=True) + 1e-06
    return (wide * lax.rsqrt(power)).astype(jnp.bfloat16)


def kernel_sums(rows, unit):
    scores = lax.dot_general(
        rows, unit, (((1,), (1,)), ((), ())), preferred_element_type=jnp.float32
    )
    return jnp.sum(jnp.exp((scores / rows.shape[1] - 1.0) / 0.1), axis=1)


def block_update(rows, slots, width):
    matches = slots[:, None] == jnp.arange(width, dtype=jnp.int32)[None, :]
    sums = lax.dot_general(
        matches.astype(jnp.bfloat16),
        rows,
        (((0,), (0,)), ((), ())),
        preferred_element_type=jnp.float32,
    )
    counts = jnp.sum(matches.astype(jnp.int32), axis=0)
    return (sums, counts)


def slot_ranks(targets, buckets):
    matches = (targets[:, None] == jnp.arange(buckets, dtype=jnp.int32)[None, :]).astype(jnp.int32)
    return jnp.sum(jnp.cumsum(matches, axis=0) * matches, axis=1) - 1


def general_body(embeddings, probes, assigned, prior_counts, centroids, candidates, centroids2):
    devices = lax.axis_size("shard")
    emb_rows, width = embeddings.shape
    probe_count = probes.shape[1]
    capacity = max(2, 2 * emb_rows * probe_count // (BLOCKS_DEV * devices))
    scaled = unit_rows(embeddings)
    units_old = unit_rows(centroids).reshape(BLOCKS_DEV, BLOCK, width)
    total = emb_rows * probe_count
    buckets = BLOCKS_DEV * devices
    flat = probes.reshape(-1)
    place = flat * capacity + slot_ranks(flat, buckets)
    leading = jnp.arange(total, dtype=jnp.int32) % probe_count == 0
    repeated = jnp.repeat(scaled, probe_count, axis=0)
    slot_values = jnp.where(leading, jnp.repeat(assigned, probe_count), -1)
    send_rows = jnp.zeros((buckets * capacity, width), jnp.bfloat16).at[place].set(repeated)
    send_slots = jnp.full((buckets * capacity,), -1, jnp.int32).at[place].set(slot_values)
    got_rows, got_slots = (
        lax.all_to_all(
            send_rows.reshape(devices, BLOCKS_DEV * capacity, width),
            "shard",
            split_axis=0,
            concat_axis=0,
            tiled=True,
        ),
        lax.all_to_all(
            send_slots.reshape(devices, BLOCKS_DEV * capacity),
            "shard",
            split_axis=0,
            concat_axis=0,
            tiled=True,
        ),
    )
    got_rows = got_rows.reshape(devices, BLOCKS_DEV, capacity, width)
    got_slots = got_slots.reshape(devices, BLOCKS_DEV, capacity)
    local = 0
    picked = got_rows[:, local].reshape(devices * capacity, width)
    slots = got_slots[:, local].reshape(-1)
    weights = [kernel_sums(picked, units_old[local]).reshape(devices, capacity)]
    more_sums, more_counts = block_update(picked, slots, BLOCK)
    sum_list = [more_sums]
    count_list = [more_counts]
    sums = jnp.stack(sum_list)
    counts = jnp.stack(count_list)
    returned = lax.all_to_all(
        jnp.stack(weights, axis=1).reshape(devices, BLOCKS_DEV * capacity),
        "shard",
        split_axis=0,
        concat_axis=0,
        tiled=True,
    )
    totals = jnp.sum(returned.reshape(-1)[place].reshape(emb_rows, probe_count), axis=1)
    density = jnp.log(totals / (probe_count * BLOCK))
    prior = prior_counts.reshape(BLOCKS_DEV, BLOCK)
    fresh = prior + counts
    updated = (
        prior.astype(jnp.float32)[:, :, None]
        * centroids.reshape(BLOCKS_DEV, BLOCK, width).astype(jnp.float32)
        + sums
    ) / fresh.astype(jnp.float32)[:, :, None]
    new_centroids = updated.astype(jnp.bfloat16).reshape(BLOCKS_DEV * BLOCK, width)
    units_new = unit_rows(updated).reshape(BLOCKS_DEV * BLOCK, width)
    rows_two = units_new.shape[0]
    second_capacity = max(2, 3 * rows_two // (2 * BLOCKS2_DEV * devices))
    buckets_two = BLOCKS2_DEV * devices
    chosen = candidates[:, 0]
    place_two = chosen * second_capacity + slot_ranks(chosen, buckets_two)
    send_two = (
        jnp.zeros((buckets_two * second_capacity, width), jnp.bfloat16).at[place_two].set(units_new)
    )
    send_two = send_two.reshape(devices, BLOCKS2_DEV, second_capacity, width)
    units_two = unit_rows(centroids2).reshape(BLOCKS2_DEV, BLOCK2, width)
    arrived = lax.all_to_all(send_two, "shard", split_axis=0, concat_axis=0, tiled=True)
    items = arrived.shape[2]
    weights_two = [
        kernel_sums(arrived[:, local].reshape(-1, width), units_two[local]).reshape(
            arrived.shape[0], items
        )
        for local in range(BLOCKS2_DEV)
    ]
    returned_two = lax.all_to_all(
        jnp.stack(weights_two, axis=1), "shard", split_axis=0, concat_axis=0, tiled=True
    )
    level_two = jnp.log(returned_two.reshape(-1)[place_two] / BLOCK2)
    return (density, new_centroids, fresh.reshape(-1), level_two)


NT = (((1,), (1,)), ((), ()))
PARAMS = pltpu.CompilerParams(vmem_limit_bytes=48 * 1024 * 1024)
META = 16
HBM = pl.BlockSpec(memory_space=pltpu.HBM)
VMEM = pl.BlockSpec(memory_space=pltpu.VMEM)


def position():
    me = lax.axis_index("shard")
    return me, me // 4, (me // 2) % 2, me % 2


def unit_wide(wide):
    power = jnp.mean(wide * wide, axis=-1, keepdims=True) + 1e-06
    return (wide * lax.rsqrt(power)).astype(jnp.bfloat16)


def weights(scores, width):
    return jnp.exp(scores * (10.0 / width) - 10.0)


def one_hot(hits):
    return jnp.where(hits, 1.0, 0.0).astype(jnp.bfloat16)


def column(row):
    return jnp.transpose(jnp.broadcast_to(row, (8, row.shape[1])))[:, 0:1]


def fetch(pairs, sems):
    copies = [pltpu.make_async_copy(src, dst, sems.at[i]) for i, (src, dst) in enumerate(pairs)]
    for copy in copies:
        copy.start()
    return copies


def pick_rows(slot, first, count):
    return one_hot(slot == lax.broadcasted_iota(jnp.int32, (count, slot.shape[1]), 0) + first)


def pack(slot, prior, cent, first, out):
    count = out.shape[0] - META
    rows = slot.shape[1]
    ident = lax.broadcasted_iota(jnp.int32, (1, rows), 1) + 1
    line = lax.broadcasted_iota(jnp.int32, (META, rows), 0)
    facts = jnp.where(line == 0, ident >> 5, jnp.where(line == 1, ident & 31, jnp.where(line == 2, prior, 0)))
    facts = facts.astype(jnp.float32).astype(jnp.bfloat16)
    pick = pick_rows(slot, first, count)
    out[0:count, :] = jnp.dot(pick, cent, preferred_element_type=jnp.float32).astype(jnp.bfloat16)
    out[count:, :] = jnp.zeros((META, out.shape[1]), jnp.bfloat16)
    out[count:, 0:count] = lax.dot_general(facts, pick, NT, preferred_element_type=jnp.float32).astype(jnp.bfloat16)


def pack_kernel(
    cap, per, cand_any, emb_any, probes_any, assigned_any, prior_any, cent_any, mine, rows2, rows3, info,
    cand_ref, emb_ref, probes_ref, assigned_ref, prior_ref, cent_ref, sems,
):
    copies = fetch(
        (
            (cand_any, cand_ref),
            (emb_any, emb_ref),
            (probes_any, probes_ref),
            (assigned_any, assigned_ref),
            (prior_any, prior_ref),
            (cent_any, cent_ref),
        ),
        sems,
    )
    me, z, y, core = position()
    rows = cand_ref.shape[1]
    buckets = 16 * per
    before = lax.broadcasted_iota(jnp.int32, (rows, rows), 0) <= lax.broadcasted_iota(jnp.int32, (rows, rows), 1)
    before = one_hot(before)
    copies[0].wait()
    cand = cand_ref[...]
    dev = sum((cand >= per * step).astype(jnp.int32) for step in range(1, 16))
    near = dev >> 2
    plane = jnp.where(z >= 2, 3 - near, near)
    rel = (((dev >> 1) & 1) ^ y) * 2 + ((dev & 1) ^ core)
    named = cand == lax.broadcasted_iota(jnp.int32, (buckets, rows), 0)
    counted = jnp.dot(one_hot(named), before, preferred_element_type=jnp.float32)
    rank = jnp.sum(jnp.where(named, counted, 0.0), axis=0, keepdims=True).astype(jnp.int32) - 1
    kind = plane * per + cand - dev * per
    slot = (rel * 4 * per + kind) * cap + rank
    info[0:1, :] = slot
    info[1:2, :] = rel * 4 + (kind >> 2)
    info[2:3, :] = (kind & 3) * cap + rank
    for copy in copies[1:5]:
        copy.wait()
    count, width = emb_ref.shape
    probe_count = probes_ref.shape[0]
    slots = assigned_ref[...]
    facts = jnp.concatenate([probes_ref[...], slots >> 5, slots & 31], axis=0).astype(jnp.float32)
    facts = jnp.concatenate([facts, jnp.zeros((128 - probe_count - 2, count), jnp.float32)], axis=0)
    same = lax.broadcasted_iota(jnp.int32, (count, count), 0) == lax.broadcasted_iota(jnp.int32, (count, count), 1)
    mine[:, 0:width] = emb_ref[...]
    mine[:, width:] = lax.dot_general(
        one_hot(same), facts.astype(jnp.bfloat16), NT, preferred_element_type=jnp.float32
    ).astype(jnp.bfloat16)
    copies[5].wait()
    pack(slot, prior_ref[...], cent_ref[...], 2 * 4 * per * cap, rows2)
    pack(slot, prior_ref[...], cent_ref[...], 3 * 4 * per * cap, rows3)


def pack_more_kernel(info, prior_ref, cent_ref, rows2, rows3):
    half = rows2.shape[0] - META
    pack(info[0:1, :], prior_ref[...], cent_ref[...], 5 * half, rows2)
    pack(info[0:1, :], prior_ref[...], cent_ref[...], 7 * half, rows3)


def order_kernel(*refs):
    pass


def first_kernel(
    mine_any, other_any, cent_ref, prior_ref, info, early2, early3,
    scaled, facts, share, fresh_rows, fresh_counts, own_rows, beside_rows, units, mine_ref, other_ref, sems,
):
    copies = fetch(((mine_any, mine_ref), (other_any, other_ref)), sems)
    me, z, y, core = position()
    half = mine_ref.shape[0]
    count = 2 * half
    rows, width = cent_ref.shape
    prior = column(prior_ref[...].astype(jnp.float32))
    copies[0].wait()
    scaled[0:half, :] = unit_wide(mine_ref[:, 0:width].astype(jnp.float32))
    copies[1].wait()
    scaled[half:count, :] = unit_wide(other_ref[:, 0:width].astype(jnp.float32))
    aux = jnp.concatenate([mine_ref[:, width:], other_ref[:, width:]], axis=0).astype(jnp.float32)
    aux = jnp.transpose(aux)[0:16, :].astype(jnp.int32)
    facts[...] = aux
    target = jnp.where(aux[0:1, :] == me, aux[8:9, :] * 32 + aux[9:10, :], -1)
    member = jnp.sum((aux[0:8, :] == me).astype(jnp.float32), axis=0, keepdims=True)
    step = 256
    total = jnp.zeros((1, count), jnp.float32)
    for start in range(0, rows, step):
        old = cent_ref[start : start + step, :].astype(jnp.float32)
        scores = lax.dot_general(unit_wide(old), scaled[...], NT, preferred_element_type=jnp.float32)
        total = total + jnp.sum(weights(scores, width), axis=0, keepdims=True)
        hits = one_hot(target == lax.broadcasted_iota(jnp.int32, (step, count), 0) + start)
        sums = jnp.dot(hits, scaled[...], preferred_element_type=jnp.float32)
        gained = jnp.sum(hits.astype(jnp.float32), axis=1, keepdims=True)
        ahead = prior[start : start + step, :]
        updated = (ahead * old + sums) / (ahead + gained)
        fresh_rows[start : start + step, :] = updated.astype(jnp.bfloat16)
        units[start : start + step, :] = unit_wide(updated)
        gained_row = lax.dot_general(
            jnp.ones((8, count), jnp.bfloat16), hits, NT, preferred_element_type=jnp.float32
        )
        fresh_counts[0:1, start : start + step] = prior_ref[0:1, start : start + step] + gained_row[0:1, :].astype(jnp.int32)
    piece = count // 16
    lane = lax.broadcasted_iota(jnp.int32, (16, count), 1)
    line = lax.broadcasted_iota(jnp.int32, (16, count), 0)
    apart = jnp.where((member > 0.0) & (lane >= line * piece) & (lane < (line + 1) * piece), total, 0.0)
    spot = lax.broadcasted_iota(jnp.int32, (count, 128), 0)
    block = sum((spot >= piece * step).astype(jnp.int32) for step in range(1, 16))
    together = jnp.where(spot - block * piece == lax.broadcasted_iota(jnp.int32, (count, 128), 1), 1.0, 0.0)
    share[...] = jnp.dot(apart, together, precision=lax.Precision.HIGHEST, preferred_element_type=jnp.float32)
    for r, out in enumerate((own_rows, beside_rows)):
        pick = pick_rows(info[0:1, :], r * out.shape[0], out.shape[0])
        out[...] = jnp.dot(pick, units[...], preferred_element_type=jnp.float32).astype(jnp.bfloat16)


def level_sums(two, rows, per):
    block = two.shape[0] // per
    lines = []
    for j in range(per):
        scores = lax.dot_general(two[j * block : (j + 1) * block, :], rows(j), NT, preferred_element_type=jnp.float32)
        lines.append(jnp.sum(weights(scores, two.shape[1]), axis=0, keepdims=True))
    return jnp.concatenate(lines, axis=0)


def second_kernel(cap, per, second, scaled, facts_in, own_any, beside_any, rows2_any, rows3_any, *refs):
    sets, refs = refs[: 2 if not second else 3], refs[2 if not second else 3 :]
    if second:
        kept, sums, own, beside, rows2, rows3, two, packed, sems = refs
    else:
        sums, own, beside, rows2, rows3, two, two_more, packed, sems = refs
    me, z, y, core = position()
    end = (z == 0) | (z == 3)
    part = per * cap
    half = pl.ds(2 * part if second else 0, 2 * part)
    pairs = [(own_any.at[half], own), (beside_any.at[half], beside), (rows2_any, rows2), (rows3_any, rows3)]
    if second:
        at_end = pltpu.make_async_copy(sets[1], two, sems.at[4])
        at_mid = pltpu.make_async_copy(sets[0], two, sems.at[4])
        pl.when(end)(at_end.start)
        pl.when(jnp.logical_not(end))(at_mid.start)
    else:
        pairs += [(sets[0], two), (sets[1], two_more)]
    copies = fetch(pairs, sems)
    probe0 = facts_in[0:1, :]
    slots = facts_in[8:9, :] * 32 + facts_in[9:10, :]
    for r, ref in ((0, own), (1, beside), (2, rows2), (3, rows3)):
        copies[r].wait()
        if r >= 2:
            facts = jnp.transpose(ref[2 * part :, 0 : 2 * part].astype(jnp.float32))
            hits = (facts[:, 0:1] * 32.0 + facts[:, 1:2]).astype(jnp.int32) == jnp.where(probe0 == (me ^ r), slots + 1, -1)
            hits = one_hot(hits)
            gained = jnp.sum(hits.astype(jnp.float32), axis=1, keepdims=True)
            added = jnp.dot(hits, scaled[...], preferred_element_type=jnp.float32)
            ahead = facts[:, 2:3]
            wide = (ahead * ref[0 : 2 * part, :].astype(jnp.float32) + added) / jnp.maximum(ahead + gained, 1.0)
            rows = unit_wide(wide)
        else:
            rows = ref[...]
        for w in range(2):
            for j in range(per):
                start = w * part + j * cap
                packed[w, j, r * cap : (r + 1) * cap, :] = rows[start : start + cap, :]
    if second:
        pl.when(end)(at_end.wait)
        pl.when(jnp.logical_not(end))(at_mid.wait)
        sums[0:per, :] = level_sums(unit_wide(two[...].astype(jnp.float32)), lambda j: packed[0, j], per)
        kept[...] = packed[1]
    else:
        copies[4].wait()
        copies[5].wait()
        own_unit = unit_wide(two[...].astype(jnp.float32))
        near_unit = unit_wide(two_more[...].astype(jnp.float32))
        first = jnp.where(end, 0, 1)
        sums[pl.ds(first * 8, per), :] = level_sums(own_unit, lambda j: packed[first, j], per)
        sums[pl.ds(8 - first * 8, per), :] = level_sums(near_unit, lambda j: packed[1 - first, j], per)


def third_kernel(cap, per, early, later, kept_any, last_any, far_any, out0, out1, out2, out3, kept, two, sems):
    me, z, y, core = position()
    end = (z == 0) | (z == 3)
    at_end = pltpu.make_async_copy(far_any, two, sems.at[1])
    at_mid = pltpu.make_async_copy(last_any, two, sems.at[1])
    pl.when(end)(at_end.start)
    pl.when(jnp.logical_not(end))(at_mid.start)
    copies = fetch([(kept_any, kept)], sems)
    pl.when(end)(at_end.wait)
    pl.when(jnp.logical_not(end))(at_mid.wait)
    two_unit = unit_wide(two[...].astype(jnp.float32))
    copies[0].wait()
    final = level_sums(two_unit, lambda j: kept[j], per)
    lines = [early[0:per, :], early[8 : 8 + per, :], later[0:per, :], final]
    together = jnp.concatenate(lines + [jnp.zeros((16 - 4 * per, 4 * cap), jnp.float32)], axis=0)
    lane = lax.broadcasted_iota(jnp.int32, together.shape, 1)
    line = lax.broadcasted_iota(jnp.int32, together.shape, 0)
    for r, out in enumerate((out0, out1, out2, out3)):
        spread = jnp.zeros_like(together)
        for s in range(4):
            turned = together if s == r else pltpu.roll(together, ((s - r) % 4) * cap, 1)
            spread = jnp.where((line % 4 == s) & (lane >= s * cap) & (lane < (s + 1) * cap), turned, spread)
        for t in range(4):
            out[t : t + 1, :] = jnp.sum(spread[4 * t : 4 * t + 4], axis=0, keepdims=True)


def last_kernel(cap, scale, info, got0, got1, got2, got3, level_two):
    values = jnp.concatenate([got[0:4, :] for got in (got0, got1, got2, got3)], axis=0)
    rows = info.shape[1]
    chosen = jnp.where(info[2:3, :] == lax.broadcasted_iota(jnp.int32, (4 * cap, rows), 0), 1.0, 0.0)
    spread = jnp.dot(values, chosen, precision=lax.Precision.HIGHEST, preferred_element_type=jnp.float32)
    found = jnp.where(info[1:2, :] == lax.broadcasted_iota(jnp.int32, (16, rows), 0), spread, 0.0)
    level_two[...] = jnp.log(jnp.sum(found, axis=0, keepdims=True) / scale)


def call(kernel, outs, scratch=(), **kw):
    return pl.pallas_call(
        kernel,
        out_shape=outs,
        scratch_shapes=list(scratch),
        compiler_params=PARAMS,
        **kw,
    )


def line_body(embeddings, probes, assigned, prior_counts, centroids, candidates, centroids2):
    emb_rows, width = embeddings.shape
    probe_count = probes.shape[1]
    rows = centroids.shape[0]
    per = BLOCKS2_DEV
    cap = max(2, 3 * rows // (2 * per * 16))
    half = 2 * per * cap
    bf16, f32, i32 = jnp.bfloat16, jnp.float32, jnp.int32
    shape = jax.ShapeDtypeStruct

    def exchange(value, apart, sources=range(16)):
        return lax.ppermute(value, "shard", [(i, i ^ apart) for i in sources])

    mids = range(4, 12)
    near_set = exchange(centroids2, 4)
    cross_set = exchange(centroids2, 12, mids)
    prior_row = prior_counts.reshape(1, rows)
    sent = shape((half + META, width), bf16)
    line = pltpu.VMEM((1, rows), i32)
    mine, early2, early3, info = call(
        functools.partial(pack_kernel, cap, per),
        (shape((emb_rows, width + 128), bf16), sent, sent, shape((8, rows), i32)),
        [
            line,
            pltpu.VMEM((emb_rows, width), bf16),
            pltpu.VMEM((probe_count, emb_rows), i32),
            pltpu.VMEM((1, emb_rows), i32),
            line,
            pltpu.VMEM((rows, width), bf16),
            pltpu.SemaphoreType.DMA((6,)),
        ],
        in_specs=[HBM] * 6,
    )(candidates.reshape(1, rows), embeddings, probes.T, assigned.reshape(1, emb_rows), prior_row, centroids)
    early2, early3 = exchange(early2, 2), exchange(early3, 3)
    late2, late3 = call(pack_more_kernel, (sent, sent))(info, prior_row, centroids)
    late2, late3 = call(
        order_kernel, (sent, sent), in_specs=[HBM] * 4, out_specs=(HBM, HBM), input_output_aliases={0: 0, 1: 1}
    )(late2, late3, early2, early3)
    late2, late3 = exchange(late2, 2), exchange(late3, 3)
    mine = jnp.concatenate([mine] + [exchange(mine, apart) for apart in (4, 8, 12)], axis=0)
    mine = jnp.concatenate([mine, exchange(mine, 2)], axis=0)
    other = exchange(mine, 1)
    passed = exchange(cross_set, 4, mids)
    last_set = exchange(near_set, 12, mids)
    far_set = exchange(last_set, 4, mids)
    gathered = pltpu.VMEM((8 * emb_rows, width + 128), bf16)
    units = shape((2 * half, width), bf16)
    scaled, facts, share, new_centroids, counts, own_rows, beside_rows = call(
        first_kernel,
        (
            shape((16 * emb_rows, width), bf16),
            shape((16, 16 * emb_rows), i32),
            shape((16, 4 * cap), f32),
            shape((rows, width), bf16),
            shape((1, rows), i32),
            units,
            units,
        ),
        [pltpu.VMEM((rows, width), bf16), gathered, gathered, pltpu.SemaphoreType.DMA((2,))],
        in_specs=[HBM, HBM, VMEM, VMEM, VMEM, HBM, HBM],
    )(mine, other, centroids, prior_row, info, early2, early3)
    beside_rows = exchange(beside_rows, 1)
    apart = jnp.arange(16, dtype=i32) ^ lax.axis_index("shard")
    share = share[((apart & 1) << 3) | ((apart & 2) << 1) | (apart >> 2)]
    share = lax.all_to_all(share, "shard", split_axis=0, concat_axis=0, tiled=True)
    density = jnp.log(jnp.sum(share, axis=0)[:emb_rows] / (probe_count * BLOCK))
    held = pltpu.VMEM((half, width), bf16)
    arrived = pltpu.VMEM((half + META, width), bf16)
    block_set = pltpu.VMEM((per * BLOCK2, width), bf16)
    packed = pltpu.VMEM((2, per, 4 * cap, width), bf16)
    early = call(
        functools.partial(second_kernel, cap, per, False),
        shape((16, 4 * cap), f32),
        [held, held, arrived, arrived, block_set, block_set, packed, pltpu.SemaphoreType.DMA((6,))],
        in_specs=[VMEM, VMEM] + [HBM] * 6,
    )(scaled, facts, own_rows, beside_rows, early2, early3, centroids2, near_set)
    kept = shape((per, 4 * cap, width), bf16)
    kept_rows, later = call(
        functools.partial(second_kernel, cap, per, True),
        (kept, shape((8, 4 * cap), f32)),
        [held, held, arrived, arrived, block_set, packed, pltpu.SemaphoreType.DMA((5,))],
        in_specs=[VMEM, VMEM] + [HBM] * 6 + [HBM],
    )(scaled, facts, own_rows, beside_rows, late2, late3, cross_set, passed, early)
    tile = shape((8, 4 * cap), f32)
    tiles = call(
        functools.partial(third_kernel, cap, per),
        (tile,) * 4,
        [pltpu.VMEM(kept.shape, bf16), block_set, pltpu.SemaphoreType.DMA((2,))],
        in_specs=[VMEM, VMEM, HBM, HBM, HBM],
    )(early, later, kept_rows, last_set, far_set)
    tiles = [tile if r == 0 else exchange(tile, r) for r, tile in enumerate(tiles)]
    level_two = call(functools.partial(last_kernel, cap, BLOCK2), shape((1, rows), f32))(info, *tiles)
    return (density, new_centroids, counts.reshape(-1), level_two.reshape(-1))


def solution(mesh):
    placed = (
        P(("groups", "shard"), None),
        P(("groups", "shard"), None),
        P(("groups", "shard")),
        P(("groups", "shard")),
        P(("groups", "shard"), None),
        P(("groups", "shard"), None),
        P(("groups", "shard"), None),
    )
    body = line_body if mesh.shape["shard"] == 16 else general_body
    return jax.shard_map(
        body,
        mesh=mesh,
        in_specs=placed,
        out_specs=(
            P(("groups", "shard")),
            P(("groups", "shard"), None),
            P(("groups", "shard")),
            P(("groups", "shard")),
        ),
        check_vma=False,
    )
```

```python
import functools

import jax
import jax.numpy as jnp
from jax import lax
from jax.experimental import pallas as pl
from jax.experimental.pallas import tpu as pltpu
from jax.sharding import PartitionSpec as P

BLOCK = 1024
BLOCKS_DEV = 1
BLOCK2 = 128
BLOCKS2_DEV = 3


def unit_rows(values):
    wide = values.astype(jnp.float32)
    power = jnp.mean(wide * wide, axis=-1, keepdims=True) + 1e-06
    return (wide * lax.rsqrt(power)).astype(jnp.bfloat16)


def kernel_sums(rows, unit):
    scores = lax.dot_general(
        rows, unit, (((1,), (1,)), ((), ())), preferred_element_type=jnp.float32
    )
    return jnp.sum(jnp.exp((scores / rows.shape[1] - 1.0) / 0.1), axis=1)


def block_update(rows, slots, width):
    matches = slots[:, None] == jnp.arange(width, dtype=jnp.int32)[None, :]
    sums = lax.dot_general(
        matches.astype(jnp.bfloat16),
        rows,
        (((0,), (0,)), ((), ())),
        preferred_element_type=jnp.float32,
    )
    counts = jnp.sum(matches.astype(jnp.int32), axis=0)
    return (sums, counts)


def slot_ranks(targets, buckets):
    matches = (targets[:, None] == jnp.arange(buckets, dtype=jnp.int32)[None, :]).astype(jnp.int32)
    return jnp.sum(jnp.cumsum(matches, axis=0) * matches, axis=1) - 1


def general_body(embeddings, probes, assigned, prior_counts, centroids, candidates, centroids2):
    devices = lax.axis_size("shard")
    emb_rows, width = embeddings.shape
    probe_count = probes.shape[1]
    capacity = max(2, 2 * emb_rows * probe_count // (BLOCKS_DEV * devices))
    scaled = unit_rows(embeddings)
    units_old = unit_rows(centroids).reshape(BLOCKS_DEV, BLOCK, width)
    total = emb_rows * probe_count
    buckets = BLOCKS_DEV * devices
    flat = probes.reshape(-1)
    place = flat * capacity + slot_ranks(flat, buckets)
    leading = jnp.arange(total, dtype=jnp.int32) % probe_count == 0
    repeated = jnp.repeat(scaled, probe_count, axis=0)
    slot_values = jnp.where(leading, jnp.repeat(assigned, probe_count), -1)
    send_rows = jnp.zeros((buckets * capacity, width), jnp.bfloat16).at[place].set(repeated)
    send_slots = jnp.full((buckets * capacity,), -1, jnp.int32).at[place].set(slot_values)
    got_rows, got_slots = (
        lax.all_to_all(
            send_rows.reshape(devices, BLOCKS_DEV * capacity, width),
            "shard",
            split_axis=0,
            concat_axis=0,
            tiled=True,
        ),
        lax.all_to_all(
            send_slots.reshape(devices, BLOCKS_DEV * capacity),
            "shard",
            split_axis=0,
            concat_axis=0,
            tiled=True,
        ),
    )
    got_rows = got_rows.reshape(devices, BLOCKS_DEV, capacity, width)
    got_slots = got_slots.reshape(devices, BLOCKS_DEV, capacity)
    local = 0
    picked = got_rows[:, local].reshape(devices * capacity, width)
    slots = got_slots[:, local].reshape(-1)
    weights = [kernel_sums(picked, units_old[local]).reshape(devices, capacity)]
    more_sums, more_counts = block_update(picked, slots, BLOCK)
    sum_list = [more_sums]
    count_list = [more_counts]
    sums = jnp.stack(sum_list)
    counts = jnp.stack(count_list)
    returned = lax.all_to_all(
        jnp.stack(weights, axis=1).reshape(devices, BLOCKS_DEV * capacity),
        "shard",
        split_axis=0,
        concat_axis=0,
        tiled=True,
    )
    totals = jnp.sum(returned.reshape(-1)[place].reshape(emb_rows, probe_count), axis=1)
    density = jnp.log(totals / (probe_count * BLOCK))
    prior = prior_counts.reshape(BLOCKS_DEV, BLOCK)
    fresh = prior + counts
    updated = (
        prior.astype(jnp.float32)[:, :, None]
        * centroids.reshape(BLOCKS_DEV, BLOCK, width).astype(jnp.float32)
        + sums
    ) / fresh.astype(jnp.float32)[:, :, None]
    new_centroids = updated.astype(jnp.bfloat16).reshape(BLOCKS_DEV * BLOCK, width)
    units_new = unit_rows(updated).reshape(BLOCKS_DEV * BLOCK, width)
    rows_two = units_new.shape[0]
    second_capacity = max(2, 3 * rows_two // (2 * BLOCKS2_DEV * devices))
    buckets_two = BLOCKS2_DEV * devices
    chosen = candidates[:, 0]
    place_two = chosen * second_capacity + slot_ranks(chosen, buckets_two)
    send_two = (
        jnp.zeros((buckets_two * second_capacity, width), jnp.bfloat16).at[place_two].set(units_new)
    )
    send_two = send_two.reshape(devices, BLOCKS2_DEV, second_capacity, width)
    units_two = unit_rows(centroids2).reshape(BLOCKS2_DEV, BLOCK2, width)
    arrived = lax.all_to_all(send_two, "shard", split_axis=0, concat_axis=0, tiled=True)
    items = arrived.shape[2]
    weights_two = [
        kernel_sums(arrived[:, local].reshape(-1, width), units_two[local]).reshape(
            arrived.shape[0], items
        )
        for local in range(BLOCKS2_DEV)
    ]
    returned_two = lax.all_to_all(
        jnp.stack(weights_two, axis=1), "shard", split_axis=0, concat_axis=0, tiled=True
    )
    level_two = jnp.log(returned_two.reshape(-1)[place_two] / BLOCK2)
    return (density, new_centroids, fresh.reshape(-1), level_two)


NT = (((1,), (1,)), ((), ()))
PARAMS = pltpu.CompilerParams(vmem_limit_bytes=48 * 1024 * 1024)
META = 16
HBM = pl.BlockSpec(memory_space=pltpu.HBM)
ANY = pl.BlockSpec(memory_space=pl.ANY)
VMEM = pl.BlockSpec(memory_space=pltpu.VMEM)


def position():
    me = lax.axis_index("shard")
    return me, me // 4, (me // 2) % 2, me % 2


def unit_wide(wide):
    power = jnp.mean(wide * wide, axis=-1, keepdims=True) + 1e-06
    return (wide * lax.rsqrt(power)).astype(jnp.bfloat16)


def weights(scores, width):
    return jnp.exp(scores * (10.0 / width) - 10.0)


def one_hot(hits):
    return jnp.where(hits, 1.0, 0.0).astype(jnp.bfloat16)


def column(row):
    return jnp.transpose(jnp.broadcast_to(row, (8, row.shape[1])))[:, 0:1]


def fetch(pairs, sems):
    copies = [pltpu.make_async_copy(src, dst, sems.at[i]) for i, (src, dst) in enumerate(pairs)]
    for copy in copies:
        copy.start()
    return copies


def pick_rows(slot, first, count):
    return one_hot(slot == lax.broadcasted_iota(jnp.int32, (count, slot.shape[1]), 0) + first)


def pack(slot, prior, cent, first, out):
    count = out.shape[0] - META
    rows = slot.shape[1]
    ident = lax.broadcasted_iota(jnp.int32, (1, rows), 1) + 1
    line = lax.broadcasted_iota(jnp.int32, (META, rows), 0)
    facts = jnp.where(line == 0, ident >> 5, jnp.where(line == 1, ident & 31, jnp.where(line == 2, prior, 0)))
    facts = facts.astype(jnp.float32).astype(jnp.bfloat16)
    pick = pick_rows(slot, first, count)
    out[0:count, :] = jnp.dot(pick, cent, preferred_element_type=jnp.float32).astype(jnp.bfloat16)
    out[count:, :] = jnp.zeros((META, out.shape[1]), jnp.bfloat16)
    out[count:, 0:count] = lax.dot_general(facts, pick, NT, preferred_element_type=jnp.float32).astype(jnp.bfloat16)


def pack_kernel(
    cap, per, cand_any, emb_any, probes_any, assigned_any, prior_any, cent_any, mine, rows2, rows3, info,
    cand_ref, emb_ref, probes_ref, assigned_ref, prior_ref, cent_ref, sems,
):
    copies = fetch(
        (
            (cand_any, cand_ref),
            (emb_any, emb_ref),
            (probes_any, probes_ref),
            (assigned_any, assigned_ref),
            (prior_any, prior_ref),
            (cent_any, cent_ref),
        ),
        sems,
    )
    me, z, y, core = position()
    rows = cand_ref.shape[1]
    buckets = 16 * per
    before = lax.broadcasted_iota(jnp.int32, (rows, rows), 0) <= lax.broadcasted_iota(jnp.int32, (rows, rows), 1)
    before = one_hot(before)
    copies[0].wait()
    cand = cand_ref[...]
    dev = sum((cand >= per * step).astype(jnp.int32) for step in range(1, 16))
    near = dev >> 2
    plane = jnp.where(z >= 2, 3 - near, near)
    rel = (((dev >> 1) & 1) ^ y) * 2 + ((dev & 1) ^ core)
    named = cand == lax.broadcasted_iota(jnp.int32, (buckets, rows), 0)
    counted = jnp.dot(one_hot(named), before, preferred_element_type=jnp.float32)
    rank = jnp.sum(jnp.where(named, counted, 0.0), axis=0, keepdims=True).astype(jnp.int32) - 1
    kind = plane * per + cand - dev * per
    slot = (rel * 4 * per + kind) * cap + rank
    info[0:1, :] = slot
    info[1:2, :] = rel * 4 + (kind >> 2)
    info[2:3, :] = (kind & 3) * cap + rank
    for copy in copies[1:5]:
        copy.wait()
    count, width = emb_ref.shape
    probe_count = probes_ref.shape[0]
    slots = assigned_ref[...]
    facts = jnp.concatenate([probes_ref[...], slots >> 5, slots & 31], axis=0).astype(jnp.float32)
    facts = jnp.concatenate([facts, jnp.zeros((128 - probe_count - 2, count), jnp.float32)], axis=0)
    same = lax.broadcasted_iota(jnp.int32, (count, count), 0) == lax.broadcasted_iota(jnp.int32, (count, count), 1)
    mine[:, 0:width] = emb_ref[...]
    mine[:, width:] = lax.dot_general(
        one_hot(same), facts.astype(jnp.bfloat16), NT, preferred_element_type=jnp.float32
    ).astype(jnp.bfloat16)
    copies[5].wait()
    pack(slot, prior_ref[...], cent_ref[...], 2 * 4 * per * cap, rows2)
    pack(slot, prior_ref[...], cent_ref[...], 3 * 4 * per * cap, rows3)


def pack_more_kernel(info, prior_ref, cent_ref, rows2, rows3):
    half = rows2.shape[0] - META
    pack(info[0:1, :], prior_ref[...], cent_ref[...], 5 * half, rows2)
    pack(info[0:1, :], prior_ref[...], cent_ref[...], 7 * half, rows3)


def order_kernel(*refs):
    pass


def first_kernel(
    mine_any, other_any, cent_ref, prior_ref, info,
    scaled, facts, share, fresh_rows, fresh_counts, own_rows, beside_rows, units, mine_ref, other_ref, sems,
):
    copies = fetch(((mine_any, mine_ref), (other_any, other_ref)), sems)
    me, z, y, core = position()
    half = mine_ref.shape[0]
    count = 2 * half
    rows, width = cent_ref.shape
    prior = column(prior_ref[...].astype(jnp.float32))
    copies[0].wait()
    scaled[0:half, :] = unit_wide(mine_ref[:, 0:width].astype(jnp.float32))
    copies[1].wait()
    scaled[half:count, :] = unit_wide(other_ref[:, 0:width].astype(jnp.float32))
    aux = jnp.concatenate([mine_ref[:, width:], other_ref[:, width:]], axis=0).astype(jnp.float32)
    aux = jnp.transpose(aux)[0:16, :].astype(jnp.int32)
    facts[...] = aux
    target = jnp.where(aux[0:1, :] == me, aux[8:9, :] * 32 + aux[9:10, :], -1)
    member = jnp.sum((aux[0:8, :] == me).astype(jnp.float32), axis=0, keepdims=True)
    step = 256
    total = jnp.zeros((1, count), jnp.float32)
    for start in range(0, rows, step):
        old = cent_ref[start : start + step, :].astype(jnp.float32)
        scores = lax.dot_general(unit_wide(old), scaled[...], NT, preferred_element_type=jnp.float32)
        total = total + jnp.sum(weights(scores, width), axis=0, keepdims=True)
        hits = one_hot(target == lax.broadcasted_iota(jnp.int32, (step, count), 0) + start)
        sums = jnp.dot(hits, scaled[...], preferred_element_type=jnp.float32)
        gained = jnp.sum(hits.astype(jnp.float32), axis=1, keepdims=True)
        ahead = prior[start : start + step, :]
        updated = (ahead * old + sums) / (ahead + gained)
        fresh_rows[start : start + step, :] = updated.astype(jnp.bfloat16)
        units[start : start + step, :] = unit_wide(updated)
        gained_row = lax.dot_general(
            jnp.ones((8, count), jnp.bfloat16), hits, NT, preferred_element_type=jnp.float32
        )
        fresh_counts[0:1, start : start + step] = prior_ref[0:1, start : start + step] + gained_row[0:1, :].astype(jnp.int32)
    piece = count // 16
    lane = lax.broadcasted_iota(jnp.int32, (16, count), 1)
    line = lax.broadcasted_iota(jnp.int32, (16, count), 0)
    apart = jnp.where((member > 0.0) & (lane >= line * piece) & (lane < (line + 1) * piece), total, 0.0)
    spot = lax.broadcasted_iota(jnp.int32, (count, 128), 0)
    block = sum((spot >= piece * step).astype(jnp.int32) for step in range(1, 16))
    together = jnp.where(spot - block * piece == lax.broadcasted_iota(jnp.int32, (count, 128), 1), 1.0, 0.0)
    share[...] = jnp.dot(apart, together, precision=lax.Precision.HIGHEST, preferred_element_type=jnp.float32)
    for r, out in enumerate((own_rows, beside_rows)):
        pick = pick_rows(info[0:1, :], r * out.shape[0], out.shape[0])
        out[...] = jnp.dot(pick, units[...], preferred_element_type=jnp.float32).astype(jnp.bfloat16)


def level_sums(two, rows, per):
    block = two.shape[0] // per
    lines = []
    for j in range(per):
        scores = lax.dot_general(two[j * block : (j + 1) * block, :], rows(j), NT, preferred_element_type=jnp.float32)
        lines.append(jnp.sum(weights(scores, two.shape[1]), axis=0, keepdims=True))
    return jnp.concatenate(lines, axis=0)


def second_kernel(cap, per, second, scaled, facts_in, own_any, beside_any, rows2_any, rows3_any, *refs):
    sets, refs = refs[: 2 if not second else 3], refs[2 if not second else 3 :]
    if second:
        kept, sums, own, beside, rows2, rows3, two, packed, sems = refs
    else:
        sums, own, beside, rows2, rows3, two, two_more, packed, sems = refs
    me, z, y, core = position()
    end = (z == 0) | (z == 3)
    part = per * cap
    half = pl.ds(2 * part if second else 0, 2 * part)
    pairs = [(own_any.at[half], own), (beside_any.at[half], beside), (rows2_any, rows2), (rows3_any, rows3)]
    if second:
        at_end = pltpu.make_async_copy(sets[1], two, sems.at[4])
        at_mid = pltpu.make_async_copy(sets[0], two, sems.at[4])
        pl.when(end)(at_end.start)
        pl.when(jnp.logical_not(end))(at_mid.start)
    else:
        pairs += [(sets[0], two), (sets[1], two_more)]
    copies = fetch(pairs, sems)
    probe0 = facts_in[0:1, :]
    slots = facts_in[8:9, :] * 32 + facts_in[9:10, :]
    for r, ref in ((0, own), (1, beside), (2, rows2), (3, rows3)):
        copies[r].wait()
        if r >= 2:
            facts = jnp.transpose(ref[2 * part :, 0 : 2 * part].astype(jnp.float32))
            hits = (facts[:, 0:1] * 32.0 + facts[:, 1:2]).astype(jnp.int32) == jnp.where(probe0 == (me ^ r), slots + 1, -1)
            hits = one_hot(hits)
            gained = jnp.sum(hits.astype(jnp.float32), axis=1, keepdims=True)
            added = jnp.dot(hits, scaled[...], preferred_element_type=jnp.float32)
            ahead = facts[:, 2:3]
            wide = (ahead * ref[0 : 2 * part, :].astype(jnp.float32) + added) / jnp.maximum(ahead + gained, 1.0)
            rows = unit_wide(wide)
        else:
            rows = ref[...]
        for w in range(2):
            for j in range(per):
                start = w * part + j * cap
                packed[w, j, r * cap : (r + 1) * cap, :] = rows[start : start + cap, :]
    if second:
        pl.when(end)(at_end.wait)
        pl.when(jnp.logical_not(end))(at_mid.wait)
        sums[0:per, :] = level_sums(unit_wide(two[...].astype(jnp.float32)), lambda j: packed[0, j], per)
        kept[...] = packed[1]
    else:
        copies[4].wait()
        copies[5].wait()
        own_unit = unit_wide(two[...].astype(jnp.float32))
        near_unit = unit_wide(two_more[...].astype(jnp.float32))
        first = jnp.where(end, 0, 1)
        sums[pl.ds(first * 8, per), :] = level_sums(own_unit, lambda j: packed[first, j], per)
        sums[pl.ds(8 - first * 8, per), :] = level_sums(near_unit, lambda j: packed[1 - first, j], per)


def third_kernel(cap, per, early, later, share, kept_any, last_any, far_any, out, kept, two, sems):
    me, z, y, core = position()
    end = (z == 0) | (z == 3)
    at_end = pltpu.make_async_copy(far_any, two, sems.at[1])
    at_mid = pltpu.make_async_copy(last_any, two, sems.at[1])
    pl.when(end)(at_end.start)
    pl.when(jnp.logical_not(end))(at_mid.start)
    copies = fetch([(kept_any, kept)], sems)
    pl.when(end)(at_end.wait)
    pl.when(jnp.logical_not(end))(at_mid.wait)
    two_unit = unit_wide(two[...].astype(jnp.float32))
    copies[0].wait()
    final = level_sums(two_unit, lambda j: kept[j], per)
    lines = [early[0:per, :], early[8 : 8 + per, :], later[0:per, :], final]
    together = jnp.concatenate(lines + [jnp.zeros((16 - 4 * per, 4 * cap), jnp.float32)], axis=0)
    lane = lax.broadcasted_iota(jnp.int32, together.shape, 1)
    line = lax.broadcasted_iota(jnp.int32, together.shape, 0)
    out[...] = jnp.zeros(out.shape, jnp.float32)
    for r in range(4):
        spread = jnp.zeros_like(together)
        for s in range(4):
            turned = together if s == r else pltpu.roll(together, ((s - r) % 4) * cap, 1)
            spread = jnp.where((line % 4 == s) & (lane >= s * cap) & (lane < (s + 1) * cap), turned, spread)
        out[me ^ r, 0:4, :] = jnp.concatenate(
            [jnp.sum(spread[4 * t : 4 * t + 4], axis=0, keepdims=True) for t in range(4)], axis=0
        )
    for b in range(16):
        apart = ((b & 1) * 4) ^ ((b >> 1 & 1) * 12) ^ ((b >> 2 & 1) * 2) ^ (b >> 3)
        out[me ^ apart, 4:5, :] = share[b : b + 1, :]


def last_kernel(cap, scale_one, scale_two, info, got, density, level_two):
    me, z, y, core = position()
    total = jnp.zeros((1, 4 * cap), jnp.float32)
    for source in range(16):
        total = total + got[source, 4:5, :]
    density[...] = jnp.log(total[:, 0 : density.shape[1]] / scale_one)
    values = jnp.concatenate([got[me ^ r, 0:4, :] for r in range(4)], axis=0)
    rows = info.shape[1]
    chosen = jnp.where(info[2:3, :] == lax.broadcasted_iota(jnp.int32, (4 * cap, rows), 0), 1.0, 0.0)
    spread = jnp.dot(values, chosen, precision=lax.Precision.HIGHEST, preferred_element_type=jnp.float32)
    found = jnp.where(info[1:2, :] == lax.broadcasted_iota(jnp.int32, (16, rows), 0), spread, 0.0)
    level_two[...] = jnp.log(jnp.sum(found, axis=0, keepdims=True) / scale_two)


def call(kernel, outs, scratch=(), in_specs=None, **kw):
    def run(*args):
        specs = in_specs or [VMEM] * len(args)
        args = [pltpu.with_memory_space_constraint(a, pltpu.HBM) if spec is HBM else a for a, spec in zip(args, specs)]
        return pl.pallas_call(
            kernel, out_shape=outs, in_specs=specs, scratch_shapes=list(scratch), compiler_params=PARAMS, **kw
        )(*args)

    return run


def in_order(*values):
    count = len(values)
    return call(
        order_kernel,
        tuple(jax.ShapeDtypeStruct(value.shape, value.dtype) for value in values),
        in_specs=[ANY] * count,
        out_specs=(ANY,) * count,
        input_output_aliases={i: i for i in range(count)},
    )(*values)


def line_body(embeddings, probes, assigned, prior_counts, centroids, candidates, centroids2):
    emb_rows, width = embeddings.shape
    probe_count = probes.shape[1]
    rows = centroids.shape[0]
    per = BLOCKS2_DEV
    cap = max(2, 3 * rows // (2 * per * 16))
    half = 2 * per * cap
    bf16, f32, i32 = jnp.bfloat16, jnp.float32, jnp.int32
    shape = jax.ShapeDtypeStruct

    def exchange(value, apart, sources=range(16)):
        return lax.ppermute(value, "shard", [(i, i ^ apart) for i in sources])

    mids = range(4, 12)
    near_set = exchange(centroids2, 4)
    cross_set = exchange(centroids2, 12, mids)
    prior_row = prior_counts.reshape(1, rows)
    sent = shape((half + META, width), bf16)
    line = pltpu.VMEM((1, rows), i32)
    mine, early2, early3, info = call(
        functools.partial(pack_kernel, cap, per),
        (shape((emb_rows, width + 128), bf16), sent, sent, shape((8, rows), i32)),
        [
            line,
            pltpu.VMEM((emb_rows, width), bf16),
            pltpu.VMEM((probe_count, emb_rows), i32),
            pltpu.VMEM((1, emb_rows), i32),
            line,
            pltpu.VMEM((rows, width), bf16),
            pltpu.SemaphoreType.DMA((6,)),
        ],
        in_specs=[HBM] * 6,
    )(candidates.reshape(1, rows), embeddings, probes.T, assigned.reshape(1, emb_rows), prior_row, centroids)
    early2, early3 = exchange(early2, 2), exchange(early3, 3)
    late2, late3 = call(pack_more_kernel, (sent, sent))(info, prior_row, centroids)
    near_set, cross_set, early2, early3, late2, late3 = in_order(near_set, cross_set, early2, early3, late2, late3)
    late2, late3 = exchange(late2, 2), exchange(late3, 3)
    passed = exchange(cross_set, 4, mids)
    last_set = exchange(near_set, 12, mids)
    passed, last_set, late2, late3 = in_order(passed, last_set, late2, late3)
    far_set = exchange(last_set, 4, mids)
    for apart in (4, 12, 2):
        mine = jnp.concatenate([mine, exchange(mine, apart)], axis=0)
    other = exchange(mine, 1)
    gathered = pltpu.VMEM((8 * emb_rows, width + 128), bf16)
    units = shape((2 * half, width), bf16)
    scaled, facts, share, new_centroids, counts, own_rows, beside_rows = call(
        first_kernel,
        (
            shape((16 * emb_rows, width), bf16),
            shape((16, 16 * emb_rows), i32),
            shape((16, 4 * cap), f32),
            shape((rows, width), bf16),
            shape((1, rows), i32),
            units,
            units,
        ),
        [pltpu.VMEM((rows, width), bf16), gathered, gathered, pltpu.SemaphoreType.DMA((2,))],
        in_specs=[ANY, ANY, VMEM, VMEM, VMEM],
    )(mine, other, centroids, prior_row, info)
    beside_rows = exchange(beside_rows, 1)
    held = pltpu.VMEM((half, width), bf16)
    arrived = pltpu.VMEM((half + META, width), bf16)
    block_set = pltpu.VMEM((per * BLOCK2, width), bf16)
    packed = pltpu.VMEM((2, per, 4 * cap, width), bf16)
    early = call(
        functools.partial(second_kernel, cap, per, False),
        shape((16, 4 * cap), f32),
        [held, held, arrived, arrived, block_set, block_set, packed, pltpu.SemaphoreType.DMA((6,))],
        in_specs=[VMEM, VMEM] + [ANY] * 4 + [HBM, ANY],
    )(scaled, facts, own_rows, beside_rows, early2, early3, centroids2, near_set)
    kept = shape((per, 4 * cap, width), bf16)
    kept_rows, later = call(
        functools.partial(second_kernel, cap, per, True),
        (kept, shape((8, 4 * cap), f32)),
        [held, held, arrived, arrived, block_set, packed, pltpu.SemaphoreType.DMA((5,))],
        in_specs=[VMEM, VMEM] + [ANY] * 7,
    )(scaled, facts, own_rows, beside_rows, late2, late3, cross_set, passed, early)
    results = call(
        functools.partial(third_kernel, cap, per),
        shape((16, 8, 4 * cap), f32),
        [pltpu.VMEM(kept.shape, bf16), block_set, pltpu.SemaphoreType.DMA((2,))],
        in_specs=[VMEM, VMEM, VMEM, ANY, ANY, ANY],
    )(early, later, share, kept_rows, last_set, far_set)
    results = lax.all_to_all(results, "shard", split_axis=0, concat_axis=0, tiled=True)
    density, level_two = call(
        functools.partial(last_kernel, cap, probe_count * BLOCK, BLOCK2), (shape((1, emb_rows), f32), shape((1, rows), f32))
    )(info, results)
    return (density.reshape(-1), new_centroids, counts.reshape(-1), level_two.reshape(-1))


def solution(mesh):
    placed = (
        P(("groups", "shard"), None),
        P(("groups", "shard"), None),
        P(("groups", "shard")),
        P(("groups", "shard")),
        P(("groups", "shard"), None),
        P(("groups", "shard"), None),
        P(("groups", "shard"), None),
    )
    body = line_body if mesh.shape["shard"] == 16 else general_body
    return jax.shard_map(
        body,
        mesh=mesh,
        in_specs=placed,
        out_specs=(
            P(("groups", "shard")),
            P(("groups", "shard"), None),
            P(("groups", "shard")),
            P(("groups", "shard")),
        ),
        check_vma=False,
    )
```

```python
import functools

import jax
import jax.numpy as jnp
from jax import lax
from jax.experimental import pallas as pl
from jax.experimental.pallas import tpu as pltpu
from jax.sharding import PartitionSpec as P

BLOCK = 1024
BLOCKS_DEV = 1
BLOCK2 = 128
BLOCKS2_DEV = 3


def unit_rows(values):
    wide = values.astype(jnp.float32)
    power = jnp.mean(wide * wide, axis=-1, keepdims=True) + 1e-06
    return (wide * lax.rsqrt(power)).astype(jnp.bfloat16)


def kernel_sums(rows, unit):
    scores = lax.dot_general(
        rows, unit, (((1,), (1,)), ((), ())), preferred_element_type=jnp.float32
    )
    return jnp.sum(jnp.exp((scores / rows.shape[1] - 1.0) / 0.1), axis=1)


def block_update(rows, slots, width):
    matches = slots[:, None] == jnp.arange(width, dtype=jnp.int32)[None, :]
    sums = lax.dot_general(
        matches.astype(jnp.bfloat16),
        rows,
        (((0,), (0,)), ((), ())),
        preferred_element_type=jnp.float32,
    )
    counts = jnp.sum(matches.astype(jnp.int32), axis=0)
    return (sums, counts)


def slot_ranks(targets, buckets):
    matches = (targets[:, None] == jnp.arange(buckets, dtype=jnp.int32)[None, :]).astype(jnp.int32)
    return jnp.sum(jnp.cumsum(matches, axis=0) * matches, axis=1) - 1


def general_body(embeddings, probes, assigned, prior_counts, centroids, candidates, centroids2):
    devices = lax.axis_size("shard")
    emb_rows, width = embeddings.shape
    probe_count = probes.shape[1]
    capacity = max(2, 2 * emb_rows * probe_count // (BLOCKS_DEV * devices))
    scaled = unit_rows(embeddings)
    units_old = unit_rows(centroids).reshape(BLOCKS_DEV, BLOCK, width)
    total = emb_rows * probe_count
    buckets = BLOCKS_DEV * devices
    flat = probes.reshape(-1)
    place = flat * capacity + slot_ranks(flat, buckets)
    leading = jnp.arange(total, dtype=jnp.int32) % probe_count == 0
    repeated = jnp.repeat(scaled, probe_count, axis=0)
    slot_values = jnp.where(leading, jnp.repeat(assigned, probe_count), -1)
    send_rows = jnp.zeros((buckets * capacity, width), jnp.bfloat16).at[place].set(repeated)
    send_slots = jnp.full((buckets * capacity,), -1, jnp.int32).at[place].set(slot_values)
    got_rows, got_slots = (
        lax.all_to_all(
            send_rows.reshape(devices, BLOCKS_DEV * capacity, width),
            "shard",
            split_axis=0,
            concat_axis=0,
            tiled=True,
        ),
        lax.all_to_all(
            send_slots.reshape(devices, BLOCKS_DEV * capacity),
            "shard",
            split_axis=0,
            concat_axis=0,
            tiled=True,
        ),
    )
    got_rows = got_rows.reshape(devices, BLOCKS_DEV, capacity, width)
    got_slots = got_slots.reshape(devices, BLOCKS_DEV, capacity)
    local = 0
    picked = got_rows[:, local].reshape(devices * capacity, width)
    slots = got_slots[:, local].reshape(-1)
    weights = [kernel_sums(picked, units_old[local]).reshape(devices, capacity)]
    more_sums, more_counts = block_update(picked, slots, BLOCK)
    sum_list = [more_sums]
    count_list = [more_counts]
    sums = jnp.stack(sum_list)
    counts = jnp.stack(count_list)
    returned = lax.all_to_all(
        jnp.stack(weights, axis=1).reshape(devices, BLOCKS_DEV * capacity),
        "shard",
        split_axis=0,
        concat_axis=0,
        tiled=True,
    )
    totals = jnp.sum(returned.reshape(-1)[place].reshape(emb_rows, probe_count), axis=1)
    density = jnp.log(totals / (probe_count * BLOCK))
    prior = prior_counts.reshape(BLOCKS_DEV, BLOCK)
    fresh = prior + counts
    updated = (
        prior.astype(jnp.float32)[:, :, None]
        * centroids.reshape(BLOCKS_DEV, BLOCK, width).astype(jnp.float32)
        + sums
    ) / fresh.astype(jnp.float32)[:, :, None]
    new_centroids = updated.astype(jnp.bfloat16).reshape(BLOCKS_DEV * BLOCK, width)
    units_new = unit_rows(updated).reshape(BLOCKS_DEV * BLOCK, width)
    rows_two = units_new.shape[0]
    second_capacity = max(2, 3 * rows_two // (2 * BLOCKS2_DEV * devices))
    buckets_two = BLOCKS2_DEV * devices
    chosen = candidates[:, 0]
    place_two = chosen * second_capacity + slot_ranks(chosen, buckets_two)
    send_two = (
        jnp.zeros((buckets_two * second_capacity, width), jnp.bfloat16).at[place_two].set(units_new)
    )
    send_two = send_two.reshape(devices, BLOCKS2_DEV, second_capacity, width)
    units_two = unit_rows(centroids2).reshape(BLOCKS2_DEV, BLOCK2, width)
    arrived = lax.all_to_all(send_two, "shard", split_axis=0, concat_axis=0, tiled=True)
    items = arrived.shape[2]
    weights_two = [
        kernel_sums(arrived[:, local].reshape(-1, width), units_two[local]).reshape(
            arrived.shape[0], items
        )
        for local in range(BLOCKS2_DEV)
    ]
    returned_two = lax.all_to_all(
        jnp.stack(weights_two, axis=1), "shard", split_axis=0, concat_axis=0, tiled=True
    )
    level_two = jnp.log(returned_two.reshape(-1)[place_two] / BLOCK2)
    return (density, new_centroids, fresh.reshape(-1), level_two)


NT = (((1,), (1,)), ((), ()))
PARAMS = pltpu.CompilerParams(vmem_limit_bytes=48 * 1024 * 1024)
META = 16
HBM = pl.BlockSpec(memory_space=pltpu.HBM)
ANY = pl.BlockSpec(memory_space=pl.ANY)
VMEM = pl.BlockSpec(memory_space=pltpu.VMEM)


def position():
    me = lax.axis_index("shard")
    return me, me // 4, (me // 2) % 2, me % 2


def unit_wide(wide):
    power = jnp.mean(wide * wide, axis=-1, keepdims=True) + 1e-06
    return (wide * lax.rsqrt(power)).astype(jnp.bfloat16)


def weights(scores, width):
    return jnp.exp(scores * (10.0 / width) - 10.0)


def one_hot(hits):
    return jnp.where(hits, 1.0, 0.0).astype(jnp.bfloat16)


def column(row):
    return jnp.transpose(jnp.broadcast_to(row, (8, row.shape[1])))[:, 0:1]


def fetch(pairs, sems):
    copies = [pltpu.make_async_copy(src, dst, sems.at[i]) for i, (src, dst) in enumerate(pairs)]
    for copy in copies:
        copy.start()
    return copies


def pick_rows(slot, first, count):
    return one_hot(slot == lax.broadcasted_iota(jnp.int32, (count, slot.shape[1]), 0) + first)


def pack(slot, prior, cent, first, out):
    count = out.shape[0] - META
    rows = slot.shape[1]
    ident = lax.broadcasted_iota(jnp.int32, (1, rows), 1) + 1
    line = lax.broadcasted_iota(jnp.int32, (META, rows), 0)
    facts = jnp.where(line == 0, ident >> 5, jnp.where(line == 1, ident & 31, jnp.where(line == 2, prior, 0)))
    facts = facts.astype(jnp.float32).astype(jnp.bfloat16)
    pick = pick_rows(slot, first, count)
    out[0:count, :] = jnp.dot(pick, cent, preferred_element_type=jnp.float32).astype(jnp.bfloat16)
    out[count:, :] = jnp.zeros((META, out.shape[1]), jnp.bfloat16)
    out[count:, 0:count] = lax.dot_general(facts, pick, NT, preferred_element_type=jnp.float32).astype(jnp.bfloat16)


def pack_kernel(
    cap, per, cand_any, emb_any, probes_any, assigned_any, prior_any, cent_any, mine, rows2, rows3, info,
    cand_ref, emb_ref, probes_ref, assigned_ref, prior_ref, cent_ref, sems,
):
    copies = fetch(
        (
            (cand_any, cand_ref),
            (emb_any, emb_ref),
            (probes_any, probes_ref),
            (assigned_any, assigned_ref),
            (prior_any, prior_ref),
            (cent_any, cent_ref),
        ),
        sems,
    )
    me, z, y, core = position()
    rows = cand_ref.shape[1]
    buckets = 16 * per
    before = lax.broadcasted_iota(jnp.int32, (rows, rows), 0) <= lax.broadcasted_iota(jnp.int32, (rows, rows), 1)
    before = one_hot(before)
    copies[0].wait()
    cand = cand_ref[...]
    dev = sum((cand >= per * step).astype(jnp.int32) for step in range(1, 16))
    near = dev >> 2
    plane = jnp.where(z >= 2, 3 - near, near)
    rel = (((dev >> 1) & 1) ^ y) * 2 + ((dev & 1) ^ core)
    named = cand == lax.broadcasted_iota(jnp.int32, (buckets, rows), 0)
    counted = jnp.dot(one_hot(named), before, preferred_element_type=jnp.float32)
    rank = jnp.sum(jnp.where(named, counted, 0.0), axis=0, keepdims=True).astype(jnp.int32) - 1
    kind = plane * per + cand - dev * per
    slot = (rel * 4 * per + kind) * cap + rank
    info[0:1, :] = slot
    info[1:2, :] = rel * 4 + (kind >> 2)
    info[2:3, :] = (kind & 3) * cap + rank
    for copy in copies[1:5]:
        copy.wait()
    count, width = emb_ref.shape
    probe_count = probes_ref.shape[0]
    slots = assigned_ref[...]
    facts = jnp.concatenate([probes_ref[...], slots >> 5, slots & 31], axis=0).astype(jnp.float32)
    facts = jnp.concatenate([facts, jnp.zeros((128 - probe_count - 2, count), jnp.float32)], axis=0)
    same = lax.broadcasted_iota(jnp.int32, (count, count), 0) == lax.broadcasted_iota(jnp.int32, (count, count), 1)
    mine[:, 0:width] = emb_ref[...]
    mine[:, width:] = lax.dot_general(
        one_hot(same), facts.astype(jnp.bfloat16), NT, preferred_element_type=jnp.float32
    ).astype(jnp.bfloat16)
    copies[5].wait()
    pack(slot, prior_ref[...], cent_ref[...], 2 * 4 * per * cap, rows2)
    pack(slot, prior_ref[...], cent_ref[...], 3 * 4 * per * cap, rows3)


def pack_more_kernel(part, info, prior_ref, cent_ref, rows0, rows1, late2, late3):
    for first, out in ((0, rows0), (4 * part, rows1), (11 * part, late2), (15 * part, late3)):
        pack(info[0:1, :], prior_ref[...], cent_ref[...], first, out)


def order_kernel(*refs):
    pass


def share_kernel(mine_any, other_any, cent_ref, scaled, facts, share, mine_ref, other_ref, sems):
    copies = fetch(((mine_any, mine_ref), (other_any, other_ref)), sems)
    me, z, y, core = position()
    half = mine_ref.shape[0]
    count = 2 * half
    rows, width = cent_ref.shape
    copies[0].wait()
    scaled[0:half, :] = unit_wide(mine_ref[:, 0:width].astype(jnp.float32))
    copies[1].wait()
    scaled[half:count, :] = unit_wide(other_ref[:, 0:width].astype(jnp.float32))
    aux = jnp.concatenate([mine_ref[:, width:], other_ref[:, width:]], axis=0).astype(jnp.float32)
    aux = jnp.transpose(aux)[0:16, :].astype(jnp.int32)
    facts[...] = aux
    member = jnp.sum((aux[0:8, :] == me).astype(jnp.float32), axis=0, keepdims=True)
    step = 256
    total = jnp.zeros((1, count), jnp.float32)
    for start in range(0, rows, step):
        old = cent_ref[start : start + step, :].astype(jnp.float32)
        scores = lax.dot_general(unit_wide(old), scaled[...], NT, preferred_element_type=jnp.float32)
        total = total + jnp.sum(weights(scores, width), axis=0, keepdims=True)
    piece = count // 16
    lane = lax.broadcasted_iota(jnp.int32, (16, count), 1)
    line = lax.broadcasted_iota(jnp.int32, (16, count), 0)
    apart = jnp.where((member > 0.0) & (lane >= line * piece) & (lane < (line + 1) * piece), total, 0.0)
    spot = lax.broadcasted_iota(jnp.int32, (count, 128), 0)
    block = sum((spot >= piece * step).astype(jnp.int32) for step in range(1, 16))
    together = jnp.where(spot - block * piece == lax.broadcasted_iota(jnp.int32, (count, 128), 1), 1.0, 0.0)
    share[...] = jnp.dot(apart, together, precision=lax.Precision.HIGHEST, preferred_element_type=jnp.float32)


def update_kernel(after, scaled, facts, cent_ref, prior_ref, fresh_rows, fresh_counts):
    me, z, y, core = position()
    rows, width = cent_ref.shape
    count = scaled.shape[0]
    prior = column(prior_ref[...].astype(jnp.float32))
    target = jnp.where(facts[0:1, :] == me, facts[8:9, :] * 32 + facts[9:10, :], -1)
    step = 256
    for start in range(0, rows, step):
        old = cent_ref[start : start + step, :].astype(jnp.float32)
        hits = one_hot(target == lax.broadcasted_iota(jnp.int32, (step, count), 0) + start)
        sums = jnp.dot(hits, scaled[...], preferred_element_type=jnp.float32)
        gained = jnp.sum(hits.astype(jnp.float32), axis=1, keepdims=True)
        ahead = prior[start : start + step, :]
        updated = (ahead * old + sums) / (ahead + gained)
        fresh_rows[start : start + step, :] = updated.astype(jnp.bfloat16)
        gained_row = lax.dot_general(
            jnp.ones((8, count), jnp.bfloat16), hits, NT, preferred_element_type=jnp.float32
        )
        fresh_counts[0:1, start : start + step] = prior_ref[0:1, start : start + step] + gained_row[0:1, :].astype(jnp.int32)


def level_sums(two, rows, per):
    block = two.shape[0] // per
    lines = []
    for j in range(per):
        scores = lax.dot_general(two[j * block : (j + 1) * block, :], rows(j), NT, preferred_element_type=jnp.float32)
        lines.append(jnp.sum(weights(scores, two.shape[1]), axis=0, keepdims=True))
    return jnp.concatenate(lines, axis=0)


def redo(cap, per, scaled, facts_in, source, ref, rows, first, packed, r):
    part = per * cap
    probe0 = facts_in[0:1, :]
    slots = facts_in[8:9, :] * 32 + facts_in[9:10, :]
    facts = jnp.transpose(ref[ref.shape[0] - META :, first : first + rows].astype(jnp.float32))
    hits = (facts[:, 0:1] * 32.0 + facts[:, 1:2]).astype(jnp.int32) == jnp.where(probe0 == source, slots + 1, -1)
    hits = one_hot(hits)
    gained = jnp.sum(hits.astype(jnp.float32), axis=1, keepdims=True)
    added = jnp.dot(hits, scaled[...], preferred_element_type=jnp.float32)
    ahead = facts[:, 2:3]
    wide = (ahead * ref[0:rows, :].astype(jnp.float32) + added) / jnp.maximum(ahead + gained, 1.0)
    unit = unit_wide(wide)
    for w in range(rows // part):
        for j in range(per):
            start = w * part + j * cap
            packed[w, j, r * cap : (r + 1) * cap, :] = unit[start : start + cap, :]


def second_kernel(
    cap, per, scaled, facts_in, own_any, near_any, cross_any, passed_any, any0, any1, any2, any3,
    sums, rows0, rows1, rows2, rows3, two, two_more, two_last, packed, sems,
):
    me, z, y, core = position()
    end = (z == 0) | (z == 3)
    at_end = pltpu.make_async_copy(passed_any, two_last, sems.at[6])
    at_mid = pltpu.make_async_copy(cross_any, two_last, sems.at[6])
    pl.when(end)(at_end.start)
    pl.when(jnp.logical_not(end))(at_mid.start)
    copies = fetch(
        [(any0, rows0), (any1, rows1), (any2, rows2), (any3, rows3), (own_any, two), (near_any, two_more)], sems
    )
    for r, ref in enumerate((rows0, rows1, rows2, rows3)):
        copies[r].wait()
        redo(cap, per, scaled, facts_in, me ^ r, ref, 3 * per * cap, 0, packed, r)
    copies[4].wait()
    copies[5].wait()
    own_unit = unit_wide(two[...].astype(jnp.float32))
    near_unit = unit_wide(two_more[...].astype(jnp.float32))
    first = jnp.where(end, 0, 1)
    sums[pl.ds(first * 8, per), :] = level_sums(own_unit, lambda j: packed[first, j], per)
    sums[pl.ds(8 - first * 8, per), :] = level_sums(near_unit, lambda j: packed[1 - first, j], per)
    pl.when(end)(at_end.wait)
    pl.when(jnp.logical_not(end))(at_mid.wait)
    sums[16 : 16 + per, :] = level_sums(unit_wide(two_last[...].astype(jnp.float32)), lambda j: packed[2, j], per)


def late_kernel(cap, per, scaled, facts_in, any0, any1, any2, any3, kept, rows0, rows1, rows2, rows3, sems):
    me, z, y, core = position()
    part = per * cap
    tail = pl.ds(3 * part, part + META)
    copies = fetch([(any0.at[tail], rows0), (any1.at[tail], rows1), (any2, rows2), (any3, rows3)], sems)
    for r, ref in enumerate((rows0, rows1, rows2, rows3)):
        copies[r].wait()
        redo(cap, per, scaled, facts_in, me ^ r, ref, part, 3 * part if r < 2 else 0, kept, r)


def third_kernel(cap, per, early, share, kept_any, last_any, far_any, out, kept, two, sems):
    me, z, y, core = position()
    end = (z == 0) | (z == 3)
    at_end = pltpu.make_async_copy(far_any, two, sems.at[1])
    at_mid = pltpu.make_async_copy(last_any, two, sems.at[1])
    pl.when(end)(at_end.start)
    pl.when(jnp.logical_not(end))(at_mid.start)
    copies = fetch([(kept_any, kept)], sems)
    pl.when(end)(at_end.wait)
    pl.when(jnp.logical_not(end))(at_mid.wait)
    two_unit = unit_wide(two[...].astype(jnp.float32))
    copies[0].wait()
    final = level_sums(two_unit, lambda j: kept[0, j], per)
    lines = [early[8 * w : 8 * w + per, :] for w in range(3)] + [final]
    together = jnp.concatenate(lines + [jnp.zeros((16 - 4 * per, 4 * cap), jnp.float32)], axis=0)
    lane = lax.broadcasted_iota(jnp.int32, together.shape, 1)
    line = lax.broadcasted_iota(jnp.int32, together.shape, 0)
    out[...] = jnp.zeros(out.shape, jnp.float32)
    for r in range(4):
        spread = jnp.zeros_like(together)
        for s in range(4):
            turned = together if s == r else pltpu.roll(together, ((s - r) % 4) * cap, 1)
            spread = jnp.where((line % 4 == s) & (lane >= s * cap) & (lane < (s + 1) * cap), turned, spread)
        out[me ^ r, 0:4, :] = jnp.concatenate(
            [jnp.sum(spread[4 * t : 4 * t + 4], axis=0, keepdims=True) for t in range(4)], axis=0
        )
    for b in range(16):
        apart = ((b & 1) * 4) ^ ((b >> 1 & 1) * 12) ^ ((b >> 2 & 1) * 2) ^ (b >> 3)
        out[me ^ apart, 4:5, :] = share[b : b + 1, :]


def last_kernel(cap, scale_one, scale_two, info, got, density, level_two):
    me, z, y, core = position()
    total = jnp.zeros((1, 4 * cap), jnp.float32)
    for source in range(16):
        total = total + got[source, 4:5, :]
    density[...] = jnp.log(total[:, 0 : density.shape[1]] / scale_one)
    values = jnp.concatenate([got[me ^ r, 0:4, :] for r in range(4)], axis=0)
    rows = info.shape[1]
    chosen = jnp.where(info[2:3, :] == lax.broadcasted_iota(jnp.int32, (4 * cap, rows), 0), 1.0, 0.0)
    spread = jnp.dot(values, chosen, precision=lax.Precision.HIGHEST, preferred_element_type=jnp.float32)
    found = jnp.where(info[1:2, :] == lax.broadcasted_iota(jnp.int32, (16, rows), 0), spread, 0.0)
    level_two[...] = jnp.log(jnp.sum(found, axis=0, keepdims=True) / scale_two)


def call(kernel, outs, scratch=(), in_specs=None, **kw):
    def run(*args):
        specs = in_specs or [VMEM] * len(args)
        args = [pltpu.with_memory_space_constraint(a, pltpu.HBM) if spec is HBM else a for a, spec in zip(args, specs)]
        return pl.pallas_call(
            kernel, out_shape=outs, in_specs=specs, scratch_shapes=list(scratch), compiler_params=PARAMS, **kw
        )(*args)

    return run


def in_order(*values, **kw):
    count = len(values)
    return call(
        order_kernel,
        tuple(jax.ShapeDtypeStruct(value.shape, value.dtype) for value in values),
        in_specs=[ANY] * count,
        out_specs=(ANY,) * count,
        input_output_aliases={i: i for i in range(count)},
        **kw,
    )(*values)


def line_body(embeddings, probes, assigned, prior_counts, centroids, candidates, centroids2):
    emb_rows, width = embeddings.shape
    probe_count = probes.shape[1]
    rows = centroids.shape[0]
    per = BLOCKS2_DEV
    cap = max(2, 3 * rows // (2 * per * 16))
    part = per * cap
    bf16, f32, i32 = jnp.bfloat16, jnp.float32, jnp.int32
    shape = jax.ShapeDtypeStruct

    def exchange(value, apart, sources=range(16)):
        return lax.ppermute(value, "shard", [(i, i ^ apart) for i in sources])

    def rows_of(planes):
        return shape((planes * part + META, width), bf16)

    def room(like):
        return pltpu.VMEM(like.shape, like.dtype)

    mids = range(4, 12)
    near_set = exchange(centroids2, 4)
    cross_set = exchange(centroids2, 12, mids)
    prior_row = prior_counts.reshape(1, rows)
    line = pltpu.VMEM((1, rows), i32)
    mine, early2, early3, info = call(
        functools.partial(pack_kernel, cap, per),
        (shape((emb_rows, width + 128), bf16), rows_of(3), rows_of(3), shape((8, rows), i32)),
        [
            line,
            pltpu.VMEM((emb_rows, width), bf16),
            pltpu.VMEM((probe_count, emb_rows), i32),
            pltpu.VMEM((1, emb_rows), i32),
            line,
            pltpu.VMEM((rows, width), bf16),
            pltpu.SemaphoreType.DMA((6,)),
        ],
        in_specs=[HBM] * 6,
    )(candidates.reshape(1, rows), embeddings, probes.T, assigned.reshape(1, emb_rows), prior_row, centroids)
    early2, early3 = exchange(early2, 2), exchange(early3, 3)
    rows0, rows1, late2, late3 = call(
        functools.partial(pack_more_kernel, part), (rows_of(4), rows_of(4), rows_of(1), rows_of(1))
    )(info, prior_row, centroids)
    rows1 = exchange(rows1, 1)
    mine = jnp.concatenate([mine, exchange(mine, 4)], axis=0)
    near_set, cross_set, mine = in_order(near_set, cross_set, mine)
    across = exchange(mine, 12)
    passed = exchange(cross_set, 4, mids)
    last_set = exchange(near_set, 12, mids)
    mine = jnp.concatenate([mine, across], axis=0)
    mine, early2, early3, late2, late3 = in_order(mine, early2, early3, late2, late3)
    mine = jnp.concatenate([mine, exchange(mine, 2)], axis=0)
    late2, late3 = exchange(late2, 2), exchange(late3, 3)
    other = exchange(mine, 1)
    step = pl.CostEstimate(flops=0, transcendentals=0, bytes_accessed=40 * centroids2.size * 2)
    passed, last_set = in_order(passed, last_set, cost_estimate=step)
    far_set = exchange(last_set, 4, mids)
    gathered = pltpu.VMEM((8 * emb_rows, width + 128), bf16)
    scaled, facts, share = call(
        share_kernel,
        (
            shape((16 * emb_rows, width), bf16),
            shape((16, 16 * emb_rows), i32),
            shape((16, 4 * cap), f32),
        ),
        [gathered, gathered, pltpu.SemaphoreType.DMA((2,))],
        in_specs=[ANY, ANY, VMEM],
    )(mine, other, centroids)
    block_set = pltpu.VMEM((per * BLOCK2, width), bf16)
    early = call(
        functools.partial(second_kernel, cap, per),
        shape((24, 4 * cap), f32),
        [room(rows_of(4))] * 2
        + [room(rows_of(3))] * 2
        + [block_set] * 3
        + [pltpu.VMEM((3, per, 4 * cap, width), bf16), pltpu.SemaphoreType.DMA((7,))],
        in_specs=[VMEM, VMEM, HBM] + [ANY] * 7,
    )(scaled, facts, centroids2, near_set, cross_set, passed, rows0, rows1, early2, early3)
    kept = shape((1, per, 4 * cap, width), bf16)
    kept_rows = call(
        functools.partial(late_kernel, cap, per),
        kept,
        [room(rows_of(1))] * 4 + [pltpu.SemaphoreType.DMA((4,))],
        in_specs=[VMEM, VMEM] + [ANY] * 4,
    )(scaled, facts, rows0, rows1, late2, late3)
    results = call(
        functools.partial(third_kernel, cap, per),
        shape((16, 8, 4 * cap), f32),
        [room(kept), block_set, pltpu.SemaphoreType.DMA((2,))],
        in_specs=[VMEM, VMEM, ANY, ANY, ANY],
    )(early, share, kept_rows, last_set, far_set)
    new_centroids, counts = call(
        update_kernel, (shape((rows, width), bf16), shape((1, rows), i32)), in_specs=[ANY] + [VMEM] * 4
    )(results, scaled, facts, centroids, prior_row)
    results = lax.all_to_all(results, "shard", split_axis=0, concat_axis=0, tiled=True)
    density, level_two = call(
        functools.partial(last_kernel, cap, probe_count * BLOCK, BLOCK2), (shape((1, emb_rows), f32), shape((1, rows), f32))
    )(info, results)
    return (density.reshape(-1), new_centroids, counts.reshape(-1), level_two.reshape(-1))


def solution(mesh):
    placed = (
        P(("groups", "shard"), None),
        P(("groups", "shard"), None),
        P(("groups", "shard")),
        P(("groups", "shard")),
        P(("groups", "shard"), None),
        P(("groups", "shard"), None),
        P(("groups", "shard"), None),
    )
    body = line_body if mesh.shape["shard"] == 16 else general_body
    return jax.shard_map(
        body,
        mesh=mesh,
        in_specs=placed,
        out_specs=(
            P(("groups", "shard")),
            P(("groups", "shard"), None),
            P(("groups", "shard")),
            P(("groups", "shard")),
        ),
        check_vma=False,
    )
```

```python
import functools

import jax
import jax.numpy as jnp
from jax import lax
from jax.experimental import pallas as pl
from jax.experimental.pallas import tpu as pltpu
from jax.sharding import PartitionSpec as P

BLOCK = 1024
BLOCKS_DEV = 1
BLOCK2 = 128
BLOCKS2_DEV = 3


def unit_rows(values):
    wide = values.astype(jnp.float32)
    power = jnp.mean(wide * wide, axis=-1, keepdims=True) + 1e-06
    return (wide * lax.rsqrt(power)).astype(jnp.bfloat16)


def kernel_sums(rows, unit):
    scores = lax.dot_general(
        rows, unit, (((1,), (1,)), ((), ())), preferred_element_type=jnp.float32
    )
    return jnp.sum(jnp.exp((scores / rows.shape[1] - 1.0) / 0.1), axis=1)


def block_update(rows, slots, width):
    matches = slots[:, None] == jnp.arange(width, dtype=jnp.int32)[None, :]
    sums = lax.dot_general(
        matches.astype(jnp.bfloat16),
        rows,
        (((0,), (0,)), ((), ())),
        preferred_element_type=jnp.float32,
    )
    counts = jnp.sum(matches.astype(jnp.int32), axis=0)
    return (sums, counts)


def slot_ranks(targets, buckets):
    matches = (targets[:, None] == jnp.arange(buckets, dtype=jnp.int32)[None, :]).astype(jnp.int32)
    return jnp.sum(jnp.cumsum(matches, axis=0) * matches, axis=1) - 1


def general_body(embeddings, probes, assigned, prior_counts, centroids, candidates, centroids2):
    devices = lax.axis_size("shard")
    emb_rows, width = embeddings.shape
    probe_count = probes.shape[1]
    capacity = max(2, 2 * emb_rows * probe_count // (BLOCKS_DEV * devices))
    scaled = unit_rows(embeddings)
    units_old = unit_rows(centroids).reshape(BLOCKS_DEV, BLOCK, width)
    total = emb_rows * probe_count
    buckets = BLOCKS_DEV * devices
    flat = probes.reshape(-1)
    place = flat * capacity + slot_ranks(flat, buckets)
    leading = jnp.arange(total, dtype=jnp.int32) % probe_count == 0
    repeated = jnp.repeat(scaled, probe_count, axis=0)
    slot_values = jnp.where(leading, jnp.repeat(assigned, probe_count), -1)
    send_rows = jnp.zeros((buckets * capacity, width), jnp.bfloat16).at[place].set(repeated)
    send_slots = jnp.full((buckets * capacity,), -1, jnp.int32).at[place].set(slot_values)
    got_rows, got_slots = (
        lax.all_to_all(
            send_rows.reshape(devices, BLOCKS_DEV * capacity, width),
            "shard",
            split_axis=0,
            concat_axis=0,
            tiled=True,
        ),
        lax.all_to_all(
            send_slots.reshape(devices, BLOCKS_DEV * capacity),
            "shard",
            split_axis=0,
            concat_axis=0,
            tiled=True,
        ),
    )
    got_rows = got_rows.reshape(devices, BLOCKS_DEV, capacity, width)
    got_slots = got_slots.reshape(devices, BLOCKS_DEV, capacity)
    local = 0
    picked = got_rows[:, local].reshape(devices * capacity, width)
    slots = got_slots[:, local].reshape(-1)
    weights = [kernel_sums(picked, units_old[local]).reshape(devices, capacity)]
    more_sums, more_counts = block_update(picked, slots, BLOCK)
    sum_list = [more_sums]
    count_list = [more_counts]
    sums = jnp.stack(sum_list)
    counts = jnp.stack(count_list)
    returned = lax.all_to_all(
        jnp.stack(weights, axis=1).reshape(devices, BLOCKS_DEV * capacity),
        "shard",
        split_axis=0,
        concat_axis=0,
        tiled=True,
    )
    totals = jnp.sum(returned.reshape(-1)[place].reshape(emb_rows, probe_count), axis=1)
    density = jnp.log(totals / (probe_count * BLOCK))
    prior = prior_counts.reshape(BLOCKS_DEV, BLOCK)
    fresh = prior + counts
    updated = (
        prior.astype(jnp.float32)[:, :, None]
        * centroids.reshape(BLOCKS_DEV, BLOCK, width).astype(jnp.float32)
        + sums
    ) / fresh.astype(jnp.float32)[:, :, None]
    new_centroids = updated.astype(jnp.bfloat16).reshape(BLOCKS_DEV * BLOCK, width)
    units_new = unit_rows(updated).reshape(BLOCKS_DEV * BLOCK, width)
    rows_two = units_new.shape[0]
    second_capacity = max(2, 3 * rows_two // (2 * BLOCKS2_DEV * devices))
    buckets_two = BLOCKS2_DEV * devices
    chosen = candidates[:, 0]
    place_two = chosen * second_capacity + slot_ranks(chosen, buckets_two)
    send_two = (
        jnp.zeros((buckets_two * second_capacity, width), jnp.bfloat16).at[place_two].set(units_new)
    )
    send_two = send_two.reshape(devices, BLOCKS2_DEV, second_capacity, width)
    units_two = unit_rows(centroids2).reshape(BLOCKS2_DEV, BLOCK2, width)
    arrived = lax.all_to_all(send_two, "shard", split_axis=0, concat_axis=0, tiled=True)
    items = arrived.shape[2]
    weights_two = [
        kernel_sums(arrived[:, local].reshape(-1, width), units_two[local]).reshape(
            arrived.shape[0], items
        )
        for local in range(BLOCKS2_DEV)
    ]
    returned_two = lax.all_to_all(
        jnp.stack(weights_two, axis=1), "shard", split_axis=0, concat_axis=0, tiled=True
    )
    level_two = jnp.log(returned_two.reshape(-1)[place_two] / BLOCK2)
    return (density, new_centroids, fresh.reshape(-1), level_two)


NT = (((1,), (1,)), ((), ()))
PARAMS = pltpu.CompilerParams(vmem_limit_bytes=48 * 1024 * 1024)
META = 16
LATE = 5
STEP = 3
HBM = pl.BlockSpec(memory_space=pltpu.HBM)
ANY = pl.BlockSpec(memory_space=pl.ANY)
VMEM = pl.BlockSpec(memory_space=pltpu.VMEM)


def position():
    me = lax.axis_index("shard")
    return me, me // 4, (me // 2) % 2, me % 2


def unit_wide(wide):
    power = jnp.mean(wide * wide, axis=-1, keepdims=True) + 1e-06
    return (wide * lax.rsqrt(power)).astype(jnp.bfloat16)


def weights(scores, width):
    return jnp.exp(scores * (10.0 / width) - 10.0)


def one_hot(hits):
    return jnp.where(hits, 1.0, 0.0).astype(jnp.bfloat16)


def column(row):
    return jnp.transpose(jnp.broadcast_to(row, (8, row.shape[1])))[:, 0:1]


def fetch(pairs, sems):
    copies = [pltpu.make_async_copy(src, dst, sems.at[i]) for i, (src, dst) in enumerate(pairs)]
    for copy in copies:
        copy.start()
    return copies


def pick_rows(slot, first, count):
    return one_hot(slot == lax.broadcasted_iota(jnp.int32, (count, slot.shape[1]), 0) + first)


def pack(slot, prior, cent, first, out):
    count = out.shape[0] - META
    rows = slot.shape[1]
    ident = lax.broadcasted_iota(jnp.int32, (1, rows), 1) + 1
    line = lax.broadcasted_iota(jnp.int32, (META, rows), 0)
    facts = jnp.where(line == 0, ident >> 5, jnp.where(line == 1, ident & 31, jnp.where(line == 2, prior, 0)))
    facts = facts.astype(jnp.float32).astype(jnp.bfloat16)
    pick = pick_rows(slot, first, count)
    out[0:count, :] = jnp.dot(pick, cent, preferred_element_type=jnp.float32).astype(jnp.bfloat16)
    out[count:, :] = jnp.zeros((META, out.shape[1]), jnp.bfloat16)
    out[count:, 0:count] = lax.dot_general(facts, pick, NT, preferred_element_type=jnp.float32).astype(jnp.bfloat16)


def pack_kernel(
    cap, per, cand_any, emb_any, probes_any, assigned_any, prior_any, cent_any, mine, rows2, rows3, info,
    cand_ref, emb_ref, probes_ref, assigned_ref, prior_ref, cent_ref, sems,
):
    copies = fetch(
        (
            (cand_any, cand_ref),
            (emb_any, emb_ref),
            (probes_any, probes_ref),
            (assigned_any, assigned_ref),
            (prior_any, prior_ref),
            (cent_any, cent_ref),
        ),
        sems,
    )
    me, z, y, core = position()
    rows = cand_ref.shape[1]
    buckets = 16 * per
    before = lax.broadcasted_iota(jnp.int32, (rows, rows), 0) <= lax.broadcasted_iota(jnp.int32, (rows, rows), 1)
    before = one_hot(before)
    copies[0].wait()
    cand = cand_ref[...]
    dev = sum((cand >= per * step).astype(jnp.int32) for step in range(1, 16))
    near = dev >> 2
    plane = jnp.where(z >= 2, 3 - near, near)
    rel = (((dev >> 1) & 1) ^ y) * 2 + ((dev & 1) ^ core)
    named = cand == lax.broadcasted_iota(jnp.int32, (buckets, rows), 0)
    counted = jnp.dot(one_hot(named), before, preferred_element_type=jnp.float32)
    rank = jnp.sum(jnp.where(named, counted, 0.0), axis=0, keepdims=True).astype(jnp.int32) - 1
    kind = plane * per + cand - dev * per
    slot = (rel * 4 * per + kind) * cap + rank
    info[0:1, :] = slot
    info[1:2, :] = rel * 4 + (kind >> 2)
    info[2:3, :] = (kind & 3) * cap + rank
    for copy in copies[1:5]:
        copy.wait()
    count, width = emb_ref.shape
    probe_count = probes_ref.shape[0]
    slots = assigned_ref[...]
    facts = jnp.concatenate([probes_ref[...], slots >> 5, slots & 31], axis=0).astype(jnp.float32)
    facts = jnp.concatenate([facts, jnp.zeros((128 - probe_count - 2, count), jnp.float32)], axis=0)
    same = lax.broadcasted_iota(jnp.int32, (count, count), 0) == lax.broadcasted_iota(jnp.int32, (count, count), 1)
    mine[:, 0:width] = emb_ref[...]
    mine[:, width:] = lax.dot_general(
        one_hot(same), facts.astype(jnp.bfloat16), NT, preferred_element_type=jnp.float32
    ).astype(jnp.bfloat16)
    copies[5].wait()
    pack(slot, prior_ref[...], cent_ref[...], 2 * 4 * per * cap, rows2)
    pack(slot, prior_ref[...], cent_ref[...], 3 * 4 * per * cap, rows3)


def pack_more_kernel(part, info, prior_ref, cent_ref, rows0, rows1, late2, late3):
    for first, out in ((0, rows0), (4 * part, rows1), (10 * part, late2), (14 * part, late3)):
        pack(info[0:1, :], prior_ref[...], cent_ref[...], first, out)


def order_kernel(*refs):
    pass


def share_kernel(mine_any, other_any, cent_ref, scaled, facts, share, mine_ref, other_ref, sems):
    copies = fetch(((mine_any, mine_ref), (other_any, other_ref)), sems)
    me, z, y, core = position()
    half = mine_ref.shape[0]
    count = 2 * half
    rows, width = cent_ref.shape
    copies[0].wait()
    scaled[0:half, :] = unit_wide(mine_ref[:, 0:width].astype(jnp.float32))
    copies[1].wait()
    scaled[half:count, :] = unit_wide(other_ref[:, 0:width].astype(jnp.float32))
    aux = jnp.concatenate([mine_ref[:, width:], other_ref[:, width:]], axis=0).astype(jnp.float32)
    aux = jnp.transpose(aux)[0:16, :].astype(jnp.int32)
    facts[...] = aux
    member = jnp.sum((aux[0:8, :] == me).astype(jnp.float32), axis=0, keepdims=True)
    step = 256
    total = jnp.zeros((1, count), jnp.float32)
    for start in range(0, rows, step):
        old = cent_ref[start : start + step, :].astype(jnp.float32)
        scores = lax.dot_general(unit_wide(old), scaled[...], NT, preferred_element_type=jnp.float32)
        total = total + jnp.sum(weights(scores, width), axis=0, keepdims=True)
    piece = count // 16
    lane = lax.broadcasted_iota(jnp.int32, (16, count), 1)
    line = lax.broadcasted_iota(jnp.int32, (16, count), 0)
    apart = jnp.where((member > 0.0) & (lane >= line * piece) & (lane < (line + 1) * piece), total, 0.0)
    spot = lax.broadcasted_iota(jnp.int32, (count, 128), 0)
    block = sum((spot >= piece * step).astype(jnp.int32) for step in range(1, 16))
    together = jnp.where(spot - block * piece == lax.broadcasted_iota(jnp.int32, (count, 128), 1), 1.0, 0.0)
    share[...] = jnp.dot(apart, together, precision=lax.Precision.HIGHEST, preferred_element_type=jnp.float32)


def update_kernel(after, scaled, facts, cent_ref, prior_ref, fresh_rows, fresh_counts):
    me, z, y, core = position()
    rows, width = cent_ref.shape
    count = scaled.shape[0]
    prior = column(prior_ref[...].astype(jnp.float32))
    target = jnp.where(facts[0:1, :] == me, facts[8:9, :] * 32 + facts[9:10, :], -1)
    step = 256
    for start in range(0, rows, step):
        old = cent_ref[start : start + step, :].astype(jnp.float32)
        hits = one_hot(target == lax.broadcasted_iota(jnp.int32, (step, count), 0) + start)
        sums = jnp.dot(hits, scaled[...], preferred_element_type=jnp.float32)
        gained = jnp.sum(hits.astype(jnp.float32), axis=1, keepdims=True)
        ahead = prior[start : start + step, :]
        updated = (ahead * old + sums) * (1.0 / (ahead + gained))
        fresh_rows[start : start + step, :] = updated.astype(jnp.bfloat16)
        gained_row = lax.dot_general(
            jnp.ones((8, count), jnp.bfloat16), hits, NT, preferred_element_type=jnp.float32
        )
        fresh_counts[0:1, start : start + step] = prior_ref[0:1, start : start + step] + gained_row[0:1, :].astype(jnp.int32)


def level_sums(two, rows, per):
    block = two.shape[0] // per
    lines = []
    for j in range(per):
        scores = lax.dot_general(two[j * block : (j + 1) * block, :], rows(j), NT, preferred_element_type=jnp.float32)
        lines.append(jnp.sum(weights(scores, two.shape[1]), axis=0, keepdims=True))
    return jnp.concatenate(lines, axis=0)


def redo(cap, per, scaled, facts_in, me, refs, firsts, packed):
    part = per * cap
    count = 2 * part
    probe0 = facts_in[0:1, :]
    slots = facts_in[8:9, :] * 32 + facts_in[9:10, :]
    for r, (ref, first) in enumerate(zip(refs, firsts)):
        facts = jnp.transpose(ref[ref.shape[0] - META :, first : first + count].astype(jnp.float32))
        hits = (facts[:, 0:1] * 32.0 + facts[:, 1:2]).astype(jnp.int32) == jnp.where(probe0 == (me ^ r), slots + 1, -1)
        hits = one_hot(hits)
        gained = jnp.sum(hits.astype(jnp.float32), axis=1, keepdims=True)
        ahead = facts[:, 2:3]
        fresh = jnp.maximum(ahead + gained, 1.0)
        floor = fresh * fresh * 1e-06
        added = jnp.dot(hits, scaled[...], preferred_element_type=jnp.float32)
        whole = ahead * ref[0:count, :].astype(jnp.float32) + added
        power = jnp.mean(whole * whole, axis=-1, keepdims=True) + floor
        unit = (whole * lax.rsqrt(power)).astype(jnp.bfloat16)
        for w in range(2):
            for j in range(per):
                start = w * part + j * cap
                packed[w, j, r * cap : (r + 1) * cap, :] = unit[start : start + cap, :]


def early_kernel(
    cap, per, scaled, facts_in, own_any, near_any, any0, any1, any2, any3,
    sums, rows0, rows1, rows2, rows3, two, two_more, packed, sems,
):
    me, z, y, core = position()
    end = (z == 0) | (z == 3)
    refs = (rows0, rows1, rows2, rows3)
    copies = fetch(list(zip((any0, any1, any2, any3, own_any, near_any), (*refs, two, two_more))), sems)
    for copy in copies:
        copy.wait()
    redo(cap, per, scaled, facts_in, me, refs, (0, 0, 0, 0), packed)
    own_unit = unit_wide(two[...].astype(jnp.float32))
    near_unit = unit_wide(two_more[...].astype(jnp.float32))
    first = jnp.where(end, 0, 1)
    sums[pl.ds(first * 8, per), :] = level_sums(own_unit, lambda j: packed[first, j], per)
    sums[pl.ds(8 - first * 8, per), :] = level_sums(near_unit, lambda j: packed[1 - first, j], per)


def late_kernel(
    cap, per, scaled, facts_in, cross_any, passed_any, any0, any1, any2, any3, after,
    sums, kept, rows0, rows1, rows2, rows3, two, packed, sems,
):
    me, z, y, core = position()
    end = (z == 0) | (z == 3)
    part = per * cap
    at_end = pltpu.make_async_copy(passed_any, two, sems.at[4])
    at_mid = pltpu.make_async_copy(cross_any, two, sems.at[4])
    pl.when(end)(at_end.start)
    pl.when(jnp.logical_not(end))(at_mid.start)
    tail = pl.ds(2 * part, 2 * part + META)
    refs = (rows0, rows1, rows2, rows3)
    copies = fetch(list(zip((any0.at[tail], any1.at[tail], any2, any3), refs)), sems)
    for copy in copies:
        copy.wait()
    redo(cap, per, scaled, facts_in, me, refs, (2 * part, 2 * part, 0, 0), packed)
    kept[...] = packed[1]
    pl.when(end)(at_end.wait)
    pl.when(jnp.logical_not(end))(at_mid.wait)
    sums[0:per, :] = level_sums(unit_wide(two[...].astype(jnp.float32)), lambda j: packed[0, j], per)


def third_kernel(cap, per, early, later, share, kept_any, last_any, far_any, out, kept, two, sems):
    me, z, y, core = position()
    end = (z == 0) | (z == 3)
    at_end = pltpu.make_async_copy(far_any, two, sems.at[1])
    at_mid = pltpu.make_async_copy(last_any, two, sems.at[1])
    pl.when(end)(at_end.start)
    pl.when(jnp.logical_not(end))(at_mid.start)
    copies = fetch([(kept_any, kept)], sems)
    pl.when(end)(at_end.wait)
    pl.when(jnp.logical_not(end))(at_mid.wait)
    two_unit = unit_wide(two[...].astype(jnp.float32))
    copies[0].wait()
    final = level_sums(two_unit, lambda j: kept[j], per)
    lines = [early[0:per, :], early[8 : 8 + per, :], later[0:per, :], final]
    together = jnp.concatenate(lines + [jnp.zeros((16 - 4 * per, 4 * cap), jnp.float32)], axis=0)
    lane = lax.broadcasted_iota(jnp.int32, together.shape, 1)
    line = lax.broadcasted_iota(jnp.int32, together.shape, 0)
    out[...] = jnp.zeros(out.shape, jnp.float32)
    for r in range(4):
        spread = jnp.zeros_like(together)
        for s in range(4):
            turned = together if s == r else pltpu.roll(together, ((s - r) % 4) * cap, 1)
            spread = jnp.where((line % 4 == s) & (lane >= s * cap) & (lane < (s + 1) * cap), turned, spread)
        out[me ^ r, 0:4, :] = jnp.concatenate(
            [jnp.sum(spread[4 * t : 4 * t + 4], axis=0, keepdims=True) for t in range(4)], axis=0
        )
    for b in range(16):
        apart = ((b & 1) * 4) ^ ((b >> 1 & 1) * 12) ^ ((b >> 2 & 1) * 2) ^ (b >> 3)
        out[me ^ apart, 4:5, :] = share[b : b + 1, :]


def last_kernel(cap, scale_one, scale_two, info, got, density, level_two):
    me, z, y, core = position()
    total = jnp.zeros((1, 4 * cap), jnp.float32)
    for source in range(16):
        total = total + got[source, 4:5, :]
    density[...] = jnp.log(total[:, 0 : density.shape[1]] / scale_one)
    values = jnp.concatenate([got[me ^ r, 0:4, :] for r in range(4)], axis=0)
    rows = info.shape[1]
    chosen = jnp.where(info[2:3, :] == lax.broadcasted_iota(jnp.int32, (4 * cap, rows), 0), 1.0, 0.0)
    spread = jnp.dot(values, chosen, precision=lax.Precision.HIGHEST, preferred_element_type=jnp.float32)
    found = jnp.where(info[1:2, :] == lax.broadcasted_iota(jnp.int32, (16, rows), 0), spread, 0.0)
    level_two[...] = jnp.log(jnp.sum(found, axis=0, keepdims=True) / scale_two)


def call(kernel, outs, scratch=(), in_specs=None, **kw):
    def run(*args):
        specs = in_specs or [VMEM] * len(args)
        args = [pltpu.with_memory_space_constraint(a, pltpu.HBM) if spec is HBM else a for a, spec in zip(args, specs)]
        return pl.pallas_call(
            kernel, out_shape=outs, in_specs=specs, scratch_shapes=list(scratch), compiler_params=PARAMS, **kw
        )(*args)

    return run


def lasting(micros):
    return pl.CostEstimate(flops=0, transcendentals=0, bytes_accessed=int(micros * 3_690_000))


def in_order(*values, **kw):
    count = len(values)
    return call(
        order_kernel,
        tuple(jax.ShapeDtypeStruct(value.shape, value.dtype) for value in values),
        in_specs=[ANY] * count,
        out_specs=(ANY,) * count,
        input_output_aliases={i: i for i in range(count)},
        **kw,
    )(*values)


def line_body(embeddings, probes, assigned, prior_counts, centroids, candidates, centroids2):
    emb_rows, width = embeddings.shape
    probe_count = probes.shape[1]
    rows = centroids.shape[0]
    per = BLOCKS2_DEV
    cap = max(2, 3 * rows // (2 * per * 16))
    part = per * cap
    bf16, f32, i32 = jnp.bfloat16, jnp.float32, jnp.int32
    shape = jax.ShapeDtypeStruct

    def exchange(value, apart, sources=range(16)):
        return lax.ppermute(value, "shard", [(i, i ^ apart) for i in sources])

    def rows_of(planes):
        return shape((planes * part + META, width), bf16)

    def room(like):
        return pltpu.VMEM(like.shape, like.dtype)

    mids = range(4, 12)
    near_set = exchange(centroids2, 4)
    cross_set = exchange(centroids2, 12, mids)
    prior_row = prior_counts.reshape(1, rows)
    line = pltpu.VMEM((1, rows), i32)
    mine, early2, early3, info = call(
        functools.partial(pack_kernel, cap, per),
        (shape((emb_rows, width + 128), bf16), rows_of(2), rows_of(2), shape((8, rows), i32)),
        [
            line,
            pltpu.VMEM((emb_rows, width), bf16),
            pltpu.VMEM((probe_count, emb_rows), i32),
            pltpu.VMEM((1, emb_rows), i32),
            line,
            pltpu.VMEM((rows, width), bf16),
            pltpu.SemaphoreType.DMA((6,)),
        ],
        in_specs=[HBM] * 6,
    )(candidates.reshape(1, rows), embeddings, probes.T, assigned.reshape(1, emb_rows), prior_row, centroids)
    early2, early3 = exchange(early2, 2), exchange(early3, 3)
    rows0, rows1, late2, late3 = call(
        functools.partial(pack_more_kernel, part), (rows_of(4), rows_of(4), rows_of(2), rows_of(2))
    )(info, prior_row, centroids)
    rows1 = exchange(rows1, 1)
    mine = jnp.concatenate([mine, exchange(mine, 4)], axis=0)
    near_set, cross_set, mine = in_order(near_set, cross_set, mine)
    across = exchange(mine, 12)
    passed = exchange(cross_set, 4, mids)
    last_set = exchange(near_set, 12, mids)
    mine = jnp.concatenate([mine, across], axis=0)
    mine, early2, early3, late2, late3 = in_order(mine, early2, early3, late2, late3)
    mine = jnp.concatenate([mine, exchange(mine, 2)], axis=0)
    late2, late3 = exchange(late2, 2), exchange(late3, 3)
    passed, last_set, mine = in_order(passed, last_set, mine, cost_estimate=lasting(STEP))
    far_set = exchange(last_set, 4, mids)
    other = exchange(mine, 1)
    gathered = pltpu.VMEM((8 * emb_rows, width + 128), bf16)
    scaled, facts, share = call(
        share_kernel,
        (
            shape((16 * emb_rows, width), bf16),
            shape((16, 16 * emb_rows), i32),
            shape((16, 4 * cap), f32),
        ),
        [gathered, gathered, pltpu.SemaphoreType.DMA((2,))],
        in_specs=[ANY, ANY, VMEM],
        cost_estimate=lasting(3),
    )(mine, other, centroids)
    block_set = pltpu.VMEM((per * BLOCK2, width), bf16)
    packed = pltpu.VMEM((2, per, 4 * cap, width), bf16)
    early = call(
        functools.partial(early_kernel, cap, per),
        shape((16, 4 * cap), f32),
        [room(rows_of(4))] * 2 + [room(rows_of(2))] * 2 + [block_set] * 2 + [packed, pltpu.SemaphoreType.DMA((6,))],
        in_specs=[VMEM, VMEM, HBM] + [ANY] * 5,
        cost_estimate=lasting(5),
    )(scaled, facts, centroids2, near_set, rows0, rows1, early2, early3)
    kept = shape((per, 4 * cap, width), bf16)
    later, kept_rows = call(
        functools.partial(late_kernel, cap, per),
        (shape((8, 4 * cap), f32), kept),
        [room(rows_of(2))] * 4 + [block_set, packed, pltpu.SemaphoreType.DMA((5,))],
        in_specs=[VMEM, VMEM] + [ANY] * 7,
        cost_estimate=lasting(LATE),
    )(scaled, facts, cross_set, passed, rows0, rows1, late2, late3, early)
    results = call(
        functools.partial(third_kernel, cap, per),
        shape((16, 8, 4 * cap), f32),
        [room(kept), block_set, pltpu.SemaphoreType.DMA((2,))],
        in_specs=[VMEM, VMEM, VMEM, ANY, ANY, ANY],
        cost_estimate=lasting(1),
    )(early, later, share, kept_rows, last_set, far_set)
    new_centroids, counts = call(
        update_kernel, (shape((rows, width), bf16), shape((1, rows), i32)), in_specs=[ANY] + [VMEM] * 4
    )(results, scaled, facts, centroids, prior_row)
    results = lax.all_to_all(results, "shard", split_axis=0, concat_axis=0, tiled=True)
    density, level_two = call(
        functools.partial(last_kernel, cap, probe_count * BLOCK, BLOCK2), (shape((1, emb_rows), f32), shape((1, rows), f32))
    )(info, results)
    return (density.reshape(-1), new_centroids, counts.reshape(-1), level_two.reshape(-1))


def solution(mesh):
    placed = (
        P(("groups", "shard"), None),
        P(("groups", "shard"), None),
        P(("groups", "shard")),
        P(("groups", "shard")),
        P(("groups", "shard"), None),
        P(("groups", "shard"), None),
        P(("groups", "shard"), None),
    )
    body = line_body if mesh.shape["shard"] == 16 else general_body
    return jax.shard_map(
        body,
        mesh=mesh,
        in_specs=placed,
        out_specs=(
            P(("groups", "shard")),
            P(("groups", "shard"), None),
            P(("groups", "shard")),
            P(("groups", "shard")),
        ),
        check_vma=False,
    )
```

```python
import functools

import jax
import jax.numpy as jnp
from jax import lax
from jax.experimental import pallas as pl
from jax.experimental.pallas import tpu as pltpu
from jax.sharding import PartitionSpec as P

BLOCK = 1024
BLOCKS_DEV = 1
BLOCK2 = 128
BLOCKS2_DEV = 3


def unit_rows(values):
    wide = values.astype(jnp.float32)
    power = jnp.mean(wide * wide, axis=-1, keepdims=True) + 1e-06
    return (wide * lax.rsqrt(power)).astype(jnp.bfloat16)


def kernel_sums(rows, unit):
    scores = lax.dot_general(
        rows, unit, (((1,), (1,)), ((), ())), preferred_element_type=jnp.float32
    )
    return jnp.sum(jnp.exp((scores / rows.shape[1] - 1.0) / 0.1), axis=1)


def block_update(rows, slots, width):
    matches = slots[:, None] == jnp.arange(width, dtype=jnp.int32)[None, :]
    sums = lax.dot_general(
        matches.astype(jnp.bfloat16),
        rows,
        (((0,), (0,)), ((), ())),
        preferred_element_type=jnp.float32,
    )
    counts = jnp.sum(matches.astype(jnp.int32), axis=0)
    return (sums, counts)


def slot_ranks(targets, buckets):
    matches = (targets[:, None] == jnp.arange(buckets, dtype=jnp.int32)[None, :]).astype(jnp.int32)
    return jnp.sum(jnp.cumsum(matches, axis=0) * matches, axis=1) - 1


def general_body(embeddings, probes, assigned, prior_counts, centroids, candidates, centroids2):
    devices = lax.axis_size("shard")
    emb_rows, width = embeddings.shape
    probe_count = probes.shape[1]
    capacity = max(2, 2 * emb_rows * probe_count // (BLOCKS_DEV * devices))
    scaled = unit_rows(embeddings)
    units_old = unit_rows(centroids).reshape(BLOCKS_DEV, BLOCK, width)
    total = emb_rows * probe_count
    buckets = BLOCKS_DEV * devices
    flat = probes.reshape(-1)
    place = flat * capacity + slot_ranks(flat, buckets)
    leading = jnp.arange(total, dtype=jnp.int32) % probe_count == 0
    repeated = jnp.repeat(scaled, probe_count, axis=0)
    slot_values = jnp.where(leading, jnp.repeat(assigned, probe_count), -1)
    send_rows = jnp.zeros((buckets * capacity, width), jnp.bfloat16).at[place].set(repeated)
    send_slots = jnp.full((buckets * capacity,), -1, jnp.int32).at[place].set(slot_values)
    got_rows, got_slots = (
        lax.all_to_all(
            send_rows.reshape(devices, BLOCKS_DEV * capacity, width),
            "shard",
            split_axis=0,
            concat_axis=0,
            tiled=True,
        ),
        lax.all_to_all(
            send_slots.reshape(devices, BLOCKS_DEV * capacity),
            "shard",
            split_axis=0,
            concat_axis=0,
            tiled=True,
        ),
    )
    got_rows = got_rows.reshape(devices, BLOCKS_DEV, capacity, width)
    got_slots = got_slots.reshape(devices, BLOCKS_DEV, capacity)
    local = 0
    picked = got_rows[:, local].reshape(devices * capacity, width)
    slots = got_slots[:, local].reshape(-1)
    weights = [kernel_sums(picked, units_old[local]).reshape(devices, capacity)]
    more_sums, more_counts = block_update(picked, slots, BLOCK)
    sum_list = [more_sums]
    count_list = [more_counts]
    sums = jnp.stack(sum_list)
    counts = jnp.stack(count_list)
    returned = lax.all_to_all(
        jnp.stack(weights, axis=1).reshape(devices, BLOCKS_DEV * capacity),
        "shard",
        split_axis=0,
        concat_axis=0,
        tiled=True,
    )
    totals = jnp.sum(returned.reshape(-1)[place].reshape(emb_rows, probe_count), axis=1)
    density = jnp.log(totals / (probe_count * BLOCK))
    prior = prior_counts.reshape(BLOCKS_DEV, BLOCK)
    fresh = prior + counts
    updated = (
        prior.astype(jnp.float32)[:, :, None]
        * centroids.reshape(BLOCKS_DEV, BLOCK, width).astype(jnp.float32)
        + sums
    ) / fresh.astype(jnp.float32)[:, :, None]
    new_centroids = updated.astype(jnp.bfloat16).reshape(BLOCKS_DEV * BLOCK, width)
    units_new = unit_rows(updated).reshape(BLOCKS_DEV * BLOCK, width)
    rows_two = units_new.shape[0]
    second_capacity = max(2, 3 * rows_two // (2 * BLOCKS2_DEV * devices))
    buckets_two = BLOCKS2_DEV * devices
    chosen = candidates[:, 0]
    place_two = chosen * second_capacity + slot_ranks(chosen, buckets_two)
    send_two = (
        jnp.zeros((buckets_two * second_capacity, width), jnp.bfloat16).at[place_two].set(units_new)
    )
    send_two = send_two.reshape(devices, BLOCKS2_DEV, second_capacity, width)
    units_two = unit_rows(centroids2).reshape(BLOCKS2_DEV, BLOCK2, width)
    arrived = lax.all_to_all(send_two, "shard", split_axis=0, concat_axis=0, tiled=True)
    items = arrived.shape[2]
    weights_two = [
        kernel_sums(arrived[:, local].reshape(-1, width), units_two[local]).reshape(
            arrived.shape[0], items
        )
        for local in range(BLOCKS2_DEV)
    ]
    returned_two = lax.all_to_all(
        jnp.stack(weights_two, axis=1), "shard", split_axis=0, concat_axis=0, tiled=True
    )
    level_two = jnp.log(returned_two.reshape(-1)[place_two] / BLOCK2)
    return (density, new_centroids, fresh.reshape(-1), level_two)


NT = (((1,), (1,)), ((), ()))
PARAMS = pltpu.CompilerParams(vmem_limit_bytes=48 * 1024 * 1024)
META = 16
LATE = 5
STEP = 40
HBM = pl.BlockSpec(memory_space=pltpu.HBM)
ANY = pl.BlockSpec(memory_space=pl.ANY)
VMEM = pl.BlockSpec(memory_space=pltpu.VMEM)


def position():
    me = lax.axis_index("shard")
    return me, me // 4, (me // 2) % 2, me % 2


def unit_wide(wide):
    power = jnp.mean(wide * wide, axis=-1, keepdims=True) + 1e-06
    return (wide * lax.rsqrt(power)).astype(jnp.bfloat16)


def weights(scores, width):
    return jnp.exp(scores * (10.0 / width) - 10.0)


def one_hot(hits):
    return jnp.where(hits, 1.0, 0.0).astype(jnp.bfloat16)


def column(row):
    return jnp.transpose(jnp.broadcast_to(row, (8, row.shape[1])))[:, 0:1]


def fetch(pairs, sems):
    copies = [pltpu.make_async_copy(src, dst, sems.at[i]) for i, (src, dst) in enumerate(pairs)]
    for copy in copies:
        copy.start()
    return copies


def pick_rows(slot, first, count):
    return one_hot(slot == lax.broadcasted_iota(jnp.int32, (count, slot.shape[1]), 0) + first)


def pack(slot, prior, cent, first, out):
    count = out.shape[0] - META
    rows = slot.shape[1]
    ident = lax.broadcasted_iota(jnp.int32, (1, rows), 1) + 1
    line = lax.broadcasted_iota(jnp.int32, (META, rows), 0)
    facts = jnp.where(line == 0, ident >> 5, jnp.where(line == 1, ident & 31, jnp.where(line == 2, prior, 0)))
    facts = facts.astype(jnp.float32).astype(jnp.bfloat16)
    pick = pick_rows(slot, first, count)
    out[0:count, :] = jnp.dot(pick, cent, preferred_element_type=jnp.float32).astype(jnp.bfloat16)
    out[count:, :] = jnp.zeros((META, out.shape[1]), jnp.bfloat16)
    out[count:, 0:count] = lax.dot_general(facts, pick, NT, preferred_element_type=jnp.float32).astype(jnp.bfloat16)


def pack_kernel(
    cap, per, cand_any, emb_any, probes_any, assigned_any, prior_any, cent_any, mine, rows2, rows3, info,
    cand_ref, emb_ref, probes_ref, assigned_ref, prior_ref, cent_ref, sems,
):
    copies = fetch(
        (
            (cand_any, cand_ref),
            (emb_any, emb_ref),
            (probes_any, probes_ref),
            (assigned_any, assigned_ref),
            (prior_any, prior_ref),
            (cent_any, cent_ref),
        ),
        sems,
    )
    me, z, y, core = position()
    rows = cand_ref.shape[1]
    buckets = 16 * per
    before = lax.broadcasted_iota(jnp.int32, (rows, rows), 0) <= lax.broadcasted_iota(jnp.int32, (rows, rows), 1)
    before = one_hot(before)
    copies[0].wait()
    cand = cand_ref[...]
    dev = sum((cand >= per * step).astype(jnp.int32) for step in range(1, 16))
    near = dev >> 2
    plane = jnp.where(z >= 2, 3 - near, near)
    rel = (((dev >> 1) & 1) ^ y) * 2 + ((dev & 1) ^ core)
    named = cand == lax.broadcasted_iota(jnp.int32, (buckets, rows), 0)
    counted = jnp.dot(one_hot(named), before, preferred_element_type=jnp.float32)
    rank = jnp.sum(jnp.where(named, counted, 0.0), axis=0, keepdims=True).astype(jnp.int32) - 1
    kind = plane * per + cand - dev * per
    slot = (rel * 4 * per + kind) * cap + rank
    info[0:1, :] = slot
    info[1:2, :] = rel * 4 + (kind >> 2)
    info[2:3, :] = (kind & 3) * cap + rank
    for copy in copies[1:5]:
        copy.wait()
    count, width = emb_ref.shape
    probe_count = probes_ref.shape[0]
    slots = assigned_ref[...]
    facts = jnp.concatenate([probes_ref[...], slots >> 5, slots & 31], axis=0).astype(jnp.float32)
    facts = jnp.concatenate([facts, jnp.zeros((128 - probe_count - 2, count), jnp.float32)], axis=0)
    same = lax.broadcasted_iota(jnp.int32, (count, count), 0) == lax.broadcasted_iota(jnp.int32, (count, count), 1)
    mine[:, 0:width] = emb_ref[...]
    mine[:, width:] = lax.dot_general(
        one_hot(same), facts.astype(jnp.bfloat16), NT, preferred_element_type=jnp.float32
    ).astype(jnp.bfloat16)
    copies[5].wait()
    pack(slot, prior_ref[...], cent_ref[...], 2 * 4 * per * cap, rows2)
    pack(slot, prior_ref[...], cent_ref[...], 3 * 4 * per * cap, rows3)


def pack_more_kernel(part, info, prior_ref, cent_ref, rows0, rows1, late2, late3):
    for first, out in ((0, rows0), (4 * part, rows1), (10 * part, late2), (14 * part, late3)):
        pack(info[0:1, :], prior_ref[...], cent_ref[...], first, out)


def order_kernel(*refs):
    pass


def share_kernel(mine_any, other_any, cent_ref, scaled, facts, share, mine_ref, other_ref, sems):
    copies = fetch(((mine_any, mine_ref), (other_any, other_ref)), sems)
    me, z, y, core = position()
    half = mine_ref.shape[0]
    count = 2 * half
    rows, width = cent_ref.shape
    copies[0].wait()
    scaled[0:half, :] = unit_wide(mine_ref[:, 0:width].astype(jnp.float32))
    copies[1].wait()
    scaled[half:count, :] = unit_wide(other_ref[:, 0:width].astype(jnp.float32))
    aux = jnp.concatenate([mine_ref[:, width:], other_ref[:, width:]], axis=0).astype(jnp.float32)
    aux = jnp.transpose(aux)[0:16, :].astype(jnp.int32)
    facts[...] = aux
    member = jnp.sum((aux[0:8, :] == me).astype(jnp.float32), axis=0, keepdims=True)
    step = 256
    total = jnp.zeros((1, count), jnp.float32)
    for start in range(0, rows, step):
        old = cent_ref[start : start + step, :].astype(jnp.float32)
        scores = lax.dot_general(unit_wide(old), scaled[...], NT, preferred_element_type=jnp.float32)
        total = total + jnp.sum(weights(scores, width), axis=0, keepdims=True)
    piece = count // 16
    lane = lax.broadcasted_iota(jnp.int32, (16, count), 1)
    line = lax.broadcasted_iota(jnp.int32, (16, count), 0)
    apart = jnp.where((member > 0.0) & (lane >= line * piece) & (lane < (line + 1) * piece), total, 0.0)
    spot = lax.broadcasted_iota(jnp.int32, (count, 128), 0)
    block = sum((spot >= piece * step).astype(jnp.int32) for step in range(1, 16))
    together = jnp.where(spot - block * piece == lax.broadcasted_iota(jnp.int32, (count, 128), 1), 1.0, 0.0)
    share[...] = jnp.dot(apart, together, precision=lax.Precision.HIGHEST, preferred_element_type=jnp.float32)


def update_kernel(after, scaled, facts, cent_ref, prior_ref, fresh_rows, fresh_counts):
    me, z, y, core = position()
    rows, width = cent_ref.shape
    count = scaled.shape[0]
    prior = column(prior_ref[...].astype(jnp.float32))
    target = jnp.where(facts[0:1, :] == me, facts[8:9, :] * 32 + facts[9:10, :], -1)
    step = 256
    for start in range(0, rows, step):
        old = cent_ref[start : start + step, :].astype(jnp.float32)
        hits = one_hot(target == lax.broadcasted_iota(jnp.int32, (step, count), 0) + start)
        sums = jnp.dot(hits, scaled[...], preferred_element_type=jnp.float32)
        gained = jnp.sum(hits.astype(jnp.float32), axis=1, keepdims=True)
        ahead = prior[start : start + step, :]
        updated = (ahead * old + sums) * (1.0 / (ahead + gained))
        fresh_rows[start : start + step, :] = updated.astype(jnp.bfloat16)
        gained_row = lax.dot_general(
            jnp.ones((8, count), jnp.bfloat16), hits, NT, preferred_element_type=jnp.float32
        )
        fresh_counts[0:1, start : start + step] = prior_ref[0:1, start : start + step] + gained_row[0:1, :].astype(jnp.int32)


def level_sums(two, rows, per):
    block = two.shape[0] // per
    lines = []
    for j in range(per):
        scores = lax.dot_general(two[j * block : (j + 1) * block, :], rows(j), NT, preferred_element_type=jnp.float32)
        lines.append(jnp.sum(weights(scores, two.shape[1]), axis=0, keepdims=True))
    return jnp.concatenate(lines, axis=0)


def redo(cap, per, scaled, facts_in, me, refs, firsts, packed):
    part = per * cap
    count = 2 * part
    probe0 = facts_in[0:1, :]
    slots = facts_in[8:9, :] * 32 + facts_in[9:10, :]
    for r, (ref, first) in enumerate(zip(refs, firsts)):
        facts = jnp.transpose(ref[ref.shape[0] - META :, first : first + count].astype(jnp.float32))
        hits = (facts[:, 0:1] * 32.0 + facts[:, 1:2]).astype(jnp.int32) == jnp.where(probe0 == (me ^ r), slots + 1, -1)
        hits = one_hot(hits)
        gained = jnp.sum(hits.astype(jnp.float32), axis=1, keepdims=True)
        ahead = facts[:, 2:3]
        fresh = jnp.maximum(ahead + gained, 1.0)
        floor = fresh * fresh * 1e-06
        added = jnp.dot(hits, scaled[...], preferred_element_type=jnp.float32)
        whole = ahead * ref[0:count, :].astype(jnp.float32) + added
        power = jnp.mean(whole * whole, axis=-1, keepdims=True) + floor
        unit = (whole * lax.rsqrt(power)).astype(jnp.bfloat16)
        for w in range(2):
            for j in range(per):
                start = w * part + j * cap
                packed[w, j, r * cap : (r + 1) * cap, :] = unit[start : start + cap, :]


def early_kernel(
    cap, per, scaled, facts_in, own_any, near_any, any0, any1, any2, any3,
    sums, rows0, rows1, rows2, rows3, two, two_more, packed, sems,
):
    me, z, y, core = position()
    end = (z == 0) | (z == 3)
    refs = (rows0, rows1, rows2, rows3)
    copies = fetch(list(zip((any0, any1, any2, any3, own_any, near_any), (*refs, two, two_more))), sems)
    for copy in copies:
        copy.wait()
    redo(cap, per, scaled, facts_in, me, refs, (0, 0, 0, 0), packed)
    own_unit = unit_wide(two[...].astype(jnp.float32))
    near_unit = unit_wide(two_more[...].astype(jnp.float32))
    first = jnp.where(end, 0, 1)
    sums[pl.ds(first * 8, per), :] = level_sums(own_unit, lambda j: packed[first, j], per)
    sums[pl.ds(8 - first * 8, per), :] = level_sums(near_unit, lambda j: packed[1 - first, j], per)


def late_kernel(
    cap, per, scaled, facts_in, cross_any, passed_any, any0, any1, any2, any3, after,
    sums, kept, rows0, rows1, rows2, rows3, two, packed, sems,
):
    me, z, y, core = position()
    end = (z == 0) | (z == 3)
    part = per * cap
    at_end = pltpu.make_async_copy(passed_any, two, sems.at[4])
    at_mid = pltpu.make_async_copy(cross_any, two, sems.at[4])
    pl.when(end)(at_end.start)
    pl.when(jnp.logical_not(end))(at_mid.start)
    tail = pl.ds(2 * part, 2 * part + META)
    refs = (rows0, rows1, rows2, rows3)
    copies = fetch(list(zip((any0.at[tail], any1.at[tail], any2, any3), refs)), sems)
    for copy in copies:
        copy.wait()
    redo(cap, per, scaled, facts_in, me, refs, (2 * part, 2 * part, 0, 0), packed)
    kept[...] = packed[1]
    pl.when(end)(at_end.wait)
    pl.when(jnp.logical_not(end))(at_mid.wait)
    sums[0:per, :] = level_sums(unit_wide(two[...].astype(jnp.float32)), lambda j: packed[0, j], per)


def third_kernel(cap, per, early, later, share, kept_any, last_any, far_any, out, kept, two, sems):
    me, z, y, core = position()
    end = (z == 0) | (z == 3)
    at_end = pltpu.make_async_copy(far_any, two, sems.at[1])
    at_mid = pltpu.make_async_copy(last_any, two, sems.at[1])
    pl.when(end)(at_end.start)
    pl.when(jnp.logical_not(end))(at_mid.start)
    copies = fetch([(kept_any, kept)], sems)
    pl.when(end)(at_end.wait)
    pl.when(jnp.logical_not(end))(at_mid.wait)
    two_unit = unit_wide(two[...].astype(jnp.float32))
    copies[0].wait()
    final = level_sums(two_unit, lambda j: kept[j], per)
    lines = [early[0:per, :], early[8 : 8 + per, :], later[0:per, :], final]
    together = jnp.concatenate(lines + [jnp.zeros((16 - 4 * per, 4 * cap), jnp.float32)], axis=0)
    lane = lax.broadcasted_iota(jnp.int32, together.shape, 1)
    line = lax.broadcasted_iota(jnp.int32, together.shape, 0)
    out[...] = jnp.zeros(out.shape, jnp.float32)
    for r in range(4):
        spread = jnp.zeros_like(together)
        for s in range(4):
            turned = together if s == r else pltpu.roll(together, ((s - r) % 4) * cap, 1)
            spread = jnp.where((line % 4 == s) & (lane >= s * cap) & (lane < (s + 1) * cap), turned, spread)
        out[me ^ r, 0:4, :] = jnp.concatenate(
            [jnp.sum(spread[4 * t : 4 * t + 4], axis=0, keepdims=True) for t in range(4)], axis=0
        )
    for b in range(16):
        apart = ((b & 1) * 4) ^ ((b >> 1 & 1) * 12) ^ ((b >> 2 & 1) * 2) ^ (b >> 3)
        out[me ^ apart, 4:5, :] = share[b : b + 1, :]


def last_kernel(cap, scale_one, scale_two, info, got, density, level_two):
    me, z, y, core = position()
    total = jnp.zeros((1, 4 * cap), jnp.float32)
    for source in range(16):
        total = total + got[source, 4:5, :]
    density[...] = jnp.log(total[:, 0 : density.shape[1]] / scale_one)
    values = jnp.concatenate([got[me ^ r, 0:4, :] for r in range(4)], axis=0)
    rows = info.shape[1]
    chosen = jnp.where(info[2:3, :] == lax.broadcasted_iota(jnp.int32, (4 * cap, rows), 0), 1.0, 0.0)
    spread = jnp.dot(values, chosen, precision=lax.Precision.HIGHEST, preferred_element_type=jnp.float32)
    found = jnp.where(info[1:2, :] == lax.broadcasted_iota(jnp.int32, (16, rows), 0), spread, 0.0)
    level_two[...] = jnp.log(jnp.sum(found, axis=0, keepdims=True) / scale_two)


def call(kernel, outs, scratch=(), in_specs=None, **kw):
    def run(*args):
        specs = in_specs or [VMEM] * len(args)
        args = [pltpu.with_memory_space_constraint(a, pltpu.HBM) if spec is HBM else a for a, spec in zip(args, specs)]
        return pl.pallas_call(
            kernel, out_shape=outs, in_specs=specs, scratch_shapes=list(scratch), compiler_params=PARAMS, **kw
        )(*args)

    return run


def lasting(micros):
    return pl.CostEstimate(flops=0, transcendentals=0, bytes_accessed=int(micros * 3_690_000))


def in_order(*values, **kw):
    count = len(values)
    return call(
        order_kernel,
        tuple(jax.ShapeDtypeStruct(value.shape, value.dtype) for value in values),
        in_specs=[ANY] * count,
        out_specs=(ANY,) * count,
        input_output_aliases={i: i for i in range(count)},
        **kw,
    )(*values)


def line_body(embeddings, probes, assigned, prior_counts, centroids, candidates, centroids2):
    emb_rows, width = embeddings.shape
    probe_count = probes.shape[1]
    rows = centroids.shape[0]
    per = BLOCKS2_DEV
    cap = max(2, 3 * rows // (2 * per * 16))
    part = per * cap
    bf16, f32, i32 = jnp.bfloat16, jnp.float32, jnp.int32
    shape = jax.ShapeDtypeStruct

    def exchange(value, apart, sources=range(16)):
        return lax.ppermute(value, "shard", [(i, i ^ apart) for i in sources])

    def rows_of(planes):
        return shape((planes * part + META, width), bf16)

    def room(like):
        return pltpu.VMEM(like.shape, like.dtype)

    mids = range(4, 12)
    near_set = exchange(centroids2, 4)
    cross_set = exchange(centroids2, 12, mids)
    prior_row = prior_counts.reshape(1, rows)
    line = pltpu.VMEM((1, rows), i32)
    mine, early2, early3, info = call(
        functools.partial(pack_kernel, cap, per),
        (shape((emb_rows, width + 128), bf16), rows_of(2), rows_of(2), shape((8, rows), i32)),
        [
            line,
            pltpu.VMEM((emb_rows, width), bf16),
            pltpu.VMEM((probe_count, emb_rows), i32),
            pltpu.VMEM((1, emb_rows), i32),
            line,
            pltpu.VMEM((rows, width), bf16),
            pltpu.SemaphoreType.DMA((6,)),
        ],
        in_specs=[HBM] * 6,
    )(candidates.reshape(1, rows), embeddings, probes.T, assigned.reshape(1, emb_rows), prior_row, centroids)
    early2, early3 = exchange(early2, 2), exchange(early3, 3)
    rows0, rows1, late2, late3 = call(
        functools.partial(pack_more_kernel, part), (rows_of(4), rows_of(4), rows_of(2), rows_of(2))
    )(info, prior_row, centroids)
    mine = jnp.concatenate([mine, exchange(mine, 4)], axis=0)
    near_set, cross_set, mine, rows0 = in_order(near_set, cross_set, mine, rows0)
    across = exchange(mine, 12)
    passed = exchange(cross_set, 4, mids)
    last_set = exchange(near_set, 12, mids)
    mine = jnp.concatenate([mine, across], axis=0)
    mine, early2, early3, late2 = in_order(mine, early2, early3, late2)
    late2 = exchange(late2, 2)
    mine = jnp.concatenate([mine, exchange(mine, 2)], axis=0)
    passed, last_set, mine, late2, late3, rows1 = in_order(passed, last_set, mine, late2, late3, rows1)
    far_set = exchange(last_set, 4, mids)
    late3 = exchange(late3, 3)
    rows1 = exchange(rows1, 1)
    other = exchange(mine, 1)
    gathered = pltpu.VMEM((8 * emb_rows, width + 128), bf16)
    scaled, facts, share = call(
        share_kernel,
        (
            shape((16 * emb_rows, width), bf16),
            shape((16, 16 * emb_rows), i32),
            shape((16, 4 * cap), f32),
        ),
        [gathered, gathered, pltpu.SemaphoreType.DMA((2,))],
        in_specs=[ANY, ANY, VMEM],
        cost_estimate=lasting(3),
    )(mine, other, centroids)
    block_set = pltpu.VMEM((per * BLOCK2, width), bf16)
    packed = pltpu.VMEM((2, per, 4 * cap, width), bf16)
    early = call(
        functools.partial(early_kernel, cap, per),
        shape((16, 4 * cap), f32),
        [room(rows_of(4))] * 2 + [room(rows_of(2))] * 2 + [block_set] * 2 + [packed, pltpu.SemaphoreType.DMA((6,))],
        in_specs=[VMEM, VMEM, HBM] + [ANY] * 5,
        cost_estimate=lasting(5),
    )(scaled, facts, centroids2, near_set, rows0, rows1, early2, early3)
    kept = shape((per, 4 * cap, width), bf16)
    later, kept_rows = call(
        functools.partial(late_kernel, cap, per),
        (shape((8, 4 * cap), f32), kept),
        [room(rows_of(2))] * 4 + [block_set, packed, pltpu.SemaphoreType.DMA((5,))],
        in_specs=[VMEM, VMEM] + [ANY] * 7,
        cost_estimate=lasting(LATE),
    )(scaled, facts, cross_set, passed, rows0, rows1, late2, late3, early)
    results = call(
        functools.partial(third_kernel, cap, per),
        shape((16, 8, 4 * cap), f32),
        [room(kept), block_set, pltpu.SemaphoreType.DMA((2,))],
        in_specs=[VMEM, VMEM, VMEM, ANY, ANY, ANY],
        cost_estimate=lasting(1),
    )(early, later, share, kept_rows, last_set, far_set)
    new_centroids, counts = call(
        update_kernel, (shape((rows, width), bf16), shape((1, rows), i32)), in_specs=[ANY] + [VMEM] * 4
    )(results, scaled, facts, centroids, prior_row)
    results = lax.all_to_all(results, "shard", split_axis=0, concat_axis=0, tiled=True)
    density, level_two = call(
        functools.partial(last_kernel, cap, probe_count * BLOCK, BLOCK2), (shape((1, emb_rows), f32), shape((1, rows), f32))
    )(info, results)
    return (density.reshape(-1), new_centroids, counts.reshape(-1), level_two.reshape(-1))


def solution(mesh):
    placed = (
        P(("groups", "shard"), None),
        P(("groups", "shard"), None),
        P(("groups", "shard")),
        P(("groups", "shard")),
        P(("groups", "shard"), None),
        P(("groups", "shard"), None),
        P(("groups", "shard"), None),
    )
    body = line_body if mesh.shape["shard"] == 16 else general_body
    return jax.shard_map(
        body,
        mesh=mesh,
        in_specs=placed,
        out_specs=(
            P(("groups", "shard")),
            P(("groups", "shard"), None),
            P(("groups", "shard")),
            P(("groups", "shard")),
        ),
        check_vma=False,
    )
```

```python
import functools

import jax
import jax.numpy as jnp
from jax import lax
from jax.experimental import pallas as pl
from jax.experimental.pallas import tpu as pltpu
from jax.sharding import PartitionSpec as P

BLOCK = 1024
BLOCKS_DEV = 1
BLOCK2 = 128
BLOCKS2_DEV = 3


def unit_rows(values):
    wide = values.astype(jnp.float32)
    power = jnp.mean(wide * wide, axis=-1, keepdims=True) + 1e-06
    return (wide * lax.rsqrt(power)).astype(jnp.bfloat16)


def kernel_sums(rows, unit):
    scores = lax.dot_general(
        rows, unit, (((1,), (1,)), ((), ())), preferred_element_type=jnp.float32
    )
    return jnp.sum(jnp.exp((scores / rows.shape[1] - 1.0) / 0.1), axis=1)


def block_update(rows, slots, width):
    matches = slots[:, None] == jnp.arange(width, dtype=jnp.int32)[None, :]
    sums = lax.dot_general(
        matches.astype(jnp.bfloat16),
        rows,
        (((0,), (0,)), ((), ())),
        preferred_element_type=jnp.float32,
    )
    counts = jnp.sum(matches.astype(jnp.int32), axis=0)
    return (sums, counts)


def slot_ranks(targets, buckets):
    matches = (targets[:, None] == jnp.arange(buckets, dtype=jnp.int32)[None, :]).astype(jnp.int32)
    return jnp.sum(jnp.cumsum(matches, axis=0) * matches, axis=1) - 1


def general_body(embeddings, probes, assigned, prior_counts, centroids, candidates, centroids2):
    devices = lax.axis_size("shard")
    emb_rows, width = embeddings.shape
    probe_count = probes.shape[1]
    capacity = max(2, 2 * emb_rows * probe_count // (BLOCKS_DEV * devices))
    scaled = unit_rows(embeddings)
    units_old = unit_rows(centroids).reshape(BLOCKS_DEV, BLOCK, width)
    total = emb_rows * probe_count
    buckets = BLOCKS_DEV * devices
    flat = probes.reshape(-1)
    place = flat * capacity + slot_ranks(flat, buckets)
    leading = jnp.arange(total, dtype=jnp.int32) % probe_count == 0
    repeated = jnp.repeat(scaled, probe_count, axis=0)
    slot_values = jnp.where(leading, jnp.repeat(assigned, probe_count), -1)
    send_rows = jnp.zeros((buckets * capacity, width), jnp.bfloat16).at[place].set(repeated)
    send_slots = jnp.full((buckets * capacity,), -1, jnp.int32).at[place].set(slot_values)
    got_rows, got_slots = (
        lax.all_to_all(
            send_rows.reshape(devices, BLOCKS_DEV * capacity, width),
            "shard",
            split_axis=0,
            concat_axis=0,
            tiled=True,
        ),
        lax.all_to_all(
            send_slots.reshape(devices, BLOCKS_DEV * capacity),
            "shard",
            split_axis=0,
            concat_axis=0,
            tiled=True,
        ),
    )
    got_rows = got_rows.reshape(devices, BLOCKS_DEV, capacity, width)
    got_slots = got_slots.reshape(devices, BLOCKS_DEV, capacity)
    local = 0
    picked = got_rows[:, local].reshape(devices * capacity, width)
    slots = got_slots[:, local].reshape(-1)
    weights = [kernel_sums(picked, units_old[local]).reshape(devices, capacity)]
    more_sums, more_counts = block_update(picked, slots, BLOCK)
    sum_list = [more_sums]
    count_list = [more_counts]
    sums = jnp.stack(sum_list)
    counts = jnp.stack(count_list)
    returned = lax.all_to_all(
        jnp.stack(weights, axis=1).reshape(devices, BLOCKS_DEV * capacity),
        "shard",
        split_axis=0,
        concat_axis=0,
        tiled=True,
    )
    totals = jnp.sum(returned.reshape(-1)[place].reshape(emb_rows, probe_count), axis=1)
    density = jnp.log(totals / (probe_count * BLOCK))
    prior = prior_counts.reshape(BLOCKS_DEV, BLOCK)
    fresh = prior + counts
    updated = (
        prior.astype(jnp.float32)[:, :, None]
        * centroids.reshape(BLOCKS_DEV, BLOCK, width).astype(jnp.float32)
        + sums
    ) / fresh.astype(jnp.float32)[:, :, None]
    new_centroids = updated.astype(jnp.bfloat16).reshape(BLOCKS_DEV * BLOCK, width)
    units_new = unit_rows(updated).reshape(BLOCKS_DEV * BLOCK, width)
    rows_two = units_new.shape[0]
    second_capacity = max(2, 3 * rows_two // (2 * BLOCKS2_DEV * devices))
    buckets_two = BLOCKS2_DEV * devices
    chosen = candidates[:, 0]
    place_two = chosen * second_capacity + slot_ranks(chosen, buckets_two)
    send_two = (
        jnp.zeros((buckets_two * second_capacity, width), jnp.bfloat16).at[place_two].set(units_new)
    )
    send_two = send_two.reshape(devices, BLOCKS2_DEV, second_capacity, width)
    units_two = unit_rows(centroids2).reshape(BLOCKS2_DEV, BLOCK2, width)
    arrived = lax.all_to_all(send_two, "shard", split_axis=0, concat_axis=0, tiled=True)
    items = arrived.shape[2]
    weights_two = [
        kernel_sums(arrived[:, local].reshape(-1, width), units_two[local]).reshape(
            arrived.shape[0], items
        )
        for local in range(BLOCKS2_DEV)
    ]
    returned_two = lax.all_to_all(
        jnp.stack(weights_two, axis=1), "shard", split_axis=0, concat_axis=0, tiled=True
    )
    level_two = jnp.log(returned_two.reshape(-1)[place_two] / BLOCK2)
    return (density, new_centroids, fresh.reshape(-1), level_two)


NT = (((1,), (1,)), ((), ()))
PARAMS = pltpu.CompilerParams(vmem_limit_bytes=48 * 1024 * 1024)
META = 16
LATE = 5
STEP = 40
HBM = pl.BlockSpec(memory_space=pltpu.HBM)
ANY = pl.BlockSpec(memory_space=pl.ANY)
VMEM = pl.BlockSpec(memory_space=pltpu.VMEM)


def position():
    me = lax.axis_index("shard")
    return me, me // 4, (me // 2) % 2, me % 2


def unit_wide(wide):
    power = jnp.mean(wide * wide, axis=-1, keepdims=True) + 1e-06
    return (wide * lax.rsqrt(power)).astype(jnp.bfloat16)


def weights(scores, width):
    return jnp.exp(scores * (10.0 / width) - 10.0)


def one_hot(hits):
    return jnp.where(hits, 1.0, 0.0).astype(jnp.bfloat16)


def column(row):
    return jnp.transpose(jnp.broadcast_to(row, (8, row.shape[1])))[:, 0:1]


def fetch(pairs, sems):
    copies = [pltpu.make_async_copy(src, dst, sems.at[i]) for i, (src, dst) in enumerate(pairs)]
    for copy in copies:
        copy.start()
    return copies


def pick_rows(slot, first, count):
    return one_hot(slot == lax.broadcasted_iota(jnp.int32, (count, slot.shape[1]), 0) + first)


def pack(slot, prior, cent, first, out):
    count = out.shape[0] - META
    rows = slot.shape[1]
    ident = lax.broadcasted_iota(jnp.int32, (1, rows), 1) + 1
    line = lax.broadcasted_iota(jnp.int32, (META, rows), 0)
    facts = jnp.where(line == 0, ident >> 5, jnp.where(line == 1, ident & 31, jnp.where(line == 2, prior, 0)))
    facts = facts.astype(jnp.float32).astype(jnp.bfloat16)
    pick = pick_rows(slot, first, count)
    out[0:count, :] = jnp.dot(pick, cent, preferred_element_type=jnp.float32).astype(jnp.bfloat16)
    out[count:, :] = jnp.zeros((META, out.shape[1]), jnp.bfloat16)
    out[count:, 0:count] = lax.dot_general(facts, pick, NT, preferred_element_type=jnp.float32).astype(jnp.bfloat16)


def pack_kernel(
    cap, per, cand_any, emb_any, probes_any, assigned_any, prior_any, cent_any, mine, rows2, rows3, info,
    cand_ref, emb_ref, probes_ref, assigned_ref, prior_ref, cent_ref, sems,
):
    copies = fetch(
        (
            (cand_any, cand_ref),
            (emb_any, emb_ref),
            (probes_any, probes_ref),
            (assigned_any, assigned_ref),
            (prior_any, prior_ref),
            (cent_any, cent_ref),
        ),
        sems,
    )
    me, z, y, core = position()
    rows = cand_ref.shape[1]
    buckets = 16 * per
    before = lax.broadcasted_iota(jnp.int32, (rows, rows), 0) <= lax.broadcasted_iota(jnp.int32, (rows, rows), 1)
    before = one_hot(before)
    copies[0].wait()
    cand = cand_ref[...]
    dev = sum((cand >= per * step).astype(jnp.int32) for step in range(1, 16))
    near = dev >> 2
    plane = jnp.where(z >= 2, 3 - near, near)
    rel = (((dev >> 1) & 1) ^ y) * 2 + ((dev & 1) ^ core)
    named = cand == lax.broadcasted_iota(jnp.int32, (buckets, rows), 0)
    counted = jnp.dot(one_hot(named), before, preferred_element_type=jnp.float32)
    rank = jnp.sum(jnp.where(named, counted, 0.0), axis=0, keepdims=True).astype(jnp.int32) - 1
    kind = plane * per + cand - dev * per
    slot = (rel * 4 * per + kind) * cap + rank
    info[0:1, :] = slot
    info[1:2, :] = rel * 4 + (kind >> 2)
    info[2:3, :] = (kind & 3) * cap + rank
    for copy in copies[1:5]:
        copy.wait()
    count, width = emb_ref.shape
    probe_count = probes_ref.shape[0]
    slots = assigned_ref[...]
    facts = jnp.concatenate([probes_ref[...], slots >> 5, slots & 31], axis=0).astype(jnp.float32)
    facts = jnp.concatenate([facts, jnp.zeros((128 - probe_count - 2, count), jnp.float32)], axis=0)
    same = lax.broadcasted_iota(jnp.int32, (count, count), 0) == lax.broadcasted_iota(jnp.int32, (count, count), 1)
    mine[:, 0:width] = emb_ref[...]
    mine[:, width:] = lax.dot_general(
        one_hot(same), facts.astype(jnp.bfloat16), NT, preferred_element_type=jnp.float32
    ).astype(jnp.bfloat16)
    copies[5].wait()
    pack(slot, prior_ref[...], cent_ref[...], 2 * 4 * per * cap, rows2)
    pack(slot, prior_ref[...], cent_ref[...], 3 * 4 * per * cap, rows3)


def pack_more_kernel(part, info, prior_ref, cent_ref, rows0, rows1, late2, late3):
    for first, out in ((0, rows0), (4 * part, rows1), (11 * part, late2), (15 * part, late3)):
        pack(info[0:1, :], prior_ref[...], cent_ref[...], first, out)


def order_kernel(*refs):
    pass


def share_kernel(mine_any, other_any, cent_ref, scaled, facts, share, mine_ref, other_ref, sems):
    copies = fetch(((mine_any, mine_ref), (other_any, other_ref)), sems)
    me, z, y, core = position()
    half = mine_ref.shape[0]
    count = 2 * half
    rows, width = cent_ref.shape
    copies[0].wait()
    scaled[0:half, :] = unit_wide(mine_ref[:, 0:width].astype(jnp.float32))
    copies[1].wait()
    scaled[half:count, :] = unit_wide(other_ref[:, 0:width].astype(jnp.float32))
    aux = jnp.concatenate([mine_ref[:, width:], other_ref[:, width:]], axis=0).astype(jnp.float32)
    aux = jnp.transpose(aux)[0:16, :].astype(jnp.int32)
    facts[...] = aux
    member = jnp.sum((aux[0:8, :] == me).astype(jnp.float32), axis=0, keepdims=True)
    step = 256
    total = jnp.zeros((1, count), jnp.float32)
    for start in range(0, rows, step):
        old = cent_ref[start : start + step, :].astype(jnp.float32)
        scores = lax.dot_general(unit_wide(old), scaled[...], NT, preferred_element_type=jnp.float32)
        total = total + jnp.sum(weights(scores, width), axis=0, keepdims=True)
    piece = count // 16
    lane = lax.broadcasted_iota(jnp.int32, (16, count), 1)
    line = lax.broadcasted_iota(jnp.int32, (16, count), 0)
    apart = jnp.where((member > 0.0) & (lane >= line * piece) & (lane < (line + 1) * piece), total, 0.0)
    spot = lax.broadcasted_iota(jnp.int32, (count, 128), 0)
    block = sum((spot >= piece * step).astype(jnp.int32) for step in range(1, 16))
    together = jnp.where(spot - block * piece == lax.broadcasted_iota(jnp.int32, (count, 128), 1), 1.0, 0.0)
    share[...] = jnp.dot(apart, together, precision=lax.Precision.HIGHEST, preferred_element_type=jnp.float32)


def update_kernel(after, scaled, facts, cent_ref, prior_ref, fresh_rows, fresh_counts):
    me, z, y, core = position()
    rows, width = cent_ref.shape
    count = scaled.shape[0]
    prior = column(prior_ref[...].astype(jnp.float32))
    target = jnp.where(facts[0:1, :] == me, facts[8:9, :] * 32 + facts[9:10, :], -1)
    step = 256
    for start in range(0, rows, step):
        old = cent_ref[start : start + step, :].astype(jnp.float32)
        hits = one_hot(target == lax.broadcasted_iota(jnp.int32, (step, count), 0) + start)
        sums = jnp.dot(hits, scaled[...], preferred_element_type=jnp.float32)
        gained = jnp.sum(hits.astype(jnp.float32), axis=1, keepdims=True)
        ahead = prior[start : start + step, :]
        updated = (ahead * old + sums) * (1.0 / (ahead + gained))
        fresh_rows[start : start + step, :] = updated.astype(jnp.bfloat16)
        gained_row = lax.dot_general(
            jnp.ones((8, count), jnp.bfloat16), hits, NT, preferred_element_type=jnp.float32
        )
        fresh_counts[0:1, start : start + step] = prior_ref[0:1, start : start + step] + gained_row[0:1, :].astype(jnp.int32)


def level_sums(two, rows, per):
    block = two.shape[0] // per
    lines = []
    for j in range(per):
        scores = lax.dot_general(two[j * block : (j + 1) * block, :], rows(j), NT, preferred_element_type=jnp.float32)
        lines.append(jnp.sum(weights(scores, two.shape[1]), axis=0, keepdims=True))
    return jnp.concatenate(lines, axis=0)


def redo(cap, per, scaled, facts_in, me, refs, firsts, packed):
    part = per * cap
    planes = packed.shape[0]
    count = planes * part
    probe0 = facts_in[0:1, :]
    slots = facts_in[8:9, :] * 32 + facts_in[9:10, :]
    for r, (ref, first) in enumerate(zip(refs, firsts)):
        facts = jnp.transpose(ref[ref.shape[0] - META :, first : first + count].astype(jnp.float32))
        hits = (facts[:, 0:1] * 32.0 + facts[:, 1:2]).astype(jnp.int32) == jnp.where(probe0 == (me ^ r), slots + 1, -1)
        hits = one_hot(hits)
        gained = jnp.sum(hits.astype(jnp.float32), axis=1, keepdims=True)
        ahead = facts[:, 2:3]
        fresh = jnp.maximum(ahead + gained, 1.0)
        floor = fresh * fresh * 1e-06
        added = jnp.dot(hits, scaled[...], preferred_element_type=jnp.float32)
        whole = ahead * ref[0:count, :].astype(jnp.float32) + added
        power = jnp.mean(whole * whole, axis=-1, keepdims=True) + floor
        unit = (whole * lax.rsqrt(power)).astype(jnp.bfloat16)
        for w in range(planes):
            for j in range(per):
                start = w * part + j * cap
                packed[w, j, r * cap : (r + 1) * cap, :] = unit[start : start + cap, :]


def early_kernel(
    cap, per, scaled, facts_in, own_any, near_any, cross_any, passed_any, any0, any1, any2, any3,
    sums, rows0, rows1, rows2, rows3, two, two_more, two_last, packed, sems,
):
    me, z, y, core = position()
    end = (z == 0) | (z == 3)
    refs = (rows0, rows1, rows2, rows3)
    at_end = pltpu.make_async_copy(passed_any, two_last, sems.at[6])
    at_mid = pltpu.make_async_copy(cross_any, two_last, sems.at[6])
    copies = fetch(list(zip((any0, any1, any2, any3, own_any, near_any), (*refs, two, two_more))), sems)
    pl.when(end)(at_end.start)
    pl.when(jnp.logical_not(end))(at_mid.start)
    for copy in copies:
        copy.wait()
    redo(cap, per, scaled, facts_in, me, refs, (0, 0, 0, 0), packed)
    own_unit = unit_wide(two[...].astype(jnp.float32))
    near_unit = unit_wide(two_more[...].astype(jnp.float32))
    first = jnp.where(end, 0, 1)
    sums[pl.ds(first * 8, per), :] = level_sums(own_unit, lambda j: packed[first, j], per)
    sums[pl.ds(8 - first * 8, per), :] = level_sums(near_unit, lambda j: packed[1 - first, j], per)
    pl.when(end)(at_end.wait)
    pl.when(jnp.logical_not(end))(at_mid.wait)
    sums[16 : 16 + per, :] = level_sums(unit_wide(two_last[...].astype(jnp.float32)), lambda j: packed[2, j], per)


def late_kernel(
    cap, per, scaled, facts_in, any0, any1, any2, any3, after, packed, rows0, rows1, rows2, rows3, sems
):
    me, z, y, core = position()
    part = per * cap
    tail = pl.ds(3 * part, part + META)
    refs = (rows0, rows1, rows2, rows3)
    copies = fetch(list(zip((any0.at[tail], any1.at[tail], any2, any3), refs)), sems)
    for copy in copies:
        copy.wait()
    redo(cap, per, scaled, facts_in, me, refs, (3 * part, 3 * part, 0, 0), packed)


def third_kernel(cap, per, early, kept_any, last_any, far_any, out0, out1, out2, out3, kept, two, sems):
    me, z, y, core = position()
    end = (z == 0) | (z == 3)
    at_end = pltpu.make_async_copy(far_any, two, sems.at[1])
    at_mid = pltpu.make_async_copy(last_any, two, sems.at[1])
    pl.when(end)(at_end.start)
    pl.when(jnp.logical_not(end))(at_mid.start)
    copies = fetch([(kept_any, kept)], sems)
    pl.when(end)(at_end.wait)
    pl.when(jnp.logical_not(end))(at_mid.wait)
    two_unit = unit_wide(two[...].astype(jnp.float32))
    copies[0].wait()
    final = level_sums(two_unit, lambda j: kept[0, j], per)
    lines = [early[8 * w : 8 * w + per, :] for w in range(3)] + [final]
    together = jnp.concatenate(lines + [jnp.zeros((16 - 4 * per, 4 * cap), jnp.float32)], axis=0)
    lane = lax.broadcasted_iota(jnp.int32, together.shape, 1)
    line = lax.broadcasted_iota(jnp.int32, together.shape, 0)
    for r, out in enumerate((out0, out1, out2, out3)):
        spread = jnp.zeros_like(together)
        for s in range(4):
            turned = together if s == r else pltpu.roll(together, ((s - r) % 4) * cap, 1)
            spread = jnp.where((line % 4 == s) & (lane >= s * cap) & (lane < (s + 1) * cap), turned, spread)
        for t in range(4):
            out[t : t + 1, :] = jnp.sum(spread[4 * t : 4 * t + 4], axis=0, keepdims=True)


def last_kernel(cap, scale_one, scale_two, info, got0, got1, got2, got3, shares, density, level_two):
    density[...] = jnp.log(shares[:, 0 : density.shape[1]] / scale_one)
    values = jnp.concatenate([got[0:4, :] for got in (got0, got1, got2, got3)], axis=0)
    rows = info.shape[1]
    chosen = jnp.where(info[2:3, :] == lax.broadcasted_iota(jnp.int32, (4 * cap, rows), 0), 1.0, 0.0)
    spread = jnp.dot(values, chosen, precision=lax.Precision.HIGHEST, preferred_element_type=jnp.float32)
    found = jnp.where(info[1:2, :] == lax.broadcasted_iota(jnp.int32, (16, rows), 0), spread, 0.0)
    level_two[...] = jnp.log(jnp.sum(found, axis=0, keepdims=True) / scale_two)


def call(kernel, outs, scratch=(), in_specs=None, **kw):
    def run(*args):
        specs = in_specs or [VMEM] * len(args)
        args = [pltpu.with_memory_space_constraint(a, pltpu.HBM) if spec is HBM else a for a, spec in zip(args, specs)]
        return pl.pallas_call(
            kernel, out_shape=outs, in_specs=specs, scratch_shapes=list(scratch), compiler_params=PARAMS, **kw
        )(*args)

    return run


def lasting(micros):
    return pl.CostEstimate(flops=0, transcendentals=0, bytes_accessed=int(micros * 3_690_000))


def in_order(*values, **kw):
    count = len(values)
    return call(
        order_kernel,
        tuple(jax.ShapeDtypeStruct(value.shape, value.dtype) for value in values),
        in_specs=[ANY] * count,
        out_specs=(ANY,) * count,
        input_output_aliases={i: i for i in range(count)},
        **kw,
    )(*values)


def line_body(embeddings, probes, assigned, prior_counts, centroids, candidates, centroids2):
    emb_rows, width = embeddings.shape
    probe_count = probes.shape[1]
    rows = centroids.shape[0]
    per = BLOCKS2_DEV
    cap = max(2, 3 * rows // (2 * per * 16))
    part = per * cap
    bf16, f32, i32 = jnp.bfloat16, jnp.float32, jnp.int32
    shape = jax.ShapeDtypeStruct

    def exchange(value, apart, sources=range(16)):
        return lax.ppermute(value, "shard", [(i, i ^ apart) for i in sources])

    def rows_of(planes):
        return shape((planes * part + META, width), bf16)

    def room(like):
        return pltpu.VMEM(like.shape, like.dtype)

    mids = range(4, 12)
    near_set = exchange(centroids2, 4)
    cross_set = exchange(centroids2, 12, mids)
    prior_row = prior_counts.reshape(1, rows)
    line = pltpu.VMEM((1, rows), i32)
    mine, early2, early3, info = call(
        functools.partial(pack_kernel, cap, per),
        (shape((emb_rows, width + 128), bf16), rows_of(3), rows_of(3), shape((8, rows), i32)),
        [
            line,
            pltpu.VMEM((emb_rows, width), bf16),
            pltpu.VMEM((probe_count, emb_rows), i32),
            pltpu.VMEM((1, emb_rows), i32),
            line,
            pltpu.VMEM((rows, width), bf16),
            pltpu.SemaphoreType.DMA((6,)),
        ],
        in_specs=[HBM] * 6,
    )(candidates.reshape(1, rows), embeddings, probes.T, assigned.reshape(1, emb_rows), prior_row, centroids)
    early2, early3 = exchange(early2, 2), exchange(early3, 3)
    rows0, rows1, late2, late3 = call(
        functools.partial(pack_more_kernel, part), (rows_of(4), rows_of(4), rows_of(1), rows_of(1))
    )(info, prior_row, centroids)
    mine = jnp.concatenate([mine, exchange(mine, 4)], axis=0)
    near_set, cross_set, mine, rows0 = in_order(near_set, cross_set, mine, rows0)
    across = exchange(mine, 12)
    passed = exchange(cross_set, 4, mids)
    last_set = exchange(near_set, 12, mids)
    mine = jnp.concatenate([mine, across], axis=0)
    mine, early2, early3, late2, late3, rows1 = in_order(mine, early2, early3, late2, late3, rows1)
    mine = jnp.concatenate([mine, exchange(mine, 2)], axis=0)
    late2, late3 = exchange(late2, 2), exchange(late3, 3)
    rows1 = exchange(rows1, 1)
    passed, last_set, mine = in_order(passed, last_set, mine)
    far_set = exchange(last_set, 4, mids)
    other = exchange(mine, 1)
    gathered = pltpu.VMEM((8 * emb_rows, width + 128), bf16)
    scaled, facts, share = call(
        share_kernel,
        (
            shape((16 * emb_rows, width), bf16),
            shape((16, 16 * emb_rows), i32),
            shape((16, 4 * cap), f32),
        ),
        [gathered, gathered, pltpu.SemaphoreType.DMA((2,))],
        in_specs=[ANY, ANY, VMEM],
        cost_estimate=lasting(3),
    )(mine, other, centroids)

    def gather(share, apart):
        half = share.shape[0] // 2
        return share[:half] + exchange(share[half:], apart)

    block_set = pltpu.VMEM((per * BLOCK2, width), bf16)
    packed = pltpu.VMEM((3, per, 4 * cap, width), bf16)
    early = call(
        functools.partial(early_kernel, cap, per),
        shape((24, 4 * cap), f32),
        [room(rows_of(4))] * 2 + [room(rows_of(3))] * 2 + [block_set] * 3 + [packed, pltpu.SemaphoreType.DMA((7,))],
        in_specs=[VMEM, VMEM, HBM] + [ANY] * 7,
        cost_estimate=lasting(7),
    )(scaled, facts, centroids2, near_set, cross_set, passed, rows0, rows1, early2, early3)
    share, early = in_order(gather(share, 1), early)
    kept = shape((1, per, 4 * cap, width), bf16)
    kept_rows = call(
        functools.partial(late_kernel, cap, per),
        kept,
        [room(rows_of(1))] * 4 + [pltpu.SemaphoreType.DMA((4,))],
        in_specs=[VMEM] * 2 + [ANY] * 5,
        cost_estimate=lasting(3),
    )(scaled, facts, rows0, rows1, late2, late3, early)
    share, kept_rows = in_order(gather(share, 2), kept_rows)
    tile = shape((8, 4 * cap), f32)
    tiles = call(
        functools.partial(third_kernel, cap, per),
        (tile,) * 4,
        [room(kept), block_set, pltpu.SemaphoreType.DMA((2,))],
        in_specs=[VMEM, ANY, ANY, ANY],
        cost_estimate=lasting(1),
    )(early, kept_rows, last_set, far_set)
    share, *tiles = in_order(gather(share, 12), *tiles)
    new_centroids, counts = call(
        update_kernel, (shape((rows, width), bf16), shape((1, rows), i32)), in_specs=[ANY] + [VMEM] * 4
    )(tiles[0], scaled, facts, centroids, prior_row)
    tiles = [tile if r == 0 else exchange(tile, r) for r, tile in enumerate(tiles)]
    share = gather(share, 4)
    density, level_two = call(
        functools.partial(last_kernel, cap, probe_count * BLOCK, BLOCK2), (shape((1, emb_rows), f32), shape((1, rows), f32))
    )(info, *tiles, share)
    return (density.reshape(-1), new_centroids, counts.reshape(-1), level_two.reshape(-1))


def solution(mesh):
    placed = (
        P(("groups", "shard"), None),
        P(("groups", "shard"), None),
        P(("groups", "shard")),
        P(("groups", "shard")),
        P(("groups", "shard"), None),
        P(("groups", "shard"), None),
        P(("groups", "shard"), None),
    )
    body = line_body if mesh.shape["shard"] == 16 else general_body
    return jax.shard_map(
        body,
        mesh=mesh,
        in_specs=placed,
        out_specs=(
            P(("groups", "shard")),
            P(("groups", "shard"), None),
            P(("groups", "shard")),
            P(("groups", "shard")),
        ),
        check_vma=False,
    )
```

```python
import functools
import math

import jax
import jax.numpy as jnp
from jax import lax
from jax.experimental import pallas as pl
from jax.experimental.pallas import tpu as pltpu
from jax.sharding import PartitionSpec as P

BLOCK = 1024
BLOCKS_DEV = 1
BLOCK2 = 128
BLOCKS2_DEV = 3


def unit_rows(values):
    wide = values.astype(jnp.float32)
    power = jnp.mean(wide * wide, axis=-1, keepdims=True) + 1e-06
    return (wide * lax.rsqrt(power)).astype(jnp.bfloat16)


def kernel_sums(rows, unit):
    scores = lax.dot_general(
        rows, unit, (((1,), (1,)), ((), ())), preferred_element_type=jnp.float32
    )
    return jnp.sum(jnp.exp((scores / rows.shape[1] - 1.0) / 0.1), axis=1)


def block_update(rows, slots, width):
    matches = slots[:, None] == jnp.arange(width, dtype=jnp.int32)[None, :]
    sums = lax.dot_general(
        matches.astype(jnp.bfloat16),
        rows,
        (((0,), (0,)), ((), ())),
        preferred_element_type=jnp.float32,
    )
    counts = jnp.sum(matches.astype(jnp.int32), axis=0)
    return (sums, counts)


def slot_ranks(targets, buckets):
    matches = (targets[:, None] == jnp.arange(buckets, dtype=jnp.int32)[None, :]).astype(jnp.int32)
    return jnp.sum(jnp.cumsum(matches, axis=0) * matches, axis=1) - 1


def general_body(embeddings, probes, assigned, prior_counts, centroids, candidates, centroids2):
    devices = lax.axis_size("shard")
    emb_rows, width = embeddings.shape
    probe_count = probes.shape[1]
    capacity = max(2, 2 * emb_rows * probe_count // (BLOCKS_DEV * devices))
    scaled = unit_rows(embeddings)
    units_old = unit_rows(centroids).reshape(BLOCKS_DEV, BLOCK, width)
    total = emb_rows * probe_count
    buckets = BLOCKS_DEV * devices
    flat = probes.reshape(-1)
    place = flat * capacity + slot_ranks(flat, buckets)
    leading = jnp.arange(total, dtype=jnp.int32) % probe_count == 0
    repeated = jnp.repeat(scaled, probe_count, axis=0)
    slot_values = jnp.where(leading, jnp.repeat(assigned, probe_count), -1)
    send_rows = jnp.zeros((buckets * capacity, width), jnp.bfloat16).at[place].set(repeated)
    send_slots = jnp.full((buckets * capacity,), -1, jnp.int32).at[place].set(slot_values)
    got_rows, got_slots = (
        lax.all_to_all(
            send_rows.reshape(devices, BLOCKS_DEV * capacity, width),
            "shard",
            split_axis=0,
            concat_axis=0,
            tiled=True,
        ),
        lax.all_to_all(
            send_slots.reshape(devices, BLOCKS_DEV * capacity),
            "shard",
            split_axis=0,
            concat_axis=0,
            tiled=True,
        ),
    )
    got_rows = got_rows.reshape(devices, BLOCKS_DEV, capacity, width)
    got_slots = got_slots.reshape(devices, BLOCKS_DEV, capacity)
    local = 0
    picked = got_rows[:, local].reshape(devices * capacity, width)
    slots = got_slots[:, local].reshape(-1)
    weights = [kernel_sums(picked, units_old[local]).reshape(devices, capacity)]
    more_sums, more_counts = block_update(picked, slots, BLOCK)
    sum_list = [more_sums]
    count_list = [more_counts]
    sums = jnp.stack(sum_list)
    counts = jnp.stack(count_list)
    returned = lax.all_to_all(
        jnp.stack(weights, axis=1).reshape(devices, BLOCKS_DEV * capacity),
        "shard",
        split_axis=0,
        concat_axis=0,
        tiled=True,
    )
    totals = jnp.sum(returned.reshape(-1)[place].reshape(emb_rows, probe_count), axis=1)
    density = jnp.log(totals / (probe_count * BLOCK))
    prior = prior_counts.reshape(BLOCKS_DEV, BLOCK)
    fresh = prior + counts
    updated = (
        prior.astype(jnp.float32)[:, :, None]
        * centroids.reshape(BLOCKS_DEV, BLOCK, width).astype(jnp.float32)
        + sums
    ) / fresh.astype(jnp.float32)[:, :, None]
    new_centroids = updated.astype(jnp.bfloat16).reshape(BLOCKS_DEV * BLOCK, width)
    units_new = unit_rows(updated).reshape(BLOCKS_DEV * BLOCK, width)
    rows_two = units_new.shape[0]
    second_capacity = max(2, 3 * rows_two // (2 * BLOCKS2_DEV * devices))
    buckets_two = BLOCKS2_DEV * devices
    chosen = candidates[:, 0]
    place_two = chosen * second_capacity + slot_ranks(chosen, buckets_two)
    send_two = (
        jnp.zeros((buckets_two * second_capacity, width), jnp.bfloat16).at[place_two].set(units_new)
    )
    send_two = send_two.reshape(devices, BLOCKS2_DEV, second_capacity, width)
    units_two = unit_rows(centroids2).reshape(BLOCKS2_DEV, BLOCK2, width)
    arrived = lax.all_to_all(send_two, "shard", split_axis=0, concat_axis=0, tiled=True)
    items = arrived.shape[2]
    weights_two = [
        kernel_sums(arrived[:, local].reshape(-1, width), units_two[local]).reshape(
            arrived.shape[0], items
        )
        for local in range(BLOCKS2_DEV)
    ]
    returned_two = lax.all_to_all(
        jnp.stack(weights_two, axis=1), "shard", split_axis=0, concat_axis=0, tiled=True
    )
    level_two = jnp.log(returned_two.reshape(-1)[place_two] / BLOCK2)
    return (density, new_centroids, fresh.reshape(-1), level_two)


NT = (((1,), (1,)), ((), ()))
PARAMS = pltpu.CompilerParams(vmem_limit_bytes=48 * 1024 * 1024)
META = 16
LATE = 5
STEP = 40
HBM = pl.BlockSpec(memory_space=pltpu.HBM)
ANY = pl.BlockSpec(memory_space=pl.ANY)
VMEM = pl.BlockSpec(memory_space=pltpu.VMEM)


def position():
    me = lax.axis_index("shard")
    return me, me // 4, (me // 2) % 2, me % 2


def unit_wide(wide):
    power = jnp.mean(wide * wide, axis=-1, keepdims=True) + 1e-06
    return (wide * lax.rsqrt(power)).astype(jnp.bfloat16)


def weights(scores, width):
    return jnp.exp(scores * (10.0 / width) - 10.0)


def one_hot(hits):
    return jnp.where(hits, 1.0, 0.0).astype(jnp.bfloat16)


def column(row):
    return jnp.transpose(jnp.broadcast_to(row, (8, row.shape[1])))[:, 0:1]


def fetch(pairs, sems):
    copies = [pltpu.make_async_copy(src, dst, sems.at[i]) for i, (src, dst) in enumerate(pairs)]
    for copy in copies:
        copy.start()
    return copies


def pick_rows(slot, first, count):
    return one_hot(slot == lax.broadcasted_iota(jnp.int32, (count, slot.shape[1]), 0) + first)


def pack(slot, prior, cent, first, out):
    count = out.shape[0] - META
    rows = slot.shape[1]
    ident = lax.broadcasted_iota(jnp.int32, (1, rows), 1) + 1
    line = lax.broadcasted_iota(jnp.int32, (META, rows), 0)
    facts = jnp.where(line == 0, ident >> 5, jnp.where(line == 1, ident & 31, jnp.where(line == 2, prior, 0)))
    facts = facts.astype(jnp.float32).astype(jnp.bfloat16)
    pick = pick_rows(slot, first, count)
    out[0:count, :] = jnp.dot(pick, cent, preferred_element_type=jnp.float32).astype(jnp.bfloat16)
    out[count:, :] = jnp.zeros((META, out.shape[1]), jnp.bfloat16)
    out[count:, 0:count] = lax.dot_general(facts, pick, NT, preferred_element_type=jnp.float32).astype(jnp.bfloat16)


def pack_kernel(
    cap, per, cand_any, emb_any, probes_any, assigned_any, prior_any, cent_any, mine, rows2, rows3, info,
    cand_ref, emb_ref, probes_ref, assigned_ref, prior_ref, cent_ref, sems,
):
    copies = fetch(
        (
            (cand_any, cand_ref),
            (emb_any, emb_ref),
            (probes_any, probes_ref),
            (assigned_any, assigned_ref),
            (prior_any, prior_ref),
            (cent_any, cent_ref),
        ),
        sems,
    )
    me, z, y, core = position()
    rows = cand_ref.shape[1]
    buckets = 16 * per
    before = lax.broadcasted_iota(jnp.int32, (rows, rows), 0) <= lax.broadcasted_iota(jnp.int32, (rows, rows), 1)
    before = one_hot(before)
    copies[0].wait()
    cand = cand_ref[...]
    dev = sum((cand >= per * step).astype(jnp.int32) for step in range(1, 16))
    near = dev >> 2
    plane = jnp.where(z >= 2, 3 - near, near)
    rel = (((dev >> 1) & 1) ^ y) * 2 + ((dev & 1) ^ core)
    named = cand == lax.broadcasted_iota(jnp.int32, (buckets, rows), 0)
    counted = jnp.dot(one_hot(named), before, preferred_element_type=jnp.float32)
    rank = jnp.sum(jnp.where(named, counted, 0.0), axis=0, keepdims=True).astype(jnp.int32) - 1
    kind = plane * per + cand - dev * per
    slot = (rel * 4 * per + kind) * cap + rank
    info[0:1, :] = slot
    info[1:2, :] = rel * 4 + (kind >> 2)
    info[2:3, :] = (kind & 3) * cap + rank
    for copy in copies[1:5]:
        copy.wait()
    count, width = emb_ref.shape
    probe_count = probes_ref.shape[0]
    slots = assigned_ref[...]
    facts = jnp.concatenate([probes_ref[...], slots >> 5, slots & 31], axis=0).astype(jnp.float32)
    facts = jnp.concatenate([facts, jnp.zeros((128 - probe_count - 2, count), jnp.float32)], axis=0)
    same = lax.broadcasted_iota(jnp.int32, (count, count), 0) == lax.broadcasted_iota(jnp.int32, (count, count), 1)
    mine[:, 0:width] = emb_ref[...]
    mine[:, width:] = lax.dot_general(
        one_hot(same), facts.astype(jnp.bfloat16), NT, preferred_element_type=jnp.float32
    ).astype(jnp.bfloat16)
    copies[5].wait()
    pack(slot, prior_ref[...], cent_ref[...], 2 * 4 * per * cap, rows2)
    pack(slot, prior_ref[...], cent_ref[...], 3 * 4 * per * cap, rows3)


def pack_more_kernel(part, info, prior_ref, cent_ref, rows0, rows1, late2, late3):
    for first, out in ((0, rows0), (4 * part, rows1), (11 * part, late2), (15 * part, late3)):
        pack(info[0:1, :], prior_ref[...], cent_ref[...], first, out)


def order_kernel(*refs):
    pass


def prepare_kernel(cent_ref, own_any, near_any, unit_old, units, own, near, sems):
    copies = fetch(((own_any, own), (near_any, near)), sems)
    step = 256
    for start in range(0, cent_ref.shape[0], step):
        unit_old[start : start + step, :] = unit_wide(cent_ref[start : start + step, :].astype(jnp.float32))
    me, z, y, core = position()
    first = jnp.where((z == 0) | (z == 3), 0, 1)
    copies[0].wait()
    units[first] = unit_wide(own[...].astype(jnp.float32))
    copies[1].wait()
    units[1 - first] = unit_wide(near[...].astype(jnp.float32))


def share_kernel(mine_any, other_any, unit_old, scaled, facts, share_low, share_high, mine_ref, other_ref, sems):
    copies = fetch(((mine_any, mine_ref), (other_any, other_ref)), sems)
    me, z, y, core = position()
    half = mine_ref.shape[0]
    count = 2 * half
    rows, width = unit_old.shape
    copies[0].wait()
    scaled[0:half, :] = unit_wide(mine_ref[:, 0:width].astype(jnp.float32))
    copies[1].wait()
    scaled[half:count, :] = unit_wide(other_ref[:, 0:width].astype(jnp.float32))
    aux = jnp.concatenate([mine_ref[:, width:], other_ref[:, width:]], axis=0).astype(jnp.float32)
    aux = jnp.transpose(aux)[0:16, :].astype(jnp.int32)
    facts[...] = aux
    member = jnp.sum((aux[0:8, :] == me).astype(jnp.float32), axis=0, keepdims=True)
    step = 256
    total = jnp.zeros((1, count), jnp.float32)
    for start in range(0, rows, step):
        scores = lax.dot_general(
            unit_old[start : start + step, :], scaled[...], NT, preferred_element_type=jnp.float32
        )
        total = total + jnp.sum(weights(scores, width), axis=0, keepdims=True)
    piece = count // 16
    lane = lax.broadcasted_iota(jnp.int32, (16, count), 1)
    line = lax.broadcasted_iota(jnp.int32, (16, count), 0)
    apart = jnp.where((member > 0.0) & (lane >= line * piece) & (lane < (line + 1) * piece), total, 0.0)
    spot = lax.broadcasted_iota(jnp.int32, (count, 128), 0)
    block = sum((spot >= piece * step).astype(jnp.int32) for step in range(1, 16))
    together = jnp.where(spot - block * piece == lax.broadcasted_iota(jnp.int32, (count, 128), 1), 1.0, 0.0)
    share = jnp.dot(apart, together, precision=lax.Precision.HIGHEST, preferred_element_type=jnp.float32)
    share_low[...] = share[0:8, :]
    share_high[...] = share[8:16, :]


def update_kernel(after, scaled, facts, cent_ref, prior_ref, fresh_rows, fresh_counts):
    me, z, y, core = position()
    rows, width = cent_ref.shape
    count = scaled.shape[0]
    prior = column(prior_ref[...].astype(jnp.float32))
    target = jnp.where(facts[0:1, :] == me, facts[8:9, :] * 32 + facts[9:10, :], -1)
    step = 256
    for start in range(0, rows, step):
        old = cent_ref[start : start + step, :].astype(jnp.float32)
        hits = one_hot(target == lax.broadcasted_iota(jnp.int32, (step, count), 0) + start)
        sums = jnp.dot(hits, scaled[...], preferred_element_type=jnp.float32)
        gained = jnp.sum(hits.astype(jnp.float32), axis=1, keepdims=True)
        ahead = prior[start : start + step, :]
        updated = (ahead * old + sums) * (1.0 / (ahead + gained))
        fresh_rows[start : start + step, :] = updated.astype(jnp.bfloat16)
        gained_row = lax.dot_general(
            jnp.ones((8, count), jnp.bfloat16), hits, NT, preferred_element_type=jnp.float32
        )
        fresh_counts[0:1, start : start + step] = prior_ref[0:1, start : start + step] + gained_row[0:1, :].astype(jnp.int32)


def level_sums(two, packed, floors, w, per):
    block, width = two.shape[0] // per, two.shape[1]
    lines = []
    for j in range(per):
        rows = packed[w, j]
        floor = floors[w, j]
        scores = lax.dot_general(two[j * block : (j + 1) * block, :], rows, NT, preferred_element_type=jnp.float32)
        power = lax.dot_general(
            jnp.ones((8, width), jnp.bfloat16), rows * rows, NT, preferred_element_type=jnp.float32
        ) + lax.dot_general(
            jnp.ones((8, floor.shape[1]), jnp.bfloat16), floor * floor, NT, preferred_element_type=jnp.float32
        )
        power = jnp.where(power > 0.0, power, 1.0) * (1.0 / width)
        lines.append(jnp.sum(weights(scores * lax.rsqrt(power[0:1, :]), width), axis=0, keepdims=True))
    return jnp.concatenate(lines, axis=0)


def redo(cap, per, scaled, facts_in, me, refs, firsts, packed, floors):
    part = per * cap
    planes = packed.shape[0]
    count = planes * part
    width = scaled.shape[1]
    probe0 = facts_in[0:1, :]
    slots = facts_in[8:9, :] * 32 + facts_in[9:10, :]
    lane = lax.broadcasted_iota(jnp.int32, (count, 128), 1)
    for r, (ref, first) in enumerate(zip(refs, firsts)):
        facts = jnp.transpose(ref[ref.shape[0] - META :, first : first + count].astype(jnp.float32))
        hits = (facts[:, 0:1] * 32.0 + facts[:, 1:2]).astype(jnp.int32) == jnp.where(probe0 == (me ^ r), slots + 1, -1)
        gained = jnp.sum(jnp.where(hits, 1.0, 0.0), axis=1, keepdims=True)
        ahead = facts[:, 2:3]
        floor = (ahead + gained) * math.sqrt(1e-06 * width)
        floor = jnp.where(lane == 0, floor, 0.0).astype(jnp.bfloat16)
        added = jnp.dot(one_hot(hits), scaled[...], preferred_element_type=jnp.float32)
        whole = (ahead * ref[0:count, :].astype(jnp.float32) + added).astype(jnp.bfloat16)
        for w in range(planes):
            for j in range(per):
                start = w * part + j * cap
                packed[w, j, r * cap : (r + 1) * cap, :] = whole[start : start + cap, :]
                floors[w, j, r * cap : (r + 1) * cap, :] = floor[start : start + cap, :]


def early_kernel(
    cap, per, scaled, facts_in, units_any, cross_any, passed_any, any0, any1, any2, any3,
    sums, rows0, rows1, rows2, rows3, units, two_last, packed, floors, sems,
):
    me, z, y, core = position()
    end = (z == 0) | (z == 3)
    refs = (rows0, rows1, rows2, rows3)
    at_end = pltpu.make_async_copy(passed_any, two_last, sems.at[5])
    at_mid = pltpu.make_async_copy(cross_any, two_last, sems.at[5])
    copies = fetch(list(zip((any0, any1, any2, any3, units_any), (*refs, units))), sems)
    pl.when(end)(at_end.start)
    pl.when(jnp.logical_not(end))(at_mid.start)
    for copy in copies:
        copy.wait()
    pl.when(end)(at_end.wait)
    pl.when(jnp.logical_not(end))(at_mid.wait)
    redo(cap, per, scaled, facts_in, me, refs, (0, 0, 0, 0), packed, floors)
    third = unit_wide(two_last[...].astype(jnp.float32))
    for w, two in enumerate((units[0], units[1], third)):
        sums[8 * w : 8 * w + per, :] = level_sums(two, packed, floors, w, per)


def late_kernel(
    cap, per, scaled, facts_in, any0, any1, any2, any3, after, packed, floors, rows0, rows1, rows2, rows3, sems
):
    me, z, y, core = position()
    part = per * cap
    tail = pl.ds(3 * part, part + META)
    refs = (rows0, rows1, rows2, rows3)
    copies = fetch(list(zip((any0.at[tail], any1.at[tail], any2, any3), refs)), sems)
    for copy in copies:
        copy.wait()
    redo(cap, per, scaled, facts_in, me, refs, (3 * part, 3 * part, 0, 0), packed, floors)


def third_kernel(cap, per, early, floors, kept_any, last_any, far_any, out0, out1, out2, out3, kept, two, sems):
    me, z, y, core = position()
    end = (z == 0) | (z == 3)
    at_end = pltpu.make_async_copy(far_any, two, sems.at[1])
    at_mid = pltpu.make_async_copy(last_any, two, sems.at[1])
    pl.when(end)(at_end.start)
    pl.when(jnp.logical_not(end))(at_mid.start)
    copies = fetch([(kept_any, kept)], sems)
    pl.when(end)(at_end.wait)
    pl.when(jnp.logical_not(end))(at_mid.wait)
    two_unit = unit_wide(two[...].astype(jnp.float32))
    copies[0].wait()
    final = level_sums(two_unit, kept, floors, 0, per)
    lines = [early[8 * w : 8 * w + per, :] for w in range(3)] + [final]
    together = jnp.concatenate(lines + [jnp.zeros((16 - 4 * per, 4 * cap), jnp.float32)], axis=0)
    lane = lax.broadcasted_iota(jnp.int32, together.shape, 1)
    line = lax.broadcasted_iota(jnp.int32, together.shape, 0)
    for r, out in enumerate((out0, out1, out2, out3)):
        spread = jnp.zeros_like(together)
        for s in range(4):
            turned = together if s == r else pltpu.roll(together, ((s - r) % 4) * cap, 1)
            spread = jnp.where((line % 4 == s) & (lane >= s * cap) & (lane < (s + 1) * cap), turned, spread)
        for t in range(4):
            out[t : t + 1, :] = jnp.sum(spread[4 * t : 4 * t + 4], axis=0, keepdims=True)


def last_kernel(cap, scale_one, scale_two, info, got0, got1, got2, got3, shares, density, level_two):
    density[...] = jnp.log(shares[:, 0 : density.shape[1]] / scale_one)
    values = jnp.concatenate([got[0:4, :] for got in (got0, got1, got2, got3)], axis=0)
    rows = info.shape[1]
    chosen = jnp.where(info[2:3, :] == lax.broadcasted_iota(jnp.int32, (4 * cap, rows), 0), 1.0, 0.0)
    spread = jnp.dot(values, chosen, precision=lax.Precision.HIGHEST, preferred_element_type=jnp.float32)
    found = jnp.where(info[1:2, :] == lax.broadcasted_iota(jnp.int32, (16, rows), 0), spread, 0.0)
    level_two[...] = jnp.log(jnp.sum(found, axis=0, keepdims=True) / scale_two)


def call(kernel, outs, scratch=(), in_specs=None, **kw):
    def run(*args):
        specs = in_specs or [VMEM] * len(args)
        args = [pltpu.with_memory_space_constraint(a, pltpu.HBM) if spec is HBM else a for a, spec in zip(args, specs)]
        return pl.pallas_call(
            kernel, out_shape=outs, in_specs=specs, scratch_shapes=list(scratch), compiler_params=PARAMS, **kw
        )(*args)

    return run


def lasting(micros):
    return pl.CostEstimate(flops=0, transcendentals=0, bytes_accessed=int(micros * 3_690_000))


def in_order(*values, **kw):
    count = len(values)
    return call(
        order_kernel,
        tuple(jax.ShapeDtypeStruct(value.shape, value.dtype) for value in values),
        in_specs=[ANY] * count,
        out_specs=(ANY,) * count,
        input_output_aliases={i: i for i in range(count)},
        **kw,
    )(*values)


def line_body(embeddings, probes, assigned, prior_counts, centroids, candidates, centroids2):
    emb_rows, width = embeddings.shape
    probe_count = probes.shape[1]
    rows = centroids.shape[0]
    per = BLOCKS2_DEV
    cap = max(2, 3 * rows // (2 * per * 16))
    part = per * cap
    bf16, f32, i32 = jnp.bfloat16, jnp.float32, jnp.int32
    shape = jax.ShapeDtypeStruct

    def exchange(value, apart, sources=range(16)):
        return lax.ppermute(value, "shard", [(i, i ^ apart) for i in sources])

    def rows_of(planes):
        return shape((planes * part + META, width), bf16)

    def room(like):
        return pltpu.VMEM(like.shape, like.dtype)

    mids = range(4, 12)
    near_set = exchange(centroids2, 4)
    cross_set = exchange(centroids2, 12, mids)
    prior_row = prior_counts.reshape(1, rows)
    line = pltpu.VMEM((1, rows), i32)
    mine, early2, early3, info = call(
        functools.partial(pack_kernel, cap, per),
        (shape((emb_rows, width + 128), bf16), rows_of(3), rows_of(3), shape((8, rows), i32)),
        [
            line,
            pltpu.VMEM((emb_rows, width), bf16),
            pltpu.VMEM((probe_count, emb_rows), i32),
            pltpu.VMEM((1, emb_rows), i32),
            line,
            pltpu.VMEM((rows, width), bf16),
            pltpu.SemaphoreType.DMA((6,)),
        ],
        in_specs=[HBM] * 6,
    )(candidates.reshape(1, rows), embeddings, probes.T, assigned.reshape(1, emb_rows), prior_row, centroids)
    early2, early3 = exchange(early2, 2), exchange(early3, 3)
    rows0, rows1, late2, late3 = call(
        functools.partial(pack_more_kernel, part), (rows_of(4), rows_of(4), rows_of(1), rows_of(1))
    )(info, prior_row, centroids)
    mine = jnp.concatenate([mine, exchange(mine, 4)], axis=0)
    near_set, cross_set, mine, rows0 = in_order(near_set, cross_set, mine, rows0)
    across = exchange(mine, 12)
    passed = exchange(cross_set, 4, mids)
    last_set = exchange(near_set, 12, mids)
    mine = jnp.concatenate([mine, across], axis=0)
    mine, early2, early3, late2, late3, rows1 = in_order(mine, early2, early3, late2, late3, rows1)
    mine = jnp.concatenate([mine, exchange(mine, 2)], axis=0)
    late2, late3 = exchange(late2, 2), exchange(late3, 3)
    rows1 = exchange(rows1, 1)
    set_rows = per * BLOCK2
    block_set = pltpu.VMEM((set_rows, width), bf16)
    unit_old, units = call(
        prepare_kernel,
        (shape((rows, width), bf16), shape((2, set_rows, width), bf16)),
        [block_set, block_set, pltpu.SemaphoreType.DMA((2,))],
        in_specs=[VMEM, HBM, ANY],
    )(centroids, centroids2, near_set)
    passed, last_set, mine, unit_old, units = in_order(passed, last_set, mine, unit_old, units)
    far_set = exchange(last_set, 4, mids)
    other = exchange(mine, 1)
    gathered = pltpu.VMEM((8 * emb_rows, width + 128), bf16)
    scaled, facts, share, share_high = call(
        share_kernel,
        (
            shape((16 * emb_rows, width), bf16),
            shape((16, 16 * emb_rows), i32),
            shape((8, 4 * cap), f32),
            shape((8, 4 * cap), f32),
        ),
        [gathered, gathered, pltpu.SemaphoreType.DMA((2,))],
        in_specs=[ANY, ANY, VMEM],
        cost_estimate=lasting(3),
    )(mine, other, unit_old)
    share = share + exchange(share_high, 1)

    def gather(share, apart):
        half = share.shape[0] // 2
        return share[:half] + exchange(share[half:], apart)

    early = call(
        functools.partial(early_kernel, cap, per),
        shape((24, 4 * cap), f32),
        [room(rows_of(4))] * 2
        + [room(rows_of(3))] * 2
        + [
            pltpu.VMEM((2, set_rows, width), bf16),
            block_set,
            pltpu.VMEM((3, per, 4 * cap, width), bf16),
            pltpu.VMEM((3, per, 4 * cap, 128), bf16),
            pltpu.SemaphoreType.DMA((6,)),
        ],
        in_specs=[VMEM, VMEM] + [ANY] * 7,
        cost_estimate=lasting(7),
    )(scaled, facts, units, cross_set, passed, rows0, rows1, early2, early3)
    share, early = in_order(gather(share, 2), early)
    kept = shape((1, per, 4 * cap, width), bf16)
    kept_rows, floors = call(
        functools.partial(late_kernel, cap, per),
        (kept, shape((1, per, 4 * cap, 128), bf16)),
        [room(rows_of(1))] * 4 + [pltpu.SemaphoreType.DMA((4,))],
        in_specs=[VMEM] * 2 + [ANY] * 5,
        cost_estimate=lasting(3),
    )(scaled, facts, rows0, rows1, late2, late3, early)
    share, kept_rows = in_order(gather(share, 12), kept_rows)
    tile = shape((8, 4 * cap), f32)
    tiles = call(
        functools.partial(third_kernel, cap, per),
        (tile,) * 4,
        [room(kept), block_set, pltpu.SemaphoreType.DMA((2,))],
        in_specs=[VMEM, VMEM, ANY, ANY, ANY],
        cost_estimate=lasting(1),
    )(early, floors, kept_rows, last_set, far_set)
    share, *tiles = in_order(share, *tiles)
    new_centroids, counts = call(
        update_kernel, (shape((rows, width), bf16), shape((1, rows), i32)), in_specs=[ANY] + [VMEM] * 4
    )(tiles[0], scaled, facts, centroids, prior_row)
    tiles = [tile if r == 0 else exchange(tile, r) for r, tile in enumerate(tiles)]
    share = gather(share, 4)
    density, level_two = call(
        functools.partial(last_kernel, cap, probe_count * BLOCK, BLOCK2), (shape((1, emb_rows), f32), shape((1, rows), f32))
    )(info, *tiles, share)
    return (density.reshape(-1), new_centroids, counts.reshape(-1), level_two.reshape(-1))


def solution(mesh):
    placed = (
        P(("groups", "shard"), None),
        P(("groups", "shard"), None),
        P(("groups", "shard")),
        P(("groups", "shard")),
        P(("groups", "shard"), None),
        P(("groups", "shard"), None),
        P(("groups", "shard"), None),
    )
    body = line_body if mesh.shape["shard"] == 16 else general_body
    return jax.shard_map(
        body,
        mesh=mesh,
        in_specs=placed,
        out_specs=(
            P(("groups", "shard")),
            P(("groups", "shard"), None),
            P(("groups", "shard")),
            P(("groups", "shard")),
        ),
        check_vma=False,
    )
```

```python
import functools
import math

import jax
import jax.numpy as jnp
from jax import lax
from jax.experimental import pallas as pl
from jax.experimental.pallas import tpu as pltpu
from jax.sharding import PartitionSpec as P

BLOCK = 1024
BLOCKS_DEV = 1
BLOCK2 = 128
BLOCKS2_DEV = 3


def unit_rows(values):
    wide = values.astype(jnp.float32)
    power = jnp.mean(wide * wide, axis=-1, keepdims=True) + 1e-06
    return (wide * lax.rsqrt(power)).astype(jnp.bfloat16)


def kernel_sums(rows, unit):
    scores = lax.dot_general(
        rows, unit, (((1,), (1,)), ((), ())), preferred_element_type=jnp.float32
    )
    return jnp.sum(jnp.exp((scores / rows.shape[1] - 1.0) / 0.1), axis=1)


def block_update(rows, slots, width):
    matches = slots[:, None] == jnp.arange(width, dtype=jnp.int32)[None, :]
    sums = lax.dot_general(
        matches.astype(jnp.bfloat16),
        rows,
        (((0,), (0,)), ((), ())),
        preferred_element_type=jnp.float32,
    )
    counts = jnp.sum(matches.astype(jnp.int32), axis=0)
    return (sums, counts)


def slot_ranks(targets, buckets):
    matches = (targets[:, None] == jnp.arange(buckets, dtype=jnp.int32)[None, :]).astype(jnp.int32)
    return jnp.sum(jnp.cumsum(matches, axis=0) * matches, axis=1) - 1


def general_body(embeddings, probes, assigned, prior_counts, centroids, candidates, centroids2):
    devices = lax.axis_size("shard")
    emb_rows, width = embeddings.shape
    probe_count = probes.shape[1]
    capacity = max(2, 2 * emb_rows * probe_count // (BLOCKS_DEV * devices))
    scaled = unit_rows(embeddings)
    units_old = unit_rows(centroids).reshape(BLOCKS_DEV, BLOCK, width)
    total = emb_rows * probe_count
    buckets = BLOCKS_DEV * devices
    flat = probes.reshape(-1)
    place = flat * capacity + slot_ranks(flat, buckets)
    leading = jnp.arange(total, dtype=jnp.int32) % probe_count == 0
    repeated = jnp.repeat(scaled, probe_count, axis=0)
    slot_values = jnp.where(leading, jnp.repeat(assigned, probe_count), -1)
    send_rows = jnp.zeros((buckets * capacity, width), jnp.bfloat16).at[place].set(repeated)
    send_slots = jnp.full((buckets * capacity,), -1, jnp.int32).at[place].set(slot_values)
    got_rows, got_slots = (
        lax.all_to_all(
            send_rows.reshape(devices, BLOCKS_DEV * capacity, width),
            "shard",
            split_axis=0,
            concat_axis=0,
            tiled=True,
        ),
        lax.all_to_all(
            send_slots.reshape(devices, BLOCKS_DEV * capacity),
            "shard",
            split_axis=0,
            concat_axis=0,
            tiled=True,
        ),
    )
    got_rows = got_rows.reshape(devices, BLOCKS_DEV, capacity, width)
    got_slots = got_slots.reshape(devices, BLOCKS_DEV, capacity)
    local = 0
    picked = got_rows[:, local].reshape(devices * capacity, width)
    slots = got_slots[:, local].reshape(-1)
    weights = [kernel_sums(picked, units_old[local]).reshape(devices, capacity)]
    more_sums, more_counts = block_update(picked, slots, BLOCK)
    sum_list = [more_sums]
    count_list = [more_counts]
    sums = jnp.stack(sum_list)
    counts = jnp.stack(count_list)
    returned = lax.all_to_all(
        jnp.stack(weights, axis=1).reshape(devices, BLOCKS_DEV * capacity),
        "shard",
        split_axis=0,
        concat_axis=0,
        tiled=True,
    )
    totals = jnp.sum(returned.reshape(-1)[place].reshape(emb_rows, probe_count), axis=1)
    density = jnp.log(totals / (probe_count * BLOCK))
    prior = prior_counts.reshape(BLOCKS_DEV, BLOCK)
    fresh = prior + counts
    updated = (
        prior.astype(jnp.float32)[:, :, None]
        * centroids.reshape(BLOCKS_DEV, BLOCK, width).astype(jnp.float32)
        + sums
    ) / fresh.astype(jnp.float32)[:, :, None]
    new_centroids = updated.astype(jnp.bfloat16).reshape(BLOCKS_DEV * BLOCK, width)
    units_new = unit_rows(updated).reshape(BLOCKS_DEV * BLOCK, width)
    rows_two = units_new.shape[0]
    second_capacity = max(2, 3 * rows_two // (2 * BLOCKS2_DEV * devices))
    buckets_two = BLOCKS2_DEV * devices
    chosen = candidates[:, 0]
    place_two = chosen * second_capacity + slot_ranks(chosen, buckets_two)
    send_two = (
        jnp.zeros((buckets_two * second_capacity, width), jnp.bfloat16).at[place_two].set(units_new)
    )
    send_two = send_two.reshape(devices, BLOCKS2_DEV, second_capacity, width)
    units_two = unit_rows(centroids2).reshape(BLOCKS2_DEV, BLOCK2, width)
    arrived = lax.all_to_all(send_two, "shard", split_axis=0, concat_axis=0, tiled=True)
    items = arrived.shape[2]
    weights_two = [
        kernel_sums(arrived[:, local].reshape(-1, width), units_two[local]).reshape(
            arrived.shape[0], items
        )
        for local in range(BLOCKS2_DEV)
    ]
    returned_two = lax.all_to_all(
        jnp.stack(weights_two, axis=1), "shard", split_axis=0, concat_axis=0, tiled=True
    )
    level_two = jnp.log(returned_two.reshape(-1)[place_two] / BLOCK2)
    return (density, new_centroids, fresh.reshape(-1), level_two)


NT = (((1,), (1,)), ((), ()))
PARAMS = pltpu.CompilerParams(vmem_limit_bytes=48 * 1024 * 1024)
META = 16
LATE = 5
STEP = 40
HBM = pl.BlockSpec(memory_space=pltpu.HBM)
ANY = pl.BlockSpec(memory_space=pl.ANY)
VMEM = pl.BlockSpec(memory_space=pltpu.VMEM)


def position():
    me = lax.axis_index("shard")
    return me, me // 4, (me // 2) % 2, me % 2


def unit_wide(wide):
    power = jnp.mean(wide * wide, axis=-1, keepdims=True) + 1e-06
    return (wide * lax.rsqrt(power)).astype(jnp.bfloat16)


def weights(scores, width):
    return jnp.exp(scores * (10.0 / width) - 10.0)


def one_hot(hits):
    return jnp.where(hits, 1.0, 0.0).astype(jnp.bfloat16)


def column(row):
    return jnp.transpose(jnp.broadcast_to(row, (8, row.shape[1])))[:, 0:1]


def fetch(pairs, sems):
    copies = [pltpu.make_async_copy(src, dst, sems.at[i]) for i, (src, dst) in enumerate(pairs)]
    for copy in copies:
        copy.start()
    return copies


def pick_rows(slot, first, count):
    return one_hot(slot == lax.broadcasted_iota(jnp.int32, (count, slot.shape[1]), 0) + first)


def pack(slot, prior, cent, first, out):
    count = out.shape[0] - META
    rows = slot.shape[1]
    ident = lax.broadcasted_iota(jnp.int32, (1, rows), 1) + 1
    line = lax.broadcasted_iota(jnp.int32, (META, rows), 0)
    facts = jnp.where(line == 0, ident >> 5, jnp.where(line == 1, ident & 31, jnp.where(line == 2, prior, 0)))
    facts = facts.astype(jnp.float32).astype(jnp.bfloat16)
    pick = pick_rows(slot, first, count)
    out[0:count, :] = jnp.dot(pick, cent, preferred_element_type=jnp.float32).astype(jnp.bfloat16)
    out[count:, :] = jnp.zeros((META, out.shape[1]), jnp.bfloat16)
    out[count:, 0:count] = lax.dot_general(facts, pick, NT, preferred_element_type=jnp.float32).astype(jnp.bfloat16)


def pack_kernel(
    cap, per, cand_any, emb_any, probes_any, assigned_any, prior_any, cent_any, mine, rows2, rows3, info,
    cand_ref, emb_ref, probes_ref, assigned_ref, prior_ref, cent_ref, sems,
):
    copies = fetch(
        (
            (cand_any, cand_ref),
            (emb_any, emb_ref),
            (probes_any, probes_ref),
            (assigned_any, assigned_ref),
            (prior_any, prior_ref),
            (cent_any, cent_ref),
        ),
        sems,
    )
    me, z, y, core = position()
    rows = cand_ref.shape[1]
    buckets = 16 * per
    before = lax.broadcasted_iota(jnp.int32, (rows, rows), 0) <= lax.broadcasted_iota(jnp.int32, (rows, rows), 1)
    before = one_hot(before)
    copies[0].wait()
    cand = cand_ref[...]
    dev = sum((cand >= per * step).astype(jnp.int32) for step in range(1, 16))
    near = dev >> 2
    plane = jnp.where(z >= 2, 3 - near, near)
    rel = (((dev >> 1) & 1) ^ y) * 2 + ((dev & 1) ^ core)
    named = cand == lax.broadcasted_iota(jnp.int32, (buckets, rows), 0)
    counted = jnp.dot(one_hot(named), before, preferred_element_type=jnp.float32)
    rank = jnp.sum(jnp.where(named, counted, 0.0), axis=0, keepdims=True).astype(jnp.int32) - 1
    kind = plane * per + cand - dev * per
    slot = (rel * 4 * per + kind) * cap + rank
    info[0:1, :] = slot
    info[1:2, :] = rel * 4 + (kind >> 2)
    info[2:3, :] = (kind & 3) * cap + rank
    for copy in copies[1:5]:
        copy.wait()
    count, width = emb_ref.shape
    probe_count = probes_ref.shape[0]
    slots = assigned_ref[...]
    facts = jnp.concatenate([probes_ref[...], slots >> 5, slots & 31], axis=0).astype(jnp.float32)
    facts = jnp.concatenate([facts, jnp.zeros((128 - probe_count - 2, count), jnp.float32)], axis=0)
    same = lax.broadcasted_iota(jnp.int32, (count, count), 0) == lax.broadcasted_iota(jnp.int32, (count, count), 1)
    mine[:, 0:width] = emb_ref[...]
    mine[:, width:] = lax.dot_general(
        one_hot(same), facts.astype(jnp.bfloat16), NT, preferred_element_type=jnp.float32
    ).astype(jnp.bfloat16)
    copies[5].wait()
    pack(slot, prior_ref[...], cent_ref[...], 2 * 4 * per * cap, rows2)
    pack(slot, prior_ref[...], cent_ref[...], 3 * 4 * per * cap, rows3)


def pack_more_kernel(part, info, prior_ref, cent_ref, rows0, rows1, late3):
    for first, out in ((0, rows0), (4 * part, rows1), (15 * part, late3)):
        pack(info[0:1, :], prior_ref[...], cent_ref[...], first, out)


def order_kernel(*refs):
    pass


def prepare_kernel(cent_ref, own_any, near_any, unit_old, units, own, near, sems):
    copies = fetch(((own_any, own), (near_any, near)), sems)
    step = 256
    for start in range(0, cent_ref.shape[0], step):
        unit_old[start : start + step, :] = unit_wide(cent_ref[start : start + step, :].astype(jnp.float32))
    me, z, y, core = position()
    first = jnp.where((z == 0) | (z == 3), 0, 1)
    copies[0].wait()
    units[first] = unit_wide(own[...].astype(jnp.float32))
    copies[1].wait()
    units[1 - first] = unit_wide(near[...].astype(jnp.float32))


def share_kernel(mine_any, other_any, unit_old, scaled, facts, share_low, share_high, mine_ref, other_ref, sems):
    copies = fetch(((mine_any, mine_ref), (other_any, other_ref)), sems)
    me, z, y, core = position()
    half = mine_ref.shape[0]
    count = 2 * half
    rows, width = unit_old.shape
    copies[0].wait()
    scaled[0:half, :] = unit_wide(mine_ref[:, 0:width].astype(jnp.float32))
    copies[1].wait()
    scaled[half:count, :] = unit_wide(other_ref[:, 0:width].astype(jnp.float32))
    aux = jnp.concatenate([mine_ref[:, width:], other_ref[:, width:]], axis=0).astype(jnp.float32)
    aux = jnp.transpose(aux)[0:16, :].astype(jnp.int32)
    facts[...] = aux
    member = jnp.sum((aux[0:8, :] == me).astype(jnp.float32), axis=0, keepdims=True)
    step = 256
    total = jnp.zeros((1, count), jnp.float32)
    for start in range(0, rows, step):
        scores = lax.dot_general(
            unit_old[start : start + step, :], scaled[...], NT, preferred_element_type=jnp.float32
        )
        total = total + jnp.sum(weights(scores, width), axis=0, keepdims=True)
    piece = count // 16
    lane = lax.broadcasted_iota(jnp.int32, (16, count), 1)
    line = lax.broadcasted_iota(jnp.int32, (16, count), 0)
    apart = jnp.where((member > 0.0) & (lane >= line * piece) & (lane < (line + 1) * piece), total, 0.0)
    spot = lax.broadcasted_iota(jnp.int32, (count, 128), 0)
    block = sum((spot >= piece * step).astype(jnp.int32) for step in range(1, 16))
    together = jnp.where(spot - block * piece == lax.broadcasted_iota(jnp.int32, (count, 128), 1), 1.0, 0.0)
    share = jnp.dot(apart, together, precision=lax.Precision.HIGHEST, preferred_element_type=jnp.float32)
    share_low[...] = share[0:8, :]
    share_high[...] = share[8:16, :]


def update_kernel(after, scaled, facts, cent_ref, prior_ref, fresh_rows, fresh_counts):
    me, z, y, core = position()
    rows, width = cent_ref.shape
    count = scaled.shape[0]
    prior = column(prior_ref[...].astype(jnp.float32))
    target = jnp.where(facts[0:1, :] == me, facts[8:9, :] * 32 + facts[9:10, :], -1)
    step = 256
    for start in range(0, rows, step):
        old = cent_ref[start : start + step, :].astype(jnp.float32)
        hits = one_hot(target == lax.broadcasted_iota(jnp.int32, (step, count), 0) + start)
        sums = jnp.dot(hits, scaled[...], preferred_element_type=jnp.float32)
        gained = jnp.sum(hits.astype(jnp.float32), axis=1, keepdims=True)
        ahead = prior[start : start + step, :]
        updated = (ahead * old + sums) * (1.0 / (ahead + gained))
        fresh_rows[start : start + step, :] = updated.astype(jnp.bfloat16)
        gained_row = lax.dot_general(
            jnp.ones((8, count), jnp.bfloat16), hits, NT, preferred_element_type=jnp.float32
        )
        fresh_counts[0:1, start : start + step] = prior_ref[0:1, start : start + step] + gained_row[0:1, :].astype(jnp.int32)


def level_sums(two, packed, floors, w, per):
    block, width = two.shape[0] // per, two.shape[1]
    lines = []
    for j in range(per):
        rows = packed[w, j]
        floor = floors[w, j]
        scores = lax.dot_general(two[j * block : (j + 1) * block, :], rows, NT, preferred_element_type=jnp.float32)
        power = lax.dot_general(
            jnp.ones((8, width), jnp.bfloat16), rows * rows, NT, preferred_element_type=jnp.float32
        ) + lax.dot_general(
            jnp.ones((8, floor.shape[1]), jnp.bfloat16), floor * floor, NT, preferred_element_type=jnp.float32
        )
        power = jnp.where(power > 0.0, power, 1.0) * (1.0 / width)
        lines.append(jnp.sum(weights(scores * lax.rsqrt(power[0:1, :]), width), axis=0, keepdims=True))
    return jnp.concatenate(lines, axis=0)


def redo(cap, per, scaled, facts_in, me, refs, firsts, packed, floors):
    part = per * cap
    planes = packed.shape[0]
    count = planes * part
    width = scaled.shape[1]
    probe0 = facts_in[0:1, :]
    slots = facts_in[8:9, :] * 32 + facts_in[9:10, :]
    lane = lax.broadcasted_iota(jnp.int32, (count, 128), 1)
    for r, (ref, first) in enumerate(zip(refs, firsts)):
        facts = jnp.transpose(ref[ref.shape[0] - META :, first : first + count].astype(jnp.float32))
        hits = (facts[:, 0:1] * 32.0 + facts[:, 1:2]).astype(jnp.int32) == jnp.where(probe0 == (me ^ r), slots + 1, -1)
        gained = jnp.sum(jnp.where(hits, 1.0, 0.0), axis=1, keepdims=True)
        ahead = facts[:, 2:3]
        floor = (ahead + gained) * math.sqrt(1e-06 * width)
        floor = jnp.where(lane == 0, floor, 0.0).astype(jnp.bfloat16)
        added = jnp.dot(one_hot(hits), scaled[...], preferred_element_type=jnp.float32)
        whole = (ahead * ref[0:count, :].astype(jnp.float32) + added).astype(jnp.bfloat16)
        for w in range(planes):
            for j in range(per):
                start = w * part + j * cap
                packed[w, j, r * cap : (r + 1) * cap, :] = whole[start : start + cap, :]
                floors[w, j, r * cap : (r + 1) * cap, :] = floor[start : start + cap, :]


def early_kernel(
    cap, per, scaled, facts_in, units_any, cross_any, passed_any, any0, any1, any2, any3,
    sums, rows0, rows1, rows2, rows3, units, two_last, packed, floors, sems,
):
    me, z, y, core = position()
    end = (z == 0) | (z == 3)
    refs = (rows0, rows1, rows2, rows3)
    at_end = pltpu.make_async_copy(passed_any, two_last, sems.at[5])
    at_mid = pltpu.make_async_copy(cross_any, two_last, sems.at[5])
    copies = fetch(list(zip((any0, any1, any2, any3, units_any), (*refs, units))), sems)
    pl.when(end)(at_end.start)
    pl.when(jnp.logical_not(end))(at_mid.start)
    for copy in copies:
        copy.wait()
    pl.when(end)(at_end.wait)
    pl.when(jnp.logical_not(end))(at_mid.wait)
    redo(cap, per, scaled, facts_in, me, refs, (0, 0, 0, 0), packed, floors)
    third = unit_wide(two_last[...].astype(jnp.float32))
    for w, two in enumerate((units[0], units[1], third)):
        sums[8 * w : 8 * w + per, :] = level_sums(two, packed, floors, w, per)


def late_kernel(
    cap, per, scaled, facts_in, any0, any1, any2, any3, after, packed, floors, rows0, rows1, rows2, rows3, sems
):
    me, z, y, core = position()
    part = per * cap
    tail = pl.ds(3 * part, part + META)
    refs = (rows0, rows1, rows2, rows3)
    copies = fetch(list(zip((any0.at[tail], any1.at[tail], any2.at[tail], any3), refs)), sems)
    for copy in copies:
        copy.wait()
    redo(cap, per, scaled, facts_in, me, refs, (3 * part, 3 * part, 3 * part, 0), packed, floors)


def third_kernel(cap, per, early, floors, kept_any, last_any, far_any, out0, out1, out2, out3, kept, two, sems):
    me, z, y, core = position()
    end = (z == 0) | (z == 3)
    at_end = pltpu.make_async_copy(far_any, two, sems.at[1])
    at_mid = pltpu.make_async_copy(last_any, two, sems.at[1])
    pl.when(end)(at_end.start)
    pl.when(jnp.logical_not(end))(at_mid.start)
    copies = fetch([(kept_any, kept)], sems)
    pl.when(end)(at_end.wait)
    pl.when(jnp.logical_not(end))(at_mid.wait)
    two_unit = unit_wide(two[...].astype(jnp.float32))
    copies[0].wait()
    final = level_sums(two_unit, kept, floors, 0, per)
    lines = [early[8 * w : 8 * w + per, :] for w in range(3)] + [final]
    together = jnp.concatenate(lines + [jnp.zeros((16 - 4 * per, 4 * cap), jnp.float32)], axis=0)
    lane = lax.broadcasted_iota(jnp.int32, together.shape, 1)
    line = lax.broadcasted_iota(jnp.int32, together.shape, 0)
    for r, out in enumerate((out0, out1, out2, out3)):
        spread = jnp.zeros_like(together)
        for s in range(4):
            turned = together if s == r else pltpu.roll(together, ((s - r) % 4) * cap, 1)
            spread = jnp.where((line % 4 == s) & (lane >= s * cap) & (lane < (s + 1) * cap), turned, spread)
        for t in range(4):
            out[t : t + 1, :] = jnp.sum(spread[4 * t : 4 * t + 4], axis=0, keepdims=True)


def last_kernel(cap, scale_one, scale_two, info, got0, got1, got2, got3, shares, density, level_two):
    density[...] = jnp.log(shares[:, 0 : density.shape[1]] / scale_one)
    values = jnp.concatenate([got[0:4, :] for got in (got0, got1, got2, got3)], axis=0)
    rows = info.shape[1]
    chosen = jnp.where(info[2:3, :] == lax.broadcasted_iota(jnp.int32, (4 * cap, rows), 0), 1.0, 0.0)
    spread = jnp.dot(values, chosen, precision=lax.Precision.HIGHEST, preferred_element_type=jnp.float32)
    found = jnp.where(info[1:2, :] == lax.broadcasted_iota(jnp.int32, (16, rows), 0), spread, 0.0)
    level_two[...] = jnp.log(jnp.sum(found, axis=0, keepdims=True) / scale_two)


def call(kernel, outs, scratch=(), in_specs=None, **kw):
    def run(*args):
        specs = in_specs or [VMEM] * len(args)
        args = [pltpu.with_memory_space_constraint(a, pltpu.HBM) if spec is HBM else a for a, spec in zip(args, specs)]
        return pl.pallas_call(
            kernel, out_shape=outs, in_specs=specs, scratch_shapes=list(scratch), compiler_params=PARAMS, **kw
        )(*args)

    return run


def lasting(micros):
    return pl.CostEstimate(flops=0, transcendentals=0, bytes_accessed=int(micros * 3_690_000))


def in_order(*values, **kw):
    count = len(values)
    return call(
        order_kernel,
        tuple(jax.ShapeDtypeStruct(value.shape, value.dtype) for value in values),
        in_specs=[ANY] * count,
        out_specs=(ANY,) * count,
        input_output_aliases={i: i for i in range(count)},
        **kw,
    )(*values)


def line_body(embeddings, probes, assigned, prior_counts, centroids, candidates, centroids2):
    emb_rows, width = embeddings.shape
    probe_count = probes.shape[1]
    rows = centroids.shape[0]
    per = BLOCKS2_DEV
    cap = max(2, 3 * rows // (2 * per * 16))
    part = per * cap
    bf16, f32, i32 = jnp.bfloat16, jnp.float32, jnp.int32
    shape = jax.ShapeDtypeStruct

    def exchange(value, apart, sources=range(16)):
        return lax.ppermute(value, "shard", [(i, i ^ apart) for i in sources])

    def rows_of(planes):
        return shape((planes * part + META, width), bf16)

    def room(like):
        return pltpu.VMEM(like.shape, like.dtype)

    mids = range(4, 12)
    near_set = exchange(centroids2, 4)
    cross_set = exchange(centroids2, 12, mids)
    prior_row = prior_counts.reshape(1, rows)
    line = pltpu.VMEM((1, rows), i32)
    mine, rows2, early3, info = call(
        functools.partial(pack_kernel, cap, per),
        (shape((emb_rows, width + 128), bf16), rows_of(4), rows_of(3), shape((8, rows), i32)),
        [
            line,
            pltpu.VMEM((emb_rows, width), bf16),
            pltpu.VMEM((probe_count, emb_rows), i32),
            pltpu.VMEM((1, emb_rows), i32),
            line,
            pltpu.VMEM((rows, width), bf16),
            pltpu.SemaphoreType.DMA((6,)),
        ],
        in_specs=[HBM] * 6,
    )(candidates.reshape(1, rows), embeddings, probes.T, assigned.reshape(1, emb_rows), prior_row, centroids)
    rows2, early3 = exchange(rows2, 2), exchange(early3, 3)
    rows0, rows1, late3 = call(
        functools.partial(pack_more_kernel, part), (rows_of(4), rows_of(4), rows_of(1))
    )(info, prior_row, centroids)
    mine = jnp.concatenate([mine, exchange(mine, 4)], axis=0)
    near_set, cross_set, mine, rows0 = in_order(near_set, cross_set, mine, rows0)
    across = exchange(mine, 12)
    passed = exchange(cross_set, 4, mids)
    last_set = exchange(near_set, 12, mids)
    mine = jnp.concatenate([mine, across], axis=0)
    mine, rows2, early3, late3, rows1 = in_order(mine, rows2, early3, late3, rows1)
    mine = jnp.concatenate([mine, exchange(mine, 2)], axis=0)
    late3 = exchange(late3, 3)
    rows1 = exchange(rows1, 1)
    set_rows = per * BLOCK2
    block_set = pltpu.VMEM((set_rows, width), bf16)
    unit_old, units = call(
        prepare_kernel,
        (shape((rows, width), bf16), shape((2, set_rows, width), bf16)),
        [block_set, block_set, pltpu.SemaphoreType.DMA((2,))],
        in_specs=[VMEM, HBM, ANY],
    )(centroids, centroids2, near_set)
    passed, last_set, mine, unit_old, units = in_order(passed, last_set, mine, unit_old, units)
    far_set = exchange(last_set, 4, mids)
    other = exchange(mine, 1)
    gathered = pltpu.VMEM((8 * emb_rows, width + 128), bf16)
    scaled, facts, share, share_high = call(
        share_kernel,
        (
            shape((16 * emb_rows, width), bf16),
            shape((16, 16 * emb_rows), i32),
            shape((8, 4 * cap), f32),
            shape((8, 4 * cap), f32),
        ),
        [gathered, gathered, pltpu.SemaphoreType.DMA((2,))],
        in_specs=[ANY, ANY, VMEM],
        cost_estimate=lasting(3),
    )(mine, other, unit_old)
    share = share + exchange(share_high, 1)

    def gather(share, apart):
        half = share.shape[0] // 2
        return share[:half] + exchange(share[half:], apart)

    early = call(
        functools.partial(early_kernel, cap, per),
        shape((24, 4 * cap), f32),
        [room(rows_of(4))] * 3
        + [room(rows_of(3))]
        + [
            pltpu.VMEM((2, set_rows, width), bf16),
            block_set,
            pltpu.VMEM((3, per, 4 * cap, width), bf16),
            pltpu.VMEM((3, per, 4 * cap, 128), bf16),
            pltpu.SemaphoreType.DMA((6,)),
        ],
        in_specs=[VMEM, VMEM] + [ANY] * 7,
        cost_estimate=lasting(7),
    )(scaled, facts, units, cross_set, passed, rows0, rows1, rows2, early3)
    share, early = in_order(gather(share, 2), early)
    kept = shape((1, per, 4 * cap, width), bf16)
    kept_rows, floors = call(
        functools.partial(late_kernel, cap, per),
        (kept, shape((1, per, 4 * cap, 128), bf16)),
        [room(rows_of(1))] * 4 + [pltpu.SemaphoreType.DMA((4,))],
        in_specs=[VMEM] * 2 + [ANY] * 5,
        cost_estimate=lasting(3),
    )(scaled, facts, rows0, rows1, rows2, late3, early)
    share, kept_rows = in_order(gather(share, 12), kept_rows)
    tile = shape((8, 4 * cap), f32)
    tiles = call(
        functools.partial(third_kernel, cap, per),
        (tile,) * 4,
        [room(kept), block_set, pltpu.SemaphoreType.DMA((2,))],
        in_specs=[VMEM, VMEM, ANY, ANY, ANY],
        cost_estimate=lasting(1),
    )(early, floors, kept_rows, last_set, far_set)
    share, *tiles = in_order(share, *tiles)
    new_centroids, counts = call(
        update_kernel, (shape((rows, width), bf16), shape((1, rows), i32)), in_specs=[ANY] + [VMEM] * 4
    )(tiles[0], scaled, facts, centroids, prior_row)
    tiles = [tile if r == 0 else exchange(tile, r) for r, tile in enumerate(tiles)]
    share = gather(share, 4)
    density, level_two = call(
        functools.partial(last_kernel, cap, probe_count * BLOCK, BLOCK2), (shape((1, emb_rows), f32), shape((1, rows), f32))
    )(info, *tiles, share)
    return (density.reshape(-1), new_centroids, counts.reshape(-1), level_two.reshape(-1))


def solution(mesh):
    placed = (
        P(("groups", "shard"), None),
        P(("groups", "shard"), None),
        P(("groups", "shard")),
        P(("groups", "shard")),
        P(("groups", "shard"), None),
        P(("groups", "shard"), None),
        P(("groups", "shard"), None),
    )
    body = line_body if mesh.shape["shard"] == 16 else general_body
    return jax.shard_map(
        body,
        mesh=mesh,
        in_specs=placed,
        out_specs=(
            P(("groups", "shard")),
            P(("groups", "shard"), None),
            P(("groups", "shard")),
            P(("groups", "shard")),
        ),
        check_vma=False,
    )
```

```python
import functools
import math

import jax
import jax.numpy as jnp
from jax import lax
from jax.experimental import pallas as pl
from jax.experimental.pallas import tpu as pltpu
from jax.sharding import PartitionSpec as P

BLOCK = 1024
BLOCKS_DEV = 1
BLOCK2 = 128
BLOCKS2_DEV = 3


def unit_rows(values):
    wide = values.astype(jnp.float32)
    power = jnp.mean(wide * wide, axis=-1, keepdims=True) + 1e-06
    return (wide * lax.rsqrt(power)).astype(jnp.bfloat16)


def kernel_sums(rows, unit):
    scores = lax.dot_general(
        rows, unit, (((1,), (1,)), ((), ())), preferred_element_type=jnp.float32
    )
    return jnp.sum(jnp.exp((scores / rows.shape[1] - 1.0) / 0.1), axis=1)


def block_update(rows, slots, width):
    matches = slots[:, None] == jnp.arange(width, dtype=jnp.int32)[None, :]
    sums = lax.dot_general(
        matches.astype(jnp.bfloat16),
        rows,
        (((0,), (0,)), ((), ())),
        preferred_element_type=jnp.float32,
    )
    counts = jnp.sum(matches.astype(jnp.int32), axis=0)
    return (sums, counts)


def slot_ranks(targets, buckets):
    matches = (targets[:, None] == jnp.arange(buckets, dtype=jnp.int32)[None, :]).astype(jnp.int32)
    return jnp.sum(jnp.cumsum(matches, axis=0) * matches, axis=1) - 1


def general_body(embeddings, probes, assigned, prior_counts, centroids, candidates, centroids2):
    devices = lax.axis_size("shard")
    emb_rows, width = embeddings.shape
    probe_count = probes.shape[1]
    capacity = max(2, 2 * emb_rows * probe_count // (BLOCKS_DEV * devices))
    scaled = unit_rows(embeddings)
    units_old = unit_rows(centroids).reshape(BLOCKS_DEV, BLOCK, width)
    total = emb_rows * probe_count
    buckets = BLOCKS_DEV * devices
    flat = probes.reshape(-1)
    place = flat * capacity + slot_ranks(flat, buckets)
    leading = jnp.arange(total, dtype=jnp.int32) % probe_count == 0
    repeated = jnp.repeat(scaled, probe_count, axis=0)
    slot_values = jnp.where(leading, jnp.repeat(assigned, probe_count), -1)
    send_rows = jnp.zeros((buckets * capacity, width), jnp.bfloat16).at[place].set(repeated)
    send_slots = jnp.full((buckets * capacity,), -1, jnp.int32).at[place].set(slot_values)
    got_rows, got_slots = (
        lax.all_to_all(
            send_rows.reshape(devices, BLOCKS_DEV * capacity, width),
            "shard",
            split_axis=0,
            concat_axis=0,
            tiled=True,
        ),
        lax.all_to_all(
            send_slots.reshape(devices, BLOCKS_DEV * capacity),
            "shard",
            split_axis=0,
            concat_axis=0,
            tiled=True,
        ),
    )
    got_rows = got_rows.reshape(devices, BLOCKS_DEV, capacity, width)
    got_slots = got_slots.reshape(devices, BLOCKS_DEV, capacity)
    local = 0
    picked = got_rows[:, local].reshape(devices * capacity, width)
    slots = got_slots[:, local].reshape(-1)
    weights = [kernel_sums(picked, units_old[local]).reshape(devices, capacity)]
    more_sums, more_counts = block_update(picked, slots, BLOCK)
    sum_list = [more_sums]
    count_list = [more_counts]
    sums = jnp.stack(sum_list)
    counts = jnp.stack(count_list)
    returned = lax.all_to_all(
        jnp.stack(weights, axis=1).reshape(devices, BLOCKS_DEV * capacity),
        "shard",
        split_axis=0,
        concat_axis=0,
        tiled=True,
    )
    totals = jnp.sum(returned.reshape(-1)[place].reshape(emb_rows, probe_count), axis=1)
    density = jnp.log(totals / (probe_count * BLOCK))
    prior = prior_counts.reshape(BLOCKS_DEV, BLOCK)
    fresh = prior + counts
    updated = (
        prior.astype(jnp.float32)[:, :, None]
        * centroids.reshape(BLOCKS_DEV, BLOCK, width).astype(jnp.float32)
        + sums
    ) / fresh.astype(jnp.float32)[:, :, None]
    new_centroids = updated.astype(jnp.bfloat16).reshape(BLOCKS_DEV * BLOCK, width)
    units_new = unit_rows(updated).reshape(BLOCKS_DEV * BLOCK, width)
    rows_two = units_new.shape[0]
    second_capacity = max(2, 3 * rows_two // (2 * BLOCKS2_DEV * devices))
    buckets_two = BLOCKS2_DEV * devices
    chosen = candidates[:, 0]
    place_two = chosen * second_capacity + slot_ranks(chosen, buckets_two)
    send_two = (
        jnp.zeros((buckets_two * second_capacity, width), jnp.bfloat16).at[place_two].set(units_new)
    )
    send_two = send_two.reshape(devices, BLOCKS2_DEV, second_capacity, width)
    units_two = unit_rows(centroids2).reshape(BLOCKS2_DEV, BLOCK2, width)
    arrived = lax.all_to_all(send_two, "shard", split_axis=0, concat_axis=0, tiled=True)
    items = arrived.shape[2]
    weights_two = [
        kernel_sums(arrived[:, local].reshape(-1, width), units_two[local]).reshape(
            arrived.shape[0], items
        )
        for local in range(BLOCKS2_DEV)
    ]
    returned_two = lax.all_to_all(
        jnp.stack(weights_two, axis=1), "shard", split_axis=0, concat_axis=0, tiled=True
    )
    level_two = jnp.log(returned_two.reshape(-1)[place_two] / BLOCK2)
    return (density, new_centroids, fresh.reshape(-1), level_two)


NT = (((1,), (1,)), ((), ()))
PARAMS = pltpu.CompilerParams(vmem_limit_bytes=48 * 1024 * 1024)
META = 16
LATE = 5
STEP = 40
HBM = pl.BlockSpec(memory_space=pltpu.HBM)
ANY = pl.BlockSpec(memory_space=pl.ANY)
VMEM = pl.BlockSpec(memory_space=pltpu.VMEM)


def position():
    me = lax.axis_index("shard")
    return me, me // 4, (me // 2) % 2, me % 2


def unit_wide(wide):
    power = jnp.mean(wide * wide, axis=-1, keepdims=True) + 1e-06
    return (wide * lax.rsqrt(power)).astype(jnp.bfloat16)


def weights(scores, width):
    return jnp.exp(scores * (10.0 / width) - 10.0)


def one_hot(hits):
    return jnp.where(hits, 1.0, 0.0).astype(jnp.bfloat16)


def column(row):
    return jnp.transpose(jnp.broadcast_to(row, (8, row.shape[1])))[:, 0:1]


def fetch(pairs, sems):
    copies = [pltpu.make_async_copy(src, dst, sems.at[i]) for i, (src, dst) in enumerate(pairs)]
    for copy in copies:
        copy.start()
    return copies


def pick_rows(slot, first, count):
    return one_hot(slot == lax.broadcasted_iota(jnp.int32, (count, slot.shape[1]), 0) + first)


def pack(slot, prior, cent, first, out):
    count = out.shape[0] - META
    rows = slot.shape[1]
    ident = lax.broadcasted_iota(jnp.int32, (1, rows), 1) + 1
    line = lax.broadcasted_iota(jnp.int32, (META, rows), 0)
    facts = jnp.where(line == 0, ident >> 5, jnp.where(line == 1, ident & 31, jnp.where(line == 2, prior, 0)))
    facts = facts.astype(jnp.float32).astype(jnp.bfloat16)
    pick = pick_rows(slot, first, count)
    out[0:count, :] = jnp.dot(pick, cent, preferred_element_type=jnp.float32).astype(jnp.bfloat16)
    out[count:, :] = jnp.zeros((META, out.shape[1]), jnp.bfloat16)
    out[count:, 0:count] = lax.dot_general(facts, pick, NT, preferred_element_type=jnp.float32).astype(jnp.bfloat16)


def pack_kernel(
    cap, per, cand_any, emb_any, probes_any, assigned_any, prior_any, cent_any, mine, rows2, rows3, info,
    cand_ref, emb_ref, probes_ref, assigned_ref, prior_ref, cent_ref, sems,
):
    copies = fetch(
        (
            (cand_any, cand_ref),
            (emb_any, emb_ref),
            (probes_any, probes_ref),
            (assigned_any, assigned_ref),
            (prior_any, prior_ref),
            (cent_any, cent_ref),
        ),
        sems,
    )
    me, z, y, core = position()
    rows = cand_ref.shape[1]
    buckets = 16 * per
    before = lax.broadcasted_iota(jnp.int32, (rows, rows), 0) <= lax.broadcasted_iota(jnp.int32, (rows, rows), 1)
    before = one_hot(before)
    copies[0].wait()
    cand = cand_ref[...]
    dev = sum((cand >= per * step).astype(jnp.int32) for step in range(1, 16))
    near = dev >> 2
    plane = jnp.where(z >= 2, 3 - near, near)
    rel = (((dev >> 1) & 1) ^ y) * 2 + ((dev & 1) ^ core)
    named = cand == lax.broadcasted_iota(jnp.int32, (buckets, rows), 0)
    counted = jnp.dot(one_hot(named), before, preferred_element_type=jnp.float32)
    rank = jnp.sum(jnp.where(named, counted, 0.0), axis=0, keepdims=True).astype(jnp.int32) - 1
    kind = plane * per + cand - dev * per
    slot = (rel * 4 * per + kind) * cap + rank
    info[0:1, :] = slot
    info[1:2, :] = rel * 4 + (kind >> 2)
    info[2:3, :] = (kind & 3) * cap + rank
    for copy in copies[1:5]:
        copy.wait()
    count, width = emb_ref.shape
    probe_count = probes_ref.shape[0]
    slots = assigned_ref[...]
    facts = jnp.concatenate([probes_ref[...], slots >> 5, slots & 31], axis=0).astype(jnp.float32)
    facts = jnp.concatenate([facts, jnp.zeros((128 - probe_count - 2, count), jnp.float32)], axis=0)
    same = lax.broadcasted_iota(jnp.int32, (count, count), 0) == lax.broadcasted_iota(jnp.int32, (count, count), 1)
    mine[:, 0:width] = emb_ref[...]
    mine[:, width:] = lax.dot_general(
        one_hot(same), facts.astype(jnp.bfloat16), NT, preferred_element_type=jnp.float32
    ).astype(jnp.bfloat16)
    copies[5].wait()
    pack(slot, prior_ref[...], cent_ref[...], 2 * 4 * per * cap, rows2)
    pack(slot, prior_ref[...], cent_ref[...], 3 * 4 * per * cap, rows3)


def pack_more_kernel(part, info, prior_ref, cent_ref, rows0, rows1, late2, late3):
    for first, out in ((0, rows0), (4 * part, rows1), (11 * part, late2), (15 * part, late3)):
        pack(info[0:1, :], prior_ref[...], cent_ref[...], first, out)


def order_kernel(*refs):
    pass


def prepare_kernel(cent_ref, own_any, near_any, unit_old, units, own, near, sems):
    copies = fetch(((own_any, own), (near_any, near)), sems)
    step = 256
    for start in range(0, cent_ref.shape[0], step):
        unit_old[start : start + step, :] = unit_wide(cent_ref[start : start + step, :].astype(jnp.float32))
    me, z, y, core = position()
    first = jnp.where((z == 0) | (z == 3), 0, 1)
    copies[0].wait()
    units[first] = unit_wide(own[...].astype(jnp.float32))
    copies[1].wait()
    units[1 - first] = unit_wide(near[...].astype(jnp.float32))


def share_kernel(mine_any, other_any, unit_old, scaled, facts, share_low, share_high, mine_ref, other_ref, sems):
    copies = fetch(((mine_any, mine_ref), (other_any, other_ref)), sems)
    me, z, y, core = position()
    half = mine_ref.shape[0]
    count = 2 * half
    rows, width = unit_old.shape
    copies[0].wait()
    scaled[0:half, :] = unit_wide(mine_ref[:, 0:width].astype(jnp.float32))
    copies[1].wait()
    scaled[half:count, :] = unit_wide(other_ref[:, 0:width].astype(jnp.float32))
    aux = jnp.concatenate([mine_ref[:, width:], other_ref[:, width:]], axis=0).astype(jnp.float32)
    aux = jnp.transpose(aux)[0:16, :].astype(jnp.int32)
    facts[...] = aux
    member = jnp.sum((aux[0:8, :] == me).astype(jnp.float32), axis=0, keepdims=True)
    step = 256
    total = jnp.zeros((1, count), jnp.float32)
    for start in range(0, rows, step):
        scores = lax.dot_general(
            unit_old[start : start + step, :], scaled[...], NT, preferred_element_type=jnp.float32
        )
        total = total + jnp.sum(weights(scores, width), axis=0, keepdims=True)
    piece = count // 16
    lane = lax.broadcasted_iota(jnp.int32, (16, count), 1)
    line = lax.broadcasted_iota(jnp.int32, (16, count), 0)
    apart = jnp.where((member > 0.0) & (lane >= line * piece) & (lane < (line + 1) * piece), total, 0.0)
    spot = lax.broadcasted_iota(jnp.int32, (count, 128), 0)
    block = sum((spot >= piece * step).astype(jnp.int32) for step in range(1, 16))
    together = jnp.where(spot - block * piece == lax.broadcasted_iota(jnp.int32, (count, 128), 1), 1.0, 0.0)
    share = jnp.dot(apart, together, precision=lax.Precision.HIGHEST, preferred_element_type=jnp.float32)
    share_low[...] = jnp.concatenate([share[0:4, :], share[8:12, :]], axis=0)
    share_high[...] = jnp.concatenate([share[4:8, :], share[12:16, :]], axis=0)


def update_kernel(after, scaled, facts, cent_ref, prior_ref, fresh_rows, fresh_counts):
    me, z, y, core = position()
    rows, width = cent_ref.shape
    count = scaled.shape[0]
    prior = column(prior_ref[...].astype(jnp.float32))
    target = jnp.where(facts[0:1, :] == me, facts[8:9, :] * 32 + facts[9:10, :], -1)
    step = 256
    for start in range(0, rows, step):
        old = cent_ref[start : start + step, :].astype(jnp.float32)
        hits = one_hot(target == lax.broadcasted_iota(jnp.int32, (step, count), 0) + start)
        sums = jnp.dot(hits, scaled[...], preferred_element_type=jnp.float32)
        gained = jnp.sum(hits.astype(jnp.float32), axis=1, keepdims=True)
        ahead = prior[start : start + step, :]
        updated = (ahead * old + sums) * (1.0 / (ahead + gained))
        fresh_rows[start : start + step, :] = updated.astype(jnp.bfloat16)
        gained_row = lax.dot_general(
            jnp.ones((8, count), jnp.bfloat16), hits, NT, preferred_element_type=jnp.float32
        )
        fresh_counts[0:1, start : start + step] = prior_ref[0:1, start : start + step] + gained_row[0:1, :].astype(jnp.int32)


def level_sums(two, packed, floors, w, per):
    block, width = two.shape[0] // per, two.shape[1]
    lines = []
    for j in range(per):
        rows = packed[w, j]
        floor = floors[w, j]
        scores = lax.dot_general(two[j * block : (j + 1) * block, :], rows, NT, preferred_element_type=jnp.float32)
        power = lax.dot_general(
            jnp.ones((8, width), jnp.bfloat16), rows * rows, NT, preferred_element_type=jnp.float32
        ) + lax.dot_general(
            jnp.ones((8, floor.shape[1]), jnp.bfloat16), floor * floor, NT, preferred_element_type=jnp.float32
        )
        power = jnp.where(power > 0.0, power, 1.0) * (1.0 / width)
        lines.append(jnp.sum(weights(scores * lax.rsqrt(power[0:1, :]), width), axis=0, keepdims=True))
    return jnp.concatenate(lines, axis=0)


def redo(cap, per, scaled, facts_in, me, refs, firsts, packed, floors):
    part = per * cap
    planes = packed.shape[0]
    count = planes * part
    width = scaled.shape[1]
    probe0 = facts_in[0:1, :]
    slots = facts_in[8:9, :] * 32 + facts_in[9:10, :]
    lane = lax.broadcasted_iota(jnp.int32, (count, 128), 1)
    for r, (ref, first) in enumerate(zip(refs, firsts)):
        facts = jnp.transpose(ref[ref.shape[0] - META :, first : first + count].astype(jnp.float32))
        hits = (facts[:, 0:1] * 32.0 + facts[:, 1:2]).astype(jnp.int32) == jnp.where(probe0 == (me ^ r), slots + 1, -1)
        gained = jnp.sum(jnp.where(hits, 1.0, 0.0), axis=1, keepdims=True)
        ahead = facts[:, 2:3]
        floor = (ahead + gained) * math.sqrt(1e-06 * width)
        floor = jnp.where(lane == 0, floor, 0.0).astype(jnp.bfloat16)
        added = jnp.dot(one_hot(hits), scaled[...], preferred_element_type=jnp.float32)
        whole = (ahead * ref[0:count, :].astype(jnp.float32) + added).astype(jnp.bfloat16)
        for w in range(planes):
            for j in range(per):
                start = w * part + j * cap
                packed[w, j, r * cap : (r + 1) * cap, :] = whole[start : start + cap, :]
                floors[w, j, r * cap : (r + 1) * cap, :] = floor[start : start + cap, :]


def early_kernel(
    cap, per, scaled, facts_in, units_any, cross_any, passed_any, any0, any1, any2, any3,
    sums, rows0, rows1, rows2, rows3, units, two_last, packed, floors, sems,
):
    me, z, y, core = position()
    end = (z == 0) | (z == 3)
    refs = (rows0, rows1, rows2, rows3)
    at_end = pltpu.make_async_copy(passed_any, two_last, sems.at[5])
    at_mid = pltpu.make_async_copy(cross_any, two_last, sems.at[5])
    copies = fetch(list(zip((any0, any1, any2, any3, units_any), (*refs, units))), sems)
    pl.when(end)(at_end.start)
    pl.when(jnp.logical_not(end))(at_mid.start)
    for copy in copies:
        copy.wait()
    pl.when(end)(at_end.wait)
    pl.when(jnp.logical_not(end))(at_mid.wait)
    redo(cap, per, scaled, facts_in, me, refs, (0, 0, 0, 0), packed, floors)
    third = unit_wide(two_last[...].astype(jnp.float32))
    for w, two in enumerate((units[0], units[1], third)):
        sums[8 * w : 8 * w + per, :] = level_sums(two, packed, floors, w, per)


def late_kernel(
    cap, per, scaled, facts_in, any0, any1, any2, any3, after, updated, packed, floors, rows0, rows1, rows2, rows3, sems
):
    me, z, y, core = position()
    part = per * cap
    tail = pl.ds(3 * part, part + META)
    refs = (rows0, rows1, rows2, rows3)
    copies = fetch(list(zip((any0.at[tail], any1.at[tail], any2, any3), refs)), sems)
    for copy in copies:
        copy.wait()
    redo(cap, per, scaled, facts_in, me, refs, (3 * part, 3 * part, 0, 0), packed, floors)


def third_kernel(cap, per, early, floors, kept_any, last_any, far_any, out0, out1, out2, out3, kept, two, sems):
    me, z, y, core = position()
    end = (z == 0) | (z == 3)
    at_end = pltpu.make_async_copy(far_any, two, sems.at[1])
    at_mid = pltpu.make_async_copy(last_any, two, sems.at[1])
    pl.when(end)(at_end.start)
    pl.when(jnp.logical_not(end))(at_mid.start)
    copies = fetch([(kept_any, kept)], sems)
    pl.when(end)(at_end.wait)
    pl.when(jnp.logical_not(end))(at_mid.wait)
    two_unit = unit_wide(two[...].astype(jnp.float32))
    copies[0].wait()
    final = level_sums(two_unit, kept, floors, 0, per)
    lines = [early[8 * w : 8 * w + per, :] for w in range(3)] + [final]
    together = jnp.concatenate(lines + [jnp.zeros((16 - 4 * per, 4 * cap), jnp.float32)], axis=0)
    lane = lax.broadcasted_iota(jnp.int32, together.shape, 1)
    line = lax.broadcasted_iota(jnp.int32, together.shape, 0)
    for r, out in enumerate((out0, out1, out2, out3)):
        spread = jnp.zeros_like(together)
        for s in range(4):
            turned = together if s == r else pltpu.roll(together, ((s - r) % 4) * cap, 1)
            spread = jnp.where((line % 4 == s) & (lane >= s * cap) & (lane < (s + 1) * cap), turned, spread)
        for t in range(4):
            out[t : t + 1, :] = jnp.sum(spread[4 * t : 4 * t + 4], axis=0, keepdims=True)


def last_kernel(cap, scale_one, scale_two, info, got0, got1, got2, got3, shares, density, level_two):
    density[...] = jnp.log(shares[:, 0 : density.shape[1]] / scale_one)
    values = jnp.concatenate([got[0:4, :] for got in (got0, got1, got2, got3)], axis=0)
    rows = info.shape[1]
    chosen = jnp.where(info[2:3, :] == lax.broadcasted_iota(jnp.int32, (4 * cap, rows), 0), 1.0, 0.0)
    spread = jnp.dot(values, chosen, precision=lax.Precision.HIGHEST, preferred_element_type=jnp.float32)
    found = jnp.where(info[1:2, :] == lax.broadcasted_iota(jnp.int32, (16, rows), 0), spread, 0.0)
    level_two[...] = jnp.log(jnp.sum(found, axis=0, keepdims=True) / scale_two)


def call(kernel, outs, scratch=(), in_specs=None, **kw):
    def run(*args):
        specs = in_specs or [VMEM] * len(args)
        args = [pltpu.with_memory_space_constraint(a, pltpu.HBM) if spec is HBM else a for a, spec in zip(args, specs)]
        return pl.pallas_call(
            kernel, out_shape=outs, in_specs=specs, scratch_shapes=list(scratch), compiler_params=PARAMS, **kw
        )(*args)

    return run


def lasting(micros):
    return pl.CostEstimate(flops=0, transcendentals=0, bytes_accessed=int(micros * 3_690_000))


def in_order(*values, **kw):
    count = len(values)
    return call(
        order_kernel,
        tuple(jax.ShapeDtypeStruct(value.shape, value.dtype) for value in values),
        in_specs=[ANY] * count,
        out_specs=(ANY,) * count,
        input_output_aliases={i: i for i in range(count)},
        **kw,
    )(*values)


def line_body(embeddings, probes, assigned, prior_counts, centroids, candidates, centroids2):
    emb_rows, width = embeddings.shape
    probe_count = probes.shape[1]
    rows = centroids.shape[0]
    per = BLOCKS2_DEV
    cap = max(2, 3 * rows // (2 * per * 16))
    part = per * cap
    bf16, f32, i32 = jnp.bfloat16, jnp.float32, jnp.int32
    shape = jax.ShapeDtypeStruct

    def exchange(value, apart, sources=range(16)):
        return lax.ppermute(value, "shard", [(i, i ^ apart) for i in sources])

    def rows_of(planes):
        return shape((planes * part + META, width), bf16)

    def room(like):
        return pltpu.VMEM(like.shape, like.dtype)

    mids = range(4, 12)
    near_set = exchange(centroids2, 4)
    cross_set = exchange(centroids2, 12, mids)
    prior_row = prior_counts.reshape(1, rows)
    line = pltpu.VMEM((1, rows), i32)
    mine, early2, early3, info = call(
        functools.partial(pack_kernel, cap, per),
        (shape((emb_rows, width + 128), bf16), rows_of(3), rows_of(3), shape((8, rows), i32)),
        [
            line,
            pltpu.VMEM((emb_rows, width), bf16),
            pltpu.VMEM((probe_count, emb_rows), i32),
            pltpu.VMEM((1, emb_rows), i32),
            line,
            pltpu.VMEM((rows, width), bf16),
            pltpu.SemaphoreType.DMA((6,)),
        ],
        in_specs=[HBM] * 6,
    )(candidates.reshape(1, rows), embeddings, probes.T, assigned.reshape(1, emb_rows), prior_row, centroids)
    early2, early3 = exchange(early2, 2), exchange(early3, 3)
    rows0, rows1, late2, late3 = call(
        functools.partial(pack_more_kernel, part), (rows_of(4), rows_of(4), rows_of(1), rows_of(1))
    )(info, prior_row, centroids)
    mine = jnp.concatenate([mine, exchange(mine, 4)], axis=0)
    near_set, cross_set, mine, rows0 = in_order(near_set, cross_set, mine, rows0)
    across = exchange(mine, 12)
    passed = exchange(cross_set, 4, mids)
    last_set = exchange(near_set, 12, mids)
    mine = jnp.concatenate([mine, across], axis=0)
    mine, early2, early3, late2, late3, rows1 = in_order(mine, early2, early3, late2, late3, rows1)
    mine = jnp.concatenate([mine, exchange(mine, 2)], axis=0)
    late2, late3 = exchange(late2, 2), exchange(late3, 3)
    rows1 = exchange(rows1, 1)
    set_rows = per * BLOCK2
    block_set = pltpu.VMEM((set_rows, width), bf16)
    unit_old, units = call(
        prepare_kernel,
        (shape((rows, width), bf16), shape((2, set_rows, width), bf16)),
        [block_set, block_set, pltpu.SemaphoreType.DMA((2,))],
        in_specs=[VMEM, HBM, ANY],
    )(centroids, centroids2, near_set)
    passed, last_set, mine, unit_old, units = in_order(passed, last_set, mine, unit_old, units)
    far_set = exchange(last_set, 4, mids)
    other = exchange(mine, 1)
    gathered = pltpu.VMEM((8 * emb_rows, width + 128), bf16)
    scaled, facts, share, share_high = call(
        share_kernel,
        (
            shape((16 * emb_rows, width), bf16),
            shape((16, 16 * emb_rows), i32),
            shape((8, 4 * cap), f32),
            shape((8, 4 * cap), f32),
        ),
        [gathered, gathered, pltpu.SemaphoreType.DMA((2,))],
        in_specs=[ANY, ANY, VMEM],
        cost_estimate=lasting(3),
    )(mine, other, unit_old)
    share = share + exchange(share_high, 2)

    def gather(share, apart):
        half = share.shape[0] // 2
        return share[:half] + exchange(share[half:], apart)

    early = call(
        functools.partial(early_kernel, cap, per),
        shape((24, 4 * cap), f32),
        [room(rows_of(4))] * 2
        + [room(rows_of(3))] * 2
        + [
            pltpu.VMEM((2, set_rows, width), bf16),
            block_set,
            pltpu.VMEM((3, per, 4 * cap, width), bf16),
            pltpu.VMEM((3, per, 4 * cap, 128), bf16),
            pltpu.SemaphoreType.DMA((6,)),
        ],
        in_specs=[VMEM, VMEM] + [ANY] * 7,
        cost_estimate=lasting(7),
    )(scaled, facts, units, cross_set, passed, rows0, rows1, early2, early3)
    share, early = in_order(gather(share, 1), early)
    new_centroids, counts = call(
        update_kernel, (shape((rows, width), bf16), shape((1, rows), i32)), in_specs=[ANY] + [VMEM] * 4
    )(early, scaled, facts, centroids, prior_row)
    kept = shape((1, per, 4 * cap, width), bf16)
    kept_rows, floors = call(
        functools.partial(late_kernel, cap, per),
        (kept, shape((1, per, 4 * cap, 128), bf16)),
        [room(rows_of(1))] * 4 + [pltpu.SemaphoreType.DMA((4,))],
        in_specs=[VMEM] * 2 + [ANY] * 6,
        cost_estimate=lasting(3),
    )(scaled, facts, rows0, rows1, late2, late3, early, counts)
    share, kept_rows = in_order(gather(share, 12), kept_rows)
    tile = shape((8, 4 * cap), f32)
    tiles = call(
        functools.partial(third_kernel, cap, per),
        (tile,) * 4,
        [room(kept), block_set, pltpu.SemaphoreType.DMA((2,))],
        in_specs=[VMEM, VMEM, ANY, ANY, ANY],
        cost_estimate=lasting(1),
    )(early, floors, kept_rows, last_set, far_set)
    tiles = [tile if r == 0 else exchange(tile, r) for r, tile in enumerate(tiles)]
    share = gather(share, 4)
    density, level_two = call(
        functools.partial(last_kernel, cap, probe_count * BLOCK, BLOCK2), (shape((1, emb_rows), f32), shape((1, rows), f32))
    )(info, *tiles, share)
    return (density.reshape(-1), new_centroids, counts.reshape(-1), level_two.reshape(-1))


def solution(mesh):
    placed = (
        P(("groups", "shard"), None),
        P(("groups", "shard"), None),
        P(("groups", "shard")),
        P(("groups", "shard")),
        P(("groups", "shard"), None),
        P(("groups", "shard"), None),
        P(("groups", "shard"), None),
    )
    body = line_body if mesh.shape["shard"] == 16 else general_body
    return jax.shard_map(
        body,
        mesh=mesh,
        in_specs=placed,
        out_specs=(
            P(("groups", "shard")),
            P(("groups", "shard"), None),
            P(("groups", "shard")),
            P(("groups", "shard")),
        ),
        check_vma=False,
    )
```

```python
import functools
import math

import jax
import jax.numpy as jnp
from jax import lax
from jax.experimental import pallas as pl
from jax.experimental.pallas import tpu as pltpu
from jax.sharding import PartitionSpec as P

BLOCK = 1024
BLOCKS_DEV = 1
BLOCK2 = 128
BLOCKS2_DEV = 3


def unit_rows(values):
    wide = values.astype(jnp.float32)
    power = jnp.mean(wide * wide, axis=-1, keepdims=True) + 1e-06
    return (wide * lax.rsqrt(power)).astype(jnp.bfloat16)


def kernel_sums(rows, unit):
    scores = lax.dot_general(
        rows, unit, (((1,), (1,)), ((), ())), preferred_element_type=jnp.float32
    )
    return jnp.sum(jnp.exp((scores / rows.shape[1] - 1.0) / 0.1), axis=1)


def block_update(rows, slots, width):
    matches = slots[:, None] == jnp.arange(width, dtype=jnp.int32)[None, :]
    sums = lax.dot_general(
        matches.astype(jnp.bfloat16),
        rows,
        (((0,), (0,)), ((), ())),
        preferred_element_type=jnp.float32,
    )
    counts = jnp.sum(matches.astype(jnp.int32), axis=0)
    return (sums, counts)


def slot_ranks(targets, buckets):
    matches = (targets[:, None] == jnp.arange(buckets, dtype=jnp.int32)[None, :]).astype(jnp.int32)
    return jnp.sum(jnp.cumsum(matches, axis=0) * matches, axis=1) - 1


def general_body(embeddings, probes, assigned, prior_counts, centroids, candidates, centroids2):
    devices = lax.axis_size("shard")
    emb_rows, width = embeddings.shape
    probe_count = probes.shape[1]
    capacity = max(2, 2 * emb_rows * probe_count // (BLOCKS_DEV * devices))
    scaled = unit_rows(embeddings)
    units_old = unit_rows(centroids).reshape(BLOCKS_DEV, BLOCK, width)
    total = emb_rows * probe_count
    buckets = BLOCKS_DEV * devices
    flat = probes.reshape(-1)
    place = flat * capacity + slot_ranks(flat, buckets)
    leading = jnp.arange(total, dtype=jnp.int32) % probe_count == 0
    repeated = jnp.repeat(scaled, probe_count, axis=0)
    slot_values = jnp.where(leading, jnp.repeat(assigned, probe_count), -1)
    send_rows = jnp.zeros((buckets * capacity, width), jnp.bfloat16).at[place].set(repeated)
    send_slots = jnp.full((buckets * capacity,), -1, jnp.int32).at[place].set(slot_values)
    got_rows, got_slots = (
        lax.all_to_all(
            send_rows.reshape(devices, BLOCKS_DEV * capacity, width),
            "shard",
            split_axis=0,
            concat_axis=0,
            tiled=True,
        ),
        lax.all_to_all(
            send_slots.reshape(devices, BLOCKS_DEV * capacity),
            "shard",
            split_axis=0,
            concat_axis=0,
            tiled=True,
        ),
    )
    got_rows = got_rows.reshape(devices, BLOCKS_DEV, capacity, width)
    got_slots = got_slots.reshape(devices, BLOCKS_DEV, capacity)
    local = 0
    picked = got_rows[:, local].reshape(devices * capacity, width)
    slots = got_slots[:, local].reshape(-1)
    weights = [kernel_sums(picked, units_old[local]).reshape(devices, capacity)]
    more_sums, more_counts = block_update(picked, slots, BLOCK)
    sum_list = [more_sums]
    count_list = [more_counts]
    sums = jnp.stack(sum_list)
    counts = jnp.stack(count_list)
    returned = lax.all_to_all(
        jnp.stack(weights, axis=1).reshape(devices, BLOCKS_DEV * capacity),
        "shard",
        split_axis=0,
        concat_axis=0,
        tiled=True,
    )
    totals = jnp.sum(returned.reshape(-1)[place].reshape(emb_rows, probe_count), axis=1)
    density = jnp.log(totals / (probe_count * BLOCK))
    prior = prior_counts.reshape(BLOCKS_DEV, BLOCK)
    fresh = prior + counts
    updated = (
        prior.astype(jnp.float32)[:, :, None]
        * centroids.reshape(BLOCKS_DEV, BLOCK, width).astype(jnp.float32)
        + sums
    ) / fresh.astype(jnp.float32)[:, :, None]
    new_centroids = updated.astype(jnp.bfloat16).reshape(BLOCKS_DEV * BLOCK, width)
    units_new = unit_rows(updated).reshape(BLOCKS_DEV * BLOCK, width)
    rows_two = units_new.shape[0]
    second_capacity = max(2, 3 * rows_two // (2 * BLOCKS2_DEV * devices))
    buckets_two = BLOCKS2_DEV * devices
    chosen = candidates[:, 0]
    place_two = chosen * second_capacity + slot_ranks(chosen, buckets_two)
    send_two = (
        jnp.zeros((buckets_two * second_capacity, width), jnp.bfloat16).at[place_two].set(units_new)
    )
    send_two = send_two.reshape(devices, BLOCKS2_DEV, second_capacity, width)
    units_two = unit_rows(centroids2).reshape(BLOCKS2_DEV, BLOCK2, width)
    arrived = lax.all_to_all(send_two, "shard", split_axis=0, concat_axis=0, tiled=True)
    items = arrived.shape[2]
    weights_two = [
        kernel_sums(arrived[:, local].reshape(-1, width), units_two[local]).reshape(
            arrived.shape[0], items
        )
        for local in range(BLOCKS2_DEV)
    ]
    returned_two = lax.all_to_all(
        jnp.stack(weights_two, axis=1), "shard", split_axis=0, concat_axis=0, tiled=True
    )
    level_two = jnp.log(returned_two.reshape(-1)[place_two] / BLOCK2)
    return (density, new_centroids, fresh.reshape(-1), level_two)


NT = (((1,), (1,)), ((), ()))
PARAMS = pltpu.CompilerParams(vmem_limit_bytes=48 * 1024 * 1024)
META = 16
LATE = 5
STEP = 40
HBM = pl.BlockSpec(memory_space=pltpu.HBM)
ANY = pl.BlockSpec(memory_space=pl.ANY)
VMEM = pl.BlockSpec(memory_space=pltpu.VMEM)


def position():
    me = lax.axis_index("shard")
    return me, me // 4, (me // 2) % 2, me % 2


def unit_wide(wide):
    power = jnp.mean(wide * wide, axis=-1, keepdims=True) + 1e-06
    return (wide * lax.rsqrt(power)).astype(jnp.bfloat16)


def weights(scores, width):
    return jnp.exp(scores * (10.0 / width) - 10.0)


def one_hot(hits):
    return jnp.where(hits, 1.0, 0.0).astype(jnp.bfloat16)


def column(row):
    return jnp.transpose(jnp.broadcast_to(row, (8, row.shape[1])))[:, 0:1]


def fetch(pairs, sems):
    copies = [pltpu.make_async_copy(src, dst, sems.at[i]) for i, (src, dst) in enumerate(pairs)]
    for copy in copies:
        copy.start()
    return copies


def pick_rows(slot, first, count):
    return one_hot(slot == lax.broadcasted_iota(jnp.int32, (count, slot.shape[1]), 0) + first)


def pack(slot, prior, cent, first, out):
    count = out.shape[0] - META
    rows = slot.shape[1]
    ident = lax.broadcasted_iota(jnp.int32, (1, rows), 1) + 1
    line = lax.broadcasted_iota(jnp.int32, (META, rows), 0)
    facts = jnp.where(line == 0, ident >> 5, jnp.where(line == 1, ident & 31, jnp.where(line == 2, prior, 0)))
    facts = facts.astype(jnp.float32).astype(jnp.bfloat16)
    pick = pick_rows(slot, first, count)
    out[0:count, :] = jnp.dot(pick, cent, preferred_element_type=jnp.float32).astype(jnp.bfloat16)
    out[count:, :] = jnp.zeros((META, out.shape[1]), jnp.bfloat16)
    out[count:, 0:count] = lax.dot_general(facts, pick, NT, preferred_element_type=jnp.float32).astype(jnp.bfloat16)


def pack_kernel(
    cap, per, cand_any, emb_any, probes_any, assigned_any, prior_any, cent_any, mine, rows2, rows3, info,
    cand_ref, emb_ref, probes_ref, assigned_ref, prior_ref, cent_ref, sems,
):
    copies = fetch(
        (
            (cand_any, cand_ref),
            (emb_any, emb_ref),
            (probes_any, probes_ref),
            (assigned_any, assigned_ref),
            (prior_any, prior_ref),
            (cent_any, cent_ref),
        ),
        sems,
    )
    me, z, y, core = position()
    rows = cand_ref.shape[1]
    buckets = 16 * per
    before = lax.broadcasted_iota(jnp.int32, (rows, rows), 0) <= lax.broadcasted_iota(jnp.int32, (rows, rows), 1)
    before = one_hot(before)
    copies[0].wait()
    cand = cand_ref[...]
    dev = sum((cand >= per * step).astype(jnp.int32) for step in range(1, 16))
    near = dev >> 2
    plane = jnp.where(z >= 2, 3 - near, near)
    rel = (((dev >> 1) & 1) ^ y) * 2 + ((dev & 1) ^ core)
    named = cand == lax.broadcasted_iota(jnp.int32, (buckets, rows), 0)
    counted = jnp.dot(one_hot(named), before, preferred_element_type=jnp.float32)
    rank = jnp.sum(jnp.where(named, counted, 0.0), axis=0, keepdims=True).astype(jnp.int32) - 1
    kind = plane * per + cand - dev * per
    slot = (rel * 4 * per + kind) * cap + rank
    info[0:1, :] = slot
    info[1:2, :] = rel * 4 + (kind >> 2)
    info[2:3, :] = (kind & 3) * cap + rank
    for copy in copies[1:5]:
        copy.wait()
    count, width = emb_ref.shape
    probe_count = probes_ref.shape[0]
    slots = assigned_ref[...]
    facts = jnp.concatenate([probes_ref[...], slots >> 5, slots & 31], axis=0).astype(jnp.float32)
    facts = jnp.concatenate([facts, jnp.zeros((128 - probe_count - 2, count), jnp.float32)], axis=0)
    same = lax.broadcasted_iota(jnp.int32, (count, count), 0) == lax.broadcasted_iota(jnp.int32, (count, count), 1)
    mine[:, 0:width] = emb_ref[...]
    mine[:, width:] = lax.dot_general(
        one_hot(same), facts.astype(jnp.bfloat16), NT, preferred_element_type=jnp.float32
    ).astype(jnp.bfloat16)
    copies[5].wait()
    pack(slot, prior_ref[...], cent_ref[...], 2 * 4 * per * cap, rows2)
    pack(slot, prior_ref[...], cent_ref[...], 3 * 4 * per * cap, rows3)


def pack_more_kernel(part, info, prior_ref, cent_ref, rows0, rows1, late2, late3):
    for first, out in ((0, rows0), (4 * part, rows1), (11 * part, late2), (15 * part, late3)):
        pack(info[0:1, :], prior_ref[...], cent_ref[...], first, out)


def order_kernel(*refs):
    pass


def prepare_kernel(cent_ref, own_any, near_any, unit_old, units, own, near, sems):
    copies = fetch(((own_any, own), (near_any, near)), sems)
    step = 256
    for start in range(0, cent_ref.shape[0], step):
        unit_old[start : start + step, :] = unit_wide(cent_ref[start : start + step, :].astype(jnp.float32))
    me, z, y, core = position()
    first = jnp.where((z == 0) | (z == 3), 0, 1)
    copies[0].wait()
    units[first] = unit_wide(own[...].astype(jnp.float32))
    copies[1].wait()
    units[1 - first] = unit_wide(near[...].astype(jnp.float32))


def share_kernel(mine_any, other_any, unit_old, scaled, facts, placed, mine_ref, other_ref, sems):
    copies = fetch(((mine_any, mine_ref), (other_any, other_ref)), sems)
    me, z, y, core = position()
    half = mine_ref.shape[0]
    count = 2 * half
    rows, width = unit_old.shape
    copies[0].wait()
    scaled[0:half, :] = unit_wide(mine_ref[:, 0:width].astype(jnp.float32))
    copies[1].wait()
    scaled[half:count, :] = unit_wide(other_ref[:, 0:width].astype(jnp.float32))
    aux = jnp.concatenate([mine_ref[:, width:], other_ref[:, width:]], axis=0).astype(jnp.float32)
    aux = jnp.transpose(aux)[0:16, :].astype(jnp.int32)
    facts[...] = aux
    member = jnp.sum((aux[0:8, :] == me).astype(jnp.float32), axis=0, keepdims=True)
    step = 256
    total = jnp.zeros((1, count), jnp.float32)
    for start in range(0, rows, step):
        scores = lax.dot_general(
            unit_old[start : start + step, :], scaled[...], NT, preferred_element_type=jnp.float32
        )
        total = total + jnp.sum(weights(scores, width), axis=0, keepdims=True)
    piece = count // 16
    lane = lax.broadcasted_iota(jnp.int32, (16, count), 1)
    line = lax.broadcasted_iota(jnp.int32, (16, count), 0)
    apart = jnp.where((member > 0.0) & (lane >= line * piece) & (lane < (line + 1) * piece), total, 0.0)
    spot = lax.broadcasted_iota(jnp.int32, (count, 128), 0)
    block = sum((spot >= piece * step).astype(jnp.int32) for step in range(1, 16))
    together = jnp.where(spot - block * piece == lax.broadcasted_iota(jnp.int32, (count, 128), 1), 1.0, 0.0)
    share = jnp.dot(apart, together, precision=lax.Precision.HIGHEST, preferred_element_type=jnp.float32)
    for b in range(16):
        apart = ((b & 1) * 4) ^ ((b >> 1 & 1) * 12) ^ ((b >> 2 & 1) * 2) ^ (b >> 3)
        placed[me ^ apart] = share[b : b + 1, :]


def update_kernel(after, scaled, facts, cent_ref, prior_ref, fresh_rows, fresh_counts):
    me, z, y, core = position()
    rows, width = cent_ref.shape
    count = scaled.shape[0]
    prior = column(prior_ref[...].astype(jnp.float32))
    target = jnp.where(facts[0:1, :] == me, facts[8:9, :] * 32 + facts[9:10, :], -1)
    step = 256
    for start in range(0, rows, step):
        old = cent_ref[start : start + step, :].astype(jnp.float32)
        hits = one_hot(target == lax.broadcasted_iota(jnp.int32, (step, count), 0) + start)
        sums = jnp.dot(hits, scaled[...], preferred_element_type=jnp.float32)
        gained = jnp.sum(hits.astype(jnp.float32), axis=1, keepdims=True)
        ahead = prior[start : start + step, :]
        updated = (ahead * old + sums) * (1.0 / (ahead + gained))
        fresh_rows[start : start + step, :] = updated.astype(jnp.bfloat16)
        gained_row = lax.dot_general(
            jnp.ones((8, count), jnp.bfloat16), hits, NT, preferred_element_type=jnp.float32
        )
        fresh_counts[0:1, start : start + step] = prior_ref[0:1, start : start + step] + gained_row[0:1, :].astype(jnp.int32)


def level_sums(two, packed, floors, w, per):
    block, width = two.shape[0] // per, two.shape[1]
    lines = []
    for j in range(per):
        rows = packed[w, j]
        floor = floors[w, j]
        scores = lax.dot_general(two[j * block : (j + 1) * block, :], rows, NT, preferred_element_type=jnp.float32)
        power = lax.dot_general(
            jnp.ones((8, width), jnp.bfloat16), rows * rows, NT, preferred_element_type=jnp.float32
        ) + lax.dot_general(
            jnp.ones((8, floor.shape[1]), jnp.bfloat16), floor * floor, NT, preferred_element_type=jnp.float32
        )
        power = jnp.where(power > 0.0, power, 1.0) * (1.0 / width)
        lines.append(jnp.sum(weights(scores * lax.rsqrt(power[0:1, :]), width), axis=0, keepdims=True))
    return jnp.concatenate(lines, axis=0)


def redo(cap, per, scaled, facts_in, me, refs, firsts, packed, floors):
    part = per * cap
    planes = packed.shape[0]
    count = planes * part
    width = scaled.shape[1]
    probe0 = facts_in[0:1, :]
    slots = facts_in[8:9, :] * 32 + facts_in[9:10, :]
    lane = lax.broadcasted_iota(jnp.int32, (count, 128), 1)
    for r, (ref, first) in enumerate(zip(refs, firsts)):
        facts = jnp.transpose(ref[ref.shape[0] - META :, first : first + count].astype(jnp.float32))
        hits = (facts[:, 0:1] * 32.0 + facts[:, 1:2]).astype(jnp.int32) == jnp.where(probe0 == (me ^ r), slots + 1, -1)
        gained = jnp.sum(jnp.where(hits, 1.0, 0.0), axis=1, keepdims=True)
        ahead = facts[:, 2:3]
        floor = (ahead + gained) * math.sqrt(1e-06 * width)
        floor = jnp.where(lane == 0, floor, 0.0).astype(jnp.bfloat16)
        added = jnp.dot(one_hot(hits), scaled[...], preferred_element_type=jnp.float32)
        whole = (ahead * ref[0:count, :].astype(jnp.float32) + added).astype(jnp.bfloat16)
        for w in range(planes):
            for j in range(per):
                start = w * part + j * cap
                packed[w, j, r * cap : (r + 1) * cap, :] = whole[start : start + cap, :]
                floors[w, j, r * cap : (r + 1) * cap, :] = floor[start : start + cap, :]


def early_kernel(
    cap, per, scaled, facts_in, units_any, cross_any, passed_any, any0, any1, any2, any3,
    sums, rows0, rows1, rows2, rows3, units, two_last, packed, floors, sems,
):
    me, z, y, core = position()
    end = (z == 0) | (z == 3)
    refs = (rows0, rows1, rows2, rows3)
    at_end = pltpu.make_async_copy(passed_any, two_last, sems.at[5])
    at_mid = pltpu.make_async_copy(cross_any, two_last, sems.at[5])
    copies = fetch(list(zip((any0, any1, any2, any3, units_any), (*refs, units))), sems)
    pl.when(end)(at_end.start)
    pl.when(jnp.logical_not(end))(at_mid.start)
    for copy in copies:
        copy.wait()
    pl.when(end)(at_end.wait)
    pl.when(jnp.logical_not(end))(at_mid.wait)
    redo(cap, per, scaled, facts_in, me, refs, (0, 0, 0, 0), packed, floors)
    third = unit_wide(two_last[...].astype(jnp.float32))
    for w, two in enumerate((units[0], units[1], third)):
        sums[8 * w : 8 * w + per, :] = level_sums(two, packed, floors, w, per)


def late_kernel(
    cap, per, scaled, facts_in, any0, any1, any2, any3, after, updated, packed, floors, rows0, rows1, rows2, rows3, sems
):
    me, z, y, core = position()
    part = per * cap
    tail = pl.ds(3 * part, part + META)
    refs = (rows0, rows1, rows2, rows3)
    copies = fetch(list(zip((any0.at[tail], any1.at[tail], any2, any3), refs)), sems)
    for copy in copies:
        copy.wait()
    redo(cap, per, scaled, facts_in, me, refs, (3 * part, 3 * part, 0, 0), packed, floors)


def third_kernel(cap, per, early, floors, kept_any, last_any, far_any, after, out0, out1, out2, out3, kept, two, sems):
    me, z, y, core = position()
    end = (z == 0) | (z == 3)
    at_end = pltpu.make_async_copy(far_any, two, sems.at[1])
    at_mid = pltpu.make_async_copy(last_any, two, sems.at[1])
    pl.when(end)(at_end.start)
    pl.when(jnp.logical_not(end))(at_mid.start)
    copies = fetch([(kept_any, kept)], sems)
    pl.when(end)(at_end.wait)
    pl.when(jnp.logical_not(end))(at_mid.wait)
    two_unit = unit_wide(two[...].astype(jnp.float32))
    copies[0].wait()
    final = level_sums(two_unit, kept, floors, 0, per)
    lines = [early[8 * w : 8 * w + per, :] for w in range(3)] + [final]
    together = jnp.concatenate(lines + [jnp.zeros((16 - 4 * per, 4 * cap), jnp.float32)], axis=0)
    lane = lax.broadcasted_iota(jnp.int32, together.shape, 1)
    line = lax.broadcasted_iota(jnp.int32, together.shape, 0)
    for r, out in enumerate((out0, out1, out2, out3)):
        spread = jnp.zeros_like(together)
        for s in range(4):
            turned = together if s == r else pltpu.roll(together, ((s - r) % 4) * cap, 1)
            spread = jnp.where((line % 4 == s) & (lane >= s * cap) & (lane < (s + 1) * cap), turned, spread)
        for t in range(4):
            out[t : t + 1, :] = jnp.sum(spread[4 * t : 4 * t + 4], axis=0, keepdims=True)


def last_kernel(cap, scale_one, scale_two, info, got0, got1, got2, got3, shares, density, level_two):
    total = shares[0]
    for source in range(1, 16):
        total = total + shares[source]
    density[...] = jnp.log(total[:, 0 : density.shape[1]] / scale_one)
    values = jnp.concatenate([got[0:4, :] for got in (got0, got1, got2, got3)], axis=0)
    rows = info.shape[1]
    chosen = jnp.where(info[2:3, :] == lax.broadcasted_iota(jnp.int32, (4 * cap, rows), 0), 1.0, 0.0)
    spread = jnp.dot(values, chosen, precision=lax.Precision.HIGHEST, preferred_element_type=jnp.float32)
    found = jnp.where(info[1:2, :] == lax.broadcasted_iota(jnp.int32, (16, rows), 0), spread, 0.0)
    level_two[...] = jnp.log(jnp.sum(found, axis=0, keepdims=True) / scale_two)


def call(kernel, outs, scratch=(), in_specs=None, **kw):
    def run(*args):
        specs = in_specs or [VMEM] * len(args)
        args = [pltpu.with_memory_space_constraint(a, pltpu.HBM) if spec is HBM else a for a, spec in zip(args, specs)]
        return pl.pallas_call(
            kernel, out_shape=outs, in_specs=specs, scratch_shapes=list(scratch), compiler_params=PARAMS, **kw
        )(*args)

    return run


def lasting(micros):
    return pl.CostEstimate(flops=0, transcendentals=0, bytes_accessed=int(micros * 3_690_000))


def in_order(*values, **kw):
    count = len(values)
    return call(
        order_kernel,
        tuple(jax.ShapeDtypeStruct(value.shape, value.dtype) for value in values),
        in_specs=[ANY] * count,
        out_specs=(ANY,) * count,
        input_output_aliases={i: i for i in range(count)},
        **kw,
    )(*values)


def line_body(embeddings, probes, assigned, prior_counts, centroids, candidates, centroids2):
    emb_rows, width = embeddings.shape
    probe_count = probes.shape[1]
    rows = centroids.shape[0]
    per = BLOCKS2_DEV
    cap = max(2, 3 * rows // (2 * per * 16))
    part = per * cap
    bf16, f32, i32 = jnp.bfloat16, jnp.float32, jnp.int32
    shape = jax.ShapeDtypeStruct

    def exchange(value, apart, sources=range(16)):
        return lax.ppermute(value, "shard", [(i, i ^ apart) for i in sources])

    def rows_of(planes):
        return shape((planes * part + META, width), bf16)

    def room(like):
        return pltpu.VMEM(like.shape, like.dtype)

    mids = range(4, 12)
    near_set = exchange(centroids2, 4)
    cross_set = exchange(centroids2, 12, mids)
    prior_row = prior_counts.reshape(1, rows)
    line = pltpu.VMEM((1, rows), i32)
    mine, early2, early3, info = call(
        functools.partial(pack_kernel, cap, per),
        (shape((emb_rows, width + 128), bf16), rows_of(3), rows_of(3), shape((8, rows), i32)),
        [
            line,
            pltpu.VMEM((emb_rows, width), bf16),
            pltpu.VMEM((probe_count, emb_rows), i32),
            pltpu.VMEM((1, emb_rows), i32),
            line,
            pltpu.VMEM((rows, width), bf16),
            pltpu.SemaphoreType.DMA((6,)),
        ],
        in_specs=[HBM] * 6,
    )(candidates.reshape(1, rows), embeddings, probes.T, assigned.reshape(1, emb_rows), prior_row, centroids)
    early2, early3 = exchange(early2, 2), exchange(early3, 3)
    rows0, rows1, late2, late3 = call(
        functools.partial(pack_more_kernel, part), (rows_of(4), rows_of(4), rows_of(1), rows_of(1))
    )(info, prior_row, centroids)
    mine = jnp.concatenate([mine, exchange(mine, 4)], axis=0)
    near_set, cross_set, mine, rows0 = in_order(near_set, cross_set, mine, rows0)
    across = exchange(mine, 12)
    passed = exchange(cross_set, 4, mids)
    last_set = exchange(near_set, 12, mids)
    mine = jnp.concatenate([mine, across], axis=0)
    mine, early2, early3, late2, late3, rows1 = in_order(mine, early2, early3, late2, late3, rows1)
    mine = jnp.concatenate([mine, exchange(mine, 2)], axis=0)
    late2, late3 = exchange(late2, 2), exchange(late3, 3)
    rows1 = exchange(rows1, 1)
    set_rows = per * BLOCK2
    block_set = pltpu.VMEM((set_rows, width), bf16)
    unit_old, units = call(
        prepare_kernel,
        (shape((rows, width), bf16), shape((2, set_rows, width), bf16)),
        [block_set, block_set, pltpu.SemaphoreType.DMA((2,))],
        in_specs=[VMEM, HBM, ANY],
    )(centroids, centroids2, near_set)
    passed, last_set, unit_old, units = in_order(passed, last_set, unit_old, units)
    far_set = exchange(last_set, 4, mids)
    other = exchange(mine, 1)
    gathered = pltpu.VMEM((8 * emb_rows, width + 128), bf16)
    scaled, facts, share = call(
        share_kernel,
        (
            shape((16 * emb_rows, width), bf16),
            shape((16, 16 * emb_rows), i32),
            shape((16, 1, 4 * cap), f32),
        ),
        [gathered, gathered, pltpu.SemaphoreType.DMA((2,))],
        in_specs=[ANY, ANY, VMEM],
    )(mine, other, unit_old)
    early = call(
        functools.partial(early_kernel, cap, per),
        shape((24, 4 * cap), f32),
        [room(rows_of(4))] * 2
        + [room(rows_of(3))] * 2
        + [
            pltpu.VMEM((2, set_rows, width), bf16),
            block_set,
            pltpu.VMEM((3, per, 4 * cap, width), bf16),
            pltpu.VMEM((3, per, 4 * cap, 128), bf16),
            pltpu.SemaphoreType.DMA((6,)),
        ],
        in_specs=[VMEM, VMEM] + [ANY] * 7,
    )(scaled, facts, units, cross_set, passed, rows0, rows1, early2, early3)
    new_centroids, counts = call(
        update_kernel, (shape((rows, width), bf16), shape((1, rows), i32)), in_specs=[ANY] + [VMEM] * 4
    )(early, scaled, facts, centroids, prior_row)
    kept = shape((1, per, 4 * cap, width), bf16)
    kept_rows, floors = call(
        functools.partial(late_kernel, cap, per),
        (kept, shape((1, per, 4 * cap, 128), bf16)),
        [room(rows_of(1))] * 4 + [pltpu.SemaphoreType.DMA((4,))],
        in_specs=[VMEM] * 2 + [ANY] * 6,
    )(scaled, facts, rows0, rows1, late2, late3, early, counts)
    share, kept_rows = in_order(share, kept_rows)
    share = lax.all_to_all(share, "shard", split_axis=0, concat_axis=0, tiled=True)
    tile = shape((8, 4 * cap), f32)
    tiles = call(
        functools.partial(third_kernel, cap, per),
        (tile,) * 4,
        [room(kept), block_set, pltpu.SemaphoreType.DMA((2,))],
        in_specs=[VMEM, VMEM] + [ANY] * 4,
    )(early, floors, kept_rows, last_set, far_set, share)
    tiles = [tile if r == 0 else exchange(tile, r) for r, tile in enumerate(tiles)]
    density, level_two = call(
        functools.partial(last_kernel, cap, probe_count * BLOCK, BLOCK2), (shape((1, emb_rows), f32), shape((1, rows), f32))
    )(info, *tiles, share)
    return (density.reshape(-1), new_centroids, counts.reshape(-1), level_two.reshape(-1))


def solution(mesh):
    placed = (
        P(("groups", "shard"), None),
        P(("groups", "shard"), None),
        P(("groups", "shard")),
        P(("groups", "shard")),
        P(("groups", "shard"), None),
        P(("groups", "shard"), None),
        P(("groups", "shard"), None),
    )
    body = line_body if mesh.shape["shard"] == 16 else general_body
    return jax.shard_map(
        body,
        mesh=mesh,
        in_specs=placed,
        out_specs=(
            P(("groups", "shard")),
            P(("groups", "shard"), None),
            P(("groups", "shard")),
            P(("groups", "shard")),
        ),
        check_vma=False,
    )
```

```python
import functools
import math

import jax
import jax.numpy as jnp
from jax import lax
from jax.experimental import pallas as pl
from jax.experimental.pallas import tpu as pltpu
from jax.sharding import PartitionSpec as P

BLOCK = 1024
BLOCKS_DEV = 1
BLOCK2 = 128
BLOCKS2_DEV = 3


def unit_rows(values):
    wide = values.astype(jnp.float32)
    power = jnp.mean(wide * wide, axis=-1, keepdims=True) + 1e-06
    return (wide * lax.rsqrt(power)).astype(jnp.bfloat16)


def kernel_sums(rows, unit):
    scores = lax.dot_general(
        rows, unit, (((1,), (1,)), ((), ())), preferred_element_type=jnp.float32
    )
    return jnp.sum(jnp.exp((scores / rows.shape[1] - 1.0) / 0.1), axis=1)


def block_update(rows, slots, width):
    matches = slots[:, None] == jnp.arange(width, dtype=jnp.int32)[None, :]
    sums = lax.dot_general(
        matches.astype(jnp.bfloat16),
        rows,
        (((0,), (0,)), ((), ())),
        preferred_element_type=jnp.float32,
    )
    counts = jnp.sum(matches.astype(jnp.int32), axis=0)
    return (sums, counts)


def slot_ranks(targets, buckets):
    matches = (targets[:, None] == jnp.arange(buckets, dtype=jnp.int32)[None, :]).astype(jnp.int32)
    return jnp.sum(jnp.cumsum(matches, axis=0) * matches, axis=1) - 1


def general_body(embeddings, probes, assigned, prior_counts, centroids, candidates, centroids2):
    devices = lax.axis_size("shard")
    emb_rows, width = embeddings.shape
    probe_count = probes.shape[1]
    capacity = max(2, 2 * emb_rows * probe_count // (BLOCKS_DEV * devices))
    scaled = unit_rows(embeddings)
    units_old = unit_rows(centroids).reshape(BLOCKS_DEV, BLOCK, width)
    total = emb_rows * probe_count
    buckets = BLOCKS_DEV * devices
    flat = probes.reshape(-1)
    place = flat * capacity + slot_ranks(flat, buckets)
    leading = jnp.arange(total, dtype=jnp.int32) % probe_count == 0
    repeated = jnp.repeat(scaled, probe_count, axis=0)
    slot_values = jnp.where(leading, jnp.repeat(assigned, probe_count), -1)
    send_rows = jnp.zeros((buckets * capacity, width), jnp.bfloat16).at[place].set(repeated)
    send_slots = jnp.full((buckets * capacity,), -1, jnp.int32).at[place].set(slot_values)
    got_rows, got_slots = (
        lax.all_to_all(
            send_rows.reshape(devices, BLOCKS_DEV * capacity, width),
            "shard",
            split_axis=0,
            concat_axis=0,
            tiled=True,
        ),
        lax.all_to_all(
            send_slots.reshape(devices, BLOCKS_DEV * capacity),
            "shard",
            split_axis=0,
            concat_axis=0,
            tiled=True,
        ),
    )
    got_rows = got_rows.reshape(devices, BLOCKS_DEV, capacity, width)
    got_slots = got_slots.reshape(devices, BLOCKS_DEV, capacity)
    local = 0
    picked = got_rows[:, local].reshape(devices * capacity, width)
    slots = got_slots[:, local].reshape(-1)
    weights = [kernel_sums(picked, units_old[local]).reshape(devices, capacity)]
    more_sums, more_counts = block_update(picked, slots, BLOCK)
    sum_list = [more_sums]
    count_list = [more_counts]
    sums = jnp.stack(sum_list)
    counts = jnp.stack(count_list)
    returned = lax.all_to_all(
        jnp.stack(weights, axis=1).reshape(devices, BLOCKS_DEV * capacity),
        "shard",
        split_axis=0,
        concat_axis=0,
        tiled=True,
    )
    totals = jnp.sum(returned.reshape(-1)[place].reshape(emb_rows, probe_count), axis=1)
    density = jnp.log(totals / (probe_count * BLOCK))
    prior = prior_counts.reshape(BLOCKS_DEV, BLOCK)
    fresh = prior + counts
    updated = (
        prior.astype(jnp.float32)[:, :, None]
        * centroids.reshape(BLOCKS_DEV, BLOCK, width).astype(jnp.float32)
        + sums
    ) / fresh.astype(jnp.float32)[:, :, None]
    new_centroids = updated.astype(jnp.bfloat16).reshape(BLOCKS_DEV * BLOCK, width)
    units_new = unit_rows(updated).reshape(BLOCKS_DEV * BLOCK, width)
    rows_two = units_new.shape[0]
    second_capacity = max(2, 3 * rows_two // (2 * BLOCKS2_DEV * devices))
    buckets_two = BLOCKS2_DEV * devices
    chosen = candidates[:, 0]
    place_two = chosen * second_capacity + slot_ranks(chosen, buckets_two)
    send_two = (
        jnp.zeros((buckets_two * second_capacity, width), jnp.bfloat16).at[place_two].set(units_new)
    )
    send_two = send_two.reshape(devices, BLOCKS2_DEV, second_capacity, width)
    units_two = unit_rows(centroids2).reshape(BLOCKS2_DEV, BLOCK2, width)
    arrived = lax.all_to_all(send_two, "shard", split_axis=0, concat_axis=0, tiled=True)
    items = arrived.shape[2]
    weights_two = [
        kernel_sums(arrived[:, local].reshape(-1, width), units_two[local]).reshape(
            arrived.shape[0], items
        )
        for local in range(BLOCKS2_DEV)
    ]
    returned_two = lax.all_to_all(
        jnp.stack(weights_two, axis=1), "shard", split_axis=0, concat_axis=0, tiled=True
    )
    level_two = jnp.log(returned_two.reshape(-1)[place_two] / BLOCK2)
    return (density, new_centroids, fresh.reshape(-1), level_two)


NT = (((1,), (1,)), ((), ()))
PARAMS = pltpu.CompilerParams(vmem_limit_bytes=48 * 1024 * 1024)
META = 16
SHARE = 1
LATE = 5
STEP = 12
HBM = pl.BlockSpec(memory_space=pltpu.HBM)
ANY = pl.BlockSpec(memory_space=pl.ANY)
VMEM = pl.BlockSpec(memory_space=pltpu.VMEM)


def position():
    me = lax.axis_index("shard")
    return me, me // 4, (me // 2) % 2, me % 2


def unit_wide(wide):
    power = jnp.mean(wide * wide, axis=-1, keepdims=True) + 1e-06
    return (wide * lax.rsqrt(power)).astype(jnp.bfloat16)


def weights(scores, width):
    return jnp.exp(scores * (10.0 / width) - 10.0)


def one_hot(hits):
    return jnp.where(hits, 1.0, 0.0).astype(jnp.bfloat16)


def column(row):
    return jnp.transpose(jnp.broadcast_to(row, (8, row.shape[1])))[:, 0:1]


def fetch(pairs, sems):
    copies = [pltpu.make_async_copy(src, dst, sems.at[i]) for i, (src, dst) in enumerate(pairs)]
    for copy in copies:
        copy.start()
    return copies


def pick_rows(slot, first, count):
    return one_hot(slot == lax.broadcasted_iota(jnp.int32, (count, slot.shape[1]), 0) + first)


def pack(slot, prior, cent, first, out):
    count = out.shape[0] - META
    rows = slot.shape[1]
    ident = lax.broadcasted_iota(jnp.int32, (1, rows), 1) + 1
    line = lax.broadcasted_iota(jnp.int32, (META, rows), 0)
    facts = jnp.where(line == 0, ident >> 5, jnp.where(line == 1, ident & 31, jnp.where(line == 2, prior, 0)))
    facts = facts.astype(jnp.float32).astype(jnp.bfloat16)
    pick = pick_rows(slot, first, count)
    out[0:count, :] = jnp.dot(pick, cent, preferred_element_type=jnp.float32).astype(jnp.bfloat16)
    out[count:, :] = jnp.zeros((META, out.shape[1]), jnp.bfloat16)
    out[count:, 0:count] = lax.dot_general(facts, pick, NT, preferred_element_type=jnp.float32).astype(jnp.bfloat16)


def pack_kernel(
    cap, per, cand_any, emb_any, probes_any, assigned_any, prior_any, cent_any, mine, rows2, rows3, info,
    cand_ref, emb_ref, probes_ref, assigned_ref, prior_ref, cent_ref, sems,
):
    copies = fetch(
        (
            (cand_any, cand_ref),
            (emb_any, emb_ref),
            (probes_any, probes_ref),
            (assigned_any, assigned_ref),
            (prior_any, prior_ref),
            (cent_any, cent_ref),
        ),
        sems,
    )
    me, z, y, core = position()
    rows = cand_ref.shape[1]
    buckets = 16 * per
    before = lax.broadcasted_iota(jnp.int32, (rows, rows), 0) <= lax.broadcasted_iota(jnp.int32, (rows, rows), 1)
    before = one_hot(before)
    copies[0].wait()
    cand = cand_ref[...]
    dev = sum((cand >= per * step).astype(jnp.int32) for step in range(1, 16))
    near = dev >> 2
    plane = jnp.where(z >= 2, 3 - near, near)
    rel = (((dev >> 1) & 1) ^ y) * 2 + ((dev & 1) ^ core)
    named = cand == lax.broadcasted_iota(jnp.int32, (buckets, rows), 0)
    counted = jnp.dot(one_hot(named), before, preferred_element_type=jnp.float32)
    rank = jnp.sum(jnp.where(named, counted, 0.0), axis=0, keepdims=True).astype(jnp.int32) - 1
    kind = plane * per + cand - dev * per
    slot = (rel * 4 * per + kind) * cap + rank
    info[0:1, :] = slot
    info[1:2, :] = rel * 4 + (kind >> 2)
    info[2:3, :] = (kind & 3) * cap + rank
    for copy in copies[1:5]:
        copy.wait()
    count, width = emb_ref.shape
    probe_count = probes_ref.shape[0]
    slots = assigned_ref[...]
    facts = jnp.concatenate([probes_ref[...], slots >> 5, slots & 31], axis=0).astype(jnp.float32)
    facts = jnp.concatenate([facts, jnp.zeros((128 - probe_count - 2, count), jnp.float32)], axis=0)
    same = lax.broadcasted_iota(jnp.int32, (count, count), 0) == lax.broadcasted_iota(jnp.int32, (count, count), 1)
    mine[:, 0:width] = emb_ref[...]
    mine[:, width:] = lax.dot_general(
        one_hot(same), facts.astype(jnp.bfloat16), NT, preferred_element_type=jnp.float32
    ).astype(jnp.bfloat16)
    copies[5].wait()
    pack(slot, prior_ref[...], cent_ref[...], 2 * 4 * per * cap, rows2)
    pack(slot, prior_ref[...], cent_ref[...], 3 * 4 * per * cap, rows3)


def pack_more_kernel(part, info, prior_ref, cent_ref, rows0, rows1, late2, late3):
    for first, out in ((0, rows0), (4 * part, rows1), (11 * part, late2), (15 * part, late3)):
        pack(info[0:1, :], prior_ref[...], cent_ref[...], first, out)


def order_kernel(*refs):
    pass


def prepare_kernel(cent_ref, own_any, near_any, unit_old, units, own, near, sems):
    copies = fetch(((own_any, own), (near_any, near)), sems)
    step = 256
    for start in range(0, cent_ref.shape[0], step):
        unit_old[start : start + step, :] = unit_wide(cent_ref[start : start + step, :].astype(jnp.float32))
    me, z, y, core = position()
    first = jnp.where((z == 0) | (z == 3), 0, 1)
    copies[0].wait()
    units[first] = unit_wide(own[...].astype(jnp.float32))
    copies[1].wait()
    units[1 - first] = unit_wide(near[...].astype(jnp.float32))


def share_kernel(mine_any, other_any, unit_old, scaled, facts, share_low, share_high, mine_ref, other_ref, sems):
    copies = fetch(((mine_any, mine_ref), (other_any, other_ref)), sems)
    me, z, y, core = position()
    half = mine_ref.shape[0]
    count = 2 * half
    rows, width = unit_old.shape
    copies[0].wait()
    scaled[0:half, :] = unit_wide(mine_ref[:, 0:width].astype(jnp.float32))
    copies[1].wait()
    scaled[half:count, :] = unit_wide(other_ref[:, 0:width].astype(jnp.float32))
    aux = jnp.concatenate([mine_ref[:, width:], other_ref[:, width:]], axis=0).astype(jnp.float32)
    aux = jnp.transpose(aux)[0:16, :].astype(jnp.int32)
    facts[...] = aux
    member = jnp.sum((aux[0:8, :] == me).astype(jnp.float32), axis=0, keepdims=True)
    step = 256
    total = jnp.zeros((1, count), jnp.float32)
    for start in range(0, rows, step):
        scores = lax.dot_general(
            unit_old[start : start + step, :], scaled[...], NT, preferred_element_type=jnp.float32
        )
        total = total + jnp.sum(weights(scores, width), axis=0, keepdims=True)
    piece = count // 16
    lane = lax.broadcasted_iota(jnp.int32, (16, count), 1)
    line = lax.broadcasted_iota(jnp.int32, (16, count), 0)
    apart = jnp.where((member > 0.0) & (lane >= line * piece) & (lane < (line + 1) * piece), total, 0.0)
    spot = lax.broadcasted_iota(jnp.int32, (count, 128), 0)
    block = sum((spot >= piece * step).astype(jnp.int32) for step in range(1, 16))
    together = jnp.where(spot - block * piece == lax.broadcasted_iota(jnp.int32, (count, 128), 1), 1.0, 0.0)
    share = jnp.dot(apart, together, precision=lax.Precision.HIGHEST, preferred_element_type=jnp.float32)
    share_low[...] = share[0:8, :]
    share_high[...] = share[8:16, :]


def update_kernel(after, scaled, facts, cent_ref, prior_ref, fresh_rows, fresh_counts):
    me, z, y, core = position()
    rows, width = cent_ref.shape
    count = scaled.shape[0]
    prior = column(prior_ref[...].astype(jnp.float32))
    target = jnp.where(facts[0:1, :] == me, facts[8:9, :] * 32 + facts[9:10, :], -1)
    step = 256
    for start in range(0, rows, step):
        old = cent_ref[start : start + step, :].astype(jnp.float32)
        hits = one_hot(target == lax.broadcasted_iota(jnp.int32, (step, count), 0) + start)
        sums = jnp.dot(hits, scaled[...], preferred_element_type=jnp.float32)
        gained = jnp.sum(hits.astype(jnp.float32), axis=1, keepdims=True)
        ahead = prior[start : start + step, :]
        updated = (ahead * old + sums) * (1.0 / (ahead + gained))
        fresh_rows[start : start + step, :] = updated.astype(jnp.bfloat16)
        gained_row = lax.dot_general(
            jnp.ones((8, count), jnp.bfloat16), hits, NT, preferred_element_type=jnp.float32
        )
        fresh_counts[0:1, start : start + step] = prior_ref[0:1, start : start + step] + gained_row[0:1, :].astype(jnp.int32)


def level_sums(two, packed, floors, w, per):
    block, width = two.shape[0] // per, two.shape[1]
    lines = []
    for j in range(per):
        rows = packed[w, j]
        floor = floors[w, j]
        scores = lax.dot_general(two[j * block : (j + 1) * block, :], rows, NT, preferred_element_type=jnp.float32)
        power = lax.dot_general(
            jnp.ones((8, width), jnp.bfloat16), rows * rows, NT, preferred_element_type=jnp.float32
        ) + lax.dot_general(
            jnp.ones((8, floor.shape[1]), jnp.bfloat16), floor * floor, NT, preferred_element_type=jnp.float32
        )
        power = jnp.where(power > 0.0, power, 1.0) * (1.0 / width)
        lines.append(jnp.sum(weights(scores * lax.rsqrt(power[0:1, :]), width), axis=0, keepdims=True))
    return jnp.concatenate(lines, axis=0)


def redo(cap, per, scaled, facts_in, me, refs, firsts, packed, floors):
    part = per * cap
    planes = packed.shape[0]
    count = planes * part
    width = scaled.shape[1]
    probe0 = facts_in[0:1, :]
    slots = facts_in[8:9, :] * 32 + facts_in[9:10, :]
    lane = lax.broadcasted_iota(jnp.int32, (count, 128), 1)
    for r, (ref, first) in enumerate(zip(refs, firsts)):
        facts = jnp.transpose(ref[ref.shape[0] - META :, first : first + count].astype(jnp.float32))
        hits = (facts[:, 0:1] * 32.0 + facts[:, 1:2]).astype(jnp.int32) == jnp.where(probe0 == (me ^ r), slots + 1, -1)
        gained = jnp.sum(jnp.where(hits, 1.0, 0.0), axis=1, keepdims=True)
        ahead = facts[:, 2:3]
        floor = (ahead + gained) * math.sqrt(1e-06 * width)
        floor = jnp.where(lane == 0, floor, 0.0).astype(jnp.bfloat16)
        added = jnp.dot(one_hot(hits), scaled[...], preferred_element_type=jnp.float32)
        whole = (ahead * ref[0:count, :].astype(jnp.float32) + added).astype(jnp.bfloat16)
        for w in range(planes):
            for j in range(per):
                start = w * part + j * cap
                packed[w, j, r * cap : (r + 1) * cap, :] = whole[start : start + cap, :]
                floors[w, j, r * cap : (r + 1) * cap, :] = floor[start : start + cap, :]


def early_kernel(
    cap, per, scaled, facts_in, units_any, cross_any, passed_any, any0, any1, any2, any3,
    sums, rows0, rows1, rows2, rows3, units, two_last, packed, floors, sems,
):
    me, z, y, core = position()
    end = (z == 0) | (z == 3)
    refs = (rows0, rows1, rows2, rows3)
    at_end = pltpu.make_async_copy(passed_any, two_last, sems.at[5])
    at_mid = pltpu.make_async_copy(cross_any, two_last, sems.at[5])
    copies = fetch(list(zip((any0, any1, any2, any3, units_any), (*refs, units))), sems)
    pl.when(end)(at_end.start)
    pl.when(jnp.logical_not(end))(at_mid.start)
    for copy in copies:
        copy.wait()
    pl.when(end)(at_end.wait)
    pl.when(jnp.logical_not(end))(at_mid.wait)
    redo(cap, per, scaled, facts_in, me, refs, (0, 0, 0, 0), packed, floors)
    third = unit_wide(two_last[...].astype(jnp.float32))
    for w, two in enumerate((units[0], units[1], third)):
        sums[8 * w : 8 * w + per, :] = level_sums(two, packed, floors, w, per)


def late_kernel(
    cap, per, scaled, facts_in, any0, any1, any2, any3, after, updated, packed, floors, rows0, rows1, rows2, rows3, sems
):
    me, z, y, core = position()
    part = per * cap
    tail = pl.ds(3 * part, part + META)
    refs = (rows0, rows1, rows2, rows3)
    copies = fetch(list(zip((any0.at[tail], any1.at[tail], any2, any3), refs)), sems)
    for copy in copies:
        copy.wait()
    redo(cap, per, scaled, facts_in, me, refs, (3 * part, 3 * part, 0, 0), packed, floors)


def third_kernel(cap, per, early, floors, kept_any, last_any, far_any, inside, across, kept, two, sems):
    me, z, y, core = position()
    end = (z == 0) | (z == 3)
    at_end = pltpu.make_async_copy(far_any, two, sems.at[1])
    at_mid = pltpu.make_async_copy(last_any, two, sems.at[1])
    pl.when(end)(at_end.start)
    pl.when(jnp.logical_not(end))(at_mid.start)
    copies = fetch([(kept_any, kept)], sems)
    pl.when(end)(at_end.wait)
    pl.when(jnp.logical_not(end))(at_mid.wait)
    two_unit = unit_wide(two[...].astype(jnp.float32))
    copies[0].wait()
    final = level_sums(two_unit, kept, floors, 0, per)
    lines = [early[8 * w : 8 * w + per, :] for w in range(3)] + [final]
    together = jnp.concatenate(lines + [jnp.zeros((16 - 4 * per, 4 * cap), jnp.float32)], axis=0)
    lane = lax.broadcasted_iota(jnp.int32, together.shape, 1)
    line = lax.broadcasted_iota(jnp.int32, together.shape, 0)
    for r in range(4):
        out, start = (inside, across)[r // 2], 4 * (r % 2)
        spread = jnp.zeros_like(together)
        for s in range(4):
            turned = together if s == r else pltpu.roll(together, ((s - r) % 4) * cap, 1)
            spread = jnp.where((line % 4 == s) & (lane >= s * cap) & (lane < (s + 1) * cap), turned, spread)
        for t in range(4):
            out[start + t : start + t + 1, :] = jnp.sum(spread[4 * t : 4 * t + 4], axis=0, keepdims=True)


def last_kernel(cap, scale_one, scale_two, info, inside, across, beside, share0, share1, share2, share3, density, level_two):
    total = share0[...] + share1[...] + share2[...] + share3[...]
    density[...] = jnp.log(total[:, 0 : density.shape[1]] / scale_one)
    values = jnp.concatenate([inside[0:4, :], beside[0:4, :], across[0:4, :], beside[4:8, :]], axis=0)
    rows = info.shape[1]
    chosen = jnp.where(info[2:3, :] == lax.broadcasted_iota(jnp.int32, (4 * cap, rows), 0), 1.0, 0.0)
    spread = jnp.dot(values, chosen, precision=lax.Precision.HIGHEST, preferred_element_type=jnp.float32)
    found = jnp.where(info[1:2, :] == lax.broadcasted_iota(jnp.int32, (16, rows), 0), spread, 0.0)
    level_two[...] = jnp.log(jnp.sum(found, axis=0, keepdims=True) / scale_two)


def call(kernel, outs, scratch=(), in_specs=None, **kw):
    def run(*args):
        specs = in_specs or [VMEM] * len(args)
        args = [pltpu.with_memory_space_constraint(a, pltpu.HBM) if spec is HBM else a for a, spec in zip(args, specs)]
        return pl.pallas_call(
            kernel, out_shape=outs, in_specs=specs, scratch_shapes=list(scratch), compiler_params=PARAMS, **kw
        )(*args)

    return run


def lasting(micros):
    return pl.CostEstimate(flops=0, transcendentals=0, bytes_accessed=int(micros * 3_690_000))


def in_order(*values, **kw):
    count = len(values)
    return call(
        order_kernel,
        tuple(jax.ShapeDtypeStruct(value.shape, value.dtype) for value in values),
        in_specs=[ANY] * count,
        out_specs=(ANY,) * count,
        input_output_aliases={i: i for i in range(count)},
        **kw,
    )(*values)


def line_body(embeddings, probes, assigned, prior_counts, centroids, candidates, centroids2):
    emb_rows, width = embeddings.shape
    probe_count = probes.shape[1]
    rows = centroids.shape[0]
    per = BLOCKS2_DEV
    cap = max(2, 3 * rows // (2 * per * 16))
    part = per * cap
    bf16, f32, i32 = jnp.bfloat16, jnp.float32, jnp.int32
    shape = jax.ShapeDtypeStruct

    def exchange(value, apart, sources=range(16)):
        return lax.ppermute(value, "shard", [(i, i ^ apart) for i in sources])

    def rows_of(planes):
        return shape((planes * part + META, width), bf16)

    def room(like):
        return pltpu.VMEM(like.shape, like.dtype)

    mids = range(4, 12)
    near_set = exchange(centroids2, 4)
    cross_set = exchange(centroids2, 12, mids)
    prior_row = prior_counts.reshape(1, rows)
    line = pltpu.VMEM((1, rows), i32)
    mine, early2, early3, info = call(
        functools.partial(pack_kernel, cap, per),
        (shape((emb_rows, width + 128), bf16), rows_of(3), rows_of(3), shape((8, rows), i32)),
        [
            line,
            pltpu.VMEM((emb_rows, width), bf16),
            pltpu.VMEM((probe_count, emb_rows), i32),
            pltpu.VMEM((1, emb_rows), i32),
            line,
            pltpu.VMEM((rows, width), bf16),
            pltpu.SemaphoreType.DMA((6,)),
        ],
        in_specs=[HBM] * 6,
    )(candidates.reshape(1, rows), embeddings, probes.T, assigned.reshape(1, emb_rows), prior_row, centroids)
    early2, early3 = exchange(early2, 2), exchange(early3, 3)
    rows0, rows1, late2, late3 = call(
        functools.partial(pack_more_kernel, part), (rows_of(4), rows_of(4), rows_of(1), rows_of(1))
    )(info, prior_row, centroids)
    mine = jnp.concatenate([mine, exchange(mine, 4)], axis=0)
    near_set, cross_set, mine, rows0 = in_order(near_set, cross_set, mine, rows0)
    across = exchange(mine, 12)
    passed = exchange(cross_set, 4, mids)
    last_set = exchange(near_set, 12, mids)
    mine = jnp.concatenate([mine, across], axis=0)
    mine, early2, early3, late2, late3, rows1 = in_order(mine, early2, early3, late2, late3, rows1)
    mine = jnp.concatenate([mine, exchange(mine, 2)], axis=0)
    late2, late3 = exchange(late2, 2), exchange(late3, 3)
    rows1 = exchange(rows1, 1)
    set_rows = per * BLOCK2
    block_set = pltpu.VMEM((set_rows, width), bf16)
    unit_old, units = call(
        prepare_kernel,
        (shape((rows, width), bf16), shape((2, set_rows, width), bf16)),
        [block_set, block_set, pltpu.SemaphoreType.DMA((2,))],
        in_specs=[VMEM, HBM, ANY],
    )(centroids, centroids2, near_set)
    passed, last_set, unit_old, units = in_order(passed, last_set, unit_old, units)
    far_set = exchange(last_set, 4, mids)
    other = exchange(mine, 1)
    gathered = pltpu.VMEM((8 * emb_rows, width + 128), bf16)
    scaled, facts, share, share_high = call(
        share_kernel,
        (
            shape((16 * emb_rows, width), bf16),
            shape((16, 16 * emb_rows), i32),
            shape((8, 4 * cap), f32),
            shape((8, 4 * cap), f32),
        ),
        [gathered, gathered, pltpu.SemaphoreType.DMA((2,))],
        in_specs=[ANY, ANY, VMEM],
    )(mine, other, unit_old)
    share = share + exchange(share_high, 1)
    share = share[0:4] + exchange(share[4:8], 2)
    early = call(
        functools.partial(early_kernel, cap, per),
        shape((24, 4 * cap), f32),
        [room(rows_of(4))] * 2
        + [room(rows_of(3))] * 2
        + [
            pltpu.VMEM((2, set_rows, width), bf16),
            block_set,
            pltpu.VMEM((3, per, 4 * cap, width), bf16),
            pltpu.VMEM((3, per, 4 * cap, 128), bf16),
            pltpu.SemaphoreType.DMA((6,)),
        ],
        in_specs=[VMEM, VMEM] + [ANY] * 7,
    )(scaled, facts, units, cross_set, passed, rows0, rows1, early2, early3)
    new_centroids, counts = call(
        update_kernel, (shape((rows, width), bf16), shape((1, rows), i32)), in_specs=[ANY] + [VMEM] * 4
    )(early, scaled, facts, centroids, prior_row)
    kept = shape((1, per, 4 * cap, width), bf16)
    kept_rows, floors = call(
        functools.partial(late_kernel, cap, per),
        (kept, shape((1, per, 4 * cap, 128), bf16)),
        [room(rows_of(1))] * 4 + [pltpu.SemaphoreType.DMA((4,))],
        in_specs=[VMEM] * 2 + [ANY] * 6,
    )(scaled, facts, rows0, rows1, late2, late3, early, counts)
    tile = shape((8, 4 * cap), f32)
    inside, across = call(
        functools.partial(third_kernel, cap, per),
        (tile,) * 2,
        [room(kept), block_set, pltpu.SemaphoreType.DMA((2,))],
        in_specs=[VMEM, VMEM] + [ANY] * 3,
    )(early, floors, kept_rows, last_set, far_set)
    across = exchange(across, 2)
    beside = exchange(jnp.concatenate([inside[4:8], across[4:8]], axis=0), 1)
    share = [share[0:1]] + [exchange(share[i : i + 1], apart) for i, apart in ((1, 4), (2, 12), (3, 8))]
    density, level_two = call(
        functools.partial(last_kernel, cap, probe_count * BLOCK, BLOCK2), (shape((1, emb_rows), f32), shape((1, rows), f32))
    )(info, inside, across, beside, *share)
    return (density.reshape(-1), new_centroids, counts.reshape(-1), level_two.reshape(-1))


def solution(mesh):
    placed = (
        P(("groups", "shard"), None),
        P(("groups", "shard"), None),
        P(("groups", "shard")),
        P(("groups", "shard")),
        P(("groups", "shard"), None),
        P(("groups", "shard"), None),
        P(("groups", "shard"), None),
    )
    body = line_body if mesh.shape["shard"] == 16 else general_body
    return jax.shard_map(
        body,
        mesh=mesh,
        in_specs=placed,
        out_specs=(
            P(("groups", "shard")),
            P(("groups", "shard"), None),
            P(("groups", "shard")),
            P(("groups", "shard")),
        ),
        check_vma=False,
    )
```

```python
import functools
import math

import jax
import jax.numpy as jnp
from jax import lax
from jax.experimental import pallas as pl
from jax.experimental.pallas import tpu as pltpu
from jax.sharding import PartitionSpec as P

BLOCK = 1024
BLOCKS_DEV = 1
BLOCK2 = 128
BLOCKS2_DEV = 3


def unit_rows(values):
    wide = values.astype(jnp.float32)
    power = jnp.mean(wide * wide, axis=-1, keepdims=True) + 1e-06
    return (wide * lax.rsqrt(power)).astype(jnp.bfloat16)


def kernel_sums(rows, unit):
    scores = lax.dot_general(
        rows, unit, (((1,), (1,)), ((), ())), preferred_element_type=jnp.float32
    )
    return jnp.sum(jnp.exp((scores / rows.shape[1] - 1.0) / 0.1), axis=1)


def block_update(rows, slots, width):
    matches = slots[:, None] == jnp.arange(width, dtype=jnp.int32)[None, :]
    sums = lax.dot_general(
        matches.astype(jnp.bfloat16),
        rows,
        (((0,), (0,)), ((), ())),
        preferred_element_type=jnp.float32,
    )
    counts = jnp.sum(matches.astype(jnp.int32), axis=0)
    return (sums, counts)


def slot_ranks(targets, buckets):
    matches = (targets[:, None] == jnp.arange(buckets, dtype=jnp.int32)[None, :]).astype(jnp.int32)
    return jnp.sum(jnp.cumsum(matches, axis=0) * matches, axis=1) - 1


def general_body(embeddings, probes, assigned, prior_counts, centroids, candidates, centroids2):
    devices = lax.axis_size("shard")
    emb_rows, width = embeddings.shape
    probe_count = probes.shape[1]
    capacity = max(2, 2 * emb_rows * probe_count // (BLOCKS_DEV * devices))
    scaled = unit_rows(embeddings)
    units_old = unit_rows(centroids).reshape(BLOCKS_DEV, BLOCK, width)
    total = emb_rows * probe_count
    buckets = BLOCKS_DEV * devices
    flat = probes.reshape(-1)
    place = flat * capacity + slot_ranks(flat, buckets)
    leading = jnp.arange(total, dtype=jnp.int32) % probe_count == 0
    repeated = jnp.repeat(scaled, probe_count, axis=0)
    slot_values = jnp.where(leading, jnp.repeat(assigned, probe_count), -1)
    send_rows = jnp.zeros((buckets * capacity, width), jnp.bfloat16).at[place].set(repeated)
    send_slots = jnp.full((buckets * capacity,), -1, jnp.int32).at[place].set(slot_values)
    got_rows, got_slots = (
        lax.all_to_all(
            send_rows.reshape(devices, BLOCKS_DEV * capacity, width),
            "shard",
            split_axis=0,
            concat_axis=0,
            tiled=True,
        ),
        lax.all_to_all(
            send_slots.reshape(devices, BLOCKS_DEV * capacity),
            "shard",
            split_axis=0,
            concat_axis=0,
            tiled=True,
        ),
    )
    got_rows = got_rows.reshape(devices, BLOCKS_DEV, capacity, width)
    got_slots = got_slots.reshape(devices, BLOCKS_DEV, capacity)
    local = 0
    picked = got_rows[:, local].reshape(devices * capacity, width)
    slots = got_slots[:, local].reshape(-1)
    weights = [kernel_sums(picked, units_old[local]).reshape(devices, capacity)]
    more_sums, more_counts = block_update(picked, slots, BLOCK)
    sum_list = [more_sums]
    count_list = [more_counts]
    sums = jnp.stack(sum_list)
    counts = jnp.stack(count_list)
    returned = lax.all_to_all(
        jnp.stack(weights, axis=1).reshape(devices, BLOCKS_DEV * capacity),
        "shard",
        split_axis=0,
        concat_axis=0,
        tiled=True,
    )
    totals = jnp.sum(returned.reshape(-1)[place].reshape(emb_rows, probe_count), axis=1)
    density = jnp.log(totals / (probe_count * BLOCK))
    prior = prior_counts.reshape(BLOCKS_DEV, BLOCK)
    fresh = prior + counts
    updated = (
        prior.astype(jnp.float32)[:, :, None]
        * centroids.reshape(BLOCKS_DEV, BLOCK, width).astype(jnp.float32)
        + sums
    ) / fresh.astype(jnp.float32)[:, :, None]
    new_centroids = updated.astype(jnp.bfloat16).reshape(BLOCKS_DEV * BLOCK, width)
    units_new = unit_rows(updated).reshape(BLOCKS_DEV * BLOCK, width)
    rows_two = units_new.shape[0]
    second_capacity = max(2, 3 * rows_two // (2 * BLOCKS2_DEV * devices))
    buckets_two = BLOCKS2_DEV * devices
    chosen = candidates[:, 0]
    place_two = chosen * second_capacity + slot_ranks(chosen, buckets_two)
    send_two = (
        jnp.zeros((buckets_two * second_capacity, width), jnp.bfloat16).at[place_two].set(units_new)
    )
    send_two = send_two.reshape(devices, BLOCKS2_DEV, second_capacity, width)
    units_two = unit_rows(centroids2).reshape(BLOCKS2_DEV, BLOCK2, width)
    arrived = lax.all_to_all(send_two, "shard", split_axis=0, concat_axis=0, tiled=True)
    items = arrived.shape[2]
    weights_two = [
        kernel_sums(arrived[:, local].reshape(-1, width), units_two[local]).reshape(
            arrived.shape[0], items
        )
        for local in range(BLOCKS2_DEV)
    ]
    returned_two = lax.all_to_all(
        jnp.stack(weights_two, axis=1), "shard", split_axis=0, concat_axis=0, tiled=True
    )
    level_two = jnp.log(returned_two.reshape(-1)[place_two] / BLOCK2)
    return (density, new_centroids, fresh.reshape(-1), level_two)


NT = (((1,), (1,)), ((), ()))
PARAMS = pltpu.CompilerParams(vmem_limit_bytes=48 * 1024 * 1024)
META = 16
SHARE = 1
LATE = 5
STEP = 12
HBM = pl.BlockSpec(memory_space=pltpu.HBM)
ANY = pl.BlockSpec(memory_space=pl.ANY)
VMEM = pl.BlockSpec(memory_space=pltpu.VMEM)


def position():
    me = lax.axis_index("shard")
    return me, me // 4, (me // 2) % 2, me % 2


def unit_wide(wide):
    power = jnp.mean(wide * wide, axis=-1, keepdims=True) + 1e-06
    return (wide * lax.rsqrt(power)).astype(jnp.bfloat16)


def weights(scores, width):
    return jnp.exp(scores * (10.0 / width) - 10.0)


def one_hot(hits):
    return jnp.where(hits, 1.0, 0.0).astype(jnp.bfloat16)


def column(row):
    return jnp.transpose(jnp.broadcast_to(row, (8, row.shape[1])))[:, 0:1]


def fetch(pairs, sems):
    copies = [pltpu.make_async_copy(src, dst, sems.at[i]) for i, (src, dst) in enumerate(pairs)]
    for copy in copies:
        copy.start()
    return copies


def pick_rows(slot, first, count):
    return one_hot(slot == lax.broadcasted_iota(jnp.int32, (count, slot.shape[1]), 0) + first)


def pack(slot, prior, cent, first, out):
    count = out.shape[0] - META
    rows = slot.shape[1]
    ident = lax.broadcasted_iota(jnp.int32, (1, rows), 1) + 1
    line = lax.broadcasted_iota(jnp.int32, (META, rows), 0)
    facts = jnp.where(line == 0, ident >> 5, jnp.where(line == 1, ident & 31, jnp.where(line == 2, prior, 0)))
    facts = facts.astype(jnp.float32).astype(jnp.bfloat16)
    pick = pick_rows(slot, first, count)
    out[0:count, :] = jnp.dot(pick, cent, preferred_element_type=jnp.float32).astype(jnp.bfloat16)
    out[count:, :] = jnp.zeros((META, out.shape[1]), jnp.bfloat16)
    out[count:, 0:count] = lax.dot_general(facts, pick, NT, preferred_element_type=jnp.float32).astype(jnp.bfloat16)


def pack_kernel(
    cap, per, cand_any, emb_any, probes_any, assigned_any, prior_any, cent_any, mine, rows2, rows3, info,
    cand_ref, emb_ref, probes_ref, assigned_ref, prior_ref, cent_ref, sems,
):
    copies = fetch(
        (
            (cand_any, cand_ref),
            (emb_any, emb_ref),
            (probes_any, probes_ref),
            (assigned_any, assigned_ref),
            (prior_any, prior_ref),
            (cent_any, cent_ref),
        ),
        sems,
    )
    me, z, y, core = position()
    rows = cand_ref.shape[1]
    buckets = 16 * per
    before = lax.broadcasted_iota(jnp.int32, (rows, rows), 0) <= lax.broadcasted_iota(jnp.int32, (rows, rows), 1)
    before = one_hot(before)
    copies[0].wait()
    cand = cand_ref[...]
    dev = sum((cand >= per * step).astype(jnp.int32) for step in range(1, 16))
    near = dev >> 2
    plane = jnp.where(z >= 2, 3 - near, near)
    rel = (((dev >> 1) & 1) ^ y) * 2 + ((dev & 1) ^ core)
    named = cand == lax.broadcasted_iota(jnp.int32, (buckets, rows), 0)
    counted = jnp.dot(one_hot(named), before, preferred_element_type=jnp.float32)
    rank = jnp.sum(jnp.where(named, counted, 0.0), axis=0, keepdims=True).astype(jnp.int32) - 1
    kind = plane * per + cand - dev * per
    slot = (rel * 4 * per + kind) * cap + rank
    info[0:1, :] = slot
    info[1:2, :] = rel * 4 + (kind >> 2)
    info[2:3, :] = (kind & 3) * cap + rank
    for copy in copies[1:5]:
        copy.wait()
    count, width = emb_ref.shape
    probe_count = probes_ref.shape[0]
    slots = assigned_ref[...]
    facts = jnp.concatenate([probes_ref[...], slots >> 5, slots & 31], axis=0).astype(jnp.float32)
    facts = jnp.concatenate([facts, jnp.zeros((128 - probe_count - 2, count), jnp.float32)], axis=0)
    same = lax.broadcasted_iota(jnp.int32, (count, count), 0) == lax.broadcasted_iota(jnp.int32, (count, count), 1)
    mine[:, 0:width] = emb_ref[...]
    mine[:, width:] = lax.dot_general(
        one_hot(same), facts.astype(jnp.bfloat16), NT, preferred_element_type=jnp.float32
    ).astype(jnp.bfloat16)
    copies[5].wait()
    pack(slot, prior_ref[...], cent_ref[...], 2 * 4 * per * cap, rows2)
    pack(slot, prior_ref[...], cent_ref[...], 3 * 4 * per * cap, rows3)


def pack_more_kernel(part, info, prior_ref, cent_ref, rows0, rows1, late2, late3):
    for first, out in ((0, rows0), (4 * part, rows1), (11 * part, late2), (15 * part, late3)):
        pack(info[0:1, :], prior_ref[...], cent_ref[...], first, out)


def order_kernel(*refs):
    pass


def prepare_kernel(cent_ref, own_any, near_any, unit_old, units, own, near, sems):
    copies = fetch(((own_any, own), (near_any, near)), sems)
    step = 256
    for start in range(0, cent_ref.shape[0], step):
        unit_old[start : start + step, :] = unit_wide(cent_ref[start : start + step, :].astype(jnp.float32))
    me, z, y, core = position()
    first = jnp.where((z == 0) | (z == 3), 0, 1)
    copies[0].wait()
    units[first] = unit_wide(own[...].astype(jnp.float32))
    copies[1].wait()
    units[1 - first] = unit_wide(near[...].astype(jnp.float32))


def share_kernel(mine_any, other_any, unit_old, scaled, facts, share0, share1, share2, share3, mine_ref, other_ref, sems):
    copies = fetch(((mine_any, mine_ref), (other_any, other_ref)), sems)
    me, z, y, core = position()
    half = mine_ref.shape[0]
    count = 2 * half
    rows, width = unit_old.shape
    copies[0].wait()
    scaled[0:half, :] = unit_wide(mine_ref[:, 0:width].astype(jnp.float32))
    copies[1].wait()
    scaled[half:count, :] = unit_wide(other_ref[:, 0:width].astype(jnp.float32))
    aux = jnp.concatenate([mine_ref[:, width:], other_ref[:, width:]], axis=0).astype(jnp.float32)
    aux = jnp.transpose(aux)[0:16, :].astype(jnp.int32)
    facts[...] = aux
    member = jnp.sum((aux[0:8, :] == me).astype(jnp.float32), axis=0, keepdims=True)
    step = 256
    total = jnp.zeros((1, count), jnp.float32)
    for start in range(0, rows, step):
        scores = lax.dot_general(
            unit_old[start : start + step, :], scaled[...], NT, preferred_element_type=jnp.float32
        )
        total = total + jnp.sum(weights(scores, width), axis=0, keepdims=True)
    piece = count // 16
    lane = lax.broadcasted_iota(jnp.int32, (16, count), 1)
    line = lax.broadcasted_iota(jnp.int32, (16, count), 0)
    apart = jnp.where((member > 0.0) & (lane >= line * piece) & (lane < (line + 1) * piece), total, 0.0)
    spot = lax.broadcasted_iota(jnp.int32, (count, 128), 0)
    block = sum((spot >= piece * step).astype(jnp.int32) for step in range(1, 16))
    together = jnp.where(spot - block * piece == lax.broadcasted_iota(jnp.int32, (count, 128), 1), 1.0, 0.0)
    share = jnp.dot(apart, together, precision=lax.Precision.HIGHEST, preferred_element_type=jnp.float32)
    for k, out in enumerate((share0, share1, share2, share3)):
        out[...] = jnp.concatenate([share[4 * g + k : 4 * g + k + 1, :] for g in range(4)], axis=0)


def update_kernel(after, scaled, facts, cent_ref, prior_ref, fresh_rows, fresh_counts):
    me, z, y, core = position()
    rows, width = cent_ref.shape
    count = scaled.shape[0]
    prior = column(prior_ref[...].astype(jnp.float32))
    target = jnp.where(facts[0:1, :] == me, facts[8:9, :] * 32 + facts[9:10, :], -1)
    step = 256
    for start in range(0, rows, step):
        old = cent_ref[start : start + step, :].astype(jnp.float32)
        hits = one_hot(target == lax.broadcasted_iota(jnp.int32, (step, count), 0) + start)
        sums = jnp.dot(hits, scaled[...], preferred_element_type=jnp.float32)
        gained = jnp.sum(hits.astype(jnp.float32), axis=1, keepdims=True)
        ahead = prior[start : start + step, :]
        updated = (ahead * old + sums) * (1.0 / (ahead + gained))
        fresh_rows[start : start + step, :] = updated.astype(jnp.bfloat16)
        gained_row = lax.dot_general(
            jnp.ones((8, count), jnp.bfloat16), hits, NT, preferred_element_type=jnp.float32
        )
        fresh_counts[0:1, start : start + step] = prior_ref[0:1, start : start + step] + gained_row[0:1, :].astype(jnp.int32)


def level_sums(two, packed, floors, w, per):
    block, width = two.shape[0] // per, two.shape[1]
    lines = []
    for j in range(per):
        rows = packed[w, j]
        floor = floors[w, j]
        scores = lax.dot_general(two[j * block : (j + 1) * block, :], rows, NT, preferred_element_type=jnp.float32)
        power = lax.dot_general(
            jnp.ones((8, width), jnp.bfloat16), rows * rows, NT, preferred_element_type=jnp.float32
        ) + lax.dot_general(
            jnp.ones((8, floor.shape[1]), jnp.bfloat16), floor * floor, NT, preferred_element_type=jnp.float32
        )
        power = jnp.where(power > 0.0, power, 1.0) * (1.0 / width)
        lines.append(jnp.sum(weights(scores * lax.rsqrt(power[0:1, :]), width), axis=0, keepdims=True))
    return jnp.concatenate(lines, axis=0)


def redo(cap, per, scaled, facts_in, me, refs, firsts, packed, floors):
    part = per * cap
    planes = packed.shape[0]
    count = planes * part
    width = scaled.shape[1]
    probe0 = facts_in[0:1, :]
    slots = facts_in[8:9, :] * 32 + facts_in[9:10, :]
    lane = lax.broadcasted_iota(jnp.int32, (count, 128), 1)
    for r, (ref, first) in enumerate(zip(refs, firsts)):
        facts = jnp.transpose(ref[ref.shape[0] - META :, first : first + count].astype(jnp.float32))
        hits = (facts[:, 0:1] * 32.0 + facts[:, 1:2]).astype(jnp.int32) == jnp.where(probe0 == (me ^ r), slots + 1, -1)
        gained = jnp.sum(jnp.where(hits, 1.0, 0.0), axis=1, keepdims=True)
        ahead = facts[:, 2:3]
        floor = (ahead + gained) * math.sqrt(1e-06 * width)
        floor = jnp.where(lane == 0, floor, 0.0).astype(jnp.bfloat16)
        added = jnp.dot(one_hot(hits), scaled[...], preferred_element_type=jnp.float32)
        whole = (ahead * ref[0:count, :].astype(jnp.float32) + added).astype(jnp.bfloat16)
        for w in range(planes):
            for j in range(per):
                start = w * part + j * cap
                packed[w, j, r * cap : (r + 1) * cap, :] = whole[start : start + cap, :]
                floors[w, j, r * cap : (r + 1) * cap, :] = floor[start : start + cap, :]


def early_kernel(
    cap, per, scaled, facts_in, units_any, cross_any, passed_any, any0, any1, any2, any3,
    sums, rows0, rows1, rows2, rows3, units, two_last, packed, floors, sems,
):
    me, z, y, core = position()
    end = (z == 0) | (z == 3)
    refs = (rows0, rows1, rows2, rows3)
    at_end = pltpu.make_async_copy(passed_any, two_last, sems.at[5])
    at_mid = pltpu.make_async_copy(cross_any, two_last, sems.at[5])
    copies = fetch(list(zip((any0, any1, any2, any3, units_any), (*refs, units))), sems)
    pl.when(end)(at_end.start)
    pl.when(jnp.logical_not(end))(at_mid.start)
    for copy in copies:
        copy.wait()
    pl.when(end)(at_end.wait)
    pl.when(jnp.logical_not(end))(at_mid.wait)
    redo(cap, per, scaled, facts_in, me, refs, (0, 0, 0, 0), packed, floors)
    third = unit_wide(two_last[...].astype(jnp.float32))
    for w, two in enumerate((units[0], units[1], third)):
        sums[8 * w : 8 * w + per, :] = level_sums(two, packed, floors, w, per)


def late_kernel(
    cap, per, scaled, facts_in, any0, any1, any2, any3, after, packed, floors, rows0, rows1, rows2, rows3, sems
):
    me, z, y, core = position()
    part = per * cap
    tail = pl.ds(3 * part, part + META)
    refs = (rows0, rows1, rows2, rows3)
    copies = fetch(list(zip((any0.at[tail], any1.at[tail], any2, any3), refs)), sems)
    for copy in copies:
        copy.wait()
    redo(cap, per, scaled, facts_in, me, refs, (3 * part, 3 * part, 0, 0), packed, floors)


def third_kernel(
    cap, per, early, floors, share0, share1, share2, share3, kept_any, last_any, far_any, inside, across, kept, two, sems
):
    me, z, y, core = position()
    end = (z == 0) | (z == 3)
    at_end = pltpu.make_async_copy(far_any, two, sems.at[1])
    at_mid = pltpu.make_async_copy(last_any, two, sems.at[1])
    pl.when(end)(at_end.start)
    pl.when(jnp.logical_not(end))(at_mid.start)
    copies = fetch([(kept_any, kept)], sems)
    pl.when(end)(at_end.wait)
    pl.when(jnp.logical_not(end))(at_mid.wait)
    two_unit = unit_wide(two[...].astype(jnp.float32))
    copies[0].wait()
    final = level_sums(two_unit, kept, floors, 0, per)
    lines = [early[8 * w : 8 * w + per, :] for w in range(3)] + [final]
    together = jnp.concatenate(lines + [jnp.zeros((16 - 4 * per, 4 * cap), jnp.float32)], axis=0)
    lane = lax.broadcasted_iota(jnp.int32, together.shape, 1)
    line = lax.broadcasted_iota(jnp.int32, together.shape, 0)
    share = share0[...] + share1[...] + share2[...] + share3[...]
    for r, g in enumerate((0, 2, 1, 3)):
        (inside, across)[r // 2][8 + r % 2 : 9 + r % 2, :] = share[g : g + 1, :]
    for r in range(4):
        out, start = (inside, across)[r // 2], 4 * (r % 2)
        spread = jnp.zeros_like(together)
        for s in range(4):
            turned = together if s == r else pltpu.roll(together, ((s - r) % 4) * cap, 1)
            spread = jnp.where((line % 4 == s) & (lane >= s * cap) & (lane < (s + 1) * cap), turned, spread)
        for t in range(4):
            out[start + t : start + t + 1, :] = jnp.sum(spread[4 * t : 4 * t + 4], axis=0, keepdims=True)


def last_kernel(cap, scale_one, scale_two, info, inside, across, beside, density, level_two):
    total = inside[8:9, :] + across[8:9, :] + beside[8:9, :]
    density[...] = jnp.log(total[:, 0 : density.shape[1]] / scale_one)
    values = jnp.concatenate([inside[0:4, :], beside[0:4, :], across[0:4, :], beside[4:8, :]], axis=0)
    rows = info.shape[1]
    chosen = jnp.where(info[2:3, :] == lax.broadcasted_iota(jnp.int32, (4 * cap, rows), 0), 1.0, 0.0)
    spread = jnp.dot(values, chosen, precision=lax.Precision.HIGHEST, preferred_element_type=jnp.float32)
    found = jnp.where(info[1:2, :] == lax.broadcasted_iota(jnp.int32, (16, rows), 0), spread, 0.0)
    level_two[...] = jnp.log(jnp.sum(found, axis=0, keepdims=True) / scale_two)


def call(kernel, outs, scratch=(), in_specs=None, **kw):
    def run(*args):
        specs = in_specs or [VMEM] * len(args)
        args = [pltpu.with_memory_space_constraint(a, pltpu.HBM) if spec is HBM else a for a, spec in zip(args, specs)]
        return pl.pallas_call(
            kernel, out_shape=outs, in_specs=specs, scratch_shapes=list(scratch), compiler_params=PARAMS, **kw
        )(*args)

    return run


def lasting(micros):
    return pl.CostEstimate(flops=0, transcendentals=0, bytes_accessed=int(micros * 3_690_000))


def in_order(*values, **kw):
    count = len(values)
    return call(
        order_kernel,
        tuple(jax.ShapeDtypeStruct(value.shape, value.dtype) for value in values),
        in_specs=[ANY] * count,
        out_specs=(ANY,) * count,
        input_output_aliases={i: i for i in range(count)},
        **kw,
    )(*values)


def line_body(embeddings, probes, assigned, prior_counts, centroids, candidates, centroids2):
    emb_rows, width = embeddings.shape
    probe_count = probes.shape[1]
    rows = centroids.shape[0]
    per = BLOCKS2_DEV
    cap = max(2, 3 * rows // (2 * per * 16))
    part = per * cap
    bf16, f32, i32 = jnp.bfloat16, jnp.float32, jnp.int32
    shape = jax.ShapeDtypeStruct

    def exchange(value, apart, sources=range(16)):
        return lax.ppermute(value, "shard", [(i, i ^ apart) for i in sources])

    def rows_of(planes):
        return shape((planes * part + META, width), bf16)

    def room(like):
        return pltpu.VMEM(like.shape, like.dtype)

    mids = range(4, 12)
    near_set = exchange(centroids2, 4)
    cross_set = exchange(centroids2, 12, mids)
    prior_row = prior_counts.reshape(1, rows)
    line = pltpu.VMEM((1, rows), i32)
    mine, early2, early3, info = call(
        functools.partial(pack_kernel, cap, per),
        (shape((emb_rows, width + 128), bf16), rows_of(3), rows_of(3), shape((8, rows), i32)),
        [
            line,
            pltpu.VMEM((emb_rows, width), bf16),
            pltpu.VMEM((probe_count, emb_rows), i32),
            pltpu.VMEM((1, emb_rows), i32),
            line,
            pltpu.VMEM((rows, width), bf16),
            pltpu.SemaphoreType.DMA((6,)),
        ],
        in_specs=[HBM] * 6,
    )(candidates.reshape(1, rows), embeddings, probes.T, assigned.reshape(1, emb_rows), prior_row, centroids)
    early2, early3 = exchange(early2, 2), exchange(early3, 3)
    rows0, rows1, late2, late3 = call(
        functools.partial(pack_more_kernel, part), (rows_of(4), rows_of(4), rows_of(1), rows_of(1))
    )(info, prior_row, centroids)
    mine = jnp.concatenate([mine, exchange(mine, 4)], axis=0)
    near_set, cross_set, mine, rows0 = in_order(near_set, cross_set, mine, rows0)
    across = exchange(mine, 12)
    passed = exchange(cross_set, 4, mids)
    last_set = exchange(near_set, 12, mids)
    mine = jnp.concatenate([mine, across], axis=0)
    mine, early2, early3, late2, late3, rows1 = in_order(mine, early2, early3, late2, late3, rows1)
    mine = jnp.concatenate([mine, exchange(mine, 2)], axis=0)
    late2, late3 = exchange(late2, 2), exchange(late3, 3)
    rows1 = exchange(rows1, 1)
    set_rows = per * BLOCK2
    block_set = pltpu.VMEM((set_rows, width), bf16)
    unit_old, units = call(
        prepare_kernel,
        (shape((rows, width), bf16), shape((2, set_rows, width), bf16)),
        [block_set, block_set, pltpu.SemaphoreType.DMA((2,))],
        in_specs=[VMEM, HBM, ANY],
    )(centroids, centroids2, near_set)
    passed, last_set, unit_old, units = in_order(passed, last_set, unit_old, units)
    far_set = exchange(last_set, 4, mids)
    other = exchange(mine, 1)
    gathered = pltpu.VMEM((8 * emb_rows, width + 128), bf16)
    scaled, facts, *share = call(
        share_kernel,
        (
            shape((16 * emb_rows, width), bf16),
            shape((16, 16 * emb_rows), i32),
            *[shape((4, 4 * cap), f32)] * 4,
        ),
        [gathered, gathered, pltpu.SemaphoreType.DMA((2,))],
        in_specs=[ANY, ANY, VMEM],
    )(mine, other, unit_old)
    share = [share[0], exchange(share[1], 4), exchange(share[2], 12), share[3]]
    early = call(
        functools.partial(early_kernel, cap, per),
        shape((24, 4 * cap), f32),
        [room(rows_of(4))] * 2
        + [room(rows_of(3))] * 2
        + [
            pltpu.VMEM((2, set_rows, width), bf16),
            block_set,
            pltpu.VMEM((3, per, 4 * cap, width), bf16),
            pltpu.VMEM((3, per, 4 * cap, 128), bf16),
            pltpu.SemaphoreType.DMA((6,)),
        ],
        in_specs=[VMEM, VMEM] + [ANY] * 7,
    )(scaled, facts, units, cross_set, passed, rows0, rows1, early2, early3)
    share[3], early = in_order(share[3], early)
    share[3] = exchange(share[3], 8)
    kept = shape((1, per, 4 * cap, width), bf16)
    kept_rows, floors = call(
        functools.partial(late_kernel, cap, per),
        (kept, shape((1, per, 4 * cap, 128), bf16)),
        [room(rows_of(1))] * 4 + [pltpu.SemaphoreType.DMA((4,))],
        in_specs=[VMEM] * 2 + [ANY] * 5,
    )(scaled, facts, rows0, rows1, late2, late3, early)
    tile = shape((16, 4 * cap), f32)
    inside, across = call(
        functools.partial(third_kernel, cap, per),
        (tile,) * 2,
        [room(kept), block_set, pltpu.SemaphoreType.DMA((2,))],
        in_specs=[VMEM] * 6 + [ANY] * 3,
    )(early, floors, *share, kept_rows, last_set, far_set)
    new_centroids, counts = call(
        update_kernel, (shape((rows, width), bf16), shape((1, rows), i32)), in_specs=[ANY] + [VMEM] * 4
    )(inside, scaled, facts, centroids, prior_row)
    across = exchange(across, 2)
    beside = exchange(jnp.concatenate([inside[4:8], across[4:8], inside[9:10] + across[9:10]], axis=0), 1)
    density, level_two = call(
        functools.partial(last_kernel, cap, probe_count * BLOCK, BLOCK2), (shape((1, emb_rows), f32), shape((1, rows), f32))
    )(info, inside, across, beside)
    return (density.reshape(-1), new_centroids, counts.reshape(-1), level_two.reshape(-1))


def solution(mesh):
    placed = (
        P(("groups", "shard"), None),
        P(("groups", "shard"), None),
        P(("groups", "shard")),
        P(("groups", "shard")),
        P(("groups", "shard"), None),
        P(("groups", "shard"), None),
        P(("groups", "shard"), None),
    )
    body = line_body if mesh.shape["shard"] == 16 else general_body
    return jax.shard_map(
        body,
        mesh=mesh,
        in_specs=placed,
        out_specs=(
            P(("groups", "shard")),
            P(("groups", "shard"), None),
            P(("groups", "shard")),
            P(("groups", "shard")),
        ),
        check_vma=False,
    )
```

```python
import functools
import math

import jax
import jax.numpy as jnp
from jax import lax
from jax.experimental import pallas as pl
from jax.experimental.pallas import tpu as pltpu
from jax.sharding import PartitionSpec as P

BLOCK = 1024
BLOCKS_DEV = 1
BLOCK2 = 128
BLOCKS2_DEV = 3


def unit_rows(values):
    wide = values.astype(jnp.float32)
    power = jnp.mean(wide * wide, axis=-1, keepdims=True) + 1e-06
    return (wide * lax.rsqrt(power)).astype(jnp.bfloat16)


def kernel_sums(rows, unit):
    scores = lax.dot_general(
        rows, unit, (((1,), (1,)), ((), ())), preferred_element_type=jnp.float32
    )
    return jnp.sum(jnp.exp((scores / rows.shape[1] - 1.0) / 0.1), axis=1)


def block_update(rows, slots, width):
    matches = slots[:, None] == jnp.arange(width, dtype=jnp.int32)[None, :]
    sums = lax.dot_general(
        matches.astype(jnp.bfloat16),
        rows,
        (((0,), (0,)), ((), ())),
        preferred_element_type=jnp.float32,
    )
    counts = jnp.sum(matches.astype(jnp.int32), axis=0)
    return (sums, counts)


def slot_ranks(targets, buckets):
    matches = (targets[:, None] == jnp.arange(buckets, dtype=jnp.int32)[None, :]).astype(jnp.int32)
    return jnp.sum(jnp.cumsum(matches, axis=0) * matches, axis=1) - 1


def general_body(embeddings, probes, assigned, prior_counts, centroids, candidates, centroids2):
    devices = lax.axis_size("shard")
    emb_rows, width = embeddings.shape
    probe_count = probes.shape[1]
    capacity = max(2, 2 * emb_rows * probe_count // (BLOCKS_DEV * devices))
    scaled = unit_rows(embeddings)
    units_old = unit_rows(centroids).reshape(BLOCKS_DEV, BLOCK, width)
    total = emb_rows * probe_count
    buckets = BLOCKS_DEV * devices
    flat = probes.reshape(-1)
    place = flat * capacity + slot_ranks(flat, buckets)
    leading = jnp.arange(total, dtype=jnp.int32) % probe_count == 0
    repeated = jnp.repeat(scaled, probe_count, axis=0)
    slot_values = jnp.where(leading, jnp.repeat(assigned, probe_count), -1)
    send_rows = jnp.zeros((buckets * capacity, width), jnp.bfloat16).at[place].set(repeated)
    send_slots = jnp.full((buckets * capacity,), -1, jnp.int32).at[place].set(slot_values)
    got_rows, got_slots = (
        lax.all_to_all(
            send_rows.reshape(devices, BLOCKS_DEV * capacity, width),
            "shard",
            split_axis=0,
            concat_axis=0,
            tiled=True,
        ),
        lax.all_to_all(
            send_slots.reshape(devices, BLOCKS_DEV * capacity),
            "shard",
            split_axis=0,
            concat_axis=0,
            tiled=True,
        ),
    )
    got_rows = got_rows.reshape(devices, BLOCKS_DEV, capacity, width)
    got_slots = got_slots.reshape(devices, BLOCKS_DEV, capacity)
    local = 0
    picked = got_rows[:, local].reshape(devices * capacity, width)
    slots = got_slots[:, local].reshape(-1)
    weights = [kernel_sums(picked, units_old[local]).reshape(devices, capacity)]
    more_sums, more_counts = block_update(picked, slots, BLOCK)
    sum_list = [more_sums]
    count_list = [more_counts]
    sums = jnp.stack(sum_list)
    counts = jnp.stack(count_list)
    returned = lax.all_to_all(
        jnp.stack(weights, axis=1).reshape(devices, BLOCKS_DEV * capacity),
        "shard",
        split_axis=0,
        concat_axis=0,
        tiled=True,
    )
    totals = jnp.sum(returned.reshape(-1)[place].reshape(emb_rows, probe_count), axis=1)
    density = jnp.log(totals / (probe_count * BLOCK))
    prior = prior_counts.reshape(BLOCKS_DEV, BLOCK)
    fresh = prior + counts
    updated = (
        prior.astype(jnp.float32)[:, :, None]
        * centroids.reshape(BLOCKS_DEV, BLOCK, width).astype(jnp.float32)
        + sums
    ) / fresh.astype(jnp.float32)[:, :, None]
    new_centroids = updated.astype(jnp.bfloat16).reshape(BLOCKS_DEV * BLOCK, width)
    units_new = unit_rows(updated).reshape(BLOCKS_DEV * BLOCK, width)
    rows_two = units_new.shape[0]
    second_capacity = max(2, 3 * rows_two // (2 * BLOCKS2_DEV * devices))
    buckets_two = BLOCKS2_DEV * devices
    chosen = candidates[:, 0]
    place_two = chosen * second_capacity + slot_ranks(chosen, buckets_two)
    send_two = (
        jnp.zeros((buckets_two * second_capacity, width), jnp.bfloat16).at[place_two].set(units_new)
    )
    send_two = send_two.reshape(devices, BLOCKS2_DEV, second_capacity, width)
    units_two = unit_rows(centroids2).reshape(BLOCKS2_DEV, BLOCK2, width)
    arrived = lax.all_to_all(send_two, "shard", split_axis=0, concat_axis=0, tiled=True)
    items = arrived.shape[2]
    weights_two = [
        kernel_sums(arrived[:, local].reshape(-1, width), units_two[local]).reshape(
            arrived.shape[0], items
        )
        for local in range(BLOCKS2_DEV)
    ]
    returned_two = lax.all_to_all(
        jnp.stack(weights_two, axis=1), "shard", split_axis=0, concat_axis=0, tiled=True
    )
    level_two = jnp.log(returned_two.reshape(-1)[place_two] / BLOCK2)
    return (density, new_centroids, fresh.reshape(-1), level_two)


NT = (((1,), (1,)), ((), ()))
PARAMS = pltpu.CompilerParams(vmem_limit_bytes=48 * 1024 * 1024)
META = 16
SHARE = 1
LATE = 5
STEP = 12
HBM = pl.BlockSpec(memory_space=pltpu.HBM)
ANY = pl.BlockSpec(memory_space=pl.ANY)
VMEM = pl.BlockSpec(memory_space=pltpu.VMEM)


def position():
    me = lax.axis_index("shard")
    return me, me // 4, (me // 2) % 2, me % 2


def unit_wide(wide):
    power = jnp.mean(wide * wide, axis=-1, keepdims=True) + 1e-06
    return (wide * lax.rsqrt(power)).astype(jnp.bfloat16)


def weights(scores, width):
    return jnp.exp(scores * (10.0 / width) - 10.0)


def one_hot(hits):
    return jnp.where(hits, 1.0, 0.0).astype(jnp.bfloat16)


def column(row):
    return jnp.transpose(jnp.broadcast_to(row, (8, row.shape[1])))[:, 0:1]


def fetch(pairs, sems):
    copies = [pltpu.make_async_copy(src, dst, sems.at[i]) for i, (src, dst) in enumerate(pairs)]
    for copy in copies:
        copy.start()
    return copies


def pick_rows(slot, first, count):
    return one_hot(slot == lax.broadcasted_iota(jnp.int32, (count, slot.shape[1]), 0) + first)


def pack(slot, prior, cent, first, out):
    count = out.shape[0] - META
    rows = slot.shape[1]
    ident = lax.broadcasted_iota(jnp.int32, (1, rows), 1) + 1
    line = lax.broadcasted_iota(jnp.int32, (META, rows), 0)
    facts = jnp.where(line == 0, ident >> 5, jnp.where(line == 1, ident & 31, jnp.where(line == 2, prior, 0)))
    facts = facts.astype(jnp.float32).astype(jnp.bfloat16)
    pick = pick_rows(slot, first, count)
    out[0:count, :] = jnp.dot(pick, cent, preferred_element_type=jnp.float32).astype(jnp.bfloat16)
    out[count:, :] = jnp.zeros((META, out.shape[1]), jnp.bfloat16)
    out[count:, 0:count] = lax.dot_general(facts, pick, NT, preferred_element_type=jnp.float32).astype(jnp.bfloat16)


def pack_kernel(
    cap, per, cand_any, emb_any, probes_any, assigned_any, prior_any, cent_any, mine, rows2, rows3, info,
    cand_ref, emb_ref, probes_ref, assigned_ref, prior_ref, cent_ref, sems,
):
    copies = fetch(
        (
            (cand_any, cand_ref),
            (emb_any, emb_ref),
            (probes_any, probes_ref),
            (assigned_any, assigned_ref),
            (prior_any, prior_ref),
            (cent_any, cent_ref),
        ),
        sems,
    )
    me, z, y, core = position()
    rows = cand_ref.shape[1]
    buckets = 16 * per
    before = lax.broadcasted_iota(jnp.int32, (rows, rows), 0) <= lax.broadcasted_iota(jnp.int32, (rows, rows), 1)
    before = one_hot(before)
    copies[0].wait()
    cand = cand_ref[...]
    dev = sum((cand >= per * step).astype(jnp.int32) for step in range(1, 16))
    near = dev >> 2
    plane = jnp.where(z >= 2, 3 - near, near)
    rel = (((dev >> 1) & 1) ^ y) * 2 + ((dev & 1) ^ core)
    named = cand == lax.broadcasted_iota(jnp.int32, (buckets, rows), 0)
    counted = jnp.dot(one_hot(named), before, preferred_element_type=jnp.float32)
    rank = jnp.sum(jnp.where(named, counted, 0.0), axis=0, keepdims=True).astype(jnp.int32) - 1
    kind = plane * per + cand - dev * per
    slot = (rel * 4 * per + kind) * cap + rank
    info[0:1, :] = slot
    info[1:2, :] = rel * 4 + (kind >> 2)
    info[2:3, :] = (kind & 3) * cap + rank
    for copy in copies[1:5]:
        copy.wait()
    count, width = emb_ref.shape
    probe_count = probes_ref.shape[0]
    slots = assigned_ref[...]
    facts = jnp.concatenate([probes_ref[...], slots >> 5, slots & 31], axis=0).astype(jnp.float32)
    facts = jnp.concatenate([facts, jnp.zeros((128 - probe_count - 2, count), jnp.float32)], axis=0)
    same = lax.broadcasted_iota(jnp.int32, (count, count), 0) == lax.broadcasted_iota(jnp.int32, (count, count), 1)
    mine[:, 0:width] = emb_ref[...]
    mine[:, width:] = lax.dot_general(
        one_hot(same), facts.astype(jnp.bfloat16), NT, preferred_element_type=jnp.float32
    ).astype(jnp.bfloat16)
    copies[5].wait()
    pack(slot, prior_ref[...], cent_ref[...], 2 * 4 * per * cap, rows2)
    pack(slot, prior_ref[...], cent_ref[...], 3 * 4 * per * cap, rows3)


def pack_more_kernel(part, info, prior_ref, cent_ref, rows0, rows1, late2, late3):
    for first, out in ((0, rows0), (4 * part, rows1), (11 * part, late2), (15 * part, late3)):
        pack(info[0:1, :], prior_ref[...], cent_ref[...], first, out)


def order_kernel(*refs):
    pass


def prepare_kernel(cent_ref, own_any, near_any, unit_old, units, own, near, sems):
    copies = fetch(((own_any, own), (near_any, near)), sems)
    step = 256
    for start in range(0, cent_ref.shape[0], step):
        unit_old[start : start + step, :] = unit_wide(cent_ref[start : start + step, :].astype(jnp.float32))
    me, z, y, core = position()
    first = jnp.where((z == 0) | (z == 3), 0, 1)
    copies[0].wait()
    units[first] = unit_wide(own[...].astype(jnp.float32))
    copies[1].wait()
    units[1 - first] = unit_wide(near[...].astype(jnp.float32))


def share_kernel(mine_any, other_any, unit_old, scaled, facts, share0, share1, share2, share3, mine_ref, other_ref, sems):
    copies = fetch(((mine_any, mine_ref), (other_any, other_ref)), sems)
    me, z, y, core = position()
    half = mine_ref.shape[0]
    count = 2 * half
    rows, width = unit_old.shape
    copies[0].wait()
    scaled[0:half, :] = unit_wide(mine_ref[:, 0:width].astype(jnp.float32))
    copies[1].wait()
    scaled[half:count, :] = unit_wide(other_ref[:, 0:width].astype(jnp.float32))
    aux = jnp.concatenate([mine_ref[:, width:], other_ref[:, width:]], axis=0).astype(jnp.float32)
    aux = jnp.transpose(aux)[0:16, :].astype(jnp.int32)
    facts[...] = aux
    member = jnp.sum((aux[0:8, :] == me).astype(jnp.float32), axis=0, keepdims=True)
    step = 256
    total = jnp.zeros((1, count), jnp.float32)
    for start in range(0, rows, step):
        scores = lax.dot_general(
            unit_old[start : start + step, :], scaled[...], NT, preferred_element_type=jnp.float32
        )
        total = total + jnp.sum(weights(scores, width), axis=0, keepdims=True)
    piece = count // 16
    lane = lax.broadcasted_iota(jnp.int32, (16, count), 1)
    line = lax.broadcasted_iota(jnp.int32, (16, count), 0)
    apart = jnp.where((member > 0.0) & (lane >= line * piece) & (lane < (line + 1) * piece), total, 0.0)
    spot = lax.broadcasted_iota(jnp.int32, (count, 128), 0)
    block = sum((spot >= piece * step).astype(jnp.int32) for step in range(1, 16))
    together = jnp.where(spot - block * piece == lax.broadcasted_iota(jnp.int32, (count, 128), 1), 1.0, 0.0)
    share = jnp.dot(apart, together, precision=lax.Precision.HIGHEST, preferred_element_type=jnp.float32)
    for k, out in enumerate((share0, share1, share2, share3)):
        out[...] = jnp.concatenate([share[4 * g + k : 4 * g + k + 1, :] for g in range(4)], axis=0)


def update_kernel(after, scaled, facts, cent_ref, prior_ref, fresh_rows, fresh_counts):
    me, z, y, core = position()
    rows, width = cent_ref.shape
    count = scaled.shape[0]
    prior = column(prior_ref[...].astype(jnp.float32))
    target = jnp.where(facts[0:1, :] == me, facts[8:9, :] * 32 + facts[9:10, :], -1)
    step = 256
    for start in range(0, rows, step):
        old = cent_ref[start : start + step, :].astype(jnp.float32)
        hits = one_hot(target == lax.broadcasted_iota(jnp.int32, (step, count), 0) + start)
        sums = jnp.dot(hits, scaled[...], preferred_element_type=jnp.float32)
        gained = jnp.sum(hits.astype(jnp.float32), axis=1, keepdims=True)
        ahead = prior[start : start + step, :]
        updated = (ahead * old + sums) * (1.0 / (ahead + gained))
        fresh_rows[start : start + step, :] = updated.astype(jnp.bfloat16)
        gained_row = lax.dot_general(
            jnp.ones((8, count), jnp.bfloat16), hits, NT, preferred_element_type=jnp.float32
        )
        fresh_counts[0:1, start : start + step] = prior_ref[0:1, start : start + step] + gained_row[0:1, :].astype(jnp.int32)


def level_sums(two, packed, floors, w, per):
    block, width = two.shape[0] // per, two.shape[1]
    lines = []
    for j in range(per):
        rows = packed[w, j]
        floor = floors[w, j]
        scores = lax.dot_general(two[j * block : (j + 1) * block, :], rows, NT, preferred_element_type=jnp.float32)
        power = lax.dot_general(
            jnp.ones((8, width), jnp.bfloat16), rows * rows, NT, preferred_element_type=jnp.float32
        ) + lax.dot_general(
            jnp.ones((8, floor.shape[1]), jnp.bfloat16), floor * floor, NT, preferred_element_type=jnp.float32
        )
        power = jnp.where(power > 0.0, power, 1.0) * (1.0 / width)
        lines.append(jnp.sum(weights(scores * lax.rsqrt(power[0:1, :]), width), axis=0, keepdims=True))
    return jnp.concatenate(lines, axis=0)


def redo(cap, per, scaled, facts_in, me, refs, firsts, packed, floors):
    part = per * cap
    planes = packed.shape[0]
    count = planes * part
    width = scaled.shape[1]
    probe0 = facts_in[0:1, :]
    slots = facts_in[8:9, :] * 32 + facts_in[9:10, :]
    lane = lax.broadcasted_iota(jnp.int32, (count, 128), 1)
    for r, (ref, first) in enumerate(zip(refs, firsts)):
        facts = jnp.transpose(ref[ref.shape[0] - META :, first : first + count].astype(jnp.float32))
        hits = (facts[:, 0:1] * 32.0 + facts[:, 1:2]).astype(jnp.int32) == jnp.where(probe0 == (me ^ r), slots + 1, -1)
        gained = jnp.sum(jnp.where(hits, 1.0, 0.0), axis=1, keepdims=True)
        ahead = facts[:, 2:3]
        floor = (ahead + gained) * math.sqrt(1e-06 * width)
        floor = jnp.where(lane == 0, floor, 0.0).astype(jnp.bfloat16)
        added = jnp.dot(one_hot(hits), scaled[...], preferred_element_type=jnp.float32)
        whole = (ahead * ref[0:count, :].astype(jnp.float32) + added).astype(jnp.bfloat16)
        for w in range(planes):
            for j in range(per):
                start = w * part + j * cap
                packed[w, j, r * cap : (r + 1) * cap, :] = whole[start : start + cap, :]
                floors[w, j, r * cap : (r + 1) * cap, :] = floor[start : start + cap, :]


def early_kernel(
    cap, per, scaled, facts_in, units_any, cross_any, passed_any, any0, any1, any2, any3,
    sums, rows0, rows1, rows2, rows3, units, two_last, packed, floors, sems,
):
    me, z, y, core = position()
    end = (z == 0) | (z == 3)
    refs = (rows0, rows1, rows2, rows3)
    at_end = pltpu.make_async_copy(passed_any, two_last, sems.at[5])
    at_mid = pltpu.make_async_copy(cross_any, two_last, sems.at[5])
    copies = fetch(list(zip((any0, any1, any2, any3, units_any), (*refs, units))), sems)
    pl.when(end)(at_end.start)
    pl.when(jnp.logical_not(end))(at_mid.start)
    for copy in copies:
        copy.wait()
    pl.when(end)(at_end.wait)
    pl.when(jnp.logical_not(end))(at_mid.wait)
    redo(cap, per, scaled, facts_in, me, refs, (0, 0, 0, 0), packed, floors)
    third = unit_wide(two_last[...].astype(jnp.float32))
    for w, two in enumerate((units[0], units[1], third)):
        sums[8 * w : 8 * w + per, :] = level_sums(two, packed, floors, w, per)


def late_kernel(
    cap, per, scaled, facts_in, any0, any1, any2, any3, after, packed, floors, rows0, rows1, rows2, rows3, sems
):
    me, z, y, core = position()
    part = per * cap
    tail = pl.ds(3 * part, part + META)
    refs = (rows0, rows1, rows2, rows3)
    copies = fetch(list(zip((any0.at[tail], any1.at[tail], any2, any3), refs)), sems)
    for copy in copies:
        copy.wait()
    redo(cap, per, scaled, facts_in, me, refs, (3 * part, 3 * part, 0, 0), packed, floors)


def third_kernel(
    cap, per, early, floors, share0, share1, share2, share3, kept_any, last_any, far_any, inside, across, kept, two, sems
):
    me, z, y, core = position()
    end = (z == 0) | (z == 3)
    at_end = pltpu.make_async_copy(far_any, two, sems.at[1])
    at_mid = pltpu.make_async_copy(last_any, two, sems.at[1])
    pl.when(end)(at_end.start)
    pl.when(jnp.logical_not(end))(at_mid.start)
    copies = fetch([(kept_any, kept)], sems)
    pl.when(end)(at_end.wait)
    pl.when(jnp.logical_not(end))(at_mid.wait)
    two_unit = unit_wide(two[...].astype(jnp.float32))
    copies[0].wait()
    final = level_sums(two_unit, kept, floors, 0, per)
    lines = [early[8 * w : 8 * w + per, :] for w in range(3)] + [final]
    together = jnp.concatenate(lines + [jnp.zeros((16 - 4 * per, 4 * cap), jnp.float32)], axis=0)
    lane = lax.broadcasted_iota(jnp.int32, together.shape, 1)
    line = lax.broadcasted_iota(jnp.int32, together.shape, 0)
    share = share0[...] + share1[...] + share2[...] + share3[...]
    for r, g in enumerate((0, 2, 1, 3)):
        (inside, across)[r // 2][8 + r % 2 : 9 + r % 2, :] = share[g : g + 1, :]
    for r in range(4):
        out, start = (inside, across)[r // 2], 4 * (r % 2)
        spread = jnp.zeros_like(together)
        for s in range(4):
            turned = together if s == r else pltpu.roll(together, ((s - r) % 4) * cap, 1)
            spread = jnp.where((line % 4 == s) & (lane >= s * cap) & (lane < (s + 1) * cap), turned, spread)
        for t in range(4):
            out[start + t : start + t + 1, :] = jnp.sum(spread[4 * t : 4 * t + 4], axis=0, keepdims=True)


def last_kernel(cap, scale_one, scale_two, info, inside, across, beside, density, level_two):
    total = inside[8:9, :] + across[8:9, :] + beside[8:9, :]
    density[...] = jnp.log(total[:, 0 : density.shape[1]] / scale_one)
    values = jnp.concatenate([inside[0:4, :], beside[0:4, :], across[0:4, :], beside[4:8, :]], axis=0)
    rows = info.shape[1]
    chosen = jnp.where(info[2:3, :] == lax.broadcasted_iota(jnp.int32, (4 * cap, rows), 0), 1.0, 0.0)
    spread = jnp.dot(values, chosen, precision=lax.Precision.HIGHEST, preferred_element_type=jnp.float32)
    found = jnp.where(info[1:2, :] == lax.broadcasted_iota(jnp.int32, (16, rows), 0), spread, 0.0)
    level_two[...] = jnp.log(jnp.sum(found, axis=0, keepdims=True) / scale_two)


def call(kernel, outs, scratch=(), in_specs=None, **kw):
    def run(*args):
        specs = in_specs or [VMEM] * len(args)
        args = [pltpu.with_memory_space_constraint(a, pltpu.HBM) if spec is HBM else a for a, spec in zip(args, specs)]
        return pl.pallas_call(
            kernel, out_shape=outs, in_specs=specs, scratch_shapes=list(scratch), compiler_params=PARAMS, **kw
        )(*args)

    return run


def lasting(micros):
    return pl.CostEstimate(flops=0, transcendentals=0, bytes_accessed=int(micros * 3_690_000))


def in_order(*values, **kw):
    count = len(values)
    return call(
        order_kernel,
        tuple(jax.ShapeDtypeStruct(value.shape, value.dtype) for value in values),
        in_specs=[ANY] * count,
        out_specs=(ANY,) * count,
        input_output_aliases={i: i for i in range(count)},
        **kw,
    )(*values)


def line_body(embeddings, probes, assigned, prior_counts, centroids, candidates, centroids2):
    emb_rows, width = embeddings.shape
    probe_count = probes.shape[1]
    rows = centroids.shape[0]
    per = BLOCKS2_DEV
    cap = max(2, 3 * rows // (2 * per * 16))
    part = per * cap
    bf16, f32, i32 = jnp.bfloat16, jnp.float32, jnp.int32
    shape = jax.ShapeDtypeStruct

    def exchange(value, apart, sources=range(16)):
        return lax.ppermute(value, "shard", [(i, i ^ apart) for i in sources])

    def rows_of(planes):
        return shape((planes * part + META, width), bf16)

    def room(like):
        return pltpu.VMEM(like.shape, like.dtype)

    mids = range(4, 12)
    near_set = exchange(centroids2, 4)
    cross_set = exchange(centroids2, 12, mids)
    prior_row = prior_counts.reshape(1, rows)
    line = pltpu.VMEM((1, rows), i32)
    mine, early2, early3, info = call(
        functools.partial(pack_kernel, cap, per),
        (shape((emb_rows, width + 128), bf16), rows_of(3), rows_of(3), shape((8, rows), i32)),
        [
            line,
            pltpu.VMEM((emb_rows, width), bf16),
            pltpu.VMEM((probe_count, emb_rows), i32),
            pltpu.VMEM((1, emb_rows), i32),
            line,
            pltpu.VMEM((rows, width), bf16),
            pltpu.SemaphoreType.DMA((6,)),
        ],
        in_specs=[HBM] * 6,
    )(candidates.reshape(1, rows), embeddings, probes.T, assigned.reshape(1, emb_rows), prior_row, centroids)
    early2, early3 = exchange(early2, 2), exchange(early3, 3)
    rows0, rows1, late2, late3 = call(
        functools.partial(pack_more_kernel, part), (rows_of(4), rows_of(4), rows_of(1), rows_of(1))
    )(info, prior_row, centroids)
    mine = jnp.concatenate([mine, exchange(mine, 4)], axis=0)
    near_set, cross_set, mine, rows0 = in_order(near_set, cross_set, mine, rows0)
    across = exchange(mine, 12)
    passed = exchange(cross_set, 4, mids)
    last_set = exchange(near_set, 12, mids)
    mine = jnp.concatenate([mine, across], axis=0)
    mine, early2, early3, late2, late3, rows1 = in_order(mine, early2, early3, late2, late3, rows1)
    mine = jnp.concatenate([mine, exchange(mine, 2)], axis=0)
    late2, late3 = exchange(late2, 2), exchange(late3, 3)
    rows1 = exchange(rows1, 1)
    set_rows = per * BLOCK2
    block_set = pltpu.VMEM((set_rows, width), bf16)
    unit_old, units = call(
        prepare_kernel,
        (shape((rows, width), bf16), shape((2, set_rows, width), bf16)),
        [block_set, block_set, pltpu.SemaphoreType.DMA((2,))],
        in_specs=[VMEM, HBM, ANY],
    )(centroids, centroids2, near_set)
    passed, last_set, unit_old, units = in_order(passed, last_set, unit_old, units)
    far_set = exchange(last_set, 4, mids)
    other = exchange(mine, 1)
    gathered = pltpu.VMEM((8 * emb_rows, width + 128), bf16)
    scaled, facts, *share = call(
        share_kernel,
        (
            shape((16 * emb_rows, width), bf16),
            shape((16, 16 * emb_rows), i32),
            *[shape((4, 4 * cap), f32)] * 4,
        ),
        [gathered, gathered, pltpu.SemaphoreType.DMA((2,))],
        in_specs=[ANY, ANY, VMEM],
    )(mine, other, unit_old)
    early = call(
        functools.partial(early_kernel, cap, per),
        shape((24, 4 * cap), f32),
        [room(rows_of(4))] * 2
        + [room(rows_of(3))] * 2
        + [
            pltpu.VMEM((2, set_rows, width), bf16),
            block_set,
            pltpu.VMEM((3, per, 4 * cap, width), bf16),
            pltpu.VMEM((3, per, 4 * cap, 128), bf16),
            pltpu.SemaphoreType.DMA((6,)),
        ],
        in_specs=[VMEM, VMEM] + [ANY] * 7,
    )(scaled, facts, units, cross_set, passed, rows0, rows1, early2, early3)
    kept = shape((1, per, 4 * cap, width), bf16)
    kept_rows, floors = call(
        functools.partial(late_kernel, cap, per),
        (kept, shape((1, per, 4 * cap, 128), bf16)),
        [room(rows_of(1))] * 4 + [pltpu.SemaphoreType.DMA((4,))],
        in_specs=[VMEM] * 2 + [ANY] * 5,
    )(scaled, facts, rows0, rows1, late2, late3, early)
    *share, kept_rows = in_order(*share, kept_rows)
    share = [share[0]] + [exchange(value, apart) for value, apart in zip(share[1:], (4, 12, 8))]
    tile = shape((16, 4 * cap), f32)
    inside, across = call(
        functools.partial(third_kernel, cap, per),
        (tile,) * 2,
        [room(kept), block_set, pltpu.SemaphoreType.DMA((2,))],
        in_specs=[VMEM] * 6 + [ANY] * 3,
    )(early, floors, *share, kept_rows, last_set, far_set)
    new_centroids, counts = call(
        update_kernel, (shape((rows, width), bf16), shape((1, rows), i32)), in_specs=[ANY] + [VMEM] * 4
    )(inside, scaled, facts, centroids, prior_row)
    across = exchange(across, 2)
    beside = jnp.concatenate([inside[4:8], across[4:8], inside[9:10] + across[9:10]], axis=0)
    beside, counts = in_order(beside, counts)
    beside = exchange(beside, 1)
    density, level_two = call(
        functools.partial(last_kernel, cap, probe_count * BLOCK, BLOCK2), (shape((1, emb_rows), f32), shape((1, rows), f32))
    )(info, inside, across, beside)
    return (density.reshape(-1), new_centroids, counts.reshape(-1), level_two.reshape(-1))


def solution(mesh):
    placed = (
        P(("groups", "shard"), None),
        P(("groups", "shard"), None),
        P(("groups", "shard")),
        P(("groups", "shard")),
        P(("groups", "shard"), None),
        P(("groups", "shard"), None),
        P(("groups", "shard"), None),
    )
    body = line_body if mesh.shape["shard"] == 16 else general_body
    return jax.shard_map(
        body,
        mesh=mesh,
        in_specs=placed,
        out_specs=(
            P(("groups", "shard")),
            P(("groups", "shard"), None),
            P(("groups", "shard")),
            P(("groups", "shard")),
        ),
        check_vma=False,
    )
```

```python
import functools
import math

import jax
import jax.numpy as jnp
from jax import lax
from jax.experimental import pallas as pl
from jax.experimental.pallas import tpu as pltpu
from jax.sharding import PartitionSpec as P

BLOCK = 1024
BLOCKS_DEV = 1
BLOCK2 = 128
BLOCKS2_DEV = 3


def unit_rows(values):
    wide = values.astype(jnp.float32)
    power = jnp.mean(wide * wide, axis=-1, keepdims=True) + 1e-06
    return (wide * lax.rsqrt(power)).astype(jnp.bfloat16)


def kernel_sums(rows, unit):
    scores = lax.dot_general(
        rows, unit, (((1,), (1,)), ((), ())), preferred_element_type=jnp.float32
    )
    return jnp.sum(jnp.exp((scores / rows.shape[1] - 1.0) / 0.1), axis=1)


def block_update(rows, slots, width):
    matches = slots[:, None] == jnp.arange(width, dtype=jnp.int32)[None, :]
    sums = lax.dot_general(
        matches.astype(jnp.bfloat16),
        rows,
        (((0,), (0,)), ((), ())),
        preferred_element_type=jnp.float32,
    )
    counts = jnp.sum(matches.astype(jnp.int32), axis=0)
    return (sums, counts)


def slot_ranks(targets, buckets):
    matches = (targets[:, None] == jnp.arange(buckets, dtype=jnp.int32)[None, :]).astype(jnp.int32)
    return jnp.sum(jnp.cumsum(matches, axis=0) * matches, axis=1) - 1


def general_body(embeddings, probes, assigned, prior_counts, centroids, candidates, centroids2):
    devices = lax.axis_size("shard")
    emb_rows, width = embeddings.shape
    probe_count = probes.shape[1]
    capacity = max(2, 2 * emb_rows * probe_count // (BLOCKS_DEV * devices))
    scaled = unit_rows(embeddings)
    units_old = unit_rows(centroids).reshape(BLOCKS_DEV, BLOCK, width)
    total = emb_rows * probe_count
    buckets = BLOCKS_DEV * devices
    flat = probes.reshape(-1)
    place = flat * capacity + slot_ranks(flat, buckets)
    leading = jnp.arange(total, dtype=jnp.int32) % probe_count == 0
    repeated = jnp.repeat(scaled, probe_count, axis=0)
    slot_values = jnp.where(leading, jnp.repeat(assigned, probe_count), -1)
    send_rows = jnp.zeros((buckets * capacity, width), jnp.bfloat16).at[place].set(repeated)
    send_slots = jnp.full((buckets * capacity,), -1, jnp.int32).at[place].set(slot_values)
    got_rows, got_slots = (
        lax.all_to_all(
            send_rows.reshape(devices, BLOCKS_DEV * capacity, width),
            "shard",
            split_axis=0,
            concat_axis=0,
            tiled=True,
        ),
        lax.all_to_all(
            send_slots.reshape(devices, BLOCKS_DEV * capacity),
            "shard",
            split_axis=0,
            concat_axis=0,
            tiled=True,
        ),
    )
    got_rows = got_rows.reshape(devices, BLOCKS_DEV, capacity, width)
    got_slots = got_slots.reshape(devices, BLOCKS_DEV, capacity)
    local = 0
    picked = got_rows[:, local].reshape(devices * capacity, width)
    slots = got_slots[:, local].reshape(-1)
    weights = [kernel_sums(picked, units_old[local]).reshape(devices, capacity)]
    more_sums, more_counts = block_update(picked, slots, BLOCK)
    sum_list = [more_sums]
    count_list = [more_counts]
    sums = jnp.stack(sum_list)
    counts = jnp.stack(count_list)
    returned = lax.all_to_all(
        jnp.stack(weights, axis=1).reshape(devices, BLOCKS_DEV * capacity),
        "shard",
        split_axis=0,
        concat_axis=0,
        tiled=True,
    )
    totals = jnp.sum(returned.reshape(-1)[place].reshape(emb_rows, probe_count), axis=1)
    density = jnp.log(totals / (probe_count * BLOCK))
    prior = prior_counts.reshape(BLOCKS_DEV, BLOCK)
    fresh = prior + counts
    updated = (
        prior.astype(jnp.float32)[:, :, None]
        * centroids.reshape(BLOCKS_DEV, BLOCK, width).astype(jnp.float32)
        + sums
    ) / fresh.astype(jnp.float32)[:, :, None]
    new_centroids = updated.astype(jnp.bfloat16).reshape(BLOCKS_DEV * BLOCK, width)
    units_new = unit_rows(updated).reshape(BLOCKS_DEV * BLOCK, width)
    rows_two = units_new.shape[0]
    second_capacity = max(2, 3 * rows_two // (2 * BLOCKS2_DEV * devices))
    buckets_two = BLOCKS2_DEV * devices
    chosen = candidates[:, 0]
    place_two = chosen * second_capacity + slot_ranks(chosen, buckets_two)
    send_two = (
        jnp.zeros((buckets_two * second_capacity, width), jnp.bfloat16).at[place_two].set(units_new)
    )
    send_two = send_two.reshape(devices, BLOCKS2_DEV, second_capacity, width)
    units_two = unit_rows(centroids2).reshape(BLOCKS2_DEV, BLOCK2, width)
    arrived = lax.all_to_all(send_two, "shard", split_axis=0, concat_axis=0, tiled=True)
    items = arrived.shape[2]
    weights_two = [
        kernel_sums(arrived[:, local].reshape(-1, width), units_two[local]).reshape(
            arrived.shape[0], items
        )
        for local in range(BLOCKS2_DEV)
    ]
    returned_two = lax.all_to_all(
        jnp.stack(weights_two, axis=1), "shard", split_axis=0, concat_axis=0, tiled=True
    )
    level_two = jnp.log(returned_two.reshape(-1)[place_two] / BLOCK2)
    return (density, new_centroids, fresh.reshape(-1), level_two)


NT = (((1,), (1,)), ((), ()))
PARAMS = pltpu.CompilerParams(vmem_limit_bytes=48 * 1024 * 1024)
META = 16
SHARE = 1
LATE = 5
STEP = 12
HBM = pl.BlockSpec(memory_space=pltpu.HBM)
ANY = pl.BlockSpec(memory_space=pl.ANY)
VMEM = pl.BlockSpec(memory_space=pltpu.VMEM)


def position():
    me = lax.axis_index("shard")
    return me, me // 4, (me // 2) % 2, me % 2


def unit_wide(wide):
    power = jnp.mean(wide * wide, axis=-1, keepdims=True) + 1e-06
    return (wide * lax.rsqrt(power)).astype(jnp.bfloat16)


def weights(scores, width):
    return jnp.exp(scores * (10.0 / width) - 10.0)


def one_hot(hits):
    return jnp.where(hits, 1.0, 0.0).astype(jnp.bfloat16)


def column(row):
    return jnp.transpose(jnp.broadcast_to(row, (8, row.shape[1])))[:, 0:1]


def fetch(pairs, sems):
    copies = [pltpu.make_async_copy(src, dst, sems.at[i]) for i, (src, dst) in enumerate(pairs)]
    for copy in copies:
        copy.start()
    return copies


def pick_rows(slot, first, count):
    return one_hot(slot == lax.broadcasted_iota(jnp.int32, (count, slot.shape[1]), 0) + first)


def pack(slot, prior, cent, first, out):
    count = out.shape[0] - META
    rows = slot.shape[1]
    ident = lax.broadcasted_iota(jnp.int32, (1, rows), 1) + 1
    line = lax.broadcasted_iota(jnp.int32, (META, rows), 0)
    facts = jnp.where(line == 0, ident >> 5, jnp.where(line == 1, ident & 31, jnp.where(line == 2, prior, 0)))
    facts = facts.astype(jnp.float32).astype(jnp.bfloat16)
    pick = pick_rows(slot, first, count)
    out[0:count, :] = jnp.dot(pick, cent, preferred_element_type=jnp.float32).astype(jnp.bfloat16)
    out[count:, :] = jnp.zeros((META, out.shape[1]), jnp.bfloat16)
    out[count:, 0:count] = lax.dot_general(facts, pick, NT, preferred_element_type=jnp.float32).astype(jnp.bfloat16)


def pack_kernel(
    cap, per, cand_any, emb_any, probes_any, assigned_any, prior_any, cent_any, mine, rows2, rows3, info,
    cand_ref, emb_ref, probes_ref, assigned_ref, prior_ref, cent_ref, sems,
):
    copies = fetch(
        (
            (cand_any, cand_ref),
            (emb_any, emb_ref),
            (probes_any, probes_ref),
            (assigned_any, assigned_ref),
            (prior_any, prior_ref),
            (cent_any, cent_ref),
        ),
        sems,
    )
    me, z, y, core = position()
    rows = cand_ref.shape[1]
    buckets = 16 * per
    before = lax.broadcasted_iota(jnp.int32, (rows, rows), 0) <= lax.broadcasted_iota(jnp.int32, (rows, rows), 1)
    before = one_hot(before)
    copies[0].wait()
    cand = cand_ref[...]
    dev = sum((cand >= per * step).astype(jnp.int32) for step in range(1, 16))
    near = dev >> 2
    plane = jnp.where(z >= 2, 3 - near, near)
    rel = (((dev >> 1) & 1) ^ y) * 2 + ((dev & 1) ^ core)
    named = cand == lax.broadcasted_iota(jnp.int32, (buckets, rows), 0)
    counted = jnp.dot(one_hot(named), before, preferred_element_type=jnp.float32)
    rank = jnp.sum(jnp.where(named, counted, 0.0), axis=0, keepdims=True).astype(jnp.int32) - 1
    kind = plane * per + cand - dev * per
    slot = (rel * 4 * per + kind) * cap + rank
    info[0:1, :] = slot
    info[1:2, :] = rel * 4 + (kind >> 2)
    info[2:3, :] = (kind & 3) * cap + rank
    for copy in copies[1:5]:
        copy.wait()
    count, width = emb_ref.shape
    probe_count = probes_ref.shape[0]
    slots = assigned_ref[...]
    facts = jnp.concatenate([probes_ref[...], slots >> 5, slots & 31], axis=0).astype(jnp.float32)
    facts = jnp.concatenate([facts, jnp.zeros((128 - probe_count - 2, count), jnp.float32)], axis=0)
    same = lax.broadcasted_iota(jnp.int32, (count, count), 0) == lax.broadcasted_iota(jnp.int32, (count, count), 1)
    mine[:, 0:width] = emb_ref[...]
    mine[:, width:] = lax.dot_general(
        one_hot(same), facts.astype(jnp.bfloat16), NT, preferred_element_type=jnp.float32
    ).astype(jnp.bfloat16)
    copies[5].wait()
    pack(slot, prior_ref[...], cent_ref[...], 2 * 4 * per * cap, rows2)
    pack(slot, prior_ref[...], cent_ref[...], 3 * 4 * per * cap, rows3)


def pack_more_kernel(part, info, prior_ref, cent_ref, rows0, rows1, late2, late3):
    for first, out in ((0, rows0), (4 * part, rows1), (11 * part, late2), (15 * part, late3)):
        pack(info[0:1, :], prior_ref[...], cent_ref[...], first, out)


def order_kernel(*refs):
    pass


def prepare_kernel(cent_ref, own_any, near_any, unit_old, units, own, near, sems):
    copies = fetch(((own_any, own), (near_any, near)), sems)
    step = 256
    for start in range(0, cent_ref.shape[0], step):
        unit_old[start : start + step, :] = unit_wide(cent_ref[start : start + step, :].astype(jnp.float32))
    me, z, y, core = position()
    first = jnp.where((z == 0) | (z == 3), 0, 1)
    copies[0].wait()
    units[first] = unit_wide(own[...].astype(jnp.float32))
    copies[1].wait()
    units[1 - first] = unit_wide(near[...].astype(jnp.float32))


def share_kernel(mine_any, other_any, unit_old, scaled, facts, share_low, share_high, mine_ref, other_ref, sems):
    copies = fetch(((mine_any, mine_ref), (other_any, other_ref)), sems)
    me, z, y, core = position()
    half = mine_ref.shape[0]
    count = 2 * half
    rows, width = unit_old.shape
    copies[0].wait()
    scaled[0:half, :] = unit_wide(mine_ref[:, 0:width].astype(jnp.float32))
    copies[1].wait()
    scaled[half:count, :] = unit_wide(other_ref[:, 0:width].astype(jnp.float32))
    aux = jnp.concatenate([mine_ref[:, width:], other_ref[:, width:]], axis=0).astype(jnp.float32)
    aux = jnp.transpose(aux)[0:16, :].astype(jnp.int32)
    facts[...] = aux
    member = jnp.sum((aux[0:8, :] == me).astype(jnp.float32), axis=0, keepdims=True)
    step = 256
    total = jnp.zeros((1, count), jnp.float32)
    for start in range(0, rows, step):
        scores = lax.dot_general(
            unit_old[start : start + step, :], scaled[...], NT, preferred_element_type=jnp.float32
        )
        total = total + jnp.sum(weights(scores, width), axis=0, keepdims=True)
    piece = count // 16
    lane = lax.broadcasted_iota(jnp.int32, (16, count), 1)
    line = lax.broadcasted_iota(jnp.int32, (16, count), 0)
    apart = jnp.where((member > 0.0) & (lane >= line * piece) & (lane < (line + 1) * piece), total, 0.0)
    spot = lax.broadcasted_iota(jnp.int32, (count, 128), 0)
    block = sum((spot >= piece * step).astype(jnp.int32) for step in range(1, 16))
    together = jnp.where(spot - block * piece == lax.broadcasted_iota(jnp.int32, (count, 128), 1), 1.0, 0.0)
    share = jnp.dot(apart, together, precision=lax.Precision.HIGHEST, preferred_element_type=jnp.float32)
    share_low[...] = share[0:8, :]
    share_high[...] = share[8:16, :]


def update_kernel(after, scaled, facts, cent_ref, prior_ref, fresh_rows, fresh_counts):
    me, z, y, core = position()
    rows, width = cent_ref.shape
    count = scaled.shape[0]
    prior = column(prior_ref[...].astype(jnp.float32))
    target = jnp.where(facts[0:1, :] == me, facts[8:9, :] * 32 + facts[9:10, :], -1)
    step = 256
    for start in range(0, rows, step):
        old = cent_ref[start : start + step, :].astype(jnp.float32)
        hits = one_hot(target == lax.broadcasted_iota(jnp.int32, (step, count), 0) + start)
        sums = jnp.dot(hits, scaled[...], preferred_element_type=jnp.float32)
        gained = jnp.sum(hits.astype(jnp.float32), axis=1, keepdims=True)
        ahead = prior[start : start + step, :]
        updated = (ahead * old + sums) * (1.0 / (ahead + gained))
        fresh_rows[start : start + step, :] = updated.astype(jnp.bfloat16)
        gained_row = lax.dot_general(
            jnp.ones((8, count), jnp.bfloat16), hits, NT, preferred_element_type=jnp.float32
        )
        fresh_counts[0:1, start : start + step] = prior_ref[0:1, start : start + step] + gained_row[0:1, :].astype(jnp.int32)


def level_sums(two, packed, floors, w, per):
    block, width = two.shape[0] // per, two.shape[1]
    lines = []
    for j in range(per):
        rows = packed[w, j]
        floor = floors[w, j]
        scores = lax.dot_general(two[j * block : (j + 1) * block, :], rows, NT, preferred_element_type=jnp.float32)
        power = lax.dot_general(
            jnp.ones((8, width), jnp.bfloat16), rows * rows, NT, preferred_element_type=jnp.float32
        ) + lax.dot_general(
            jnp.ones((8, floor.shape[1]), jnp.bfloat16), floor * floor, NT, preferred_element_type=jnp.float32
        )
        power = jnp.where(power > 0.0, power, 1.0) * (1.0 / width)
        lines.append(jnp.sum(weights(scores * lax.rsqrt(power[0:1, :]), width), axis=0, keepdims=True))
    return jnp.concatenate(lines, axis=0)


def redo(cap, per, scaled, facts_in, me, refs, firsts, packed, floors):
    part = per * cap
    planes = packed.shape[0]
    count = planes * part
    width = scaled.shape[1]
    probe0 = facts_in[0:1, :]
    slots = facts_in[8:9, :] * 32 + facts_in[9:10, :]
    lane = lax.broadcasted_iota(jnp.int32, (count, 128), 1)
    for r, (ref, first) in enumerate(zip(refs, firsts)):
        facts = jnp.transpose(ref[ref.shape[0] - META :, first : first + count].astype(jnp.float32))
        hits = (facts[:, 0:1] * 32.0 + facts[:, 1:2]).astype(jnp.int32) == jnp.where(probe0 == (me ^ r), slots + 1, -1)
        gained = jnp.sum(jnp.where(hits, 1.0, 0.0), axis=1, keepdims=True)
        ahead = facts[:, 2:3]
        floor = (ahead + gained) * math.sqrt(1e-06 * width)
        floor = jnp.where(lane == 0, floor, 0.0).astype(jnp.bfloat16)
        added = jnp.dot(one_hot(hits), scaled[...], preferred_element_type=jnp.float32)
        whole = (ahead * ref[0:count, :].astype(jnp.float32) + added).astype(jnp.bfloat16)
        for w in range(planes):
            for j in range(per):
                start = w * part + j * cap
                packed[w, j, r * cap : (r + 1) * cap, :] = whole[start : start + cap, :]
                floors[w, j, r * cap : (r + 1) * cap, :] = floor[start : start + cap, :]


def early_kernel(
    cap, per, scaled, facts_in, units_any, cross_any, passed_any, any0, any1, any2, any3,
    sums, rows0, rows1, rows2, rows3, units, two_last, packed, floors, sems,
):
    me, z, y, core = position()
    end = (z == 0) | (z == 3)
    refs = (rows0, rows1, rows2, rows3)
    at_end = pltpu.make_async_copy(passed_any, two_last, sems.at[5])
    at_mid = pltpu.make_async_copy(cross_any, two_last, sems.at[5])
    copies = fetch(list(zip((any0, any1, any2, any3, units_any), (*refs, units))), sems)
    pl.when(end)(at_end.start)
    pl.when(jnp.logical_not(end))(at_mid.start)
    for copy in copies:
        copy.wait()
    pl.when(end)(at_end.wait)
    pl.when(jnp.logical_not(end))(at_mid.wait)
    redo(cap, per, scaled, facts_in, me, refs, (0, 0, 0, 0), packed, floors)
    third = unit_wide(two_last[...].astype(jnp.float32))
    for w, two in enumerate((units[0], units[1], third)):
        sums[8 * w : 8 * w + per, :] = level_sums(two, packed, floors, w, per)


def late_kernel(
    cap, per, scaled, facts_in, any0, any1, any2, any3, after, packed, floors, rows0, rows1, rows2, rows3, sems
):
    me, z, y, core = position()
    part = per * cap
    tail = pl.ds(3 * part, part + META)
    refs = (rows0, rows1, rows2, rows3)
    copies = fetch(list(zip((any0.at[tail], any1.at[tail], any2, any3), refs)), sems)
    for copy in copies:
        copy.wait()
    redo(cap, per, scaled, facts_in, me, refs, (3 * part, 3 * part, 0, 0), packed, floors)


def third_kernel(cap, per, early, floors, kept_any, last_any, far_any, inside, across, kept, two, sems):
    me, z, y, core = position()
    end = (z == 0) | (z == 3)
    at_end = pltpu.make_async_copy(far_any, two, sems.at[1])
    at_mid = pltpu.make_async_copy(last_any, two, sems.at[1])
    pl.when(end)(at_end.start)
    pl.when(jnp.logical_not(end))(at_mid.start)
    copies = fetch([(kept_any, kept)], sems)
    pl.when(end)(at_end.wait)
    pl.when(jnp.logical_not(end))(at_mid.wait)
    two_unit = unit_wide(two[...].astype(jnp.float32))
    copies[0].wait()
    final = level_sums(two_unit, kept, floors, 0, per)
    lines = [early[8 * w : 8 * w + per, :] for w in range(3)] + [final]
    together = jnp.concatenate(lines + [jnp.zeros((16 - 4 * per, 4 * cap), jnp.float32)], axis=0)
    lane = lax.broadcasted_iota(jnp.int32, together.shape, 1)
    line = lax.broadcasted_iota(jnp.int32, together.shape, 0)
    for r in range(4):
        out, start = (inside, across)[r // 2], 4 * (r % 2)
        spread = jnp.zeros_like(together)
        for s in range(4):
            turned = together if s == r else pltpu.roll(together, ((s - r) % 4) * cap, 1)
            spread = jnp.where((line % 4 == s) & (lane >= s * cap) & (lane < (s + 1) * cap), turned, spread)
        for t in range(4):
            out[start + t : start + t + 1, :] = jnp.sum(spread[4 * t : 4 * t + 4], axis=0, keepdims=True)


def last_kernel(cap, scale_one, scale_two, info, inside, across, beside, share, density, level_two):
    total = share[...]
    density[...] = jnp.log(total[:, 0 : density.shape[1]] / scale_one)
    values = jnp.concatenate([inside[0:4, :], beside[0:4, :], across[0:4, :], beside[4:8, :]], axis=0)
    rows = info.shape[1]
    chosen = jnp.where(info[2:3, :] == lax.broadcasted_iota(jnp.int32, (4 * cap, rows), 0), 1.0, 0.0)
    spread = jnp.dot(values, chosen, precision=lax.Precision.HIGHEST, preferred_element_type=jnp.float32)
    found = jnp.where(info[1:2, :] == lax.broadcasted_iota(jnp.int32, (16, rows), 0), spread, 0.0)
    level_two[...] = jnp.log(jnp.sum(found, axis=0, keepdims=True) / scale_two)


def call(kernel, outs, scratch=(), in_specs=None, **kw):
    def run(*args):
        specs = in_specs or [VMEM] * len(args)
        args = [pltpu.with_memory_space_constraint(a, pltpu.HBM) if spec is HBM else a for a, spec in zip(args, specs)]
        return pl.pallas_call(
            kernel, out_shape=outs, in_specs=specs, scratch_shapes=list(scratch), compiler_params=PARAMS, **kw
        )(*args)

    return run


def lasting(micros):
    return pl.CostEstimate(flops=0, transcendentals=0, bytes_accessed=int(micros * 3_690_000))


def in_order(*values, **kw):
    count = len(values)
    return call(
        order_kernel,
        tuple(jax.ShapeDtypeStruct(value.shape, value.dtype) for value in values),
        in_specs=[ANY] * count,
        out_specs=(ANY,) * count,
        input_output_aliases={i: i for i in range(count)},
        **kw,
    )(*values)


def line_body(embeddings, probes, assigned, prior_counts, centroids, candidates, centroids2):
    emb_rows, width = embeddings.shape
    probe_count = probes.shape[1]
    rows = centroids.shape[0]
    per = BLOCKS2_DEV
    cap = max(2, 3 * rows // (2 * per * 16))
    part = per * cap
    bf16, f32, i32 = jnp.bfloat16, jnp.float32, jnp.int32
    shape = jax.ShapeDtypeStruct

    def exchange(value, apart, sources=range(16)):
        return lax.ppermute(value, "shard", [(i, i ^ apart) for i in sources])

    def rows_of(planes):
        return shape((planes * part + META, width), bf16)

    def room(like):
        return pltpu.VMEM(like.shape, like.dtype)

    mids = range(4, 12)
    near_set = exchange(centroids2, 4)
    cross_set = exchange(centroids2, 12, mids)
    prior_row = prior_counts.reshape(1, rows)
    line = pltpu.VMEM((1, rows), i32)
    mine, early2, early3, info = call(
        functools.partial(pack_kernel, cap, per),
        (shape((emb_rows, width + 128), bf16), rows_of(3), rows_of(3), shape((8, rows), i32)),
        [
            line,
            pltpu.VMEM((emb_rows, width), bf16),
            pltpu.VMEM((probe_count, emb_rows), i32),
            pltpu.VMEM((1, emb_rows), i32),
            line,
            pltpu.VMEM((rows, width), bf16),
            pltpu.SemaphoreType.DMA((6,)),
        ],
        in_specs=[HBM] * 6,
    )(candidates.reshape(1, rows), embeddings, probes.T, assigned.reshape(1, emb_rows), prior_row, centroids)
    early2, early3 = exchange(early2, 2), exchange(early3, 3)
    rows0, rows1, late2, late3 = call(
        functools.partial(pack_more_kernel, part), (rows_of(4), rows_of(4), rows_of(1), rows_of(1))
    )(info, prior_row, centroids)
    mine = jnp.concatenate([mine, exchange(mine, 4)], axis=0)
    near_set, cross_set, mine, rows0 = in_order(near_set, cross_set, mine, rows0)
    across = exchange(mine, 12)
    passed = exchange(cross_set, 4, mids)
    last_set = exchange(near_set, 12, mids)
    mine = jnp.concatenate([mine, across], axis=0)
    mine, early2, early3, late2, late3, rows1 = in_order(mine, early2, early3, late2, late3, rows1)
    mine = jnp.concatenate([mine, exchange(mine, 2)], axis=0)
    late2, late3 = exchange(late2, 2), exchange(late3, 3)
    rows1 = exchange(rows1, 1)
    set_rows = per * BLOCK2
    block_set = pltpu.VMEM((set_rows, width), bf16)
    unit_old, units = call(
        prepare_kernel,
        (shape((rows, width), bf16), shape((2, set_rows, width), bf16)),
        [block_set, block_set, pltpu.SemaphoreType.DMA((2,))],
        in_specs=[VMEM, HBM, ANY],
    )(centroids, centroids2, near_set)
    passed, last_set, mine, unit_old, units = in_order(passed, last_set, mine, unit_old, units)
    far_set = exchange(last_set, 4, mids)
    other = exchange(mine, 1)
    gathered = pltpu.VMEM((8 * emb_rows, width + 128), bf16)
    scaled, facts, share, share_high = call(
        share_kernel,
        (
            shape((16 * emb_rows, width), bf16),
            shape((16, 16 * emb_rows), i32),
            shape((8, 4 * cap), f32),
            shape((8, 4 * cap), f32),
        ),
        [gathered, gathered, pltpu.SemaphoreType.DMA((2,))],
        in_specs=[ANY, ANY, VMEM],
    )(mine, other, unit_old)
    share = share + exchange(share_high, 1)
    share = share[0:4] + exchange(share[4:8], 2)
    early = call(
        functools.partial(early_kernel, cap, per),
        shape((24, 4 * cap), f32),
        [room(rows_of(4))] * 2
        + [room(rows_of(3))] * 2
        + [
            pltpu.VMEM((2, set_rows, width), bf16),
            block_set,
            pltpu.VMEM((3, per, 4 * cap, width), bf16),
            pltpu.VMEM((3, per, 4 * cap, 128), bf16),
            pltpu.SemaphoreType.DMA((6,)),
        ],
        in_specs=[VMEM, VMEM] + [ANY] * 7,
    )(scaled, facts, units, cross_set, passed, rows0, rows1, early2, early3)
    kept = shape((1, per, 4 * cap, width), bf16)
    kept_rows, floors = call(
        functools.partial(late_kernel, cap, per),
        (kept, shape((1, per, 4 * cap, 128), bf16)),
        [room(rows_of(1))] * 4 + [pltpu.SemaphoreType.DMA((4,))],
        in_specs=[VMEM] * 2 + [ANY] * 5,
    )(scaled, facts, rows0, rows1, late2, late3, early)
    share, kept_rows = in_order(share, kept_rows)
    share = share[0:2] + exchange(share[2:4], 12)
    share = share[0:1] + exchange(share[1:2], 4)
    tile = shape((8, 4 * cap), f32)
    inside, across = call(
        functools.partial(third_kernel, cap, per),
        (tile,) * 2,
        [room(kept), block_set, pltpu.SemaphoreType.DMA((2,))],
        in_specs=[VMEM, VMEM] + [ANY] * 3,
    )(early, floors, kept_rows, last_set, far_set)
    new_centroids, counts = call(
        update_kernel, (shape((rows, width), bf16), shape((1, rows), i32)), in_specs=[ANY] + [VMEM] * 4
    )(inside, scaled, facts, centroids, prior_row)
    across = exchange(across, 2)
    beside = jnp.concatenate([inside[4:8], across[4:8]], axis=0)
    beside, counts = in_order(beside, counts)
    beside = exchange(beside, 1)
    density, level_two = call(
        functools.partial(last_kernel, cap, probe_count * BLOCK, BLOCK2), (shape((1, emb_rows), f32), shape((1, rows), f32))
    )(info, inside, across, beside, share)
    return (density.reshape(-1), new_centroids, counts.reshape(-1), level_two.reshape(-1))


def solution(mesh):
    placed = (
        P(("groups", "shard"), None),
        P(("groups", "shard"), None),
        P(("groups", "shard")),
        P(("groups", "shard")),
        P(("groups", "shard"), None),
        P(("groups", "shard"), None),
        P(("groups", "shard"), None),
    )
    body = line_body if mesh.shape["shard"] == 16 else general_body
    return jax.shard_map(
        body,
        mesh=mesh,
        in_specs=placed,
        out_specs=(
            P(("groups", "shard")),
            P(("groups", "shard"), None),
            P(("groups", "shard")),
            P(("groups", "shard")),
        ),
        check_vma=False,
    )
```

```python
import functools
import math

import jax
import jax.numpy as jnp
from jax import lax
from jax.experimental import pallas as pl
from jax.experimental.pallas import tpu as pltpu
from jax.sharding import PartitionSpec as P

BLOCK = 1024
BLOCKS_DEV = 1
BLOCK2 = 128
BLOCKS2_DEV = 3


def unit_rows(values):
    wide = values.astype(jnp.float32)
    power = jnp.mean(wide * wide, axis=-1, keepdims=True) + 1e-06
    return (wide * lax.rsqrt(power)).astype(jnp.bfloat16)


def kernel_sums(rows, unit):
    scores = lax.dot_general(
        rows, unit, (((1,), (1,)), ((), ())), preferred_element_type=jnp.float32
    )
    return jnp.sum(jnp.exp((scores / rows.shape[1] - 1.0) / 0.1), axis=1)


def block_update(rows, slots, width):
    matches = slots[:, None] == jnp.arange(width, dtype=jnp.int32)[None, :]
    sums = lax.dot_general(
        matches.astype(jnp.bfloat16),
        rows,
        (((0,), (0,)), ((), ())),
        preferred_element_type=jnp.float32,
    )
    counts = jnp.sum(matches.astype(jnp.int32), axis=0)
    return (sums, counts)


def slot_ranks(targets, buckets):
    matches = (targets[:, None] == jnp.arange(buckets, dtype=jnp.int32)[None, :]).astype(jnp.int32)
    return jnp.sum(jnp.cumsum(matches, axis=0) * matches, axis=1) - 1


def general_body(embeddings, probes, assigned, prior_counts, centroids, candidates, centroids2):
    devices = lax.axis_size("shard")
    emb_rows, width = embeddings.shape
    probe_count = probes.shape[1]
    capacity = max(2, 2 * emb_rows * probe_count // (BLOCKS_DEV * devices))
    scaled = unit_rows(embeddings)
    units_old = unit_rows(centroids).reshape(BLOCKS_DEV, BLOCK, width)
    total = emb_rows * probe_count
    buckets = BLOCKS_DEV * devices
    flat = probes.reshape(-1)
    place = flat * capacity + slot_ranks(flat, buckets)
    leading = jnp.arange(total, dtype=jnp.int32) % probe_count == 0
    repeated = jnp.repeat(scaled, probe_count, axis=0)
    slot_values = jnp.where(leading, jnp.repeat(assigned, probe_count), -1)
    send_rows = jnp.zeros((buckets * capacity, width), jnp.bfloat16).at[place].set(repeated)
    send_slots = jnp.full((buckets * capacity,), -1, jnp.int32).at[place].set(slot_values)
    got_rows, got_slots = (
        lax.all_to_all(
            send_rows.reshape(devices, BLOCKS_DEV * capacity, width),
            "shard",
            split_axis=0,
            concat_axis=0,
            tiled=True,
        ),
        lax.all_to_all(
            send_slots.reshape(devices, BLOCKS_DEV * capacity),
            "shard",
            split_axis=0,
            concat_axis=0,
            tiled=True,
        ),
    )
    got_rows = got_rows.reshape(devices, BLOCKS_DEV, capacity, width)
    got_slots = got_slots.reshape(devices, BLOCKS_DEV, capacity)
    local = 0
    picked = got_rows[:, local].reshape(devices * capacity, width)
    slots = got_slots[:, local].reshape(-1)
    weights = [kernel_sums(picked, units_old[local]).reshape(devices, capacity)]
    more_sums, more_counts = block_update(picked, slots, BLOCK)
    sum_list = [more_sums]
    count_list = [more_counts]
    sums = jnp.stack(sum_list)
    counts = jnp.stack(count_list)
    returned = lax.all_to_all(
        jnp.stack(weights, axis=1).reshape(devices, BLOCKS_DEV * capacity),
        "shard",
        split_axis=0,
        concat_axis=0,
        tiled=True,
    )
    totals = jnp.sum(returned.reshape(-1)[place].reshape(emb_rows, probe_count), axis=1)
    density = jnp.log(totals / (probe_count * BLOCK))
    prior = prior_counts.reshape(BLOCKS_DEV, BLOCK)
    fresh = prior + counts
    updated = (
        prior.astype(jnp.float32)[:, :, None]
        * centroids.reshape(BLOCKS_DEV, BLOCK, width).astype(jnp.float32)
        + sums
    ) / fresh.astype(jnp.float32)[:, :, None]
    new_centroids = updated.astype(jnp.bfloat16).reshape(BLOCKS_DEV * BLOCK, width)
    units_new = unit_rows(updated).reshape(BLOCKS_DEV * BLOCK, width)
    rows_two = units_new.shape[0]
    second_capacity = max(2, 3 * rows_two // (2 * BLOCKS2_DEV * devices))
    buckets_two = BLOCKS2_DEV * devices
    chosen = candidates[:, 0]
    place_two = chosen * second_capacity + slot_ranks(chosen, buckets_two)
    send_two = (
        jnp.zeros((buckets_two * second_capacity, width), jnp.bfloat16).at[place_two].set(units_new)
    )
    send_two = send_two.reshape(devices, BLOCKS2_DEV, second_capacity, width)
    units_two = unit_rows(centroids2).reshape(BLOCKS2_DEV, BLOCK2, width)
    arrived = lax.all_to_all(send_two, "shard", split_axis=0, concat_axis=0, tiled=True)
    items = arrived.shape[2]
    weights_two = [
        kernel_sums(arrived[:, local].reshape(-1, width), units_two[local]).reshape(
            arrived.shape[0], items
        )
        for local in range(BLOCKS2_DEV)
    ]
    returned_two = lax.all_to_all(
        jnp.stack(weights_two, axis=1), "shard", split_axis=0, concat_axis=0, tiled=True
    )
    level_two = jnp.log(returned_two.reshape(-1)[place_two] / BLOCK2)
    return (density, new_centroids, fresh.reshape(-1), level_two)


NT = (((1,), (1,)), ((), ()))
PARAMS = pltpu.CompilerParams(vmem_limit_bytes=48 * 1024 * 1024)
META = 16
SHARE = 1
LATE = 5
STEP = 12
HBM = pl.BlockSpec(memory_space=pltpu.HBM)
ANY = pl.BlockSpec(memory_space=pl.ANY)
VMEM = pl.BlockSpec(memory_space=pltpu.VMEM)


def position():
    me = lax.axis_index("shard")
    return me, me // 4, (me // 2) % 2, me % 2


def unit_wide(wide):
    power = jnp.mean(wide * wide, axis=-1, keepdims=True) + 1e-06
    return (wide * lax.rsqrt(power)).astype(jnp.bfloat16)


def weights(scores, width):
    return jnp.exp(scores * (10.0 / width) - 10.0)


def one_hot(hits):
    return jnp.where(hits, 1.0, 0.0).astype(jnp.bfloat16)


def column(row):
    return jnp.transpose(jnp.broadcast_to(row, (8, row.shape[1])))[:, 0:1]


def fetch(pairs, sems):
    copies = [pltpu.make_async_copy(src, dst, sems.at[i]) for i, (src, dst) in enumerate(pairs)]
    for copy in copies:
        copy.start()
    return copies


def pick_rows(slot, first, count):
    return one_hot(slot == lax.broadcasted_iota(jnp.int32, (count, slot.shape[1]), 0) + first)


def pack(slot, prior, cent, first, out):
    count = out.shape[0] - META
    rows = slot.shape[1]
    ident = lax.broadcasted_iota(jnp.int32, (1, rows), 1) + 1
    line = lax.broadcasted_iota(jnp.int32, (META, rows), 0)
    facts = jnp.where(line == 0, ident >> 5, jnp.where(line == 1, ident & 31, jnp.where(line == 2, prior, 0)))
    facts = facts.astype(jnp.float32).astype(jnp.bfloat16)
    pick = pick_rows(slot, first, count)
    out[0:count, :] = jnp.dot(pick, cent, preferred_element_type=jnp.float32).astype(jnp.bfloat16)
    out[count:, :] = jnp.zeros((META, out.shape[1]), jnp.bfloat16)
    out[count:, 0:count] = lax.dot_general(facts, pick, NT, preferred_element_type=jnp.float32).astype(jnp.bfloat16)


def pack_kernel(
    cap, per, cand_any, emb_any, probes_any, assigned_any, prior_any, cent_any, mine, rows2, rows3, info,
    cand_ref, emb_ref, probes_ref, assigned_ref, prior_ref, cent_ref, sems,
):
    copies = fetch(
        (
            (cand_any, cand_ref),
            (emb_any, emb_ref),
            (probes_any, probes_ref),
            (assigned_any, assigned_ref),
            (prior_any, prior_ref),
            (cent_any, cent_ref),
        ),
        sems,
    )
    me, z, y, core = position()
    rows = cand_ref.shape[1]
    buckets = 16 * per
    before = lax.broadcasted_iota(jnp.int32, (rows, rows), 0) <= lax.broadcasted_iota(jnp.int32, (rows, rows), 1)
    before = one_hot(before)
    copies[0].wait()
    cand = cand_ref[...]
    dev = sum((cand >= per * step).astype(jnp.int32) for step in range(1, 16))
    near = dev >> 2
    plane = jnp.where(z >= 2, 3 - near, near)
    rel = (((dev >> 1) & 1) ^ y) * 2 + ((dev & 1) ^ core)
    named = cand == lax.broadcasted_iota(jnp.int32, (buckets, rows), 0)
    counted = jnp.dot(one_hot(named), before, preferred_element_type=jnp.float32)
    rank = jnp.sum(jnp.where(named, counted, 0.0), axis=0, keepdims=True).astype(jnp.int32) - 1
    kind = plane * per + cand - dev * per
    slot = (rel * 4 * per + kind) * cap + rank
    info[0:1, :] = slot
    info[1:2, :] = rel * 4 + (kind >> 2)
    info[2:3, :] = (kind & 3) * cap + rank
    for copy in copies[1:5]:
        copy.wait()
    count, width = emb_ref.shape
    probe_count = probes_ref.shape[0]
    slots = assigned_ref[...]
    facts = jnp.concatenate([probes_ref[...], slots >> 5, slots & 31], axis=0).astype(jnp.float32)
    facts = jnp.concatenate([facts, jnp.zeros((128 - probe_count - 2, count), jnp.float32)], axis=0)
    same = lax.broadcasted_iota(jnp.int32, (count, count), 0) == lax.broadcasted_iota(jnp.int32, (count, count), 1)
    mine[:, 0:width] = emb_ref[...]
    mine[:, width:] = lax.dot_general(
        one_hot(same), facts.astype(jnp.bfloat16), NT, preferred_element_type=jnp.float32
    ).astype(jnp.bfloat16)
    copies[5].wait()
    pack(slot, prior_ref[...], cent_ref[...], 2 * 4 * per * cap, rows2)
    pack(slot, prior_ref[...], cent_ref[...], 3 * 4 * per * cap, rows3)


def pack_more_kernel(part, info, prior_ref, cent_ref, rows0, rows1, late2, late3):
    for first, out in ((0, rows0), (4 * part, rows1), (11 * part, late2), (15 * part, late3)):
        pack(info[0:1, :], prior_ref[...], cent_ref[...], first, out)


def order_kernel(*refs):
    pass


def prepare_kernel(cent_ref, own_any, near_any, unit_old, units, own, near, sems):
    copies = fetch(((own_any, own), (near_any, near)), sems)
    step = 256
    for start in range(0, cent_ref.shape[0], step):
        unit_old[start : start + step, :] = unit_wide(cent_ref[start : start + step, :].astype(jnp.float32))
    me, z, y, core = position()
    first = jnp.where((z == 0) | (z == 3), 0, 1)
    copies[0].wait()
    units[first] = unit_wide(own[...].astype(jnp.float32))
    copies[1].wait()
    units[1 - first] = unit_wide(near[...].astype(jnp.float32))


def share_kernel(mine_any, other_any, unit_old, scaled, facts, share_low, share_high, mine_ref, other_ref, sems):
    copies = fetch(((mine_any, mine_ref), (other_any, other_ref)), sems)
    me, z, y, core = position()
    half = mine_ref.shape[0]
    count = 2 * half
    rows, width = unit_old.shape
    copies[0].wait()
    scaled[0:half, :] = unit_wide(mine_ref[:, 0:width].astype(jnp.float32))
    copies[1].wait()
    scaled[half:count, :] = unit_wide(other_ref[:, 0:width].astype(jnp.float32))
    aux = jnp.concatenate([mine_ref[:, width:], other_ref[:, width:]], axis=0).astype(jnp.float32)
    aux = jnp.transpose(aux)[0:16, :].astype(jnp.int32)
    facts[...] = aux
    member = jnp.sum((aux[0:8, :] == me).astype(jnp.float32), axis=0, keepdims=True)
    step = 256
    total = jnp.zeros((1, count), jnp.float32)
    for start in range(0, rows, step):
        scores = lax.dot_general(
            unit_old[start : start + step, :], scaled[...], NT, preferred_element_type=jnp.float32
        )
        total = total + jnp.sum(weights(scores, width), axis=0, keepdims=True)
    piece = count // 16
    lane = lax.broadcasted_iota(jnp.int32, (16, count), 1)
    line = lax.broadcasted_iota(jnp.int32, (16, count), 0)
    apart = jnp.where((member > 0.0) & (lane >= line * piece) & (lane < (line + 1) * piece), total, 0.0)
    spot = lax.broadcasted_iota(jnp.int32, (count, 128), 0)
    block = sum((spot >= piece * step).astype(jnp.int32) for step in range(1, 16))
    together = jnp.where(spot - block * piece == lax.broadcasted_iota(jnp.int32, (count, 128), 1), 1.0, 0.0)
    share = jnp.dot(apart, together, precision=lax.Precision.HIGHEST, preferred_element_type=jnp.float32)
    share_low[...] = share[0:8, :]
    share_high[...] = share[8:16, :]


def update_kernel(after, scaled, facts, cent_ref, prior_ref, fresh_rows, fresh_counts):
    me, z, y, core = position()
    rows, width = cent_ref.shape
    count = scaled.shape[0]
    prior = column(prior_ref[...].astype(jnp.float32))
    target = jnp.where(facts[0:1, :] == me, facts[8:9, :] * 32 + facts[9:10, :], -1)
    step = 256
    for start in range(0, rows, step):
        old = cent_ref[start : start + step, :].astype(jnp.float32)
        hits = one_hot(target == lax.broadcasted_iota(jnp.int32, (step, count), 0) + start)
        sums = jnp.dot(hits, scaled[...], preferred_element_type=jnp.float32)
        gained = jnp.sum(hits.astype(jnp.float32), axis=1, keepdims=True)
        ahead = prior[start : start + step, :]
        updated = (ahead * old + sums) * (1.0 / (ahead + gained))
        fresh_rows[start : start + step, :] = updated.astype(jnp.bfloat16)
        gained_row = lax.dot_general(
            jnp.ones((8, count), jnp.bfloat16), hits, NT, preferred_element_type=jnp.float32
        )
        fresh_counts[0:1, start : start + step] = prior_ref[0:1, start : start + step] + gained_row[0:1, :].astype(jnp.int32)


def level_sums(two, packed, floors, w, per):
    block, width = two.shape[0] // per, two.shape[1]
    lines = []
    for j in range(per):
        rows = packed[w, j]
        floor = floors[w, j]
        scores = lax.dot_general(two[j * block : (j + 1) * block, :], rows, NT, preferred_element_type=jnp.float32)
        power = lax.dot_general(
            jnp.ones((8, width), jnp.bfloat16), rows * rows, NT, preferred_element_type=jnp.float32
        ) + lax.dot_general(
            jnp.ones((8, floor.shape[1]), jnp.bfloat16), floor * floor, NT, preferred_element_type=jnp.float32
        )
        power = jnp.where(power > 0.0, power, 1.0) * (1.0 / width)
        lines.append(jnp.sum(weights(scores * lax.rsqrt(power[0:1, :]), width), axis=0, keepdims=True))
    return jnp.concatenate(lines, axis=0)


def redo(cap, per, scaled, facts_in, me, refs, firsts, packed, floors):
    part = per * cap
    planes = packed.shape[0]
    count = planes * part
    width = scaled.shape[1]
    probe0 = facts_in[0:1, :]
    slots = facts_in[8:9, :] * 32 + facts_in[9:10, :]
    lane = lax.broadcasted_iota(jnp.int32, (count, 128), 1)
    for r, (ref, first) in enumerate(zip(refs, firsts)):
        facts = jnp.transpose(ref[ref.shape[0] - META :, first : first + count].astype(jnp.float32))
        hits = (facts[:, 0:1] * 32.0 + facts[:, 1:2]).astype(jnp.int32) == jnp.where(probe0 == (me ^ r), slots + 1, -1)
        gained = jnp.sum(jnp.where(hits, 1.0, 0.0), axis=1, keepdims=True)
        ahead = facts[:, 2:3]
        floor = (ahead + gained) * math.sqrt(1e-06 * width)
        floor = jnp.where(lane == 0, floor, 0.0).astype(jnp.bfloat16)
        added = jnp.dot(one_hot(hits), scaled[...], preferred_element_type=jnp.float32)
        whole = (ahead * ref[0:count, :].astype(jnp.float32) + added).astype(jnp.bfloat16)
        for w in range(planes):
            for j in range(per):
                start = w * part + j * cap
                packed[w, j, r * cap : (r + 1) * cap, :] = whole[start : start + cap, :]
                floors[w, j, r * cap : (r + 1) * cap, :] = floor[start : start + cap, :]


def early_kernel(
    cap, per, scaled, facts_in, units_any, cross_any, passed_any, any0, any1, any2, any3,
    sums, rows0, rows1, rows2, rows3, units, two_last, packed, floors, sems,
):
    me, z, y, core = position()
    end = (z == 0) | (z == 3)
    refs = (rows0, rows1, rows2, rows3)
    at_end = pltpu.make_async_copy(passed_any, two_last, sems.at[5])
    at_mid = pltpu.make_async_copy(cross_any, two_last, sems.at[5])
    copies = fetch(list(zip((any0, any1, any2, any3, units_any), (*refs, units))), sems)
    pl.when(end)(at_end.start)
    pl.when(jnp.logical_not(end))(at_mid.start)
    for copy in copies:
        copy.wait()
    pl.when(end)(at_end.wait)
    pl.when(jnp.logical_not(end))(at_mid.wait)
    redo(cap, per, scaled, facts_in, me, refs, (0, 0, 0, 0), packed, floors)
    third = unit_wide(two_last[...].astype(jnp.float32))
    for w, two in enumerate((units[0], units[1], third)):
        sums[8 * w : 8 * w + per, :] = level_sums(two, packed, floors, w, per)


def late_kernel(
    cap, per, scaled, facts_in, any0, any1, any2, any3, after, packed, floors, rows0, rows1, rows2, rows3, sems
):
    me, z, y, core = position()
    part = per * cap
    tail = pl.ds(3 * part, part + META)
    refs = (rows0, rows1, rows2, rows3)
    copies = fetch(list(zip((any0.at[tail], any1.at[tail], any2, any3), refs)), sems)
    for copy in copies:
        copy.wait()
    redo(cap, per, scaled, facts_in, me, refs, (3 * part, 3 * part, 0, 0), packed, floors)


def third_kernel(cap, per, early, floors, kept_any, last_any, far_any, inside, across, kept, two, sems):
    me, z, y, core = position()
    end = (z == 0) | (z == 3)
    at_end = pltpu.make_async_copy(far_any, two, sems.at[1])
    at_mid = pltpu.make_async_copy(last_any, two, sems.at[1])
    pl.when(end)(at_end.start)
    pl.when(jnp.logical_not(end))(at_mid.start)
    copies = fetch([(kept_any, kept)], sems)
    pl.when(end)(at_end.wait)
    pl.when(jnp.logical_not(end))(at_mid.wait)
    two_unit = unit_wide(two[...].astype(jnp.float32))
    copies[0].wait()
    final = level_sums(two_unit, kept, floors, 0, per)
    lines = [early[8 * w : 8 * w + per, :] for w in range(3)] + [final]
    together = jnp.concatenate(lines + [jnp.zeros((16 - 4 * per, 4 * cap), jnp.float32)], axis=0)
    lane = lax.broadcasted_iota(jnp.int32, together.shape, 1)
    line = lax.broadcasted_iota(jnp.int32, together.shape, 0)
    for r in range(4):
        out, start = (inside, across)[r // 2], 4 * (r % 2)
        spread = jnp.zeros_like(together)
        for s in range(4):
            turned = together if s == r else pltpu.roll(together, ((s - r) % 4) * cap, 1)
            spread = jnp.where((line % 4 == s) & (lane >= s * cap) & (lane < (s + 1) * cap), turned, spread)
        for t in range(4):
            out[start + t : start + t + 1, :] = jnp.sum(spread[4 * t : 4 * t + 4], axis=0, keepdims=True)


def last_kernel(cap, scale_one, scale_two, info, inside, across, beside, share, density, level_two):
    total = share[...]
    density[...] = jnp.log(total[:, 0 : density.shape[1]] / scale_one)
    values = jnp.concatenate([inside[0:4, :], beside[0:4, :], across[0:4, :], beside[4:8, :]], axis=0)
    rows = info.shape[1]
    chosen = jnp.where(info[2:3, :] == lax.broadcasted_iota(jnp.int32, (4 * cap, rows), 0), 1.0, 0.0)
    spread = jnp.dot(values, chosen, precision=lax.Precision.HIGHEST, preferred_element_type=jnp.float32)
    found = jnp.where(info[1:2, :] == lax.broadcasted_iota(jnp.int32, (16, rows), 0), spread, 0.0)
    level_two[...] = jnp.log(jnp.sum(found, axis=0, keepdims=True) / scale_two)


def call(kernel, outs, scratch=(), in_specs=None, **kw):
    def run(*args):
        specs = in_specs or [VMEM] * len(args)
        args = [pltpu.with_memory_space_constraint(a, pltpu.HBM) if spec is HBM else a for a, spec in zip(args, specs)]
        return pl.pallas_call(
            kernel, out_shape=outs, in_specs=specs, scratch_shapes=list(scratch), compiler_params=PARAMS, **kw
        )(*args)

    return run


def lasting(micros):
    return pl.CostEstimate(flops=0, transcendentals=0, bytes_accessed=int(micros * 3_690_000))


def in_order(*values, **kw):
    count = len(values)
    return call(
        order_kernel,
        tuple(jax.ShapeDtypeStruct(value.shape, value.dtype) for value in values),
        in_specs=[ANY] * count,
        out_specs=(ANY,) * count,
        input_output_aliases={i: i for i in range(count)},
        **kw,
    )(*values)


def line_body(embeddings, probes, assigned, prior_counts, centroids, candidates, centroids2):
    emb_rows, width = embeddings.shape
    probe_count = probes.shape[1]
    rows = centroids.shape[0]
    per = BLOCKS2_DEV
    cap = max(2, 3 * rows // (2 * per * 16))
    part = per * cap
    bf16, f32, i32 = jnp.bfloat16, jnp.float32, jnp.int32
    shape = jax.ShapeDtypeStruct

    def exchange(value, apart, sources=range(16)):
        return lax.ppermute(value, "shard", [(i, i ^ apart) for i in sources])

    def rows_of(planes):
        return shape((planes * part + META, width), bf16)

    def room(like):
        return pltpu.VMEM(like.shape, like.dtype)

    mids = range(4, 12)
    near_set = exchange(centroids2, 4)
    cross_set = exchange(centroids2, 12, mids)
    prior_row = prior_counts.reshape(1, rows)
    line = pltpu.VMEM((1, rows), i32)
    mine, early2, early3, info = call(
        functools.partial(pack_kernel, cap, per),
        (shape((emb_rows, width + 128), bf16), rows_of(3), rows_of(3), shape((8, rows), i32)),
        [
            line,
            pltpu.VMEM((emb_rows, width), bf16),
            pltpu.VMEM((probe_count, emb_rows), i32),
            pltpu.VMEM((1, emb_rows), i32),
            line,
            pltpu.VMEM((rows, width), bf16),
            pltpu.SemaphoreType.DMA((6,)),
        ],
        in_specs=[HBM] * 6,
    )(candidates.reshape(1, rows), embeddings, probes.T, assigned.reshape(1, emb_rows), prior_row, centroids)
    early2, early3 = exchange(early2, 2), exchange(early3, 3)
    rows0, rows1, late2, late3 = call(
        functools.partial(pack_more_kernel, part), (rows_of(4), rows_of(4), rows_of(1), rows_of(1))
    )(info, prior_row, centroids)
    mine = jnp.concatenate([mine, exchange(mine, 4)], axis=0)
    near_set, cross_set, mine, rows0 = in_order(near_set, cross_set, mine, rows0)
    across = exchange(mine, 12)
    passed = exchange(cross_set, 4, mids)
    last_set = exchange(near_set, 12, mids)
    mine = jnp.concatenate([mine, across], axis=0)
    mine, early2, early3, late2, late3, rows1 = in_order(mine, early2, early3, late2, late3, rows1)
    mine = jnp.concatenate([mine, exchange(mine, 2)], axis=0)
    late2, late3 = exchange(late2, 2), exchange(late3, 3)
    rows1 = exchange(rows1, 1)
    set_rows = per * BLOCK2
    block_set = pltpu.VMEM((set_rows, width), bf16)
    unit_old, units = call(
        prepare_kernel,
        (shape((rows, width), bf16), shape((2, set_rows, width), bf16)),
        [block_set, block_set, pltpu.SemaphoreType.DMA((2,))],
        in_specs=[VMEM, HBM, ANY],
    )(centroids, centroids2, near_set)
    passed, last_set, mine, unit_old, units = in_order(passed, last_set, mine, unit_old, units)
    far_set = exchange(last_set, 4, mids)
    other = exchange(mine, 1)
    gathered = pltpu.VMEM((8 * emb_rows, width + 128), bf16)
    scaled, facts, share, share_high = call(
        share_kernel,
        (
            shape((16 * emb_rows, width), bf16),
            shape((16, 16 * emb_rows), i32),
            shape((8, 4 * cap), f32),
            shape((8, 4 * cap), f32),
        ),
        [gathered, gathered, pltpu.SemaphoreType.DMA((2,))],
        in_specs=[ANY, ANY, VMEM],
    )(mine, other, unit_old)
    share = share + exchange(share_high, 1)
    share = share[0:4] + exchange(share[4:8], 2)
    early = call(
        functools.partial(early_kernel, cap, per),
        shape((24, 4 * cap), f32),
        [room(rows_of(4))] * 2
        + [room(rows_of(3))] * 2
        + [
            pltpu.VMEM((2, set_rows, width), bf16),
            block_set,
            pltpu.VMEM((3, per, 4 * cap, width), bf16),
            pltpu.VMEM((3, per, 4 * cap, 128), bf16),
            pltpu.SemaphoreType.DMA((6,)),
        ],
        in_specs=[VMEM, VMEM] + [ANY] * 7,
    )(scaled, facts, units, cross_set, passed, rows0, rows1, early2, early3)
    kept = shape((1, per, 4 * cap, width), bf16)
    kept_rows, floors = call(
        functools.partial(late_kernel, cap, per),
        (kept, shape((1, per, 4 * cap, 128), bf16)),
        [room(rows_of(1))] * 4 + [pltpu.SemaphoreType.DMA((4,))],
        in_specs=[VMEM] * 2 + [ANY] * 5,
    )(scaled, facts, rows0, rows1, late2, late3, early)
    share, kept_rows = in_order(share, kept_rows)
    share = share[0:2] + exchange(share[2:4], 12)
    share = share[0:1] + exchange(share[1:2], 4)
    tile = shape((8, 4 * cap), f32)
    inside, across = call(
        functools.partial(third_kernel, cap, per),
        (tile,) * 2,
        [room(kept), block_set, pltpu.SemaphoreType.DMA((2,))],
        in_specs=[VMEM, VMEM] + [ANY] * 3,
    )(early, floors, kept_rows, last_set, far_set)
    new_centroids, counts = call(
        update_kernel, (shape((rows, width), bf16), shape((1, rows), i32)), in_specs=[ANY] + [VMEM] * 4
    )(inside, scaled, facts, centroids, prior_row)
    across = exchange(across, 2)
    beside = jnp.concatenate([inside[4:8], across[4:8]], axis=0)
    beside = exchange(beside, 1)
    density, level_two = call(
        functools.partial(last_kernel, cap, probe_count * BLOCK, BLOCK2), (shape((1, emb_rows), f32), shape((1, rows), f32))
    )(info, inside, across, beside, share)
    return (density.reshape(-1), new_centroids, counts.reshape(-1), level_two.reshape(-1))


def solution(mesh):
    placed = (
        P(("groups", "shard"), None),
        P(("groups", "shard"), None),
        P(("groups", "shard")),
        P(("groups", "shard")),
        P(("groups", "shard"), None),
        P(("groups", "shard"), None),
        P(("groups", "shard"), None),
    )
    body = line_body if mesh.shape["shard"] == 16 else general_body
    return jax.shard_map(
        body,
        mesh=mesh,
        in_specs=placed,
        out_specs=(
            P(("groups", "shard")),
            P(("groups", "shard"), None),
            P(("groups", "shard")),
            P(("groups", "shard")),
        ),
        check_vma=False,
    )
```
